32 devices in a mesh: dp: 4 (over y, core), seq: 8 (over z, x).
Axes of the slice: x: 2, y: 2, z: 4, core: 2. Of those that a mesh axis runs over, the one named last changes fastest.
Arguments:
- tokens: bfloat16 [4096, 1600], P(('dp', 'seq')), may hold values from -6 to 6
- cotangent: bfloat16 [4096, 1600], P(('dp', 'seq')), may hold values from -6 to 6
- positions: int32 [4096], P(('dp', 'seq')), may hold values from 0 to 511, as said below
- qkv_weight: float32 [1600, 4800], P('dp', 'seq'), may hold values from -0.15625 to 0.15625
- qkv_first: float32 [1600, 4800], P('dp', 'seq'), may hold values from -56 to 56
- qkv_second: float32 [1600, 4800], P('dp', 'seq'), may hold values from 180.224 to 2908.16
- out_weight: float32 [1600, 1600], P('dp', 'seq'), may hold values from -1.5 to 1.5
- out_first: float32 [1600, 1600], P('dp', 'seq'), may hold values from -6 to 6
- out_second: float32 [1600, 1600], P('dp', 'seq'), may hold values from 1.04 to 16.8
- fc_weight: float32 [1600, 6400], P('dp', 'seq'), may hold values from -0.15625 to 0.15625
- fc_first: float32 [1600, 6400], P('dp', 'seq'), may hold values from -6 to 6
- fc_second: float32 [1600, 6400], P('dp', 'seq'), may hold values from 9.4208 to 155.648
- proj_weight: float32 [6400, 1600], P('seq', 'dp'), may hold values from -0.078125 to 0.078125
- proj_first: float32 [6400, 1600], P('seq', 'dp'), may hold values from -28 to 28
- proj_second: float32 [6400, 1600], P('seq', 'dp'), may hold values from 45.056 to 737.28
- small_weight: float32 [12, 1600], P(None, 'seq'), may hold values from -0.6 to 1.6, as said below
- small_first: float32 [12, 1600], P(None, 'seq'), may hold values from -40 to 40
- small_second: float32 [12, 1600], P(None, 'seq'), may hold values from 40.96 to 2048
Outputs:
- block_output: bfloat16 [4096, 1600], P(('dp', 'seq'))
- input_grad: bfloat16 [4096, 1600], P(('dp', 'seq'))
- qkv_moment: float32 [1600, 4800], P('dp', 'seq')
- qkv_square: float32 [1600, 4800], P('dp', 'seq')
- qkv_master: float32 [1600, 4800], P('dp', 'seq')
- out_moment: float32 [1600, 1600], P('dp', 'seq')
- out_square: float32 [1600, 1600], P('dp', 'seq')
- out_master: float32 [1600, 1600], P('dp', 'seq')
- fc_moment: float32 [1600, 6400], P('dp', 'seq')
- fc_square: float32 [1600, 6400], P('dp', 'seq')
- fc_master: float32 [1600, 6400], P('dp', 'seq')
- proj_moment: float32 [6400, 1600], P('seq', 'dp')
- proj_square: float32 [6400, 1600], P('seq', 'dp')
- proj_master: float32 [6400, 1600], P('seq', 'dp')
- small_moment: float32 [12, 1600], P(None, 'seq')
- small_square: float32 [12, 1600], P(None, 'seq')
- small_master: float32 [12, 1600], P(None, 'seq')
- proj_bias_grad: float32 [1600], P('seq')
The draws below stay inside these ranges and needn't reach their ends.
Inputs may be any that keep to these rules, and one draw needn't show every extreme that they name: Within each sequence the positions are a permutation of 0 to 511, laid over the sequence's rows in order as runs of 32 consecutive positions, each starting at a multiple of 32. `small_weight`: rows 8 and 10 lie around 1, the others around 0.
All inputs are finite; a program needn't handle non-finite values.
Results may differ from the reference program's by a relative error of at most 0.018.
Values may be sent and summed in bfloat16 or wider, within the bound.
No kernel may reach another device: no remote copies, remote signals or barrier semaphores. Data moves between devices by JAX's collectives and lax.ppermute only.
A program may use at most 320 MiB of HBM per device.

```python
import math
import jax
import jax.numpy as jnp
from jax import lax

D = 1600
HEADS = 25
HD = 64
FF = 6400
SEQ_DEV = 64
SEQS = 2
STEP = 10
SEQLEN = 512
TOKENS = 4096


def draw_positions(key, part):
    key = jax.random.fold_in(key, 11)
    stretch_count = SEQLEN // SEQ_DEV
    groups = TOKENS // (SEQS * SEQLEN)
    run_length = SEQ_DEV // 2
    run_count = SEQLEN // run_length
    group_keys = jax.random.split(key, groups * SEQS)

    def one_order(group_key):
        return jax.random.permutation(group_key, run_count).astype(jnp.int32)
    orders = jax.vmap(one_order)(group_keys)
    offsets = jnp.arange(run_length, dtype=jnp.int32)
    placed = orders[:, :, None] * run_length + offsets[None, None, :]
    laid = placed.reshape(groups, SEQS, stretch_count, SEQ_DEV).transpose(0, 2, 1, 3)
    return laid.reshape(TOKENS).astype(jnp.int32)


def draw_small_weight(key, part):
    key = jax.random.fold_in(key, 23)
    spread = jnp.clip(0.2 * jax.random.normal(key, (12, D), jnp.float32), -0.6, 0.6)
    row_index = jnp.arange(12)[:, None]
    gain_rows = (row_index == 8) | (row_index == 10)
    return jnp.where(gain_rows, 1.0 + spread, spread).astype(jnp.float32)


def block_scale(rng, extent, pieces, smallest, high):
    loudness = 1.0
    for position, blocks in pieces:
        draws = jax.random.uniform(jax.random.fold_in(jax.random.fold_in(rng, 6), position), (blocks,), jnp.float32, smallest / len(pieces), high / len(pieces))
        loudness = loudness * jnp.repeat(jnp.exp(draws), extent[position] // blocks).reshape((-1,) + (1,) * (len(extent) - 1 - position))
    return loudness


def bell_draw(rng, shape, scale, most, cuts=(), kind=jnp.bfloat16):
    factor_of = block_scale(rng, shape, cuts, -0.22, 0.18) if cuts else 1.0
    values = jax.random.normal(rng, shape, jnp.float32) * scale * factor_of
    return jnp.minimum(jnp.maximum(values, -most), most).astype(kind)


def setup_inputs(seed: int = 0) -> dict:
    splits = jax.random.split(jax.random.key(seed), 19)
    return {
        "tokens": bell_draw(splits[0], (TOKENS, D), 1.0, 6.0, ((0, 32),)),
        "cotangent": bell_draw(splits[1], (TOKENS, D), 1.0, 6.0, ((0, 32),)),
        "positions": draw_positions(jax.random.fold_in(splits[18], 71), 0),
        "qkv_weight": bell_draw(splits[3], (D, 3 * D), D ** -0.5, 0.15625, ((0, 4), (1, 8)), jnp.float32),
        "qkv_first": bell_draw(splits[4], (D, 3 * D), (0.144 * TOKENS ** 0.5), 56.0, ((0, 4), (1, 8)), jnp.float32),
        "qkv_second": jnp.clip(jnp.exp(math.log(2908.16) - 2.7810753 * jax.random.uniform(splits[5], (D, 3 * D), jnp.float32) ** block_scale(splits[5], (D, 3 * D), ((0, 4), (1, 8)), -0.2, 0.2)), 180.224, 2908.16),
        "out_weight": bell_draw(splits[6], (D, D), (max(1, 5 * D // SEQLEN)) ** -0.5, 1.5, ((0, 4), (1, 8)), jnp.float32),
        "out_first": bell_draw(splits[7], (D, D), (0.111 * (5 * TOKENS // SEQLEN) ** 0.5), 6.0, ((0, 4), (1, 8)), jnp.float32),
        "out_second": jnp.clip(jnp.exp(math.log(16.8) - 2.7821582 * jax.random.uniform(splits[8], (D, D), jnp.float32) ** block_scale(splits[8], (D, D), ((0, 4), (1, 8)), -0.2, 0.2)), 1.04, 16.8),
        "fc_weight": bell_draw(splits[9], (D, FF), D ** -0.5, 0.15625, ((0, 4), (1, 8)), jnp.float32),
        "fc_first": bell_draw(splits[10], (D, FF), (0.033 * TOKENS ** 0.5), 6.0, ((0, 4), (1, 8)), jnp.float32),
        "fc_second": jnp.clip(jnp.exp(math.log(155.648) - 2.804677 * jax.random.uniform(splits[11], (D, FF), jnp.float32) ** block_scale(splits[11], (D, FF), ((0, 4), (1, 8)), -0.2, 0.2)), 9.4208, 155.648),
        "proj_weight": bell_draw(splits[12], (FF, D), FF ** -0.5, 0.078125, ((0, 8), (1, 4)), jnp.float32),
        "proj_first": bell_draw(splits[13], (FF, D), (0.072 * TOKENS ** 0.5), 28.0, ((0, 8), (1, 4)), jnp.float32),
        "proj_second": jnp.clip(jnp.exp(math.log(737.28) - 2.7950616 * jax.random.uniform(splits[14], (FF, D), jnp.float32) ** block_scale(splits[14], (FF, D), ((0, 8), (1, 4)), -0.2, 0.2)), 45.056, 737.28),
        "small_weight": draw_small_weight(jax.random.fold_in(splits[18], 71), 0),
        "small_first": bell_draw(splits[16], (12, D), (0.111 * TOKENS ** 0.5), 40.0, ((1, 8),), jnp.float32),
        "small_second": jnp.clip(jnp.exp(math.log(2048.0) - 3.912023 * jax.random.uniform(splits[17], (12, D), jnp.float32) ** block_scale(splits[17], (12, D), ((1, 8),), -0.2, 0.2)), 40.96, 2048.0),
    }


@jax.custom_vjp
def low(v):
    return lax.optimization_barrier(v.astype(jnp.bfloat16)).astype(jnp.float32)

@jax.custom_vjp
def low_back(v):
    return v

def low_keep(v):
    return (low(v), None)

def low_pass(kept, grad):
    return (grad,)

def back_keep(v):
    return (v, None)

def back_low(kept, grad):
    return (low(grad),)
low.defvjp(low_keep, low_pass)
low_back.defvjp(back_keep, back_low)
NORM_EPS = 1e-05
SCORE_SCALE = 0.125
MASKED_SCORE = -1e+30
BETA_ONE = 0.9
BETA_TWO = 0.95
ADAM_EPS = 1e-08

def layer_norm(values, gain_row, shift_row):
    row_mean = lax.optimization_barrier(jnp.mean(values, axis=-1, keepdims=True))
    centred = values - row_mean
    spread = lax.optimization_barrier(jnp.mean(centred * centred, axis=-1, keepdims=True))
    return centred * lax.rsqrt(spread + NORM_EPS) * gain_row + shift_row

def gelu_tanh(values):
    inner = 0.7978845608028654 * (values + 0.044715 * values * values * values)
    return 0.5 * values * (1.0 + jnp.tanh(inner))

def head_attention(operands):
    query_rows, key_part, value_part, group_pos = operands
    raw_scores = low_back(jnp.dot(query_rows, key_part.T, precision=lax.Precision.HIGHEST) * SCORE_SCALE)
    allowed = group_pos[None, :] <= group_pos[:, None]
    scores = jnp.where(allowed, raw_scores, MASKED_SCORE)
    row_max = lax.optimization_barrier(jnp.max(scores, axis=1, keepdims=True))
    log_total = row_max + jnp.log(lax.optimization_barrier(jnp.sum(jnp.exp(scores - row_max), axis=1, keepdims=True)))
    soft_probs = low(jnp.exp(scores - log_total))
    return jnp.dot(soft_probs, value_part, precision=lax.Precision.HIGHEST)

def group_attention(operands):
    triple, group_pos = operands
    pos_heads = jnp.broadcast_to(group_pos, (HEADS, SEQLEN))
    return lax.map(jax.checkpoint(head_attention), (triple[0], triple[1], triple[2], pos_heads))

def attention(qkv_rows, positions):
    stretch_count = SEQLEN // SEQ_DEV
    groups = qkv_rows.shape[0] // (SEQS * SEQLEN)
    laid = qkv_rows.reshape(groups, stretch_count, SEQS, SEQ_DEV, 3, HEADS, HD)
    grouped = laid.transpose(0, 2, 4, 5, 1, 3, 6).reshape(groups * SEQS, 3, HEADS, SEQLEN, HD)
    pos_groups = positions.reshape(groups, stretch_count, SEQS, SEQ_DEV).transpose(0, 2, 1, 3).reshape(groups * SEQS, SEQLEN)
    head_outputs = lax.map(jax.checkpoint(group_attention), (grouped, pos_groups))
    spread_back = head_outputs.reshape(groups, SEQS, HEADS, stretch_count, SEQ_DEV, HD).transpose(0, 3, 1, 4, 2, 5)
    return spread_back.reshape(groups * SEQS * SEQLEN, HEADS * HD)

def forward(inputs, w_qkv, w_out, w_fc, w_proj, small_rows, positions):
    normed_one = low(layer_norm(inputs, small_rows[8], small_rows[9]))
    qkv_bias = jnp.concatenate([small_rows[0], jnp.zeros_like(small_rows[0]), small_rows[1]])
    qkv_rows = low_back(low(jnp.dot(normed_one, w_qkv, precision=lax.Precision.HIGHEST) + qkv_bias))
    context = low_back(low(attention(qkv_rows, positions)))
    attn_out = low_back(jnp.dot(context, w_out, precision=lax.Precision.HIGHEST) + small_rows[2])
    residual = inputs + attn_out
    normed_two = low(layer_norm(residual, small_rows[10], small_rows[11]))
    hidden_pre = low_back(jnp.dot(normed_two, w_fc, precision=lax.Precision.HIGHEST) + small_rows[3:7].reshape(-1))
    hidden = low(gelu_tanh(hidden_pre))
    return residual + jnp.dot(hidden, w_proj, precision=lax.Precision.HIGHEST) + small_rows[7]

def adam_update(weight, first_moment, second, gradient, step_rate, decay_rate):
    moment_new = BETA_ONE * first_moment + (1.0 - BETA_ONE) * gradient
    second_new = BETA_TWO * second + (1.0 - BETA_TWO) * gradient * gradient
    direction = moment_new / (1.0 - BETA_ONE ** STEP) / (jnp.sqrt(second_new / (1.0 - BETA_TWO ** STEP)) + ADAM_EPS)
    return (moment_new, second_new, weight - step_rate * (direction + decay_rate * weight))

def reference(tokens, cotangent, positions, qkv_weight, qkv_first, qkv_second, out_weight, out_first, out_second, fc_weight, fc_first, fc_second, proj_weight, proj_first, proj_second, small_weight, small_first, small_second):
    inputs = tokens.astype(jnp.float32)
    rounded = (low(qkv_weight), low(out_weight), low(fc_weight), low(proj_weight), low(small_weight))

    def whole(inputs_in, w_qkv, w_out, w_fc, w_proj, small_rows):
        return forward(inputs_in, w_qkv, w_out, w_fc, w_proj, small_rows, positions)
    output, backward = jax.vjp(whole, inputs, *rounded)
    grads = backward(cotangent.astype(jnp.float32))
    qkv_new = adam_update(qkv_weight, qkv_first, qkv_second, grads[1], 0.02, 0.1)
    out_new = adam_update(out_weight, out_first, out_second, grads[2], 0.3, 0.1)
    fc_new = adam_update(fc_weight, fc_first, fc_second, grads[3], 0.02, 0.1)
    proj_new = adam_update(proj_weight, proj_first, proj_second, grads[4], 0.02, 0.1)
    small_new = adam_update(small_weight, small_first, small_second, grads[5], 0.3, 0.0)
    return (output.astype(jnp.bfloat16), grads[0].astype(jnp.bfloat16), qkv_new[0], qkv_new[1], qkv_new[2], out_new[0], out_new[1], out_new[2], fc_new[0], fc_new[1], fc_new[2], proj_new[0], proj_new[1], proj_new[2], small_new[0], small_new[1], small_new[2], grads[5][7])
```

```python
import functools

import jax
import jax.numpy as jnp
import numpy as np
from jax import lax
from jax.experimental import pallas as pl
from jax.experimental.pallas import tpu as pltpu
from jax.sharding import PartitionSpec as P

HEADS = 25
HD = 64
SEQS = 2
STEP = 10

NORM_EPS = 1e-05
SCORE_SCALE = 0.125
MASKED_SCORE = -1e30
BETA_ONE = 0.9
BETA_TWO = 0.95
ADAM_EPS = 1e-08
BF16 = jnp.bfloat16
F32 = jnp.float32


def layer_norm(values, gain_row, shift_row):
    row_mean = jnp.mean(values, axis=-1, keepdims=True)
    centred = values - row_mean
    spread = jnp.mean(centred * centred, axis=-1, keepdims=True)
    return centred * lax.rsqrt(spread + NORM_EPS) * gain_row + shift_row


def gelu_tanh(values):
    inner = 0.7978845608028654 * (values + 0.044715 * values * values * values)
    return 0.5 * values * (1.0 + jnp.tanh(inner))


def adam_update(weight, first_moment, second, gradient, step_rate, decay_rate):
    moment_new = BETA_ONE * first_moment + (1.0 - BETA_ONE) * gradient
    second_new = BETA_TWO * second + (1.0 - BETA_TWO) * gradient * gradient
    direction = (
        moment_new
        / (1.0 - BETA_ONE**STEP)
        / (jnp.sqrt(second_new / (1.0 - BETA_TWO**STEP)) + ADAM_EPS)
    )
    return (moment_new, second_new, weight - step_rate * (direction + decay_rate * weight))


def dot(left, right):
    return jnp.dot(left, right, preferred_element_type=F32)


def dot_nt(left, right):
    return lax.dot_general(left, right, (((1,), (1,)), ((), ())), preferred_element_type=F32)


def dot_tn(left, right):
    return lax.dot_general(left, right, (((0,), (0,)), ((), ())), preferred_element_type=F32)


class Ring:
    def __init__(self, count):
        self.count = count
        self.sides = 2 if count % 2 == 0 else 1
        self.steps = count // self.sides
        sides, steps = self.sides, self.steps
        self.swap = [(j, j ^ 1) for j in range(count)]
        self.ahead = [
            (z * sides + x, ((z + 1) % steps) * sides + x)
            for z in range(steps)
            for x in range(sides)
        ]
        self.behind = [(dst, src) for src, dst in self.ahead]

    def owners(self):
        me = lax.axis_index("seq")
        place, side = me // self.sides, me % self.sides
        return [
            ((place + self.steps - t) % self.steps) * self.sides + (side + b) % self.sides
            for t in range(self.steps)
            for b in range(self.sides)
        ]

    def gather(self, block):
        pieces = []
        current = block
        for t in range(self.steps):
            pieces.append(current)
            if self.sides == 2:
                pieces.append(lax.ppermute(current, "seq", self.swap))
            if t + 1 < self.steps:
                current = lax.ppermute(current, "seq", self.ahead)
        return pieces

    def reorder(self, pieces):
        ordered = []
        for place, piece in enumerate(pieces):
            t, b = divmod(place, self.sides)
            blocks = piece.reshape((self.steps, self.sides, -1) + piece.shape[1:])
            blocks = jnp.roll(blocks, t, axis=0)
            if b:
                blocks = blocks[:, ::-1]
            ordered.append(blocks.reshape(piece.shape))
        return ordered

    def scatter_sum(self, partial_of):
        total = None
        for t in reversed(range(self.steps)):
            parts = partial_of(t)
            mine = parts[0]
            if self.sides == 2:
                mine = mine + lax.ppermute(parts[1].astype(BF16), "seq", self.swap).astype(F32)
            if total is not None:
                mine = mine + lax.ppermute(total.astype(BF16), "seq", self.behind).astype(F32)
            total = mine
        return total


def head_tables(count, model_width, window):
    slots = -(-HEADS // count)
    wide = slots * HD
    lists = [[[] for _ in range(count)] for _ in range(count)]
    for column in range(3 * model_width):
        src, local = divmod(column, window)
        part, within = divmod(column, model_width)
        head, lane = divmod(within, HD)
        dst, slot = head % count, head // count
        lists[src][dst].append((local, part * wide + slot * HD + lane))
    most = max(len(entry) for row in lists for entry in row)
    most = -(-most // 64) * 64
    pack = np.full((count, count * most), -1, np.int32)
    unpack = np.full((count, count * most), -1, np.int32)
    for src in range(count):
        for dst in range(count):
            for place, (local, target) in enumerate(lists[src][dst]):
                pack[src, dst * most + place] = local
                unpack[dst, src * most + place] = target
    return pack, unpack, most


def pick_row(table, index):
    return lax.dynamic_index_in_dim(jnp.asarray(table), index, 0, keepdims=False)


def one_hot(rows, size):
    return (lax.broadcasted_iota(jnp.int32, (size, rows.shape[0]), 0) == rows[None, :]).astype(BF16)


def forward_kernel(pos_col, pos_row, query_ref, full_ref, context_ref, probs_ref, *, wide):
    slots, _, run, width = query_ref.shape
    rows = slots * run
    keys_total = full_ref.shape[0] * run
    query = query_ref[:, 0].reshape(rows, width)[:, :wide]
    full = full_ref[:, 0].reshape(keys_total, width)
    key, value = full[:, wide : 2 * wide], full[:, 2 * wide :]
    seen = pos_row[0] <= pos_col[0]
    lane_head = lax.broadcasted_iota(jnp.int32, (1, wide), 1) // HD
    context = jnp.zeros((rows, wide), F32)
    for head in range(wide // HD):
        mine = lane_head == head
        scores = dot_nt(jnp.where(mine, query, jnp.zeros_like(query)), key) * SCORE_SCALE
        scores = jnp.where(seen, scores, MASKED_SCORE)
        top = jnp.max(scores, axis=1, keepdims=True)
        raw = jnp.exp(scores - top)
        probs = (raw * (1.0 / jnp.sum(raw, axis=1, keepdims=True))).astype(BF16)
        probs_ref[0, head] = probs
        context = jnp.where(mine, dot(probs, value), context)
    context_ref[:, 0] = context.astype(BF16).reshape(slots, run, wide)


def backward_kernel(query_ref, full_ref, grad_ref, probs_ref, out_ref, key_sum, value_sum, *, wide):
    step = pl.program_id(1)
    slots, _, run, width = query_ref.shape
    rows = slots * run
    count = full_ref.shape[0]
    keys_total = count * run
    query = query_ref[:, 0].reshape(rows, width)[:, :wide]
    full = full_ref[:, 0].reshape(keys_total, width)
    key, value = full[:, wide : 2 * wide], full[:, 2 * wide :]
    grad = grad_ref[:, 0].reshape(rows, wide)
    lane_head = lax.broadcasted_iota(jnp.int32, (1, wide), 1) // HD

    @pl.when(step == 0)
    def _():
        key_sum[...] = jnp.zeros_like(key_sum)
        value_sum[...] = jnp.zeros_like(value_sum)

    query_grad = jnp.zeros((rows, wide), F32)
    key_grad = jnp.zeros((keys_total, wide), F32)
    value_grad = jnp.zeros((keys_total, wide), F32)
    for head in range(wide // HD):
        mine = lane_head == head
        probs_low = probs_ref[0, head]
        probs = probs_low.astype(F32)
        grad_probs = dot_nt(jnp.where(mine, grad, jnp.zeros_like(grad)), value)
        weighted = probs * grad_probs
        delta = jnp.sum(weighted, axis=1, keepdims=True)
        grad_scores = (weighted - probs * delta).astype(BF16)
        query_grad = jnp.where(mine, dot(grad_scores, key), query_grad)
        key_grad = jnp.where(mine, dot_tn(grad_scores, query), key_grad)
        value_grad = jnp.where(mine, dot_tn(probs_low, grad), value_grad)
    key_sum[...] += key_grad
    value_sum[...] += value_grad
    out_ref[pl.ds(step * slots, slots), 0, :, :wide] = (
        (query_grad * SCORE_SCALE).astype(BF16).reshape(slots, run, wide)
    )

    @pl.when(step == pl.num_programs(1) - 1)
    def _():
        out_ref[:, 0, :, wide : 2 * wide] = (
            (key_sum[...] * SCORE_SCALE).astype(BF16).reshape(count, run, wide)
        )
        out_ref[:, 0, :, 2 * wide :] = value_sum[...].astype(BF16).reshape(count, run, wide)


def attention_forward(qkv_rows, positions):
    count, _, run, width = qkv_rows.shape
    wide = width // 3
    heads = wide // HD
    length = count * run
    block = min(length, 512)
    slots = block // run
    steps = length // block
    by_sequence = positions.reshape(count, SEQS, run).transpose(1, 0, 2).reshape(SEQS, length)
    return pl.pallas_call(
        functools.partial(forward_kernel, wide=wide),
        grid=(SEQS, steps),
        in_specs=[
            pl.BlockSpec((1, block, 1), lambda s, i: (s, i, 0)),
            pl.BlockSpec((1, 1, length), lambda s, i: (s, 0, 0)),
            pl.BlockSpec((slots, 1, run, width), lambda s, i: (i, s, 0, 0)),
            pl.BlockSpec((count, 1, run, width), lambda s, i: (0, s, 0, 0)),
        ],
        out_specs=[
            pl.BlockSpec((slots, 1, run, wide), lambda s, i: (i, s, 0, 0)),
            pl.BlockSpec((1, heads, block, length), lambda s, i: (s, 0, i, 0)),
        ],
        out_shape=[
            jax.ShapeDtypeStruct((count, SEQS, run, wide), BF16),
            jax.ShapeDtypeStruct((SEQS, heads, length, length), BF16),
        ],
        compiler_params=pltpu.CompilerParams(vmem_limit_bytes=48 * 1024 * 1024),
        cost_estimate=pl.CostEstimate(
            flops=4 * SEQS * heads * length * length * 256,
            bytes_accessed=8 * 1024 * 1024,
            transcendentals=SEQS * heads * length * length,
        ),
        name="attention_forward",
    )(by_sequence[:, :, None], by_sequence[:, None, :], qkv_rows, qkv_rows)


def attention_backward(qkv_rows, grad_context, probs):
    count, _, run, width = qkv_rows.shape
    wide = width // 3
    heads = wide // HD
    length = count * run
    block = min(length, 512)
    slots = block // run
    steps = length // block
    return pl.pallas_call(
        functools.partial(backward_kernel, wide=wide),
        grid=(SEQS, steps),
        in_specs=[
            pl.BlockSpec((slots, 1, run, width), lambda s, i: (i, s, 0, 0)),
            pl.BlockSpec((count, 1, run, width), lambda s, i: (0, s, 0, 0)),
            pl.BlockSpec((slots, 1, run, wide), lambda s, i: (i, s, 0, 0)),
            pl.BlockSpec((1, heads, block, length), lambda s, i: (s, 0, i, 0)),
        ],
        out_specs=pl.BlockSpec((count, 1, run, width), lambda s, i: (0, s, 0, 0)),
        out_shape=jax.ShapeDtypeStruct((count, SEQS, run, width), BF16),
        scratch_shapes=[pltpu.VMEM((length, wide), F32), pltpu.VMEM((length, wide), F32)],
        compiler_params=pltpu.CompilerParams(vmem_limit_bytes=48 * 1024 * 1024),
        cost_estimate=pl.CostEstimate(
            flops=8 * SEQS * heads * length * length * 256,
            bytes_accessed=8 * 1024 * 1024,
            transcendentals=0,
        ),
        name="attention_backward",
    )(qkv_rows, qkv_rows, grad_context, probs)


def shards(
    tokens,
    cotangent,
    positions,
    qkv_weight,
    qkv_first,
    qkv_second,
    out_weight,
    out_first,
    out_second,
    fc_weight,
    fc_first,
    fc_second,
    proj_weight,
    proj_first,
    proj_second,
    small_weight,
    small_first,
    small_second,
):
    count = lax.axis_size("seq")
    ring = Ring(count)
    me = lax.axis_index("seq")
    owners = ring.owners()
    owner_index = jnp.stack(owners)
    rows, width = tokens.shape
    seq_rows = rows // SEQS
    window = qkv_weight.shape[1]
    depth = qkv_weight.shape[0]
    slots = -(-HEADS // count)
    wide = slots * HD
    small_count, small_width = small_weight.shape
    hidden = fc_weight.shape[1]
    all_rows = count * rows
    pair = ring.sides * rows

    extra = -(-rows // small_width) * small_width
    pos_parts = jnp.stack([positions // 32, positions % 32]).astype(BF16)
    pos_parts = jnp.pad(pos_parts, ((0, 0), (0, extra - rows))).reshape(-1, small_width)
    small_pack = jnp.concatenate([small_weight.astype(BF16), pos_parts], axis=0)
    small_all = lax.all_to_all(
        jnp.broadcast_to(small_pack[None], (count,) + small_pack.shape), "seq", 0, 0
    ).astype(F32)
    small_rows = small_all[:, :small_count].transpose(1, 0, 2).reshape(small_count, width)
    pos_all = small_all[:, small_count:].reshape(count, 2, extra)[:, :, :rows]
    pos_all = (pos_all[:, 0] * 32.0 + pos_all[:, 1]).astype(jnp.int32)
    pos_rel = jnp.take(pos_all, owner_index, axis=0)

    pack, unpack, most = head_tables(count, width, window)
    pack_hot = one_hot(pick_row(pack, me), window)
    unpack_hot = one_hot(pick_row(unpack, me), 3 * wide)
    packed = jnp.einsum(
        "rc,cdl->drl",
        qkv_weight.astype(BF16),
        pack_hot.reshape(window, count, most),
        preferred_element_type=BF16,
    )
    received = lax.all_to_all(packed, "seq", 0, 0)
    head_part = jnp.einsum(
        "srl,ksl->rk",
        received,
        unpack_hot.reshape(3 * wide, count, most),
        preferred_element_type=BF16,
    )
    w_head = lax.all_gather(head_part, "dp", axis=0, tiled=True)
    out_part = lax.all_gather(out_weight.astype(BF16), "seq", axis=1, tiled=True)
    w_out = lax.all_gather(out_part, "dp", axis=0, tiled=True)
    w_fc = lax.all_gather(fc_weight.astype(BF16), "dp", axis=0, tiled=True)
    w_proj = lax.all_gather(proj_weight.astype(BF16), "dp", axis=1, tiled=True)

    token_pieces = ring.gather(tokens)

    def own_heads(row):
        padded = jnp.pad(row, (0, slots * count * HD - width)).reshape(slots, count, HD)
        return lax.dynamic_index_in_dim(padded, me, 1, keepdims=False).reshape(wide)

    head_bias = jnp.concatenate(
        [own_heads(small_rows[0]), jnp.zeros((wide,), F32), own_heads(small_rows[1])]
    )
    fc_bias = lax.dynamic_slice_in_dim(small_rows[3:7].reshape(-1), me * hidden, hidden, 0)

    normed_parts, qkv_parts = [], []
    for t in range(ring.steps):
        part = jnp.concatenate(token_pieces[t * ring.sides : (t + 1) * ring.sides], axis=0)
        normed = layer_norm(part.astype(F32), small_rows[8], small_rows[9]).astype(BF16)
        normed_parts.append(normed)
        qkv_parts.append((dot(normed, w_head) + head_bias).astype(BF16))
    tokens_all = jnp.concatenate(token_pieces, axis=0)
    normed_all = jnp.concatenate(normed_parts, axis=0)
    qkv_all = jnp.concatenate(qkv_parts, axis=0).reshape(count, SEQS, seq_rows, 3 * wide)

    context, probs = attention_forward(qkv_all, pos_rel)
    context = context.reshape(all_rows, wide)

    context_all = jnp.concatenate(ring.reorder(ring.gather(context)), axis=1)
    w_out_heads = jnp.pad(w_out, ((0, slots * count * HD - width), (0, 0)))
    w_out_heads = (
        w_out_heads.reshape(slots, count, HD, width)
        .transpose(1, 0, 2, 3)
        .reshape(count, wide, width)
    )
    w_out_rel = jnp.take(w_out_heads, owner_index, axis=0).reshape(count * wide, width)
    residual_all = tokens_all.astype(F32) + dot(context_all, w_out_rel) + small_rows[2]
    normed_two_all = layer_norm(residual_all, small_rows[10], small_rows[11]).astype(BF16)
    hidden_pre = dot(normed_two_all, w_fc) + fc_bias
    hidden_act, hidden_back = jax.vjp(gelu_tanh, hidden_pre)
    hidden_low = hidden_act.astype(BF16)

    cot_all = jnp.concatenate(ring.gather(cotangent), axis=0)
    grad_hidden = dot_nt(cot_all, w_proj)
    grad_pre_low = hidden_back(grad_hidden)[0].astype(BF16)

    def chunk(values, t):
        return values[t * pair : (t + 1) * pair]

    def sides_of(values):
        return [values[b * rows : (b + 1) * rows] for b in range(ring.sides)]

    grad_normed_two = ring.scatter_sum(lambda t: sides_of(dot_nt(chunk(grad_pre_low, t), w_fc)))
    residual = residual_all[:rows]
    norm_back_two = jax.vjp(layer_norm, residual, small_rows[10], small_rows[11])[1]
    grad_res_norm, grad_gain_two, grad_shift_two = norm_back_two(grad_normed_two)
    grad_residual = cotangent.astype(F32) + grad_res_norm
    grad_attn_low = grad_residual.astype(BF16)

    grad_context = dot_nt(grad_attn_low, w_out_heads.reshape(count * wide, width)).astype(BF16)
    grad_context = lax.all_to_all(
        grad_context.reshape(rows, count, wide).transpose(1, 0, 2), "seq", 0, 0
    )
    grad_context = jnp.take(grad_context, owner_index, axis=0)
    grad_qkv = attention_backward(
        qkv_all, grad_context.reshape(count, SEQS, seq_rows, wide), probs
    ).reshape(all_rows, 3 * wide)

    grad_normed_one = ring.scatter_sum(lambda t: sides_of(dot_nt(chunk(grad_qkv, t), w_head)))
    norm_back_one = jax.vjp(layer_norm, tokens.astype(F32), small_rows[8], small_rows[9])[1]
    grad_input_norm, grad_gain_one, grad_shift_one = norm_back_one(grad_normed_one)
    input_grad = (grad_residual + grad_input_norm).astype(BF16)

    output = (
        residual
        + ring.scatter_sum(lambda t: sides_of(dot(chunk(hidden_low, t), w_proj)))
        + small_rows[7]
    ).astype(BF16)

    fc_grad = lax.psum_scatter(
        dot_tn(normed_two_all, grad_pre_low).astype(BF16), "dp", scatter_dimension=0, tiled=True
    ).astype(F32)
    proj_grad = lax.psum_scatter(
        dot_tn(hidden_low, cot_all).astype(BF16), "dp", scatter_dimension=1, tiled=True
    ).astype(F32)
    out_columns = out_weight.shape[1]
    attn_columns = lax.all_to_all(
        grad_attn_low.reshape(rows, count, out_columns).transpose(1, 0, 2), "seq", 0, 0
    )
    attn_columns = jnp.take(attn_columns, owner_index, axis=0).reshape(all_rows, out_columns)
    out_rel = dot_tn(context_all, attn_columns).astype(BF16).reshape(count, wide, out_columns)
    slot_of = jnp.zeros((count,), jnp.int32).at[owner_index].set(jnp.arange(count, dtype=jnp.int32))
    out_abs = jnp.take(out_rel, slot_of, axis=0).reshape(count, slots, HD, out_columns)
    out_sum = out_abs.transpose(1, 0, 2, 3).reshape(slots * count * HD, out_columns)[:width]
    out_grad = lax.psum_scatter(out_sum, "dp", scatter_dimension=0, tiled=True).astype(F32)
    head_grad = lax.psum_scatter(
        dot_tn(normed_all, grad_qkv).astype(BF16), "dp", scatter_dimension=0, tiled=True
    )
    head_packed = jnp.einsum(
        "rk,ksl->srl",
        head_grad,
        unpack_hot.reshape(3 * wide, count, most),
        preferred_element_type=BF16,
    )
    head_back = lax.all_to_all(head_packed, "seq", 0, 0)
    qkv_grad = jnp.einsum(
        "drl,cdl->rc",
        head_back,
        pack_hot.reshape(window, count, most),
        preferred_element_type=F32,
    )

    def place_heads(values):
        spread = (jnp.arange(count) == me).astype(F32)[None, :, None]
        placed = values.reshape(slots, 1, HD) * spread
        return placed.reshape(-1)[:width]

    grad_qkv_sum = jnp.sum(grad_qkv.astype(F32), axis=0)
    grad_bias_fc = jnp.sum(grad_pre_low.astype(F32), axis=0)
    grad_bias_fc = grad_bias_fc[None, :] * (jnp.arange(count) == me).astype(F32)[:, None]
    grad_small = jnp.concatenate(
        [
            place_heads(grad_qkv_sum[:wide])[None],
            place_heads(grad_qkv_sum[2 * wide :])[None],
            jnp.sum(grad_attn_low.astype(F32), axis=0)[None],
            grad_bias_fc.reshape(-1, width),
            jnp.sum(cotangent.astype(F32), axis=0)[None],
            grad_gain_one[None],
            grad_shift_one[None],
            grad_gain_two[None],
            grad_shift_two[None],
        ],
        axis=0,
    )
    small_sent = grad_small.astype(BF16).reshape(small_count, count, small_width)
    small_part = jnp.sum(
        lax.all_to_all(small_sent.transpose(1, 0, 2), "seq", 0, 0).astype(F32), axis=0
    )
    small_grad = lax.psum(small_part, "dp")

    qkv_new = adam_update(qkv_weight, qkv_first, qkv_second, qkv_grad, 0.02, 0.1)
    out_new = adam_update(out_weight, out_first, out_second, out_grad, 0.3, 0.1)
    fc_new = adam_update(fc_weight, fc_first, fc_second, fc_grad, 0.02, 0.1)
    proj_new = adam_update(proj_weight, proj_first, proj_second, proj_grad, 0.02, 0.1)
    small_new = adam_update(small_weight, small_first, small_second, small_grad, 0.3, 0.0)
    return (
        output,
        input_grad,
        *qkv_new,
        *out_new,
        *fc_new,
        *proj_new,
        *small_new,
        small_grad[7],
    )


def solution(mesh):
    rows = P(("dp", "seq"), None)
    matrix = P("dp", "seq")
    turned = P("seq", "dp")
    small = P(None, "seq")
    in_specs = (
        (rows, rows, P(("dp", "seq"))) + (matrix,) * 9 + (turned,) * 3 + (small,) * 3
    )
    out_specs = (rows, rows) + (matrix,) * 9 + (turned,) * 3 + (small,) * 3 + (P("seq"),)
    return jax.shard_map(shards, mesh=mesh, in_specs=in_specs, out_specs=out_specs, check_vma=False)
```

```python
import functools

import jax
import jax.numpy as jnp
import numpy as np
from jax import lax
from jax.experimental import pallas as pl
from jax.experimental.pallas import tpu as pltpu
from jax.sharding import PartitionSpec as P

HEADS = 25
HD = 64
SEQS = 2
STEP = 10

NORM_EPS = 1e-05
SCORE_SCALE = 0.125
MASKED_SCORE = -1e30
BETA_ONE = 0.9
BETA_TWO = 0.95
ADAM_EPS = 1e-08
BF16 = jnp.bfloat16
F32 = jnp.float32


def layer_norm(values, gain_row, shift_row):
    row_mean = jnp.mean(values, axis=-1, keepdims=True)
    centred = values - row_mean
    spread = jnp.mean(centred * centred, axis=-1, keepdims=True)
    return centred * lax.rsqrt(spread + NORM_EPS) * gain_row + shift_row


def gelu_tanh(values):
    inner = 0.7978845608028654 * (values + 0.044715 * values * values * values)
    return 0.5 * values * (1.0 + jnp.tanh(inner))


def adam_update(weight, first_moment, second, gradient, step_rate, decay_rate):
    moment_new = BETA_ONE * first_moment + (1.0 - BETA_ONE) * gradient
    second_new = BETA_TWO * second + (1.0 - BETA_TWO) * gradient * gradient
    direction = (
        moment_new
        / (1.0 - BETA_ONE**STEP)
        / (jnp.sqrt(second_new / (1.0 - BETA_TWO**STEP)) + ADAM_EPS)
    )
    return (moment_new, second_new, weight - step_rate * (direction + decay_rate * weight))


def dot(left, right):
    return jnp.dot(left, right, preferred_element_type=F32)


def dot_nt(left, right):
    return lax.dot_general(left, right, (((1,), (1,)), ((), ())), preferred_element_type=F32)


def dot_tn(left, right):
    return lax.dot_general(left, right, (((0,), (0,)), ((), ())), preferred_element_type=F32)


def after(value, *others):
    return lax.optimization_barrier((value,) + others)[0]


class Ring:
    def __init__(self, count):
        self.sides = 2
        self.steps = count // self.sides
        sides, steps = self.sides, self.steps
        self.swap = [(j, j ^ 1) for j in range(count)]
        self.ahead = [
            (z * sides + x, ((z + 1) % steps) * sides + x)
            for z in range(steps)
            for x in range(sides)
        ]
        self.behind = [(dst, src) for src, dst in self.ahead]
        me = lax.axis_index("seq")
        self.place, self.side = me // sides, me % sides

    def position(self, t):
        return (self.place + self.steps - t) % self.steps

    def pair(self, own, other, axis):
        first = jnp.concatenate([own, other], axis=axis)
        second = jnp.concatenate([other, own], axis=axis)
        return jnp.where(self.side == 0, first, second)

    def gather(self, block, axis=0):
        tour = Tour(self, block, axis)
        for _ in range(self.steps):
            tour.step()
        return tour

    def halves(self, block):
        rows = block.shape[0] // self.sides
        own = lax.dynamic_slice_in_dim(block, self.side * rows, rows, 0)
        other = lax.dynamic_slice_in_dim(block, (1 - self.side) * rows, rows, 0)
        return own, other.astype(BF16)

    def scatter_sum(self, partials):
        fold = Fold(self, partials)
        for _ in range(self.steps):
            fold.step()
        return fold.total, fold.swapped[0]


class Fold:
    def __init__(self, ring, partials):
        self.ring, self.partials = ring, partials
        self.total, self.swapped = None, []

    def step(self, *begin):
        ring = self.ring
        mine, other = ring.halves(self.partials[ring.steps - 1 - len(self.swapped)])
        carried = self.total
        if begin:
            other = after(other, *begin)
        if len(self.swapped) > 1:
            other = after(other, self.swapped[-2])
        other = lax.ppermute(other, "seq", ring.swap)
        if carried is not None:
            carried = carried.astype(BF16)
            carried = after(carried, *begin) if begin else carried
            mine = mine + lax.ppermute(carried, "seq", ring.behind).astype(F32)
        self.swapped.append(other)
        self.total = mine + other.astype(F32)
        return self.total


class Tour:
    def __init__(self, ring, block, axis=0, back=False):
        self.ring, self.current, self.axis, self.back = ring, block, axis, back
        self.pairs = [None] * ring.steps
        self.moved = []

    def step(self, *begin):
        ring, t = self.ring, len(self.moved)
        if begin:
            self.current = after(self.current, *begin)
        if t:
            sent = after(self.current, self.moved[-2]) if t > 1 else self.current
            self.current = lax.ppermute(sent, "seq", ring.behind if self.back else ring.ahead)
        other = lax.ppermute(self.current, "seq", ring.swap)
        self.pairs[-t if self.back else t] = ring.pair(self.current, other, self.axis)
        self.moved.append(other)


class Square:
    def __init__(self):
        me = lax.axis_index("dp")
        self.far, self.near = me // 2, me % 2
        self.far_swap = [(j, j ^ 2) for j in range(4)]
        self.near_swap = [(j, j ^ 1) for j in range(4)]

    def gather(self, block):
        far = lax.ppermute(block, "dp", self.far_swap)
        column = jnp.where(self.far == 0, jnp.stack([block, far]), jnp.stack([far, block]))
        near = lax.ppermute(column, "dp", self.near_swap)
        whole = jnp.where(
            self.near == 0, jnp.stack([column, near], axis=1), jnp.stack([near, column], axis=1)
        )
        return whole.reshape((4 * block.shape[0],) + block.shape[1:]), far

    def scatter_sum(self, partial):
        parts = partial.reshape((2, 2, partial.shape[0] // 4) + partial.shape[1:])
        mine = lax.dynamic_index_in_dim(parts, self.near, 1, keepdims=False)
        other = lax.dynamic_index_in_dim(parts, 1 - self.near, 1, keepdims=False)
        column = mine.astype(F32) + lax.ppermute(
            other.astype(BF16), "dp", self.near_swap
        ).astype(F32)
        return self.finish_sum(column), column

    def finish_sum(self, column):
        mine = lax.dynamic_index_in_dim(column, self.far, 0, keepdims=False)
        other = lax.dynamic_index_in_dim(column, 1 - self.far, 0, keepdims=False)
        return mine + lax.ppermute(other.astype(BF16), "dp", self.far_swap).astype(F32)

    def sum(self, values):
        values = values + lax.ppermute(values, "dp", self.near_swap)
        return values + lax.ppermute(values, "dp", self.far_swap)


def head_tables(count, model_width, window):
    slots = -(-HEADS // count)
    wide = slots * HD
    lists = [[[] for _ in range(count)] for _ in range(count)]
    for column in range(3 * model_width):
        src, local = divmod(column, window)
        part, within = divmod(column, model_width)
        head, lane = divmod(within, HD)
        dst, slot = head % count, head // count
        lists[src][dst].append((local, part * wide + slot * HD + lane))
    most = max(len(entry) for row in lists for entry in row)
    most = -(-most // 64) * 64
    pack = np.full((count, count * most), -1, np.int32)
    unpack = np.full((count, count * most), -1, np.int32)
    for src in range(count):
        for dst in range(count):
            for place, (local, target) in enumerate(lists[src][dst]):
                pack[src, dst * most + place] = local
                unpack[dst, src * most + place] = target
    return pack, unpack, most


def pick_row(table, index):
    return lax.dynamic_index_in_dim(jnp.asarray(table), index, 0, keepdims=False)


def one_hot(rows, size):
    return (lax.broadcasted_iota(jnp.int32, (size, rows.shape[0]), 0) == rows[None, :]).astype(BF16)


def forward_kernel(pos_col, pos_row, query_ref, full_ref, context_ref, probs_ref, *, wide):
    slots, _, run, width = query_ref.shape
    rows = slots * run
    keys_total = full_ref.shape[0] * run
    query = query_ref[:, 0].reshape(rows, width)[:, :wide]
    full = full_ref[:, 0].reshape(keys_total, width)
    key, value = full[:, wide : 2 * wide], full[:, 2 * wide :]
    seen = pos_row[0] <= pos_col[0]
    lane_head = lax.broadcasted_iota(jnp.int32, (1, wide), 1) // HD
    context = jnp.zeros((rows, wide), F32)
    for head in range(wide // HD):
        mine = lane_head == head
        scores = dot_nt(jnp.where(mine, query, jnp.zeros_like(query)), key) * SCORE_SCALE
        scores = jnp.where(seen, scores, MASKED_SCORE)
        top = jnp.max(scores, axis=1, keepdims=True)
        raw = jnp.exp(scores - top)
        probs = (raw * (1.0 / jnp.sum(raw, axis=1, keepdims=True))).astype(BF16)
        probs_ref[0, head] = probs
        context = jnp.where(mine, dot(probs, value), context)
    context_ref[:, 0] = context.astype(BF16).reshape(slots, run, wide)


def backward_kernel(query_ref, full_ref, grad_ref, probs_ref, out_ref, key_sum, value_sum, *, wide):
    step = pl.program_id(1)
    slots, _, run, width = query_ref.shape
    rows = slots * run
    count = full_ref.shape[0]
    keys_total = count * run
    query = query_ref[:, 0].reshape(rows, width)[:, :wide]
    full = full_ref[:, 0].reshape(keys_total, width)
    key, value = full[:, wide : 2 * wide], full[:, 2 * wide :]
    grad = grad_ref[:, 0].reshape(rows, wide)
    lane_head = lax.broadcasted_iota(jnp.int32, (1, wide), 1) // HD

    @pl.when(step == 0)
    def _():
        key_sum[...] = jnp.zeros_like(key_sum)
        value_sum[...] = jnp.zeros_like(value_sum)

    query_grad = jnp.zeros((rows, wide), F32)
    key_grad = jnp.zeros((keys_total, wide), F32)
    value_grad = jnp.zeros((keys_total, wide), F32)
    for head in range(wide // HD):
        mine = lane_head == head
        probs_low = probs_ref[0, head]
        probs = probs_low.astype(F32)
        grad_probs = dot_nt(jnp.where(mine, grad, jnp.zeros_like(grad)), value)
        weighted = probs * grad_probs
        delta = jnp.sum(weighted, axis=1, keepdims=True)
        grad_scores = (weighted - probs * delta).astype(BF16)
        query_grad = jnp.where(mine, dot(grad_scores, key), query_grad)
        key_grad = jnp.where(mine, dot_tn(grad_scores, query), key_grad)
        value_grad = jnp.where(mine, dot_tn(probs_low, grad), value_grad)
    key_sum[...] += key_grad
    value_sum[...] += value_grad
    out_ref[pl.ds(step * slots, slots), 0, :, :wide] = (
        (query_grad * SCORE_SCALE).astype(BF16).reshape(slots, run, wide)
    )

    @pl.when(step == pl.num_programs(1) - 1)
    def _():
        out_ref[:, 0, :, wide : 2 * wide] = (
            (key_sum[...] * SCORE_SCALE).astype(BF16).reshape(count, run, wide)
        )
        out_ref[:, 0, :, 2 * wide :] = value_sum[...].astype(BF16).reshape(count, run, wide)


def attention_forward(qkv_rows, positions):
    count, _, run, width = qkv_rows.shape
    wide = width // 3
    heads = wide // HD
    length = count * run
    block = min(length, 512)
    slots = block // run
    steps = length // block
    by_sequence = positions.reshape(count, SEQS, run).transpose(1, 0, 2).reshape(SEQS, length)
    return pl.pallas_call(
        functools.partial(forward_kernel, wide=wide),
        grid=(SEQS, steps),
        in_specs=[
            pl.BlockSpec((1, block, 1), lambda s, i: (s, i, 0)),
            pl.BlockSpec((1, 1, length), lambda s, i: (s, 0, 0)),
            pl.BlockSpec((slots, 1, run, width), lambda s, i: (i, s, 0, 0)),
            pl.BlockSpec((count, 1, run, width), lambda s, i: (0, s, 0, 0)),
        ],
        out_specs=[
            pl.BlockSpec((slots, 1, run, wide), lambda s, i: (i, s, 0, 0)),
            pl.BlockSpec((1, heads, block, length), lambda s, i: (s, 0, i, 0)),
        ],
        out_shape=[
            jax.ShapeDtypeStruct((count, SEQS, run, wide), BF16),
            jax.ShapeDtypeStruct((SEQS, heads, length, length), BF16),
        ],
        compiler_params=pltpu.CompilerParams(vmem_limit_bytes=48 * 1024 * 1024),
        cost_estimate=pl.CostEstimate(
            flops=4 * SEQS * heads * length * length * 256,
            bytes_accessed=8 * 1024 * 1024,
            transcendentals=SEQS * heads * length * length,
        ),
        name="attention_forward",
    )(by_sequence[:, :, None], by_sequence[:, None, :], qkv_rows, qkv_rows)


def attention_backward(qkv_rows, grad_context, probs):
    count, _, run, width = qkv_rows.shape
    wide = width // 3
    heads = wide // HD
    length = count * run
    block = min(length, 512)
    slots = block // run
    steps = length // block
    return pl.pallas_call(
        functools.partial(backward_kernel, wide=wide),
        grid=(SEQS, steps),
        in_specs=[
            pl.BlockSpec((slots, 1, run, width), lambda s, i: (i, s, 0, 0)),
            pl.BlockSpec((count, 1, run, width), lambda s, i: (0, s, 0, 0)),
            pl.BlockSpec((slots, 1, run, wide), lambda s, i: (i, s, 0, 0)),
            pl.BlockSpec((1, heads, block, length), lambda s, i: (s, 0, i, 0)),
        ],
        out_specs=pl.BlockSpec((count, 1, run, width), lambda s, i: (0, s, 0, 0)),
        out_shape=jax.ShapeDtypeStruct((count, SEQS, run, width), BF16),
        scratch_shapes=[pltpu.VMEM((length, wide), F32), pltpu.VMEM((length, wide), F32)],
        compiler_params=pltpu.CompilerParams(vmem_limit_bytes=48 * 1024 * 1024),
        cost_estimate=pl.CostEstimate(
            flops=8 * SEQS * heads * length * length * 256,
            bytes_accessed=8 * 1024 * 1024,
            transcendentals=0,
        ),
        name="attention_backward",
    )(qkv_rows, qkv_rows, grad_context, probs)


def shards(
    tokens,
    cotangent,
    positions,
    qkv_weight,
    qkv_first,
    qkv_second,
    out_weight,
    out_first,
    out_second,
    fc_weight,
    fc_first,
    fc_second,
    proj_weight,
    proj_first,
    proj_second,
    small_weight,
    small_first,
    small_second,
):
    count = lax.axis_size("seq")
    ring = Ring(count)
    square = Square()
    me = lax.axis_index("seq")
    rows, width = tokens.shape
    seq_rows = rows // SEQS
    window = qkv_weight.shape[1]
    slots = -(-HEADS // count)
    wide = slots * HD
    small_count, small_width = small_weight.shape
    hidden = fc_weight.shape[1]
    all_rows = count * rows
    pair = ring.sides * rows
    pair_slots = ring.sides
    steps = ring.steps

    extra = -(-rows // small_width) * small_width
    pos_parts = jnp.stack([positions // 32, positions % 32]).astype(BF16)
    pos_parts = jnp.pad(pos_parts, ((0, 0), (0, extra - rows))).reshape(-1, small_width)
    small_pack = jnp.concatenate([small_weight.astype(BF16), pos_parts], axis=0)
    small_all = lax.all_to_all(
        jnp.broadcast_to(small_pack[None], (count,) + small_pack.shape), "seq", 0, 0
    ).astype(F32)
    small_rows = small_all[:, :small_count].transpose(1, 0, 2).reshape(small_count, width)
    pos_all = small_all[:, small_count:].reshape(count, 2, extra)[:, :, :rows]
    pos_all = (pos_all[:, 0] * 32.0 + pos_all[:, 1]).astype(jnp.int32)

    token_tour = ring.gather(tokens)
    token_pairs = token_tour.pairs
    pack, unpack, most = head_tables(count, width, window)
    pack_hot = one_hot(pick_row(pack, me), window)
    unpack_hot = one_hot(pick_row(unpack, me), 3 * wide)
    packed = jnp.einsum(
        "rc,cdl->drl",
        qkv_weight.astype(BF16),
        pack_hot.reshape(window, count, most),
        preferred_element_type=BF16,
    )
    received = lax.all_to_all(packed, "seq", 0, 0)
    received = after(received, token_tour.moved[0])
    head_part = jnp.einsum(
        "srl,ksl->rk",
        received,
        unpack_hot.reshape(3 * wide, count, most),
        preferred_element_type=BF16,
    )
    w_head, far_head = square.gather(head_part)
    out_part = lax.all_gather(out_weight.astype(BF16), "seq", axis=1, tiled=True)
    w_out, far_out = square.gather(after(out_part, far_head))
    w_fc, far_fc = square.gather(after(fc_weight.astype(BF16), far_out))
    w_proj, far_proj = square.gather(after(proj_weight.T.astype(BF16), far_fc))
    w_out_heads = jnp.pad(w_out, ((0, slots * count * HD - width), (0, 0)))
    w_out_heads = w_out_heads.reshape(slots, count, HD, width).transpose(1, 0, 2, 3)
    w_out_heads = w_out_heads.reshape(count * wide, width)

    def own_heads(row):
        padded = jnp.pad(row, (0, slots * count * HD - width)).reshape(slots, count, HD)
        return lax.dynamic_index_in_dim(padded, me, 1, keepdims=False).reshape(wide)

    head_bias = jnp.concatenate(
        [own_heads(small_rows[0]), jnp.zeros((wide,), F32), own_heads(small_rows[1])]
    )
    fc_bias = lax.dynamic_slice_in_dim(small_rows[3:7].reshape(-1), me * hidden, hidden, 0)

    tokens_all = jnp.zeros((all_rows, width), BF16)
    qkv_all = jnp.zeros((count, SEQS, seq_rows, 3 * wide), BF16)
    for t in range(steps):
        place = ring.position(t)
        tokens_all = lax.dynamic_update_slice_in_dim(
            tokens_all, token_pairs[t], place * pair, axis=0
        )
        normed = layer_norm(token_pairs[t].astype(F32), small_rows[8], small_rows[9]).astype(BF16)
        part = (dot(normed, w_head) + head_bias).astype(BF16)
        qkv_all = lax.dynamic_update_slice_in_dim(
            qkv_all, part.reshape(pair_slots, SEQS, seq_rows, 3 * wide), place * pair_slots, axis=0
        )

    context, probs = attention_forward(qkv_all, pos_all)
    context = context.reshape(all_rows, wide)

    half = steps // 2
    cot_middle = cotangent
    cot_tour = Tour(ring, cotangent, back=True)
    cot_tour.step(token_tour.moved[-1])
    for t in range(1, half):
        cot_tour.step()
    context_tour = Tour(ring, after(context, far_out, cot_tour.moved[-1]), axis=1)
    for t in range(steps):
        context_tour.step(*((far_fc, far_proj, w_out_heads) if t == half else ()))
    for t in range(half, steps):
        cot_tour.step(context_tour.moved[-1])
        cot_middle = cot_tour.current if t == half else cot_middle
    context_pairs, cot_pairs = context_tour.pairs, cot_tour.pairs
    residual_all = tokens_all.astype(F32) + small_rows[2]
    pair_wide = ring.sides * wide
    group = -(-steps // 4)
    for begin in range(0, steps, group):
        taken = range(begin, min(begin + group, steps))
        rows_out = [
            lax.dynamic_slice_in_dim(w_out_heads, ring.position(t) * pair_wide, pair_wide, axis=0)
            for t in taken
        ]
        block = jnp.concatenate([context_pairs[t] for t in taken], axis=1)
        residual_all = residual_all + dot(block, jnp.concatenate(rows_out, axis=0))
    normed_two_all = layer_norm(residual_all, small_rows[10], small_rows[11]).astype(BF16)
    normed_two_all = after(normed_two_all, cot_middle)

    normed_two, grad_pre, hidden_act, partial = [], [], [], []
    for t in range(steps):
        block = lax.dynamic_slice_in_dim(normed_two_all, ring.position(t) * pair, pair, axis=0)
        hidden_pre = dot(block, w_fc) + fc_bias
        act, hidden_back = jax.vjp(gelu_tanh, hidden_pre)
        grad_low = hidden_back(dot(cot_pairs[t], w_proj))[0].astype(BF16)
        normed_two.append(block)
        hidden_act.append(act.astype(BF16))
        grad_pre.append(grad_low)
        partial.append(dot_nt(grad_low, w_fc))
    grad_normed_two, _ = ring.scatter_sum(partial)

    hidden_low = jnp.concatenate(hidden_act, axis=0)
    grad_pre_low = jnp.concatenate(grad_pre, axis=0)
    fc_sum = dot_tn(after(jnp.concatenate(normed_two, axis=0), partial[0]), grad_pre_low).astype(BF16)
    proj_sum = dot_tn(hidden_low, jnp.concatenate(cot_pairs, axis=0)).astype(BF16)
    fc_grad, fc_column = square.scatter_sum(fc_sum)
    proj_grad = lax.psum_scatter(proj_sum, "dp", scatter_dimension=1, tiled=True).astype(F32)
    output_partial = dot_nt(hidden_low, w_proj)
    normed_tokens = layer_norm(tokens_all.astype(F32), 1.0, 0.0).astype(BF16)
    grad_normed_two = after(
        grad_normed_two, fc_column, proj_sum, output_partial, normed_tokens
    )

    residual = lax.dynamic_slice_in_dim(residual_all, me * rows, rows, axis=0)
    norm_back_two = jax.vjp(layer_norm, residual, small_rows[10], small_rows[11])[1]
    grad_res_norm, grad_gain_two, grad_shift_two = norm_back_two(grad_normed_two)
    grad_residual = cotangent.astype(F32) + grad_res_norm
    grad_attn_low = grad_residual.astype(BF16)

    output_fold = Fold(ring, [output_partial[t * pair : (t + 1) * pair] for t in range(steps)])
    output_fold.step(grad_normed_two)
    grad_context = dot_nt(grad_attn_low, w_out_heads).astype(BF16)
    grad_context = after(grad_context, output_fold.swapped[0])
    grad_context = lax.all_to_all(
        grad_context.reshape(rows, count, wide).transpose(1, 0, 2), "seq", 0, 0
    )
    grad_qkv = attention_backward(
        qkv_all, grad_context.reshape(count, SEQS, seq_rows, wide), probs
    ).reshape(all_rows, 3 * wide)

    output_fold.step(grad_context)
    grad_qkv = after(grad_qkv, output_fold.total)
    partial = [
        dot_nt(lax.dynamic_slice_in_dim(grad_qkv, ring.position(t) * pair, pair, axis=0), w_head)
        for t in range(steps)
    ]
    grad_normed_one, first_moved = ring.scatter_sum(partial)

    query_raw = dot_tn(after(normed_tokens, *partial), grad_qkv[:, :wide])
    other_raw = dot_tn(after(normed_tokens, first_moved), grad_qkv[:, wide:])
    raw_grad = jnp.concatenate([query_raw, other_raw], axis=1)
    grad_qkv_sum = jnp.sum(grad_qkv.astype(F32), axis=0)
    weight_head = w_head.astype(F32)
    grad_gain_one = jnp.sum(raw_grad * weight_head, axis=1)
    grad_shift_one = jnp.sum(weight_head * grad_qkv_sum, axis=1)
    head_sum = raw_grad * small_rows[8][:, None] + small_rows[9][:, None] * grad_qkv_sum
    head_grad = square.scatter_sum(head_sum.astype(BF16))[0].astype(BF16)
    head_packed = jnp.einsum(
        "rk,ksl->srl",
        head_grad,
        unpack_hot.reshape(3 * wide, count, most),
        preferred_element_type=BF16,
    )
    head_back = lax.all_to_all(head_packed, "seq", 0, 0)
    qkv_grad = jnp.einsum(
        "drl,cdl->rc",
        head_back,
        pack_hot.reshape(window, count, most),
        preferred_element_type=F32,
    )

    norm_back_one = jax.vjp(
        lambda v: layer_norm(v, small_rows[8], small_rows[9]), tokens.astype(F32)
    )[1]
    input_grad = (grad_residual + norm_back_one(grad_normed_one)[0]).astype(BF16)
    for t in range(2, steps):
        output_sum = output_fold.step(*((grad_normed_one,) if t == steps - 1 else ()))
    output = (residual + output_sum + small_rows[7]).astype(BF16)

    out_columns = out_weight.shape[1]
    attn_columns = after(grad_attn_low, grad_context)
    attn_columns = lax.all_to_all(
        attn_columns.reshape(rows, count, out_columns).transpose(1, 0, 2), "seq", 0, 0
    ).reshape(all_rows, out_columns)
    out_sum = jnp.zeros((count * wide, out_columns), BF16)
    for t in range(steps):
        out_sum = lax.dynamic_update_slice_in_dim(
            out_sum,
            dot_tn(context_pairs[t], attn_columns).astype(BF16),
            ring.position(t) * pair_wide,
            axis=0,
        )
    out_sum = out_sum.reshape(count, slots, HD, out_columns).transpose(1, 0, 2, 3)
    out_sum = out_sum.reshape(slots * count * HD, out_columns)[:width]
    out_grad, _ = square.scatter_sum(out_sum)

    def place_heads(values):
        spread = (jnp.arange(count) == me).astype(F32)[None, :, None]
        placed = values.reshape(slots, 1, HD) * spread
        return placed.reshape(-1)[:width]

    grad_bias_fc = jnp.sum(grad_pre_low.astype(F32), axis=0)
    grad_bias_fc = grad_bias_fc[None, :] * (jnp.arange(count) == me).astype(F32)[:, None]
    grad_small = jnp.concatenate(
        [
            place_heads(grad_qkv_sum[:wide])[None],
            place_heads(grad_qkv_sum[2 * wide :])[None],
            jnp.sum(grad_attn_low.astype(F32), axis=0)[None],
            grad_bias_fc.reshape(-1, width),
            jnp.sum(cotangent.astype(F32), axis=0)[None],
            grad_gain_one[None],
            grad_shift_one[None],
            grad_gain_two[None],
            grad_shift_two[None],
        ],
        axis=0,
    )
    small_sent = grad_small.astype(BF16).reshape(small_count, count, small_width)
    small_part = jnp.sum(
        lax.all_to_all(small_sent.transpose(1, 0, 2), "seq", 0, 0).astype(F32), axis=0
    )
    small_grad = square.sum(small_part)

    qkv_new = adam_update(qkv_weight, qkv_first, qkv_second, qkv_grad, 0.02, 0.1)
    out_new = adam_update(out_weight, out_first, out_second, out_grad, 0.3, 0.1)
    fc_new = adam_update(fc_weight, fc_first, fc_second, fc_grad, 0.02, 0.1)
    proj_new = adam_update(proj_weight, proj_first, proj_second, proj_grad, 0.02, 0.1)
    small_new = adam_update(small_weight, small_first, small_second, small_grad, 0.3, 0.0)
    return (
        output,
        input_grad,
        *qkv_new,
        *out_new,
        *fc_new,
        *proj_new,
        *small_new,
        small_grad[7],
    )


def solution(mesh):
    rows = P(("dp", "seq"), None)
    matrix = P("dp", "seq")
    turned = P("seq", "dp")
    small = P(None, "seq")
    in_specs = (
        (rows, rows, P(("dp", "seq"))) + (matrix,) * 9 + (turned,) * 3 + (small,) * 3
    )
    out_specs = (rows, rows) + (matrix,) * 9 + (turned,) * 3 + (small,) * 3 + (P("seq"),)
    return jax.shard_map(shards, mesh=mesh, in_specs=in_specs, out_specs=out_specs, check_vma=False)
```

```python
import functools
import math

import jax
import jax.numpy as jnp
import numpy as np
from jax import lax
from jax.experimental import pallas as pl
from jax.experimental.layout import Layout, with_layout_constraint
from jax.experimental.pallas import tpu as pltpu
from jax.sharding import PartitionSpec as P

HEADS = 25
HD = 64
SEQS = 2
STEP = 10

NORM_EPS = 1e-05
SCORE_SCALE = 0.125
MASKED_SCORE = -1e30
BETA_ONE = 0.9
BETA_TWO = 0.95
ADAM_EPS = 1e-08
BF16 = jnp.bfloat16
F32 = jnp.float32


def adam_update(weight, first_moment, second, gradient, step_rate, decay_rate):
    moment_new = BETA_ONE * first_moment + (1.0 - BETA_ONE) * gradient
    second_new = BETA_TWO * second + (1.0 - BETA_TWO) * gradient * gradient
    direction = (
        moment_new
        / (1.0 - BETA_ONE**STEP)
        / (jnp.sqrt(second_new / (1.0 - BETA_TWO**STEP)) + ADAM_EPS)
    )
    return (moment_new, second_new, weight - step_rate * (direction + decay_rate * weight))


def dot(left, right):
    return jnp.dot(left, right, preferred_element_type=F32)


def dot_nt(left, right):
    return lax.dot_general(left, right, (((1,), (1,)), ((), ())), preferred_element_type=F32)


def dot_tn(left, right):
    return lax.dot_general(left, right, (((0,), (0,)), ((), ())), preferred_element_type=F32)


def after(value, *others):
    return lax.optimization_barrier((value,) + others)[0]


def by_rows(value):
    return with_layout_constraint(value, Layout(major_to_minor=(0, 1)))


def call(kernel, out, blocks, grid=None, in_blocks=None, scalars=None, alias=None, flops=0, name=None):
    operands = 0 if scalars is None else 1
    spec = dict(
        in_specs=in_blocks,
        out_specs=blocks,
        grid=grid or (1,),
    )
    if operands:
        spec = dict(grid_spec=pltpu.PrefetchScalarGridSpec(num_scalar_prefetch=1, **spec))
    run = pl.pallas_call(
        kernel,
        out_shape=out,
        input_output_aliases=alias or {},
        compiler_params=pltpu.CompilerParams(vmem_limit_bytes=48 * 1024 * 1024),
        cost_estimate=pl.CostEstimate(
            flops=flops, bytes_accessed=8 * 1024 * 1024, transcendentals=0
        ),
        name=name,
        **spec,
    )
    if operands:
        return lambda *given: run(scalars, *given)
    return run


def whole(shape):
    return pl.BlockSpec(shape, lambda *_: (0,) * len(shape))


def struct(shape, dtype):
    return jax.ShapeDtypeStruct(shape, dtype)


class Ring:
    def __init__(self, count):
        self.sides = 2
        self.steps = count // 2
        steps = self.steps
        self.swap = [(j, j ^ 1) for j in range(count)]
        self.ahead = [(z * 2 + x, ((z + 1) % steps) * 2 + x) for z in range(steps) for x in range(2)]
        self.behind = [(dst, src) for src, dst in self.ahead]
        me = lax.axis_index("seq")
        self.place, self.side = me // 2, me % 2

    def position(self, t):
        return (self.place + self.steps - t) % self.steps

    def gather(self, block):
        tour = Tour(self, block)
        for _ in range(self.steps):
            tour.step()
        return tour


class Tour:
    def __init__(self, ring, block, back=False):
        self.ring, self.current, self.back = ring, block, back
        self.pieces = [None] * ring.steps
        self.moved = []

    def step(self, *begin):
        ring, t = self.ring, len(self.moved)
        if begin:
            self.current = after(self.current, *begin)
        if t:
            sent = after(self.current, self.moved[-2]) if t > 1 else self.current
            self.current = lax.ppermute(sent, "seq", ring.behind if self.back else ring.ahead)
        other = lax.ppermute(self.current, "seq", ring.swap)
        self.pieces[-t if self.back else t] = (self.current, other)
        self.moved.append(other)


class Fold:
    def __init__(self, ring, parts):
        self.ring, self.parts = ring, parts
        self.terms, self.swapped, self.carried = None, [], []

    def step(self, *begin):
        ring = self.ring
        mine, other = self.parts[ring.steps - 1 - len(self.swapped)]
        if begin:
            other = after(other, *begin)
        if len(self.swapped) > 1:
            other = after(other, self.swapped[-2])
        other = lax.ppermute(other, "seq", ring.swap)
        self.swapped.append(other)
        if self.terms is None:
            self.terms = (mine, other)
            return
        carried = sum(term.astype(F32) for term in self.terms).astype(BF16)
        self.carried.append(carried)
        sent = after(carried, *begin) if begin else carried
        self.terms = (mine, other, lax.ppermute(sent, "seq", ring.behind))

    def total(self):
        return sum(term.astype(F32) for term in self.terms)


class Square:
    def __init__(self):
        me = lax.axis_index("dp")
        self.me, self.far, self.near = me, me // 2, me % 2
        self.far_swap = [(j, j ^ 2) for j in range(4)]
        self.near_swap = [(j, j ^ 1) for j in range(4)]

    def gather(self, block):
        near = lax.ppermute(block, "dp", self.near_swap)
        far = lax.ppermute(block, "dp", self.far_swap)
        return (block, near, far, lax.ppermute(far, "dp", self.near_swap))

    def place(self, pieces):
        rows, width = pieces[0].shape

        def kernel(me, *refs):
            out, sems = refs[4], refs[5]
            copies = [
                pltpu.make_async_copy(
                    refs[r], out.at[pl.ds((me[0] ^ r) * rows, rows)], sems.at[r]
                )
                for r in range(4)
            ]
            for copy in copies:
                copy.start()
            for copy in copies:
                copy.wait()

        return pl.pallas_call(
            kernel,
            grid_spec=pltpu.PrefetchScalarGridSpec(
                num_scalar_prefetch=1,
                grid=(1,),
                in_specs=[pl.BlockSpec(memory_space=pl.ANY)] * 4,
                out_specs=pl.BlockSpec(memory_space=pl.ANY),
                scratch_shapes=[pltpu.SemaphoreType.DMA((4,))],
            ),
            out_shape=struct((4 * rows, width), BF16),
            name="place_rows",
        )(self.me[None], *pieces)

    def scatter_sum(self, partial):
        parts = partial.reshape((2, 2, partial.shape[0] // 4) + partial.shape[1:])
        mine = lax.dynamic_index_in_dim(parts, self.near, 1, keepdims=False)
        other = lax.dynamic_index_in_dim(parts, 1 - self.near, 1, keepdims=False)
        column = mine.astype(F32) + lax.ppermute(other, "dp", self.near_swap).astype(F32)
        mine = lax.dynamic_index_in_dim(column, self.far, 0, keepdims=False)
        other = lax.dynamic_index_in_dim(column, 1 - self.far, 0, keepdims=False)
        return mine + lax.ppermute(other.astype(BF16), "dp", self.far_swap).astype(F32), column

    def sum(self, values):
        values = values + lax.ppermute(values, "dp", self.near_swap)
        return values + lax.ppermute(values, "dp", self.far_swap)


def head_tables(count, model_width, window):
    slots = -(-HEADS // count)
    wide = slots * HD
    lists = [[[] for _ in range(count)] for _ in range(count)]
    for column in range(3 * model_width):
        src, local = divmod(column, window)
        part, within = divmod(column, model_width)
        head, lane = divmod(within, HD)
        dst, slot = head % count, head // count
        lists[src][dst].append((local, part * wide + slot * HD + lane))
    most = max(len(entry) for row in lists for entry in row)
    most = -(-most // 64) * 64
    pack = np.full((count, count * most), -1, np.int32)
    unpack = np.full((count, count * most), -1, np.int32)
    for src in range(count):
        for dst in range(count):
            for place, (local, target) in enumerate(lists[src][dst]):
                pack[src, dst * most + place] = local
                unpack[dst, src * most + place] = target
    return pack, unpack, most


def pick_row(table, index):
    return lax.dynamic_index_in_dim(jnp.asarray(table), index, 0, keepdims=False)


def one_hot(rows, size):
    return (lax.broadcasted_iota(jnp.int32, (size, rows.shape[0]), 0) == rows[None, :]).astype(BF16)


def forward_kernel(pos_col, pos_row, query_ref, full_ref, context_ref, probs_ref, *, wide):
    slots, _, run, width = query_ref.shape
    rows = slots * run
    keys_total = full_ref.shape[0] * run
    query = query_ref[:, 0].reshape(rows, width)[:, :wide]
    full = full_ref[:, 0].reshape(keys_total, width)
    key, value = full[:, wide : 2 * wide], full[:, 2 * wide :]
    seen = pos_row[0] <= pos_col[0]
    lane_head = lax.broadcasted_iota(jnp.int32, (1, wide), 1) // HD
    context = jnp.zeros((rows, wide), F32)
    for head in range(wide // HD):
        mine = lane_head == head
        scores = dot_nt(jnp.where(mine, query, jnp.zeros_like(query)), key) * SCORE_SCALE
        scores = jnp.where(seen, scores, MASKED_SCORE)
        top = jnp.max(scores, axis=1, keepdims=True)
        raw = jnp.exp(scores - top)
        probs = (raw * (1.0 / jnp.sum(raw, axis=1, keepdims=True))).astype(BF16)
        probs_ref[0, head] = probs
        context = jnp.where(mine, dot(probs, value), context)
    context_ref[:, 0] = context.astype(BF16).reshape(slots, run, wide)


def backward_kernel(query_ref, full_ref, grad_ref, probs_ref, out_ref, key_sum, value_sum, *, wide):
    step = pl.program_id(1)
    slots, _, run, width = query_ref.shape
    rows = slots * run
    count = full_ref.shape[0]
    keys_total = count * run
    query = query_ref[:, 0].reshape(rows, width)[:, :wide]
    full = full_ref[:, 0].reshape(keys_total, width)
    key, value = full[:, wide : 2 * wide], full[:, 2 * wide :]
    grad = grad_ref[:, 0].reshape(rows, wide)
    lane_head = lax.broadcasted_iota(jnp.int32, (1, wide), 1) // HD

    @pl.when(step == 0)
    def _():
        key_sum[...] = jnp.zeros_like(key_sum)
        value_sum[...] = jnp.zeros_like(value_sum)

    query_grad = jnp.zeros((rows, wide), F32)
    key_grad = jnp.zeros((keys_total, wide), F32)
    value_grad = jnp.zeros((keys_total, wide), F32)
    for head in range(wide // HD):
        mine = lane_head == head
        probs_low = probs_ref[0, head]
        probs = probs_low.astype(F32)
        grad_probs = dot_nt(jnp.where(mine, grad, jnp.zeros_like(grad)), value)
        weighted = probs * grad_probs
        delta = jnp.sum(weighted, axis=1, keepdims=True)
        grad_scores = (weighted - probs * delta).astype(BF16)
        query_grad = jnp.where(mine, dot(grad_scores, key), query_grad)
        key_grad = jnp.where(mine, dot_tn(grad_scores, query), key_grad)
        value_grad = jnp.where(mine, dot_tn(probs_low, grad), value_grad)
    key_sum[...] += key_grad
    value_sum[...] += value_grad
    out_ref[pl.ds(step * slots, slots), 0, :, :wide] = (
        (query_grad * SCORE_SCALE).astype(BF16).reshape(slots, run, wide)
    )

    @pl.when(step == pl.num_programs(1) - 1)
    def _():
        out_ref[:, 0, :, wide : 2 * wide] = (
            (key_sum[...] * SCORE_SCALE).astype(BF16).reshape(count, run, wide)
        )
        out_ref[:, 0, :, 2 * wide :] = value_sum[...].astype(BF16).reshape(count, run, wide)


def attention_forward(qkv_rows, positions):
    count, _, run, width = qkv_rows.shape
    wide = width // 3
    heads = wide // HD
    length = count * run
    block = min(length, 512)
    slots = block // run
    steps = length // block
    by_sequence = positions.reshape(count, SEQS, run).transpose(1, 0, 2).reshape(SEQS, length)
    return pl.pallas_call(
        functools.partial(forward_kernel, wide=wide),
        grid=(SEQS, steps),
        in_specs=[
            pl.BlockSpec((1, block, 1), lambda s, i: (s, i, 0)),
            pl.BlockSpec((1, 1, length), lambda s, i: (s, 0, 0)),
            pl.BlockSpec((slots, 1, run, width), lambda s, i: (i, s, 0, 0)),
            pl.BlockSpec((count, 1, run, width), lambda s, i: (0, s, 0, 0)),
        ],
        out_specs=[
            pl.BlockSpec((slots, 1, run, wide), lambda s, i: (i, s, 0, 0)),
            pl.BlockSpec((1, heads, block, length), lambda s, i: (s, 0, i, 0)),
        ],
        out_shape=[
            jax.ShapeDtypeStruct((count, SEQS, run, wide), BF16),
            jax.ShapeDtypeStruct((SEQS, heads, length, length), BF16),
        ],
        compiler_params=pltpu.CompilerParams(vmem_limit_bytes=48 * 1024 * 1024),
        cost_estimate=pl.CostEstimate(
            flops=4 * SEQS * heads * length * length * 256,
            bytes_accessed=8 * 1024 * 1024,
            transcendentals=SEQS * heads * length * length,
        ),
        name="attention_forward",
    )(by_sequence[:, :, None], by_sequence[:, None, :], qkv_rows, qkv_rows)


def attention_backward(qkv_rows, grad_context, probs):
    count, _, run, width = qkv_rows.shape
    wide = width // 3
    heads = wide // HD
    length = count * run
    block = min(length, 512)
    slots = block // run
    steps = length // block
    return pl.pallas_call(
        functools.partial(backward_kernel, wide=wide),
        grid=(SEQS, steps),
        in_specs=[
            pl.BlockSpec((slots, 1, run, width), lambda s, i: (i, s, 0, 0)),
            pl.BlockSpec((count, 1, run, width), lambda s, i: (0, s, 0, 0)),
            pl.BlockSpec((slots, 1, run, wide), lambda s, i: (i, s, 0, 0)),
            pl.BlockSpec((1, heads, block, length), lambda s, i: (s, 0, i, 0)),
        ],
        out_specs=pl.BlockSpec((count, 1, run, width), lambda s, i: (0, s, 0, 0)),
        out_shape=jax.ShapeDtypeStruct((count, SEQS, run, width), BF16),
        scratch_shapes=[pltpu.VMEM((length, wide), F32), pltpu.VMEM((length, wide), F32)],
        compiler_params=pltpu.CompilerParams(vmem_limit_bytes=48 * 1024 * 1024),
        cost_estimate=pl.CostEstimate(
            flops=8 * SEQS * heads * length * length * 256,
            bytes_accessed=8 * 1024 * 1024,
            transcendentals=0,
        ),
        name="attention_backward",
    )(qkv_rows, qkv_rows, grad_context, probs)


def in_order(side, own, other, axis=0):
    first = jnp.where(side == 0, own, other)
    second = jnp.where(side == 0, other, own)
    return jnp.concatenate([first, second], axis=axis)


def normalize(values):
    centred = values - jnp.mean(values, axis=1, keepdims=True)
    spread = lax.rsqrt(jnp.mean(centred * centred, axis=1, keepdims=True) + NORM_EPS)
    return centred * spread, spread


def normalize_back(normal, spread, gain, grad):
    scaled = grad * gain
    along = jnp.mean(scaled * normal, axis=1, keepdims=True)
    return spread * (scaled - jnp.mean(scaled, axis=1, keepdims=True) - normal * along)


def first_rows(pieces, scalars, weight, gain, shift, bias):
    rows, width = pieces[0][0].shape
    steps = len(pieces)
    total = 2 * steps * rows
    columns = weight.shape[1]

    def kernel(marks, *refs):
        given, (w, g, s, b), outs = refs[: 2 * steps], refs[2 * steps : 2 * steps + 4], refs[-3:]
        for t in range(steps):

            @pl.when(pl.program_id(0) == t)
            def _(t=t):
                outs[0][...] = in_order(marks[0], given[2 * t][...], given[2 * t + 1][...])

        normal, _ = normalize(outs[0][...].astype(F32))
        outs[1][...] = normal.astype(BF16)
        scaled = (normal * g[...] + s[...]).astype(BF16)
        outs[2][...] = (dot(scaled, w[...]) + b[...]).astype(BF16)

    def block(width):
        return pl.BlockSpec((2 * rows, width), lambda t, marks: (marks[1 + t], 0))

    flat = [piece for pair in pieces for piece in pair]
    return call(
        kernel,
        [struct((total, width), BF16), struct((total, width), BF16), struct((total, columns), BF16)],
        [block(width), block(width), block(columns)],
        grid=(steps,),
        in_blocks=[whole((rows, width))] * (2 * steps)
        + [whole(weight.shape), whole((1, width)), whole((1, width)), whole((1, columns))],
        scalars=scalars,
        flops=2 * total * width * columns,
        name="first_rows",
    )(*flat, weight, gain, shift, bias)


def second_rows(tokens_all, pieces, scalars, weight, bias, gain, shift):
    total, width = tokens_all.shape
    steps = len(pieces)
    wide = pieces[0][0].shape[1]
    rows = total // steps

    def kernel(marks, tokens, *refs):
        given = refs[: 2 * steps]
        w, b, g, s, normed, own, context = refs[2 * steps :]
        for t in range(steps):
            pair = in_order(marks[0], given[2 * t][...], given[2 * t + 1][...], axis=1)
            begin = pl.multiple_of(marks[1 + t] * (2 * wide), 2 * wide)
            context[:, pl.ds(begin, 2 * wide)] = pair
        residual = tokens[...].astype(F32) + dot(context[...], w[...]) + b[...]
        normal, _ = normalize(residual)
        normed[...] = (normal * g[...] + s[...]).astype(BF16)

        @pl.when(pl.program_id(0) == marks[1])
        def _():
            own[...] = jnp.where(marks[0] == 0, residual[: rows // 2], residual[rows // 2 :])

    return pl.pallas_call(
        kernel,
        grid_spec=pltpu.PrefetchScalarGridSpec(
            num_scalar_prefetch=1,
            grid=(steps,),
            in_specs=[pl.BlockSpec((rows, width), lambda i, marks: (i, 0))]
            + [pl.BlockSpec((rows, wide), lambda i, marks: (i, 0))] * (2 * steps)
            + [whole(weight.shape), whole((1, width)), whole((1, width)), whole((1, width))],
            out_specs=[
                pl.BlockSpec((rows, width), lambda i, marks: (i, 0)),
                whole((rows // 2, width)),
            ],
            scratch_shapes=[pltpu.VMEM((rows, 2 * steps * wide), BF16)],
        ),
        out_shape=[struct((total, width), BF16), struct((rows // 2, width), F32)],
        compiler_params=pltpu.CompilerParams(vmem_limit_bytes=48 * 1024 * 1024),
        cost_estimate=pl.CostEstimate(
            flops=2 * total * width * 2 * steps * wide,
            bytes_accessed=16 * 1024 * 1024,
            transcendentals=0,
        ),
        name="second_rows",
    )(scalars, tokens_all, *[piece for pair in pieces for piece in pair], weight, bias, gain, shift)


def hidden_rows(normed, pair, marks_t, w_fc, w_proj, bias, kept):
    total, width = normed.shape
    rows = pair[0].shape[0]
    hidden = w_fc.shape[1]

    def kernel(marks, block, own, other, fc, proj, b, *refs):
        act_ref, grad_ref, cot_ref, mine_ref, other_ref = refs[-5:]
        z = dot(block[...], fc[...]) + b[...]
        inner = 0.7978845608028654 * (z + 0.044715 * z * z * z)
        tanh = jnp.tanh(inner)
        half = 0.5 * (1.0 + tanh)
        slope = half + 0.5 * z * (1.0 - tanh * tanh) * 0.7978845608028654 * (
            1.0 + 3.0 * 0.044715 * z * z
        )
        act_ref[...] = (z * half).astype(BF16)
        cot = in_order(marks[0], own[...], other[...])
        cot_ref[...] = cot
        grad = (dot(cot, proj[...]) * slope).astype(BF16)
        grad_ref[...] = grad
        part = dot_nt(grad, fc[...])
        mine_ref[...] = jnp.where(marks[0] == 0, part[:rows], part[rows:])
        other_ref[...] = jnp.where(marks[0] == 0, part[rows:], part[:rows]).astype(BF16)

    def block(width):
        return pl.BlockSpec((2 * rows, width), lambda i, marks: (marks[1], 0))

    operands = [normed, pair[0], pair[1], w_fc, w_proj, bias]
    blocks = [
        block(width),
        whole((rows, width)),
        whole((rows, width)),
        whole(w_fc.shape),
        whole(w_proj.shape),
        whole((1, hidden)),
    ]
    alias = {}
    if kept is not None:
        alias = {1 + len(operands) + i: i for i in range(3)}
        operands += list(kept)
        blocks += [pl.BlockSpec(memory_space=pl.ANY)] * 3
    act, grad, cot, mine, other = call(
        kernel,
        [
            struct((total, hidden), BF16),
            struct((total, hidden), BF16),
            struct((total, width), BF16),
            struct((rows, width), F32),
            struct((rows, width), BF16),
        ],
        [block(hidden), block(hidden), block(width), whole((rows, width)), whole((rows, width))],
        in_blocks=blocks,
        scalars=marks_t,
        alias=alias,
        flops=12 * rows * width * hidden,
        name="hidden_rows",
    )(*operands)
    return (act, grad, cot), (mine, other)


def turned_product(left, right, name):
    total, width = left.shape
    columns = right.shape[1]
    tile = 256

    def kernel(left_ref, right_ref, out_ref):
        out_ref[...] = dot_tn(left_ref[...], right_ref[...]).astype(BF16)

    return call(
        kernel,
        struct((width, columns), BF16),
        pl.BlockSpec((tile, columns), lambda i: (i, 0)),
        grid=(pl.cdiv(width, tile),),
        in_blocks=[pl.BlockSpec((total, tile), lambda i: (0, i)), whole(right.shape)],
        flops=2 * total * width * columns,
        name=name,
    )(left, right)


def head_product(normal, grad, weight, gain, shift):
    total, width = normal.shape
    columns = grad.shape[1]
    tile = 256

    def kernel(left, right, w, g, s, out, gain_sum, shift_sum, grad_sum):
        @pl.when(pl.program_id(0) == 0)
        def _():
            grad_sum[...] = jnp.sum(right[...].astype(F32), axis=0, keepdims=True)

        raw = dot_tn(left[...], right[...])
        sums = grad_sum[...]
        low = w[...].astype(F32)
        gain_sum[...] = jnp.sum(raw * low, axis=1, keepdims=True)
        shift_sum[...] = jnp.sum(low * sums, axis=1, keepdims=True)
        out[...] = (raw * g[...] + s[...] * sums).astype(BF16)

    column = pl.BlockSpec((tile, 1), lambda i: (i, 0))
    return call(
        kernel,
        [
            struct((width, columns), BF16),
            struct((width, 1), F32),
            struct((width, 1), F32),
            struct((1, columns), F32),
        ],
        [pl.BlockSpec((tile, columns), lambda i: (i, 0)), column, column, whole((1, columns))],
        grid=(pl.cdiv(width, tile),),
        in_blocks=[
            pl.BlockSpec((total, tile), lambda i: (0, i)),
            whole(grad.shape),
            pl.BlockSpec((tile, columns), lambda i: (i, 0)),
            column,
            column,
        ],
        flops=2 * total * width * columns,
        name="head_product",
    )(normal, grad, weight, gain, shift)


def ring_parts(left, right, scalars, steps, name):
    total, inner = left.shape
    width = right.shape[0]
    rows = total // (2 * steps)

    def kernel(marks, left_ref, right_ref, *outs):
        for t in range(steps):
            for part in range(2):
                side = marks[0] if part == 0 else 1 - marks[0]
                begin = pl.multiple_of((marks[1 + t] * 2 + side) * rows, rows)
                value = dot_nt(left_ref[pl.ds(begin, rows)], right_ref[...])
                outs[2 * t + part][...] = value.astype(outs[2 * t + part].dtype)

    outs = call(
        kernel,
        [struct((rows, width), dtype) for _ in range(steps) for dtype in (F32, BF16)],
        [whole((rows, width))] * (2 * steps),
        in_blocks=[whole(left.shape), whole(right.shape)],
        scalars=scalars,
        flops=2 * total * width * inner,
        name=name,
    )(left, right)
    return [(outs[2 * t], outs[2 * t + 1]) for t in range(steps)]


def second_back(residual, terms, cotangent, gain, weight, count):
    rows, width = residual.shape
    wide = weight.shape[0] // count

    def kernel(res, mine, swapped, carried, cot, g, w, grad_ref, low_ref, sums_ref, out_ref):
        @pl.when(pl.program_id(0) == 0)
        def _():
            grad = mine[...] + swapped[...].astype(F32) + carried[...].astype(F32)
            normal, spread = normalize(res[...])
            total = cot[...].astype(F32) + normalize_back(normal, spread, g[...], grad)
            grad_ref[...] = total
            low = total.astype(BF16)
            low_ref[...] = low
            sums_ref[0:1] = jnp.sum(grad * normal, axis=0, keepdims=True)
            sums_ref[1:2] = jnp.sum(grad, axis=0, keepdims=True)
            sums_ref[2:3] = jnp.sum(low.astype(F32), axis=0, keepdims=True)
            sums_ref[3:4] = jnp.sum(cot[...].astype(F32), axis=0, keepdims=True)

        out_ref[0] = dot_nt(low_ref[...], w[...]).astype(BF16)

    row = whole((rows, width))
    return call(
        kernel,
        [
            struct((rows, width), F32),
            struct((rows, width), BF16),
            struct((4, width), F32),
            struct((count, rows, wide), BF16),
        ],
        [row, row, whole((4, width)), pl.BlockSpec((1, rows, wide), lambda i: (i, 0, 0))],
        grid=(count,),
        in_blocks=[row] * 5 + [whole((1, width)), pl.BlockSpec((wide, width), lambda i: (i, 0))],
        flops=2 * rows * width * count * wide,
        name="second_back",
    )(residual, *terms, cotangent, gain, weight)


def first_back(tokens, terms, residual_grad, gain):
    rows, width = tokens.shape

    def kernel(x, mine, swapped, carried, res, g, out_ref):
        grad = mine[...] + swapped[...].astype(F32) + carried[...].astype(F32)
        normal, spread = normalize(x[...].astype(F32))
        out_ref[...] = (res[...] + normalize_back(normal, spread, g[...], grad)).astype(BF16)

    row = whole((rows, width))
    return call(
        kernel,
        struct((rows, width), BF16),
        row,
        in_blocks=[row] * 5 + [whole((1, width))],
        flops=rows * width * 20,
        name="first_back",
    )(tokens, *terms, residual_grad, gain)


def heads_rows(me, pieces, count, slots):
    rows, width = pieces[0].shape
    unit = math.gcd(rows, HD)
    empty = [(h % count, h // count) for h in range(HEADS, count * slots)]

    def kernel(mark, *refs):
        out, blank, sems = refs[4], refs[5], refs[6]
        blank[...] = jnp.zeros_like(blank)
        copies = []
        for r in range(4):
            for piece in range(rows // unit):
                row = (mark[0] ^ r) * rows + piece * unit
                head = row // HD
                target = ((head % count) * slots + head // count) * HD + row % HD
                copies.append((refs[r].at[pl.ds(piece * unit, unit)], target, unit))
        for device, slot in empty:
            copies.append((blank, (device * slots + slot) * HD, HD))
        copies = [
            pltpu.make_async_copy(
                source, out.at[pl.ds(pl.multiple_of(target, unit), size)], sems.at[i]
            )
            for i, (source, target, size) in enumerate(copies)
        ]
        for copy in copies:
            copy.start()
        for copy in copies:
            copy.wait()

    return pl.pallas_call(
        kernel,
        grid_spec=pltpu.PrefetchScalarGridSpec(
            num_scalar_prefetch=1,
            grid=(1,),
            in_specs=[pl.BlockSpec(memory_space=pl.ANY)] * 4,
            out_specs=pl.BlockSpec(memory_space=pl.ANY),
            scratch_shapes=[
                pltpu.VMEM((HD, width), BF16),
                pltpu.SemaphoreType.DMA((4 * (rows // unit) + len(empty),)),
            ],
        ),
        out_shape=struct((count * slots * HD, width), BF16),
        name="heads_rows",
    )(me[None], *pieces)


def shards(
    tokens,
    cotangent,
    positions,
    qkv_weight,
    qkv_first,
    qkv_second,
    out_weight,
    out_first,
    out_second,
    fc_weight,
    fc_first,
    fc_second,
    proj_weight,
    proj_first,
    proj_second,
    small_weight,
    small_first,
    small_second,
):
    count = lax.axis_size("seq")
    ring = Ring(count)
    square = Square()
    me = lax.axis_index("seq")
    rows, width = tokens.shape
    seq_rows = rows // SEQS
    window = qkv_weight.shape[1]
    slots = -(-HEADS // count)
    wide = slots * HD
    small_count, small_width = small_weight.shape
    hidden = fc_weight.shape[1]
    all_rows = count * rows
    steps = ring.steps
    marks = jnp.stack([ring.side] + [ring.position(t) for t in range(steps)])
    tokens = by_rows(tokens)
    cotangent = by_rows(cotangent)

    token_tour = Tour(ring, tokens)
    token_tour.step()
    token_tour.step()
    pack, unpack, most = head_tables(count, width, window)
    pack_hot = one_hot(pick_row(pack, me), window)
    packed = jnp.einsum(
        "rc,cdl->drl",
        qkv_weight.astype(BF16),
        pack_hot.reshape(window, count, most),
        preferred_element_type=BF16,
    )
    received = lax.all_to_all(packed, "seq", 0, 0)

    extra = -(-rows // small_width) * small_width
    pos_parts = jnp.stack([positions // 32, positions % 32]).astype(BF16)
    pos_parts = jnp.pad(pos_parts, ((0, 0), (0, extra - rows))).reshape(-1, small_width)
    small_pack = jnp.concatenate([small_weight.astype(BF16), pos_parts], axis=0)
    small_pack = after(small_pack, packed)
    small_all = lax.all_to_all(
        jnp.broadcast_to(small_pack[None], (count,) + small_pack.shape), "seq", 0, 0
    ).astype(F32)

    unpack_hot = one_hot(pick_row(unpack, me), 3 * wide)
    head_part = jnp.einsum(
        "srl,ksl->rk",
        received,
        unpack_hot.reshape(3 * wide, count, most),
        preferred_element_type=BF16,
    )
    head_pieces = square.gather(head_part)
    for t in range(2, steps):
        token_tour.step(*((head_part,) if t == steps - 1 else ()))
    w_head = square.place(head_pieces)

    small_rows = small_all[:, :small_count].transpose(1, 0, 2).reshape(small_count, width)
    pos_all = small_all[:, small_count:].reshape(count, 2, extra)[:, :, :rows]
    pos_all = (pos_all[:, 0] * 32.0 + pos_all[:, 1]).astype(jnp.int32)

    def own_heads(row):
        padded = jnp.pad(row, (0, slots * count * HD - width)).reshape(slots, count, HD)
        return lax.dynamic_index_in_dim(padded, me, 1, keepdims=False).reshape(wide)

    head_bias = jnp.concatenate(
        [own_heads(small_rows[0]), jnp.zeros((wide,), F32), own_heads(small_rows[1])]
    )
    fc_bias = lax.dynamic_slice_in_dim(small_rows[3:7].reshape(-1), me * hidden, hidden, 0)
    gain_one, shift_one = small_rows[8][None], small_rows[9][None]
    gain_two, shift_two = small_rows[10][None], small_rows[11][None]

    fc_pieces = square.gather(after(fc_weight, head_pieces[2]).astype(BF16))
    proj_pieces = square.gather(after(proj_weight, fc_pieces[2]).T.astype(BF16))
    out_part = lax.all_gather(
        after(out_weight, token_tour.current).astype(BF16), "seq", axis=1, tiled=True
    )
    out_pieces = square.gather(after(by_rows(out_part), proj_pieces[2]))

    tokens_all, normal_all, qkv_rows = first_rows(
        token_tour.pieces, marks, w_head, gain_one, shift_one, head_bias[None]
    )
    qkv_all = qkv_rows.reshape(count, SEQS, seq_rows, 3 * wide)
    context, probs = attention_forward(qkv_all, pos_all)
    context = context.reshape(all_rows, wide)

    half = steps // 2
    cot_tour = Tour(ring, cotangent, back=True)
    cot_tour.step(token_tour.moved[-1])
    for t in range(1, half):
        cot_tour.step()
    context_tour = Tour(ring, after(context, cot_tour.moved[-1]))
    w_fc, w_proj, w_out = None, None, None
    for t in range(steps):
        if t == 1:
            context_tour.step(proj_pieces[2])
            w_fc = square.place(after(fc_pieces, context_tour.moved[0]))
        elif t == steps - 1:
            w_proj = square.place(after(proj_pieces, context_tour.moved[-2]))
            context_tour.step(out_pieces[2], w_fc)
        else:
            context_tour.step()
    w_out = heads_rows(square.me, out_pieces, count, slots)
    cot_middle = cotangent
    for t in range(half, steps):
        cot_tour.step(context_tour.current)
        cot_middle = cot_tour.current if t == half else cot_middle
    normed_all, residual = second_rows(
        tokens_all, context_tour.pieces, marks, w_out, small_rows[2][None], gain_two, shift_two
    )
    normed_all = after(normed_all, cot_middle)

    kept, parts = None, [None] * steps
    for t in reversed(range(steps)):
        kept, parts[t] = hidden_rows(
            normed_all,
            cot_tour.pieces[t],
            jnp.stack([ring.side, ring.position(t)]),
            w_fc,
            w_proj,
            fc_bias[None],
            kept,
        )
    hidden_low, grad_pre_low, cot_all = kept
    grad_fold = Fold(ring, parts)
    grad_fold.step()
    grad_fold.step()
    first = grad_fold.carried[-1]
    fc_sum = turned_product(after(normed_all, first), grad_pre_low, "fc_product")
    fc_grad, fc_column = square.scatter_sum(fc_sum)
    for _ in range(2, steps):
        grad_fold.step()
    proj_sum = turned_product(after(cot_all, grad_fold.carried[1], fc_sum), hidden_low, "proj_product")
    proj_grad = lax.psum_scatter(proj_sum, "dp", scatter_dimension=0, tiled=True).astype(F32)
    output_parts = ring_parts(
        after(hidden_low, grad_fold.carried[-1], proj_sum), w_proj, marks, steps, "output_parts"
    )
    terms = list(grad_fold.terms)
    terms[0] = after(terms[0], fc_column, *output_parts[-1])
    output_fold = Fold(ring, output_parts)
    output_fold.step(grad_fold.swapped[-1])
    grad_residual, grad_attn_low, row_sums, grad_context = second_back(
        residual, terms, cotangent, gain_two, w_out, count
    )

    grad_context = lax.all_to_all(after(grad_context, output_fold.swapped[0]), "seq", 0, 0)
    output_fold.step(grad_context)
    grad_qkv = attention_backward(
        qkv_all, grad_context.reshape(count, SEQS, seq_rows, wide), probs
    ).reshape(all_rows, 3 * wide)
    parts = ring_parts(
        after(grad_qkv, output_fold.terms[-1]), w_head, marks, steps, "input_parts"
    )
    input_fold = Fold(ring, parts)
    input_fold.step()
    head_sum, grad_gain_one, grad_shift_one, grad_qkv_sum = head_product(
        after(normal_all, *parts[0]), grad_qkv, w_head, small_rows[8][:, None], small_rows[9][:, None]
    )
    input_fold.step()
    head_sum = after(head_sum, input_fold.carried[0])
    head_grad = square.scatter_sum(head_sum)[0].astype(BF16)
    for _ in range(2, steps):
        input_fold.step()
    input_grad = first_back(tokens, input_fold.terms, grad_residual, gain_one)

    unpack_back = unpack_hot.reshape(3 * wide, count, most)
    head_packed = jnp.einsum("rk,ksl->srl", head_grad, unpack_back, preferred_element_type=BF16)
    head_back = lax.all_to_all(head_packed, "seq", 0, 0)
    qkv_grad = jnp.einsum(
        "drl,cdl->rc",
        head_back,
        pack_hot.reshape(window, count, most),
        preferred_element_type=F32,
    )
    for t in range(2, steps):
        output_fold.step(*((input_fold.terms[-1],) if t == steps - 1 else ()))
    output = (residual + output_fold.total() + small_rows[7]).astype(BF16)

    out_columns = out_weight.shape[1]
    attn_columns = after(grad_attn_low, grad_context)
    attn_columns = lax.all_to_all(
        attn_columns.reshape(rows, count, out_columns).transpose(1, 0, 2), "seq", 0, 0
    ).reshape(all_rows, out_columns)
    attn_columns = after(attn_columns, input_fold.carried[0])
    out_sum = jnp.zeros((count * wide, out_columns), BF16)
    for t in range(steps):
        for b in range(2):
            owner = ring.position(t) * 2 + (ring.side + b) % 2
            out_sum = lax.dynamic_update_slice_in_dim(
                out_sum,
                dot_tn(context_tour.pieces[t][b], attn_columns).astype(BF16),
                owner * wide,
                axis=0,
            )
    out_sum = out_sum.reshape(count, slots, HD, out_columns).transpose(1, 0, 2, 3)
    out_sum = out_sum.reshape(slots * count * HD, out_columns)[:width]
    out_grad, _ = square.scatter_sum(out_sum)

    def place_heads(values):
        spread = (jnp.arange(count) == me).astype(F32)[None, :, None]
        placed = values.reshape(slots, 1, HD) * spread
        return placed.reshape(-1)[:width]

    grad_bias_fc = jnp.sum(after(grad_pre_low, grad_fold.carried[-1]).astype(F32), axis=0)
    grad_bias_fc = grad_bias_fc[None, :] * (jnp.arange(count) == me).astype(F32)[:, None]
    grad_qkv_sum = after(grad_qkv_sum, input_fold.carried[0])[0]
    grad_small = jnp.concatenate(
        [
            place_heads(grad_qkv_sum[:wide])[None],
            place_heads(grad_qkv_sum[2 * wide :])[None],
            row_sums[2:3],
            grad_bias_fc.reshape(-1, width),
            row_sums[3:4],
            grad_gain_one[:, 0][None],
            grad_shift_one[:, 0][None],
            row_sums[0:1],
            row_sums[1:2],
        ],
        axis=0,
    )
    small_sent = grad_small.astype(BF16).reshape(small_count, count, small_width)
    small_part = jnp.sum(
        lax.all_to_all(small_sent.transpose(1, 0, 2), "seq", 0, 0).astype(F32), axis=0
    )
    small_grad = square.sum(small_part)

    qkv_new = adam_update(qkv_weight, qkv_first, qkv_second, qkv_grad, 0.02, 0.1)
    out_new = adam_update(out_weight, out_first, out_second, out_grad, 0.3, 0.1)
    fc_new = adam_update(fc_weight, fc_first, fc_second, fc_grad, 0.02, 0.1)
    proj_new = adam_update(
        proj_weight.T, proj_first.T, proj_second.T, proj_grad, 0.02, 0.1
    )
    proj_new = [value.T for value in proj_new]
    small_new = adam_update(small_weight, small_first, small_second, small_grad, 0.3, 0.0)
    return (
        output,
        input_grad,
        *qkv_new,
        *out_new,
        *fc_new,
        *proj_new,
        *small_new,
        small_grad[7],
    )


def solution(mesh):
    rows = P(("dp", "seq"), None)
    matrix = P("dp", "seq")
    turned = P("seq", "dp")
    small = P(None, "seq")
    in_specs = (
        (rows, rows, P(("dp", "seq"))) + (matrix,) * 9 + (turned,) * 3 + (small,) * 3
    )
    out_specs = (rows, rows) + (matrix,) * 9 + (turned,) * 3 + (small,) * 3 + (P("seq"),)
    return jax.shard_map(shards, mesh=mesh, in_specs=in_specs, out_specs=out_specs, check_vma=False)
```

```python
import functools
import math

import jax
import jax.numpy as jnp
import numpy as np
from jax import lax
from jax.experimental import pallas as pl
from jax.experimental.layout import Layout, with_layout_constraint
from jax.experimental.pallas import tpu as pltpu
from jax.sharding import PartitionSpec as P

HEADS = 25
HD = 64
SEQS = 2
STEP = 10

NORM_EPS = 1e-05
SCORE_SCALE = 0.125
MASKED_SCORE = -1e30
BETA_ONE = 0.9
BETA_TWO = 0.95
ADAM_EPS = 1e-08
BF16 = jnp.bfloat16
F32 = jnp.float32
SMALL_COST = pl.CostEstimate(flops=1024, bytes_accessed=1024, transcendentals=0)


def adam_update(weight, first_moment, second, gradient, step_rate, decay_rate):
    moment_new = BETA_ONE * first_moment + (1.0 - BETA_ONE) * gradient
    second_new = BETA_TWO * second + (1.0 - BETA_TWO) * gradient * gradient
    direction = (
        moment_new
        / (1.0 - BETA_ONE**STEP)
        / (jnp.sqrt(second_new / (1.0 - BETA_TWO**STEP)) + ADAM_EPS)
    )
    return (moment_new, second_new, weight - step_rate * (direction + decay_rate * weight))


def dot(left, right):
    return jnp.dot(left, right, preferred_element_type=F32)


def dot_nt(left, right):
    return lax.dot_general(left, right, (((1,), (1,)), ((), ())), preferred_element_type=F32)


def dot_tn(left, right):
    return lax.dot_general(left, right, (((0,), (0,)), ((), ())), preferred_element_type=F32)


def after(value, *others):
    return lax.optimization_barrier((value,) + others)[0]


def by_rows(value):
    return with_layout_constraint(value, Layout(major_to_minor=(0, 1)))


def call(kernel, out, blocks, grid=None, in_blocks=None, scalars=None, alias=None, name=None):
    operands = 0 if scalars is None else 1
    spec = dict(
        in_specs=in_blocks,
        out_specs=blocks,
        grid=grid or (1,),
    )
    if operands:
        spec = dict(grid_spec=pltpu.PrefetchScalarGridSpec(num_scalar_prefetch=1, **spec))
    run = pl.pallas_call(
        kernel,
        out_shape=out,
        input_output_aliases=alias or {},
        compiler_params=pltpu.CompilerParams(vmem_limit_bytes=48 * 1024 * 1024),
        cost_estimate=SMALL_COST,
        name=name,
        **spec,
    )
    if operands:
        return lambda *given: run(scalars, *given)
    return run


def whole(shape):
    return pl.BlockSpec(shape, lambda *_: (0,) * len(shape))


def struct(shape, dtype):
    return jax.ShapeDtypeStruct(shape, dtype)


class Ring:
    def __init__(self, count):
        self.sides = 2
        self.steps = count // 2
        steps = self.steps
        self.swap = [(j, j ^ 1) for j in range(count)]
        self.ahead = [(z * 2 + x, ((z + 1) % steps) * 2 + x) for z in range(steps) for x in range(2)]
        self.behind = [(dst, src) for src, dst in self.ahead]
        me = lax.axis_index("seq")
        self.place, self.side = me // 2, me % 2

    def position(self, t):
        return (self.place + self.steps - t) % self.steps

    def gather(self, block):
        tour = Tour(self, block)
        for _ in range(self.steps):
            tour.step()
        return tour


class Tour:
    def __init__(self, ring, block, back=False):
        self.ring, self.current, self.back = ring, block, back
        self.pieces = [None] * ring.steps
        self.moved = []

    def step(self, *begin):
        ring, t = self.ring, len(self.moved)
        if begin:
            self.current = after(self.current, *begin)
        if t:
            sent = after(self.current, self.moved[-2]) if t > 1 else self.current
            self.current = lax.ppermute(sent, "seq", ring.behind if self.back else ring.ahead)
        other = lax.ppermute(self.current, "seq", ring.swap)
        self.pieces[-t if self.back else t] = (self.current, other)
        self.moved.append(other)


class Fold:
    def __init__(self, ring, parts):
        self.ring, self.parts = ring, parts
        self.terms, self.count, self.carried = None, 0, None
        self.step()

    def step(self):
        ring = self.ring
        mine, other = self.parts[ring.steps - 1 - self.count]
        self.count += 1
        sent = None
        if self.terms is not None:
            sent = sum(term.astype(F32) for term in self.terms).astype(BF16)
            self.carried = sent
            other = after(other, sent)
        self.terms = [mine, lax.ppermute(other, "seq", ring.swap)]
        if sent is not None:
            self.terms.append(lax.ppermute(sent, "seq", ring.behind))

    def beside(self, *work):
        self.terms = list(lax.optimization_barrier((tuple(self.terms),) + work)[0])


class Square:
    def __init__(self):
        me = lax.axis_index("dp")
        self.me, self.far, self.near = me, me // 2, me % 2
        self.far_swap = [(j, j ^ 2) for j in range(4)]
        self.near_swap = [(j, j ^ 1) for j in range(4)]

    def gather(self, block, *begin):
        near = lax.ppermute(block, "dp", self.near_swap)
        far = lax.ppermute(block, "dp", self.far_swap)
        far = after(far, *begin) if begin else far
        return (block, near, far, lax.ppermute(far, "dp", self.near_swap))

    def place(self, pieces):
        rows, width = pieces[0].shape

        def kernel(me, *refs):
            for r in range(4):
                begin = pl.multiple_of((me[0] ^ r) * rows, 16)
                refs[4][pl.ds(begin, rows)] = refs[r][...]

        return call(
            kernel,
            struct((4 * rows, width), BF16),
            whole((4 * rows, width)),
            in_blocks=[whole((rows, width))] * 4,
            scalars=self.me[None],
            name="place_rows",
        )(*pieces)

    def half_sum(self, partial):
        parts = partial.reshape((2, 2, partial.shape[0] // 4) + partial.shape[1:])
        mine = lax.dynamic_index_in_dim(parts, self.near, 1, keepdims=False)
        other = lax.dynamic_index_in_dim(parts, 1 - self.near, 1, keepdims=False)
        return mine.astype(F32) + lax.ppermute(other, "dp", self.near_swap).astype(F32)

    def other_sum(self, column):
        mine = lax.dynamic_index_in_dim(column, self.far, 0, keepdims=False)
        other = lax.dynamic_index_in_dim(column, 1 - self.far, 0, keepdims=False)
        return mine + lax.ppermute(other.astype(BF16), "dp", self.far_swap).astype(F32)

    def sum(self, values):
        values = values + lax.ppermute(values, "dp", self.near_swap)
        return values + lax.ppermute(values, "dp", self.far_swap)


def head_tables(count, model_width, window):
    slots = -(-HEADS // count)
    wide = slots * HD
    lists = [[[] for _ in range(count)] for _ in range(count)]
    for column in range(3 * model_width):
        src, local = divmod(column, window)
        part, within = divmod(column, model_width)
        head, lane = divmod(within, HD)
        dst, slot = head % count, head // count
        lists[src][dst].append((local, part * wide + slot * HD + lane))
    most = max(len(entry) for row in lists for entry in row)
    most = -(-most // 64) * 64
    pack = np.full((count, count * most), -1, np.int32)
    unpack = np.full((count, count * most), -1, np.int32)
    for src in range(count):
        for dst in range(count):
            for place, (local, target) in enumerate(lists[src][dst]):
                pack[src, dst * most + place] = local
                unpack[dst, src * most + place] = target
    return pack, unpack, most


def pick_row(table, index):
    return lax.dynamic_index_in_dim(jnp.asarray(table), index, 0, keepdims=False)


def one_hot(rows, size):
    return (lax.broadcasted_iota(jnp.int32, (size, rows.shape[0]), 0) == rows[None, :]).astype(BF16)


def forward_kernel(pos_col, pos_row, query_ref, full_ref, context_ref, probs_ref, *, wide):
    slots, _, run, width = query_ref.shape
    rows = slots * run
    keys_total = full_ref.shape[0] * run
    query = query_ref[:, 0].reshape(rows, width)[:, :wide]
    full = full_ref[:, 0].reshape(keys_total, width)
    key, value = full[:, wide : 2 * wide], full[:, 2 * wide :]
    seen = pos_row[0] <= pos_col[0]
    lane_head = lax.broadcasted_iota(jnp.int32, (1, wide), 1) // HD
    context = jnp.zeros((rows, wide), F32)
    for head in range(wide // HD):
        mine = lane_head == head
        scores = dot_nt(jnp.where(mine, query, jnp.zeros_like(query)), key) * SCORE_SCALE
        scores = jnp.where(seen, scores, MASKED_SCORE)
        top = jnp.max(scores, axis=1, keepdims=True)
        raw = jnp.exp(scores - top)
        probs = (raw * (1.0 / jnp.sum(raw, axis=1, keepdims=True))).astype(BF16)
        probs_ref[0, head] = probs
        context = jnp.where(mine, dot(probs, value), context)
    context_ref[:, 0] = context.astype(BF16).reshape(slots, run, wide)


def backward_kernel(query_ref, full_ref, grad_ref, probs_ref, out_ref, key_sum, value_sum, *, wide):
    step = pl.program_id(1)
    slots, _, run, width = query_ref.shape
    rows = slots * run
    count = full_ref.shape[0]
    keys_total = count * run
    query = query_ref[:, 0].reshape(rows, width)[:, :wide]
    full = full_ref[:, 0].reshape(keys_total, width)
    key, value = full[:, wide : 2 * wide], full[:, 2 * wide :]
    grad = grad_ref[:, 0].reshape(rows, wide)
    lane_head = lax.broadcasted_iota(jnp.int32, (1, wide), 1) // HD

    @pl.when(step == 0)
    def _():
        key_sum[...] = jnp.zeros_like(key_sum)
        value_sum[...] = jnp.zeros_like(value_sum)

    query_grad = jnp.zeros((rows, wide), F32)
    key_grad = jnp.zeros((keys_total, wide), F32)
    value_grad = jnp.zeros((keys_total, wide), F32)
    for head in range(wide // HD):
        mine = lane_head == head
        probs_low = probs_ref[0, head]
        probs = probs_low.astype(F32)
        grad_probs = dot_nt(jnp.where(mine, grad, jnp.zeros_like(grad)), value)
        weighted = probs * grad_probs
        delta = jnp.sum(weighted, axis=1, keepdims=True)
        grad_scores = (weighted - probs * delta).astype(BF16)
        query_grad = jnp.where(mine, dot(grad_scores, key), query_grad)
        key_grad = jnp.where(mine, dot_tn(grad_scores, query), key_grad)
        value_grad = jnp.where(mine, dot_tn(probs_low, grad), value_grad)
    key_sum[...] += key_grad
    value_sum[...] += value_grad
    out_ref[pl.ds(step * slots, slots), 0, :, :wide] = (
        (query_grad * SCORE_SCALE).astype(BF16).reshape(slots, run, wide)
    )

    @pl.when(step == pl.num_programs(1) - 1)
    def _():
        out_ref[:, 0, :, wide : 2 * wide] = (
            (key_sum[...] * SCORE_SCALE).astype(BF16).reshape(count, run, wide)
        )
        out_ref[:, 0, :, 2 * wide :] = value_sum[...].astype(BF16).reshape(count, run, wide)


def attention_forward(qkv_rows, positions):
    count, _, run, width = qkv_rows.shape
    wide = width // 3
    heads = wide // HD
    length = count * run
    block = min(length, 512)
    slots = block // run
    steps = length // block
    by_sequence = positions.reshape(count, SEQS, run).transpose(1, 0, 2).reshape(SEQS, length)
    return pl.pallas_call(
        functools.partial(forward_kernel, wide=wide),
        grid=(SEQS, steps),
        in_specs=[
            pl.BlockSpec((1, block, 1), lambda s, i: (s, i, 0)),
            pl.BlockSpec((1, 1, length), lambda s, i: (s, 0, 0)),
            pl.BlockSpec((slots, 1, run, width), lambda s, i: (i, s, 0, 0)),
            pl.BlockSpec((count, 1, run, width), lambda s, i: (0, s, 0, 0)),
        ],
        out_specs=[
            pl.BlockSpec((slots, 1, run, wide), lambda s, i: (i, s, 0, 0)),
            pl.BlockSpec((1, heads, block, length), lambda s, i: (s, 0, i, 0)),
        ],
        out_shape=[
            jax.ShapeDtypeStruct((count, SEQS, run, wide), BF16),
            jax.ShapeDtypeStruct((SEQS, heads, length, length), BF16),
        ],
        compiler_params=pltpu.CompilerParams(vmem_limit_bytes=48 * 1024 * 1024),
        cost_estimate=SMALL_COST,
        name="attention_forward",
    )(by_sequence[:, :, None], by_sequence[:, None, :], qkv_rows, qkv_rows)


def attention_backward(qkv_rows, grad_context, probs):
    count, _, run, width = qkv_rows.shape
    wide = width // 3
    heads = wide // HD
    length = count * run
    block = min(length, 512)
    slots = block // run
    steps = length // block
    return pl.pallas_call(
        functools.partial(backward_kernel, wide=wide),
        grid=(SEQS, steps),
        in_specs=[
            pl.BlockSpec((slots, 1, run, width), lambda s, i: (i, s, 0, 0)),
            pl.BlockSpec((count, 1, run, width), lambda s, i: (0, s, 0, 0)),
            pl.BlockSpec((slots, 1, run, wide), lambda s, i: (i, s, 0, 0)),
            pl.BlockSpec((1, heads, block, length), lambda s, i: (s, 0, i, 0)),
        ],
        out_specs=pl.BlockSpec((count, 1, run, width), lambda s, i: (0, s, 0, 0)),
        out_shape=jax.ShapeDtypeStruct((count, SEQS, run, width), BF16),
        scratch_shapes=[pltpu.VMEM((length, wide), F32), pltpu.VMEM((length, wide), F32)],
        compiler_params=pltpu.CompilerParams(vmem_limit_bytes=48 * 1024 * 1024),
        cost_estimate=SMALL_COST,
        name="attention_backward",
    )(qkv_rows, qkv_rows, grad_context, probs)


def in_order(side, own, other, axis=0):
    first = jnp.where(side == 0, own, other)
    second = jnp.where(side == 0, other, own)
    return jnp.concatenate([first, second], axis=axis)


def normalize(values):
    centred = values - jnp.mean(values, axis=1, keepdims=True)
    spread = lax.rsqrt(jnp.mean(centred * centred, axis=1, keepdims=True) + NORM_EPS)
    return centred * spread, spread


def normalize_back(normal, spread, gain, grad):
    scaled = grad * gain
    along = jnp.mean(scaled * normal, axis=1, keepdims=True)
    return spread * (scaled - jnp.mean(scaled, axis=1, keepdims=True) - normal * along)


def first_rows(pieces, scalars, weight, gain, shift, bias):
    rows, width = pieces[0][0].shape
    steps = len(pieces)
    total = 2 * steps * rows
    columns = weight.shape[1]

    def kernel(marks, *refs):
        given, (w, g, s, b), outs = refs[: 2 * steps], refs[2 * steps : 2 * steps + 4], refs[-3:]
        for t in range(steps):

            @pl.when(pl.program_id(0) == t)
            def _(t=t):
                outs[0][...] = in_order(marks[0], given[2 * t][...], given[2 * t + 1][...])

        normal, _ = normalize(outs[0][...].astype(F32))
        outs[1][...] = normal.astype(BF16)
        scaled = (normal * g[...] + s[...]).astype(BF16)
        outs[2][...] = (dot(scaled, w[...]) + b[...]).astype(BF16)

    def block(width):
        return pl.BlockSpec((2 * rows, width), lambda t, marks: (marks[1 + t], 0))

    flat = [piece for pair in pieces for piece in pair]
    return call(
        kernel,
        [struct((total, width), BF16), struct((total, width), BF16), struct((total, columns), BF16)],
        [block(width), block(width), block(columns)],
        grid=(steps,),
        in_blocks=[whole((rows, width))] * (2 * steps)
        + [whole(weight.shape), whole((1, width)), whole((1, width)), whole((1, columns))],
        scalars=scalars,
        name="first_rows",
    )(*flat, weight, gain, shift, bias)


def second_rows(tokens_all, pieces, scalars, weight, bias, gain, shift):
    total, width = tokens_all.shape
    steps = len(pieces)
    wide = pieces[0][0].shape[1]
    own_rows = total // (2 * steps)
    rows = min(total, 512)
    inside = rows // own_rows

    def kernel(marks, tokens, *refs):
        given = refs[: 2 * steps]
        w, b, g, s, normed, own, context = refs[2 * steps :]
        for t in range(steps):
            pair = in_order(marks[0], given[2 * t][...], given[2 * t + 1][...], axis=1)
            begin = pl.multiple_of(marks[1 + t] * (2 * wide), 2 * wide)
            context[:, pl.ds(begin, 2 * wide)] = pair
        residual = tokens[...].astype(F32) + dot(context[...], w[...]) + b[...]
        normal, _ = normalize(residual)
        normed[...] = (normal * g[...] + s[...]).astype(BF16)

        mine = marks[1] * 2 + marks[0]
        for i in range(inside):

            @pl.when(pl.program_id(0) * inside + i == mine)
            def _(i=i):
                own[...] = residual[i * own_rows : (i + 1) * own_rows]

    return pl.pallas_call(
        kernel,
        grid_spec=pltpu.PrefetchScalarGridSpec(
            num_scalar_prefetch=1,
            grid=(total // rows,),
            in_specs=[pl.BlockSpec((rows, width), lambda i, marks: (i, 0))]
            + [pl.BlockSpec((rows, wide), lambda i, marks: (i, 0))] * (2 * steps)
            + [whole(weight.shape), whole((1, width)), whole((1, width)), whole((1, width))],
            out_specs=[
                pl.BlockSpec((rows, width), lambda i, marks: (i, 0)),
                whole((own_rows, width)),
            ],
            scratch_shapes=[pltpu.VMEM((rows, 2 * steps * wide), BF16)],
        ),
        out_shape=[struct((total, width), BF16), struct((own_rows, width), F32)],
        compiler_params=pltpu.CompilerParams(vmem_limit_bytes=48 * 1024 * 1024),
        cost_estimate=SMALL_COST,
        name="second_rows",
    )(scalars, tokens_all, *[piece for pair in pieces for piece in pair], weight, bias, gain, shift)


def hidden_rows(normed, cot, scalars, w_fc, w_proj, bias, kept, taken, rows):
    total, width = normed.shape
    hidden = w_fc.shape[1]
    many = len(taken)

    def kernel(marks, block, cot_ref, fc, proj, b, *refs):
        outs = refs[-2 - 2 * many :]
        z = dot(block[...], fc[...]) + b[...]
        tanh = jnp.tanh(0.7978845608028654 * (z + 0.044715 * z * z * z))
        half = 0.5 * (1.0 + tanh)
        slope = half + 0.5 * z * (1.0 - tanh * tanh) * 0.7978845608028654 * (
            1.0 + 3.0 * 0.044715 * z * z
        )
        outs[0][...] = (z * half).astype(BF16)
        grad = (dot(cot_ref[...], proj[...]) * slope).astype(BF16)
        outs[1][...] = grad
        part = dot_nt(grad, fc[...])
        mine = jnp.where(marks[0] == 0, part[:rows], part[rows:])
        other = jnp.where(marks[0] == 0, part[rows:], part[:rows]).astype(BF16)
        for i in range(many):

            @pl.when(pl.program_id(0) == i)
            def _(i=i):
                outs[2 + 2 * i][...] = mine
                outs[3 + 2 * i][...] = other

    def block(width):
        return pl.BlockSpec((2 * rows, width), lambda i, marks: (marks[1 + i], 0))

    operands = [normed, cot, w_fc, w_proj, bias]
    blocks = [block(width), block(width), whole(w_fc.shape), whole(w_proj.shape), whole((1, hidden))]
    alias = {}
    if kept is not None:
        alias = {1 + len(operands) + i: i for i in range(2)}
        operands += list(kept)
        blocks += [pl.BlockSpec(memory_space=pl.ANY)] * 2
    outs = call(
        kernel,
        [struct((total, hidden), BF16), struct((total, hidden), BF16)]
        + [struct((rows, width), dtype) for _ in taken for dtype in (F32, BF16)],
        [block(hidden), block(hidden)] + [whole((rows, width))] * (2 * many),
        grid=(many,),
        in_blocks=blocks,
        scalars=scalars,
        alias=alias,
        name="hidden_rows",
    )(*operands)
    return outs[:2], {t: (outs[2 + 2 * i], outs[3 + 2 * i]) for i, t in enumerate(taken)}


def turned_product(left, right, name):
    total, width = left.shape
    columns = right.shape[1]
    tile = 256

    def kernel(left_ref, right_ref, out_ref):
        out_ref[...] = dot_tn(left_ref[...], right_ref[...]).astype(BF16)

    return call(
        kernel,
        struct((width, columns), BF16),
        pl.BlockSpec((tile, columns), lambda i: (i, 0)),
        grid=(pl.cdiv(width, tile),),
        in_blocks=[pl.BlockSpec((total, tile), lambda i: (0, i)), whole(right.shape)],
        name=name,
    )(left, right)


def head_product(normal, grad, weight, gain, shift):
    total, width = normal.shape
    columns = grad.shape[1]
    tile = 256

    def kernel(left, right, w, g, s, out, gain_sum, shift_sum, grad_sum):
        @pl.when(pl.program_id(0) == 0)
        def _():
            grad_sum[...] = jnp.sum(right[...].astype(F32), axis=0, keepdims=True)

        raw = dot_tn(left[...], right[...])
        sums = grad_sum[...]
        low = w[...].astype(F32)
        gain_sum[...] = jnp.sum(raw * low, axis=1, keepdims=True)
        shift_sum[...] = jnp.sum(low * sums, axis=1, keepdims=True)
        out[...] = (raw * g[...] + s[...] * sums).astype(BF16)

    column = pl.BlockSpec((tile, 1), lambda i: (i, 0))
    return call(
        kernel,
        [
            struct((width, columns), BF16),
            struct((width, 1), F32),
            struct((width, 1), F32),
            struct((1, columns), F32),
        ],
        [pl.BlockSpec((tile, columns), lambda i: (i, 0)), column, column, whole((1, columns))],
        grid=(pl.cdiv(width, tile),),
        in_blocks=[
            pl.BlockSpec((total, tile), lambda i: (0, i)),
            whole(grad.shape),
            pl.BlockSpec((tile, columns), lambda i: (i, 0)),
            column,
            column,
        ],
        name="head_product",
    )(normal, grad, weight, gain, shift)


def ring_parts(left, right, scalars, steps, name):
    total, inner = left.shape
    width = right.shape[0]
    rows = total // (2 * steps)

    def kernel(marks, left_ref, right_ref, *outs):
        for t in range(steps):
            begin = pl.multiple_of(marks[1 + t] * (2 * rows), 2 * rows)
            part = dot_nt(left_ref[pl.ds(begin, 2 * rows)], right_ref[...])
            outs[2 * t][...] = jnp.where(marks[0] == 0, part[:rows], part[rows:])
            outs[2 * t + 1][...] = jnp.where(marks[0] == 0, part[rows:], part[:rows]).astype(BF16)

    outs = call(
        kernel,
        [struct((rows, width), dtype) for _ in range(steps) for dtype in (F32, BF16)],
        [whole((rows, width))] * (2 * steps),
        in_blocks=[whole(left.shape), whole(right.shape)],
        scalars=scalars,
        name=name,
    )(left, right)
    return [(outs[2 * t], outs[2 * t + 1]) for t in range(steps)]


def second_back(residual, terms, cotangent, gain, weight, count):
    rows, width = residual.shape
    wide = weight.shape[0] // count

    def kernel(res, mine, swapped, carried, cot, g, w, grad_ref, low_ref, sums_ref, out_ref):
        @pl.when(pl.program_id(0) == 0)
        def _():
            grad = mine[...] + swapped[...].astype(F32) + carried[...].astype(F32)
            normal, spread = normalize(res[...])
            total = cot[...].astype(F32) + normalize_back(normal, spread, g[...], grad)
            grad_ref[...] = total
            low = total.astype(BF16)
            low_ref[...] = low
            sums_ref[0:1] = jnp.sum(grad * normal, axis=0, keepdims=True)
            sums_ref[1:2] = jnp.sum(grad, axis=0, keepdims=True)
            sums_ref[2:3] = jnp.sum(low.astype(F32), axis=0, keepdims=True)
            sums_ref[3:4] = jnp.sum(cot[...].astype(F32), axis=0, keepdims=True)

        out_ref[0] = dot_nt(low_ref[...], w[...]).astype(BF16)

    row = whole((rows, width))
    return call(
        kernel,
        [
            struct((rows, width), F32),
            struct((rows, width), BF16),
            struct((4, width), F32),
            struct((count, rows, wide), BF16),
        ],
        [row, row, whole((4, width)), pl.BlockSpec((1, rows, wide), lambda i: (i, 0, 0))],
        grid=(count,),
        in_blocks=[row] * 5 + [whole((1, width)), pl.BlockSpec((wide, width), lambda i: (i, 0))],
        name="second_back",
    )(residual, *terms, cotangent, gain, weight)


def first_back(tokens, terms, residual_grad, gain):
    rows, width = tokens.shape

    def kernel(x, mine, swapped, carried, res, g, out_ref):
        grad = mine[...] + swapped[...].astype(F32) + carried[...].astype(F32)
        normal, spread = normalize(x[...].astype(F32))
        out_ref[...] = (res[...] + normalize_back(normal, spread, g[...], grad)).astype(BF16)

    row = whole((rows, width))
    return call(
        kernel,
        struct((rows, width), BF16),
        row,
        in_blocks=[row] * 5 + [whole((1, width))],
        name="first_back",
    )(tokens, *terms, residual_grad, gain)


def heads_rows(me, pieces, count, slots):
    rows, width = pieces[0].shape
    unit = math.gcd(rows, HD)

    def kernel(mark, *refs):
        out = refs[4]
        for h in range(HEADS, count * slots):
            place = ((h % count) * slots + h // count) * HD
            out[place : place + HD] = jnp.zeros((HD, width), BF16)
        for r in range(4):
            for piece in range(rows // unit):
                row = (mark[0] ^ r) * rows + piece * unit
                head = row // HD
                target = ((head % count) * slots + head // count) * HD + row % HD
                out[pl.ds(pl.multiple_of(target, unit), unit)] = refs[r][
                    piece * unit : (piece + 1) * unit
                ]

    return call(
        kernel,
        struct((count * slots * HD, width), BF16),
        whole((count * slots * HD, width)),
        in_blocks=[whole((rows, width))] * 4,
        scalars=me[None],
        name="heads_rows",
    )(*pieces)


def out_product(pieces, columns, scalars, count, slots):
    total, width = columns.shape
    wide = slots * HD
    steps = len(pieces)

    def kernel(marks, *refs):
        given, right, out = refs[: 2 * steps], refs[2 * steps], refs[-1]
        for t in range(steps):
            for b in range(2):
                owner = marks[1 + t] * 2 + (marks[0] if b == 0 else 1 - marks[0])
                value = dot_tn(given[2 * t + b][...], right[...]).astype(BF16)
                for slot in range(slots):
                    begin = pl.multiple_of((slot * count + owner) * HD, HD)
                    out[pl.ds(begin, HD)] = value[slot * HD : (slot + 1) * HD]

    return call(
        kernel,
        struct((slots * count * HD, width), BF16),
        whole((slots * count * HD, width)),
        in_blocks=[whole((total, wide))] * (2 * steps) + [whole(columns.shape)],
        scalars=scalars,
        name="out_product",
    )(*[piece for pair in pieces for piece in pair], columns)


def rows_product(left, right, name):
    total, inner = left.shape
    width = right.shape[0]
    block = min(total, 512)

    def kernel(left_ref, right_ref, out_ref):
        out_ref[...] = dot_nt(left_ref[...], right_ref[...]).astype(BF16)

    return call(
        kernel,
        struct((total, width), BF16),
        pl.BlockSpec((block, width), lambda i: (i, 0)),
        grid=(total // block,),
        in_blocks=[pl.BlockSpec((block, inner), lambda i: (i, 0)), whole(right.shape)],
        name=name,
    )(left, right)


def shards(
    tokens,
    cotangent,
    positions,
    qkv_weight,
    qkv_first,
    qkv_second,
    out_weight,
    out_first,
    out_second,
    fc_weight,
    fc_first,
    fc_second,
    proj_weight,
    proj_first,
    proj_second,
    small_weight,
    small_first,
    small_second,
):
    count = lax.axis_size("seq")
    ring = Ring(count)
    square = Square()
    me = lax.axis_index("seq")
    rows, width = tokens.shape
    seq_rows = rows // SEQS
    window = qkv_weight.shape[1]
    slots = -(-HEADS // count)
    wide = slots * HD
    small_count, small_width = small_weight.shape
    hidden = fc_weight.shape[1]
    all_rows = count * rows
    steps = ring.steps
    marks = jnp.stack([ring.side] + [ring.position(t) for t in range(steps)])
    tokens = by_rows(tokens)
    cotangent = by_rows(cotangent)

    token_tour = Tour(ring, tokens)
    token_tour.step()
    token_tour.step()
    pack, unpack, most = head_tables(count, width, window)
    pack_hot = one_hot(pick_row(pack, me), window)
    packed = jnp.einsum(
        "rc,cdl->drl",
        qkv_weight.astype(BF16),
        pack_hot.reshape(window, count, most),
        preferred_element_type=BF16,
    )
    depth = packed.shape[1]
    small_flat = jnp.concatenate(
        [
            small_weight.reshape(-1).astype(BF16),
            (positions // 32).astype(BF16),
            (positions % 32).astype(BF16),
        ]
    )
    small_depth = -(-small_flat.shape[0] // most)
    small_depth += -small_depth % 16
    small_flat = jnp.pad(small_flat, (0, small_depth * most - small_flat.shape[0]))
    small_pack = jnp.broadcast_to(
        small_flat.reshape(1, small_depth, most), (count, small_depth, most)
    )
    received = lax.all_to_all(jnp.concatenate([packed, small_pack], axis=1), "seq", 0, 0)
    received = after(received, token_tour.moved[0], token_tour.current)

    unpack_hot = one_hot(pick_row(unpack, me), 3 * wide)
    head_part = jnp.einsum(
        "srl,ksl->rk",
        received[:, :depth],
        unpack_hot.reshape(3 * wide, count, most),
        preferred_element_type=BF16,
    )
    token_tour.step()
    head_pieces = square.gather(head_part, token_tour.current, token_tour.moved[1])
    for t in range(3, steps):
        token_tour.step(*((head_part,) if t == steps - 1 else ()))
    w_head = square.place(after(head_pieces, token_tour.moved[2], token_tour.current))

    small_all = received[:, depth:].reshape(count, small_depth * most).astype(F32)
    small_rows = small_all[:, : small_count * small_width].reshape(count, small_count, small_width)
    small_rows = small_rows.transpose(1, 0, 2).reshape(small_count, width)
    pos_all = small_all[:, small_count * small_width :][:, : 2 * rows].reshape(count, 2, rows)
    pos_all = (pos_all[:, 0] * 32.0 + pos_all[:, 1]).astype(jnp.int32)

    def own_heads(row):
        padded = jnp.pad(row, (0, slots * count * HD - width)).reshape(slots, count, HD)
        return lax.dynamic_index_in_dim(padded, me, 1, keepdims=False).reshape(wide)

    head_bias = jnp.concatenate(
        [own_heads(small_rows[0]), jnp.zeros((wide,), F32), own_heads(small_rows[1])]
    )
    fc_bias = lax.dynamic_slice_in_dim(small_rows[3:7].reshape(-1), me * hidden, hidden, 0)
    gain_one, shift_one = small_rows[8][None], small_rows[9][None]
    gain_two, shift_two = small_rows[10][None], small_rows[11][None]

    ready = head_pieces[3]
    out_part = lax.all_gather(
        after(out_weight, head_part).astype(BF16), "seq", axis=1, tiled=True
    )
    cot_all = lax.all_gather(after(cotangent, ready, out_part), "seq", axis=0, tiled=True)
    fc_pieces = square.gather(after(fc_weight, ready).astype(BF16))
    proj_pieces = square.gather(after(proj_weight, fc_pieces[2]).T.astype(BF16))
    out_pieces = square.gather(after(by_rows(out_part), proj_pieces[2]))

    tokens_all, normal_all, qkv_rows = first_rows(
        token_tour.pieces, marks, w_head, gain_one, shift_one, head_bias[None]
    )
    qkv_all = qkv_rows.reshape(count, SEQS, seq_rows, 3 * wide)
    context, probs = attention_forward(qkv_all, pos_all)
    context = context.reshape(all_rows, wide)

    context_tour = Tour(ring, context)
    w_fc, w_proj = None, None
    for t in range(steps):
        if t == 1:
            context_tour.step(proj_pieces[2])
            w_fc = square.place(after(fc_pieces, context_tour.moved[0]))
        elif t == steps - 1:
            w_proj = square.place(after(proj_pieces, context_tour.moved[-2]))
            context_tour.step(out_pieces[2], w_fc)
        else:
            context_tour.step()
    w_out = heads_rows(square.me, out_pieces, count, slots)
    normed_all, residual = second_rows(
        tokens_all, context_tour.pieces, marks, w_out, small_rows[2][None], gain_two, shift_two
    )

    kept, parts = None, {}
    for taken in ([steps - 1], list(reversed(range(steps - 1)))):
        kept, more = hidden_rows(
            normed_all,
            cot_all,
            jnp.stack([ring.side] + [ring.position(t) for t in taken]),
            w_fc,
            w_proj,
            fc_bias[None],
            kept,
            taken,
            rows,
        )
        parts.update(more)
    hidden_low, grad_pre_low = kept
    grad_fold = Fold(ring, parts)
    grad_fold.beside(*parts[0])
    grad_fold.step()
    proj_sum = turned_product(after(cot_all, grad_fold.carried), hidden_low, "proj_product")
    grad_fold.beside(proj_sum)
    proj_grad = lax.psum_scatter(proj_sum, "dp", scatter_dimension=0, tiled=True).astype(F32)
    grad_fold.step()
    fc_sum = turned_product(after(normed_all, grad_fold.carried), grad_pre_low, "fc_product")
    grad_fold.beside(fc_sum)
    grad_bias_fc = jnp.sum(grad_pre_low.astype(F32), axis=0)
    for _ in range(3, steps):
        grad_fold.step()
    output_partial = rows_product(
        after(hidden_low, grad_fold.carried), w_proj, "output_product"
    )
    grad_fold.beside(output_partial, grad_bias_fc)
    fc_column = square.half_sum(after(fc_sum, output_partial))
    output_sum = lax.psum_scatter(
        after(output_partial, proj_grad), "seq", scatter_dimension=0, tiled=True
    )
    terms = grad_fold.terms
    grad_residual, grad_attn_low, row_sums, grad_context = second_back(
        residual, terms, cotangent, gain_two, w_out, count
    )

    grad_context = lax.all_to_all(grad_context, "seq", 0, 0)
    out_columns = out_weight.shape[1]
    attn_columns = after(grad_attn_low, grad_context)
    attn_columns = lax.all_to_all(
        attn_columns.reshape(rows, count, out_columns).transpose(1, 0, 2), "seq", 0, 0
    ).reshape(all_rows, out_columns)
    grad_qkv = attention_backward(
        qkv_all, grad_context.reshape(count, SEQS, seq_rows, wide), probs
    ).reshape(all_rows, 3 * wide)
    fc_grad = after(square.other_sum(fc_column), grad_qkv)
    parts = ring_parts(after(grad_qkv, attn_columns), w_head, marks, steps, "input_parts")
    input_fold = Fold(ring, parts)
    head_sum, grad_gain_one, grad_shift_one, grad_qkv_sum = head_product(
        after(normal_all, *parts[0]), grad_qkv, w_head, small_rows[8][:, None], small_rows[9][:, None]
    )
    input_fold.beside(head_sum)
    input_fold.step()

    attn_columns = after(attn_columns, input_fold.carried)
    out_sum = out_product(context_tour.pieces, attn_columns, marks, count, slots)[:width]
    input_fold.beside(out_sum)
    small_begin = input_fold.carried
    head_column = square.half_sum(after(head_sum, input_fold.carried))
    out_column = square.half_sum(out_sum)
    input_fold.step()
    fc_new = adam_update(
        fc_weight, fc_first, fc_second, after(fc_grad, input_fold.carried), 0.02, 0.1
    )
    input_fold.beside(fc_new[0], head_column, out_column)
    for _ in range(3, steps):
        input_fold.step()
    input_fold.beside(output_sum)
    head_grad = square.other_sum(head_column).astype(BF16)
    out_grad = square.other_sum(out_column)
    input_grad = first_back(tokens, input_fold.terms, grad_residual, gain_one)

    unpack_back = unpack_hot.reshape(3 * wide, count, most)
    head_packed = jnp.einsum("rk,ksl->srl", head_grad, unpack_back, preferred_element_type=BF16)
    head_back = lax.all_to_all(head_packed, "seq", 0, 0)
    qkv_grad = jnp.einsum(
        "drl,cdl->rc",
        head_back,
        pack_hot.reshape(window, count, most),
        preferred_element_type=F32,
    )
    output = (residual + output_sum.astype(F32) + small_rows[7]).astype(BF16)

    def place_heads(values):
        spread = (jnp.arange(count) == me).astype(F32)[None, :, None]
        placed = values.reshape(slots, 1, HD) * spread
        return placed.reshape(-1)[:width]

    grad_bias_fc = grad_bias_fc[None, :] * (jnp.arange(count) == me).astype(F32)[:, None]
    grad_qkv_sum = after(grad_qkv_sum, small_begin, head_column)[0]
    grad_small = jnp.concatenate(
        [
            place_heads(grad_qkv_sum[:wide])[None],
            place_heads(grad_qkv_sum[2 * wide :])[None],
            row_sums[2:3],
            grad_bias_fc.reshape(-1, width),
            row_sums[3:4],
            grad_gain_one[:, 0][None],
            grad_shift_one[:, 0][None],
            row_sums[0:1],
            row_sums[1:2],
        ],
        axis=0,
    )
    small_sent = grad_small.astype(BF16).reshape(small_count, count, small_width)
    small_part = jnp.sum(
        lax.all_to_all(small_sent.transpose(1, 0, 2), "seq", 0, 0).astype(F32), axis=0
    )
    small_grad = square.sum(small_part)

    qkv_new = adam_update(qkv_weight, qkv_first, qkv_second, qkv_grad, 0.02, 0.1)
    out_new = adam_update(out_weight, out_first, out_second, out_grad, 0.3, 0.1)
    proj_new = adam_update(
        proj_weight.T, proj_first.T, proj_second.T, proj_grad, 0.02, 0.1
    )
    proj_new = [value.T for value in proj_new]
    small_new = adam_update(small_weight, small_first, small_second, small_grad, 0.3, 0.0)
    return (
        output,
        input_grad,
        *qkv_new,
        *out_new,
        *fc_new,
        *proj_new,
        *small_new,
        small_grad[7],
    )


def solution(mesh):
    rows = P(("dp", "seq"), None)
    matrix = P("dp", "seq")
    turned = P("seq", "dp")
    small = P(None, "seq")
    in_specs = (
        (rows, rows, P(("dp", "seq"))) + (matrix,) * 9 + (turned,) * 3 + (small,) * 3
    )
    out_specs = (rows, rows) + (matrix,) * 9 + (turned,) * 3 + (small,) * 3 + (P("seq"),)
    return jax.shard_map(shards, mesh=mesh, in_specs=in_specs, out_specs=out_specs, check_vma=False)
```

```python
import functools
import math

import jax
import jax.numpy as jnp
import numpy as np
from jax import lax
from jax.experimental import pallas as pl
from jax.experimental.layout import Layout, with_layout_constraint
from jax.experimental.pallas import tpu as pltpu
from jax.sharding import PartitionSpec as P

HEADS = 25
HD = 64
SEQS = 2
STEP = 10

NORM_EPS = 1e-05
SCORE_SCALE = 0.125
MASKED_SCORE = -1e30
BETA_ONE = 0.9
BETA_TWO = 0.95
ADAM_EPS = 1e-08
BF16 = jnp.bfloat16
F32 = jnp.float32
SMALL_COST = pl.CostEstimate(flops=1024, bytes_accessed=1024, transcendentals=0)


def adam_update(weight, first_moment, second, gradient, step_rate, decay_rate):
    moment_new = BETA_ONE * first_moment + (1.0 - BETA_ONE) * gradient
    second_new = BETA_TWO * second + (1.0 - BETA_TWO) * gradient * gradient
    direction = (
        moment_new
        / (1.0 - BETA_ONE**STEP)
        / (jnp.sqrt(second_new / (1.0 - BETA_TWO**STEP)) + ADAM_EPS)
    )
    return (moment_new, second_new, weight - step_rate * (direction + decay_rate * weight))


def dot(left, right):
    return jnp.dot(left, right, preferred_element_type=F32)


def dot_nt(left, right):
    return lax.dot_general(left, right, (((1,), (1,)), ((), ())), preferred_element_type=F32)


def dot_tn(left, right):
    return lax.dot_general(left, right, (((0,), (0,)), ((), ())), preferred_element_type=F32)


def after(value, *others):
    return lax.optimization_barrier((value,) + others)[0]


def by_rows(value):
    return with_layout_constraint(value, Layout(major_to_minor=(0, 1)))


def call(
    kernel, out, blocks, grid=None, in_blocks=None, scalars=None, alias=None, scratch=(), name=None
):
    operands = 0 if scalars is None else 1
    spec = dict(
        in_specs=in_blocks,
        out_specs=blocks,
        grid=grid or (1,),
        scratch_shapes=list(scratch),
    )
    if operands:
        spec = dict(grid_spec=pltpu.PrefetchScalarGridSpec(num_scalar_prefetch=1, **spec))
    run = pl.pallas_call(
        kernel,
        out_shape=out,
        input_output_aliases=alias or {},
        compiler_params=pltpu.CompilerParams(vmem_limit_bytes=48 * 1024 * 1024),
        cost_estimate=SMALL_COST,
        name=name,
        **spec,
    )
    if operands:
        return lambda *given: run(scalars, *given)
    return run


def whole(shape):
    return pl.BlockSpec(shape, lambda *_: (0,) * len(shape))


def struct(shape, dtype):
    return jax.ShapeDtypeStruct(shape, dtype)


class Ring:
    def __init__(self, count):
        self.sides = 2
        self.steps = count // 2
        steps = self.steps
        self.swap = [(j, j ^ 1) for j in range(count)]
        self.ahead = [(z * 2 + x, ((z + 1) % steps) * 2 + x) for z in range(steps) for x in range(2)]
        self.behind = [(dst, src) for src, dst in self.ahead]
        me = lax.axis_index("seq")
        self.place, self.side = me // 2, me % 2

    def position(self, t):
        return (self.place + self.steps - t) % self.steps

    def gather(self, block):
        tour = Tour(self, block)
        for _ in range(self.steps):
            tour.step()
        return tour


class Tour:
    def __init__(self, ring, block, back=False):
        self.ring, self.current, self.back = ring, block, back
        self.pieces = [None] * ring.steps
        self.moved = []

    def step(self, *begin):
        ring, t = self.ring, len(self.moved)
        if begin:
            self.current = after(self.current, *begin)
        if t:
            sent = after(self.current, self.moved[-2]) if t > 1 else self.current
            self.current = lax.ppermute(sent, "seq", ring.behind if self.back else ring.ahead)
        crossing = after(self.current, self.moved[-1]) if t > 1 else self.current
        other = lax.ppermute(crossing, "seq", ring.swap)
        self.pieces[-t if self.back else t] = (self.current, other)
        self.moved.append(other)


class Fold:
    def __init__(self, ring, parts):
        self.ring, self.parts = ring, parts
        self.terms, self.count, self.carried = None, 0, None
        self.step()

    def step(self):
        ring = self.ring
        mine, other = self.parts[ring.steps - 1 - self.count]
        self.count += 1
        sent = None
        if self.terms is not None:
            sent = sum(term.astype(F32) for term in self.terms).astype(BF16)
            self.carried = sent
            other = after(other, sent)
        self.terms = [mine, lax.ppermute(other, "seq", ring.swap)]
        if sent is not None:
            self.terms.append(lax.ppermute(sent, "seq", ring.behind))

    def beside(self, *work):
        self.terms = list(lax.optimization_barrier((tuple(self.terms),) + work)[0])


class Square:
    def __init__(self):
        me = lax.axis_index("dp")
        self.me, self.far, self.near = me, me // 2, me % 2
        self.far_swap = [(j, j ^ 2) for j in range(4)]
        self.near_swap = [(j, j ^ 1) for j in range(4)]

    def gather(self, block, *begin):
        near = lax.ppermute(block, "dp", self.near_swap)
        far = lax.ppermute(block, "dp", self.far_swap)
        far = after(far, *begin) if begin else far
        return (block, near, far, lax.ppermute(far, "dp", self.near_swap))

    def place(self, pieces):
        rows, width = pieces[0].shape

        def kernel(me, *refs):
            for r in range(4):
                begin = pl.multiple_of((me[0] ^ r) * rows, 16)
                refs[4][pl.ds(begin, rows)] = refs[r][...]

        return call(
            kernel,
            struct((4 * rows, width), BF16),
            whole((4 * rows, width)),
            in_blocks=[whole((rows, width))] * 4,
            scalars=self.me[None],
            name="place_rows",
        )(*pieces)

    def half_sum(self, partial):
        parts = partial.reshape((2, 2, partial.shape[0] // 4) + partial.shape[1:])
        mine = lax.dynamic_index_in_dim(parts, self.near, 1, keepdims=False)
        other = lax.dynamic_index_in_dim(parts, 1 - self.near, 1, keepdims=False)
        return mine.astype(F32) + lax.ppermute(other, "dp", self.near_swap).astype(F32)

    def other_sum(self, column):
        mine = lax.dynamic_index_in_dim(column, self.far, 0, keepdims=False)
        other = lax.dynamic_index_in_dim(column, 1 - self.far, 0, keepdims=False)
        return mine + lax.ppermute(other.astype(BF16), "dp", self.far_swap).astype(F32)

    def sum(self, values):
        values = values + lax.ppermute(values, "dp", self.near_swap)
        return values + lax.ppermute(values, "dp", self.far_swap)


def head_tables(count, model_width, window):
    slots = -(-HEADS // count)
    wide = slots * HD
    lists = [[[] for _ in range(count)] for _ in range(count)]
    for column in range(3 * model_width):
        src, local = divmod(column, window)
        part, within = divmod(column, model_width)
        head, lane = divmod(within, HD)
        dst, slot = head % count, head // count
        lists[src][dst].append((local, part * wide + slot * HD + lane))
    most = max(len(entry) for row in lists for entry in row)
    most = -(-most // 64) * 64
    pack = np.full((count, count * most), -1, np.int32)
    unpack = np.full((count, count * most), -1, np.int32)
    for src in range(count):
        for dst in range(count):
            for place, (local, target) in enumerate(lists[src][dst]):
                pack[src, dst * most + place] = local
                unpack[dst, src * most + place] = target
    return pack, unpack, most


def pick_row(table, index):
    return lax.dynamic_index_in_dim(jnp.asarray(table), index, 0, keepdims=False)


def one_hot(rows, size):
    return (lax.broadcasted_iota(jnp.int32, (size, rows.shape[0]), 0) == rows[None, :]).astype(BF16)


def forward_kernel(pos_col, pos_row, query_ref, full_ref, context_ref, probs_ref, *, wide):
    slots, _, run, width = query_ref.shape
    rows = slots * run
    keys_total = full_ref.shape[0] * run
    query = query_ref[:, 0].reshape(rows, width)[:, :wide]
    full = full_ref[:, 0].reshape(keys_total, width)
    key, value = full[:, wide : 2 * wide], full[:, 2 * wide :]
    seen = pos_row[0] <= pos_col[0]
    lane_head = lax.broadcasted_iota(jnp.int32, (1, wide), 1) // HD
    context = jnp.zeros((rows, wide), F32)
    for head in range(wide // HD):
        mine = lane_head == head
        scores = dot_nt(jnp.where(mine, query, jnp.zeros_like(query)), key) * SCORE_SCALE
        scores = jnp.where(seen, scores, MASKED_SCORE)
        top = jnp.max(scores, axis=1, keepdims=True)
        raw = jnp.exp(scores - top)
        probs = (raw * (1.0 / jnp.sum(raw, axis=1, keepdims=True))).astype(BF16)
        probs_ref[0, head] = probs
        context = jnp.where(mine, dot(probs, value), context)
    context_ref[:, 0] = context.astype(BF16).reshape(slots, run, wide)


def backward_kernel(query_ref, full_ref, grad_ref, probs_ref, out_ref, key_sum, value_sum, *, wide):
    step = pl.program_id(1)
    slots, _, run, width = query_ref.shape
    rows = slots * run
    count = full_ref.shape[0]
    keys_total = count * run
    query = query_ref[:, 0].reshape(rows, width)[:, :wide]
    full = full_ref[:, 0].reshape(keys_total, width)
    key, value = full[:, wide : 2 * wide], full[:, 2 * wide :]
    grad = grad_ref[:, 0].reshape(rows, wide)
    lane_head = lax.broadcasted_iota(jnp.int32, (1, wide), 1) // HD

    @pl.when(step == 0)
    def _():
        key_sum[...] = jnp.zeros_like(key_sum)
        value_sum[...] = jnp.zeros_like(value_sum)

    query_grad = jnp.zeros((rows, wide), F32)
    key_grad = jnp.zeros((keys_total, wide), F32)
    value_grad = jnp.zeros((keys_total, wide), F32)
    for head in range(wide // HD):
        mine = lane_head == head
        probs_low = probs_ref[0, head]
        probs = probs_low.astype(F32)
        grad_probs = dot_nt(jnp.where(mine, grad, jnp.zeros_like(grad)), value)
        weighted = probs * grad_probs
        delta = jnp.sum(weighted, axis=1, keepdims=True)
        grad_scores = (weighted - probs * delta).astype(BF16)
        query_grad = jnp.where(mine, dot(grad_scores, key), query_grad)
        key_grad = jnp.where(mine, dot_tn(grad_scores, query), key_grad)
        value_grad = jnp.where(mine, dot_tn(probs_low, grad), value_grad)
    key_sum[...] += key_grad
    value_sum[...] += value_grad
    out_ref[pl.ds(step * slots, slots), 0, :, :wide] = (
        (query_grad * SCORE_SCALE).astype(BF16).reshape(slots, run, wide)
    )

    @pl.when(step == pl.num_programs(1) - 1)
    def _():
        out_ref[:, 0, :, wide : 2 * wide] = (
            (key_sum[...] * SCORE_SCALE).astype(BF16).reshape(count, run, wide)
        )
        out_ref[:, 0, :, 2 * wide :] = value_sum[...].astype(BF16).reshape(count, run, wide)


def attention_forward(qkv_rows, positions):
    count, _, run, width = qkv_rows.shape
    wide = width // 3
    heads = wide // HD
    length = count * run
    block = min(length, 512)
    slots = block // run
    steps = length // block
    by_sequence = positions.reshape(count, SEQS, run).transpose(1, 0, 2).reshape(SEQS, length)
    return pl.pallas_call(
        functools.partial(forward_kernel, wide=wide),
        grid=(SEQS, steps),
        in_specs=[
            pl.BlockSpec((1, block, 1), lambda s, i: (s, i, 0)),
            pl.BlockSpec((1, 1, length), lambda s, i: (s, 0, 0)),
            pl.BlockSpec((slots, 1, run, width), lambda s, i: (i, s, 0, 0)),
            pl.BlockSpec((count, 1, run, width), lambda s, i: (0, s, 0, 0)),
        ],
        out_specs=[
            pl.BlockSpec((slots, 1, run, wide), lambda s, i: (i, s, 0, 0)),
            pl.BlockSpec((1, heads, block, length), lambda s, i: (s, 0, i, 0)),
        ],
        out_shape=[
            jax.ShapeDtypeStruct((count, SEQS, run, wide), BF16),
            jax.ShapeDtypeStruct((SEQS, heads, length, length), BF16),
        ],
        compiler_params=pltpu.CompilerParams(vmem_limit_bytes=48 * 1024 * 1024),
        cost_estimate=SMALL_COST,
        name="attention_forward",
    )(by_sequence[:, :, None], by_sequence[:, None, :], qkv_rows, qkv_rows)


def attention_backward(qkv_rows, grad_context, probs):
    count, _, run, width = qkv_rows.shape
    wide = width // 3
    heads = wide // HD
    length = count * run
    block = min(length, 512)
    slots = block // run
    steps = length // block
    return pl.pallas_call(
        functools.partial(backward_kernel, wide=wide),
        grid=(SEQS, steps),
        in_specs=[
            pl.BlockSpec((slots, 1, run, width), lambda s, i: (i, s, 0, 0)),
            pl.BlockSpec((count, 1, run, width), lambda s, i: (0, s, 0, 0)),
            pl.BlockSpec((slots, 1, run, wide), lambda s, i: (i, s, 0, 0)),
            pl.BlockSpec((1, heads, block, length), lambda s, i: (s, 0, i, 0)),
        ],
        out_specs=pl.BlockSpec((count, 1, run, width), lambda s, i: (0, s, 0, 0)),
        out_shape=jax.ShapeDtypeStruct((count, SEQS, run, width), BF16),
        scratch_shapes=[pltpu.VMEM((length, wide), F32), pltpu.VMEM((length, wide), F32)],
        compiler_params=pltpu.CompilerParams(vmem_limit_bytes=48 * 1024 * 1024),
        cost_estimate=SMALL_COST,
        name="attention_backward",
    )(qkv_rows, qkv_rows, grad_context, probs)


CHUNK = 32


def in_chunks(rows, body):
    def step(i, carry):
        body(pl.ds(pl.multiple_of(i * CHUNK, CHUNK), CHUNK))
        return carry

    lax.fori_loop(0, rows // CHUNK, step, 0)


def in_order(side, own, other, axis=0):
    first = jnp.where(side == 0, own, other)
    second = jnp.where(side == 0, other, own)
    return jnp.concatenate([first, second], axis=axis)


def normalize(values):
    centred = values - jnp.mean(values, axis=1, keepdims=True)
    spread = lax.rsqrt(jnp.mean(centred * centred, axis=1, keepdims=True) + NORM_EPS)
    return centred * spread, spread


def normalize_back(normal, spread, gain, grad):
    scaled = grad * gain
    along = jnp.mean(scaled * normal, axis=1, keepdims=True)
    return spread * (scaled - jnp.mean(scaled, axis=1, keepdims=True) - normal * along)


def first_rows(pieces, scalars, weight, gain, shift, bias):
    rows, width = pieces[0][0].shape
    steps = len(pieces)
    total = 2 * steps * rows
    columns = weight.shape[1]

    def kernel(marks, *refs):
        given, (w, g, s, b) = refs[: 2 * steps], refs[2 * steps : 2 * steps + 4]
        outs, scaled = refs[-4:-1], refs[-1]
        for t in range(steps):

            @pl.when(pl.program_id(0) == t)
            def _(t=t):
                outs[0][...] = in_order(marks[0], given[2 * t][...], given[2 * t + 1][...])

        def body(part):
            normal, _ = normalize(outs[0][part].astype(F32))
            outs[1][part] = normal.astype(BF16)
            scaled[part] = (normal * g[...] + s[...]).astype(BF16)

        in_chunks(2 * rows, body)
        outs[2][...] = (dot(scaled[...], w[...]) + b[...]).astype(BF16)

    def block(width):
        return pl.BlockSpec((2 * rows, width), lambda t, marks: (marks[1 + t], 0))

    flat = [piece for pair in pieces for piece in pair]
    return call(
        kernel,
        [struct((total, width), BF16), struct((total, width), BF16), struct((total, columns), BF16)],
        [block(width), block(width), block(columns)],
        grid=(steps,),
        in_blocks=[whole((rows, width))] * (2 * steps)
        + [whole(weight.shape), whole((1, width)), whole((1, width)), whole((1, columns))],
        scalars=scalars,
        scratch=[pltpu.VMEM((2 * rows, width), BF16)],
        name="first_rows",
    )(*flat, weight, gain, shift, bias)


def second_rows(tokens_all, pieces, scalars, weight, bias, gain, shift):
    total, width = tokens_all.shape
    steps = len(pieces)
    wide = pieces[0][0].shape[1]
    own_rows = total // (2 * steps)
    rows = min(total, 512)
    inside = rows // own_rows

    def kernel(marks, tokens, *refs):
        given = refs[: 2 * steps]
        w, b, g, s, normed, own, context, total_ref = refs[2 * steps :]
        for t in range(steps):
            pair = in_order(marks[0], given[2 * t][...], given[2 * t + 1][...], axis=1)
            begin = pl.multiple_of(marks[1 + t] * (2 * wide), 2 * wide)
            context[:, pl.ds(begin, 2 * wide)] = pair
        total_ref[...] = dot(context[...], w[...])

        def body(part):
            residual = tokens[part].astype(F32) + total_ref[part] + b[...]
            total_ref[part] = residual
            normal, _ = normalize(residual)
            normed[part] = (normal * g[...] + s[...]).astype(BF16)

        in_chunks(rows, body)
        mine = marks[1] * 2 + marks[0]
        for i in range(inside):

            @pl.when(pl.program_id(0) * inside + i == mine)
            def _(i=i):
                own[...] = total_ref[i * own_rows : (i + 1) * own_rows]

    return pl.pallas_call(
        kernel,
        grid_spec=pltpu.PrefetchScalarGridSpec(
            num_scalar_prefetch=1,
            grid=(total // rows,),
            in_specs=[pl.BlockSpec((rows, width), lambda i, marks: (i, 0))]
            + [pl.BlockSpec((rows, wide), lambda i, marks: (i, 0))] * (2 * steps)
            + [whole(weight.shape), whole((1, width)), whole((1, width)), whole((1, width))],
            out_specs=[
                pl.BlockSpec((rows, width), lambda i, marks: (i, 0)),
                whole((own_rows, width)),
            ],
            scratch_shapes=[
                pltpu.VMEM((rows, 2 * steps * wide), BF16),
                pltpu.VMEM((rows, width), F32),
            ],
        ),
        out_shape=[struct((total, width), BF16), struct((own_rows, width), F32)],
        compiler_params=pltpu.CompilerParams(vmem_limit_bytes=48 * 1024 * 1024),
        cost_estimate=SMALL_COST,
        name="second_rows",
    )(scalars, tokens_all, *[piece for pair in pieces for piece in pair], weight, bias, gain, shift)


def hidden_rows(normed, pairs, scalars, w_fc, w_proj, bias, kept, taken, rows):
    total, width = normed.shape
    hidden = w_fc.shape[1]
    many = len(taken)

    def kernel(marks, block, *refs):
        given, (fc, proj, b) = refs[: 2 * many], refs[2 * many : 2 * many + 3]
        act_ref, grad_ref, cot_ref = refs[-5 - 2 * many : -2 - 2 * many]
        parts, before, back = refs[-2 - 2 * many : -2], refs[-2], refs[-1]
        for i in range(many):

            @pl.when(pl.program_id(0) == i)
            def _(i=i):
                cot_ref[...] = in_order(marks[0], given[2 * i][...], given[2 * i + 1][...])

        before[...] = dot(block[...], fc[...])
        back[...] = dot(cot_ref[...], proj[...])

        def body(part):
            z = before[part] + b[...]
            square = z * z
            tanh = jnp.tanh(0.7978845608028654 * (z + 0.044715 * (square * z)))
            half = 0.5 * (1.0 + tanh)
            slope = half + 0.5 * z * (1.0 - tanh * tanh) * (
                0.7978845608028654 + (0.7978845608028654 * 3.0 * 0.044715) * square
            )
            act_ref[part] = (z * half).astype(BF16)
            grad_ref[part] = (back[part] * slope).astype(BF16)

        in_chunks(2 * rows, body)
        part = dot_nt(grad_ref[...], fc[...])
        mine = jnp.where(marks[0] == 0, part[:rows], part[rows:])
        other = jnp.where(marks[0] == 0, part[rows:], part[:rows]).astype(BF16)
        for i in range(many):

            @pl.when(pl.program_id(0) == i)
            def _(i=i):
                parts[2 * i][...] = mine
                parts[2 * i + 1][...] = other

    def block(width):
        return pl.BlockSpec((2 * rows, width), lambda i, marks: (marks[1 + i], 0))

    operands = [normed] + [piece for pair in pairs for piece in pair] + [w_fc, w_proj, bias]
    blocks = [block(width)] + [whole((rows, width))] * (2 * many)
    blocks += [whole(w_fc.shape), whole(w_proj.shape), whole((1, hidden))]
    alias = {}
    if kept is not None:
        alias = {1 + len(operands) + i: i for i in range(3)}
        operands += list(kept)
        blocks += [pl.BlockSpec(memory_space=pl.ANY)] * 3
    outs = call(
        kernel,
        [struct((total, hidden), BF16), struct((total, hidden), BF16), struct((total, width), BF16)]
        + [struct((rows, width), dtype) for _ in taken for dtype in (F32, BF16)],
        [block(hidden), block(hidden), block(width)] + [whole((rows, width))] * (2 * many),
        grid=(many,),
        in_blocks=blocks,
        scalars=scalars,
        alias=alias,
        scratch=[pltpu.VMEM((2 * rows, hidden), F32)] * 2,
        name="hidden_rows",
    )(*operands)
    return outs[:3], {t: (outs[3 + 2 * i], outs[4 + 2 * i]) for i, t in enumerate(taken)}


def turned_product(left, right, name):
    total, width = left.shape
    columns = right.shape[1]
    tile = 256

    def kernel(left_ref, right_ref, out_ref):
        out_ref[...] = dot(left_ref[...].T, right_ref[...]).astype(BF16)

    return call(
        kernel,
        struct((width, columns), BF16),
        pl.BlockSpec((tile, columns), lambda i: (i, 0)),
        grid=(pl.cdiv(width, tile),),
        in_blocks=[pl.BlockSpec((total, tile), lambda i: (0, i)), whole(right.shape)],
        name=name,
    )(left, right)


def head_product(normal, grad, weight, gain, shift):
    total, width = normal.shape
    columns = grad.shape[1]
    tile = 256

    def kernel(left, right, w, g, s, out, gain_sum, shift_sum, grad_sum):
        @pl.when(pl.program_id(0) == 0)
        def _():
            grad_sum[...] = jnp.sum(right[...].astype(F32), axis=0, keepdims=True)

        raw = dot(left[...].T, right[...])
        sums = grad_sum[...]
        low = w[...].astype(F32)
        gain_sum[...] = jnp.sum(raw * low, axis=1, keepdims=True)
        shift_sum[...] = jnp.sum(low * sums, axis=1, keepdims=True)
        out[...] = (raw * g[...] + s[...] * sums).astype(BF16)

    column = pl.BlockSpec((tile, 1), lambda i: (i, 0))
    return call(
        kernel,
        [
            struct((width, columns), BF16),
            struct((width, 1), F32),
            struct((width, 1), F32),
            struct((1, columns), F32),
        ],
        [pl.BlockSpec((tile, columns), lambda i: (i, 0)), column, column, whole((1, columns))],
        grid=(pl.cdiv(width, tile),),
        in_blocks=[
            pl.BlockSpec((total, tile), lambda i: (0, i)),
            whole(grad.shape),
            pl.BlockSpec((tile, columns), lambda i: (i, 0)),
            column,
            column,
        ],
        name="head_product",
    )(normal, grad, weight, gain, shift)


def ring_parts(left, right, scalars, steps, name):
    total, inner = left.shape
    width = right.shape[0]
    rows = total // (2 * steps)

    def kernel(marks, left_ref, right_ref, *outs):
        for t in range(steps):
            begin = pl.multiple_of(marks[1 + t] * (2 * rows), 2 * rows)
            part = dot_nt(left_ref[pl.ds(begin, 2 * rows)], right_ref[...])
            outs[2 * t][...] = jnp.where(marks[0] == 0, part[:rows], part[rows:])
            outs[2 * t + 1][...] = jnp.where(marks[0] == 0, part[rows:], part[:rows]).astype(BF16)

    outs = call(
        kernel,
        [struct((rows, width), dtype) for _ in range(steps) for dtype in (F32, BF16)],
        [whole((rows, width))] * (2 * steps),
        in_blocks=[whole(left.shape), whole(right.shape)],
        scalars=scalars,
        name=name,
    )(left, right)
    return [(outs[2 * t], outs[2 * t + 1]) for t in range(steps)]


def second_back(residual, terms, cotangent, gain, weight, count):
    rows, width = residual.shape
    wide = weight.shape[0] // count

    def kernel(res, mine, swapped, carried, cot, g, w, grad_ref, low_ref, sums_ref, out_ref):
        @pl.when(pl.program_id(0) == 0)
        def _():
            sums_ref[...] = jnp.zeros_like(sums_ref)

            def body(part):
                grad = mine[part] + swapped[part].astype(F32) + carried[part].astype(F32)
                normal, spread = normalize(res[part])
                given = cot[part].astype(F32)
                total = given + normalize_back(normal, spread, g[...], grad)
                grad_ref[part] = total
                low = total.astype(BF16)
                low_ref[part] = low
                sums_ref[0:1] += jnp.sum(grad * normal, axis=0, keepdims=True)
                sums_ref[1:2] += jnp.sum(grad, axis=0, keepdims=True)
                sums_ref[2:3] += jnp.sum(low.astype(F32), axis=0, keepdims=True)
                sums_ref[3:4] += jnp.sum(given, axis=0, keepdims=True)

            in_chunks(rows, body)

        out_ref[0] = dot_nt(low_ref[...], w[...]).astype(BF16)

    row = whole((rows, width))
    return call(
        kernel,
        [
            struct((rows, width), F32),
            struct((rows, width), BF16),
            struct((4, width), F32),
            struct((count, rows, wide), BF16),
        ],
        [row, row, whole((4, width)), pl.BlockSpec((1, rows, wide), lambda i: (i, 0, 0))],
        grid=(count,),
        in_blocks=[row] * 5 + [whole((1, width)), pl.BlockSpec((wide, width), lambda i: (i, 0))],
        name="second_back",
    )(residual, *terms, cotangent, gain, weight)


def first_back(tokens, terms, residual_grad, gain):
    rows, width = tokens.shape

    def kernel(x, mine, swapped, carried, res, g, out_ref):
        def body(part):
            grad = mine[part] + swapped[part].astype(F32) + carried[part].astype(F32)
            normal, spread = normalize(x[part].astype(F32))
            out_ref[part] = (res[part] + normalize_back(normal, spread, g[...], grad)).astype(BF16)

        in_chunks(rows, body)

    row = whole((rows, width))
    return call(
        kernel,
        struct((rows, width), BF16),
        row,
        in_blocks=[row] * 5 + [whole((1, width))],
        name="first_back",
    )(tokens, *terms, residual_grad, gain)


def heads_rows(me, pieces, count, slots):
    rows, width = pieces[0].shape
    unit = math.gcd(rows, HD)

    def kernel(mark, *refs):
        out = refs[4]
        for h in range(HEADS, count * slots):
            place = ((h % count) * slots + h // count) * HD
            out[place : place + HD] = jnp.zeros((HD, width), BF16)
        for r in range(4):
            for piece in range(rows // unit):
                row = (mark[0] ^ r) * rows + piece * unit
                head = row // HD
                target = ((head % count) * slots + head // count) * HD + row % HD
                out[pl.ds(pl.multiple_of(target, unit), unit)] = refs[r][
                    piece * unit : (piece + 1) * unit
                ]

    return call(
        kernel,
        struct((count * slots * HD, width), BF16),
        whole((count * slots * HD, width)),
        in_blocks=[whole((rows, width))] * 4,
        scalars=me[None],
        name="heads_rows",
    )(*pieces)


def out_product(pieces, columns, scalars, count, slots):
    total, width = columns.shape
    wide = slots * HD
    steps = len(pieces)

    def kernel(marks, *refs):
        given, right, out = refs[: 2 * steps], refs[2 * steps], refs[-1]
        for t in range(steps):
            for b in range(2):
                owner = marks[1 + t] * 2 + (marks[0] if b == 0 else 1 - marks[0])
                value = dot_tn(given[2 * t + b][...], right[...]).astype(BF16)
                for slot in range(slots):
                    begin = pl.multiple_of((slot * count + owner) * HD, HD)
                    out[pl.ds(begin, HD)] = value[slot * HD : (slot + 1) * HD]

    return call(
        kernel,
        struct((slots * count * HD, width), BF16),
        whole((slots * count * HD, width)),
        in_blocks=[whole((total, wide))] * (2 * steps) + [whole(columns.shape)],
        scalars=scalars,
        name="out_product",
    )(*[piece for pair in pieces for piece in pair], columns)


def rows_product(left, right, name):
    total, inner = left.shape
    width = right.shape[0]
    block = min(total, 512)

    def kernel(left_ref, right_ref, out_ref):
        out_ref[...] = dot_nt(left_ref[...], right_ref[...]).astype(BF16)

    return call(
        kernel,
        struct((total, width), BF16),
        pl.BlockSpec((block, width), lambda i: (i, 0)),
        grid=(total // block,),
        in_blocks=[pl.BlockSpec((block, inner), lambda i: (i, 0)), whole(right.shape)],
        name=name,
    )(left, right)


def shards(
    tokens,
    cotangent,
    positions,
    qkv_weight,
    qkv_first,
    qkv_second,
    out_weight,
    out_first,
    out_second,
    fc_weight,
    fc_first,
    fc_second,
    proj_weight,
    proj_first,
    proj_second,
    small_weight,
    small_first,
    small_second,
):
    count = lax.axis_size("seq")
    ring = Ring(count)
    square = Square()
    me = lax.axis_index("seq")
    rows, width = tokens.shape
    seq_rows = rows // SEQS
    window = qkv_weight.shape[1]
    slots = -(-HEADS // count)
    wide = slots * HD
    small_count, small_width = small_weight.shape
    hidden = fc_weight.shape[1]
    all_rows = count * rows
    steps = ring.steps
    marks = jnp.stack([ring.side] + [ring.position(t) for t in range(steps)])
    tokens = by_rows(tokens)
    cotangent = by_rows(cotangent)

    token_tour = Tour(ring, tokens)
    token_tour.step()
    token_tour.step()
    pack, unpack, most = head_tables(count, width, window)
    pack_hot = one_hot(pick_row(pack, me), window)
    packed = jnp.einsum(
        "rc,cdl->drl",
        qkv_weight.astype(BF16),
        pack_hot.reshape(window, count, most),
        preferred_element_type=BF16,
    )
    depth = packed.shape[1]
    small_flat = jnp.concatenate(
        [
            small_weight.reshape(-1).astype(BF16),
            (positions // 32).astype(BF16),
            (positions % 32).astype(BF16),
        ]
    )
    small_depth = -(-small_flat.shape[0] // most)
    small_depth += -small_depth % 16
    small_flat = jnp.pad(small_flat, (0, small_depth * most - small_flat.shape[0]))
    small_pack = jnp.broadcast_to(
        small_flat.reshape(1, small_depth, most), (count, small_depth, most)
    )
    received = lax.all_to_all(jnp.concatenate([packed, small_pack], axis=1), "seq", 0, 0)
    token_tour.step()
    received = after(received, token_tour.moved[1], token_tour.current)

    unpack_hot = one_hot(pick_row(unpack, me), 3 * wide)
    head_part = jnp.einsum(
        "srl,ksl->rk",
        received[:, :depth],
        unpack_hot.reshape(3 * wide, count, most),
        preferred_element_type=BF16,
    )
    for t in range(3, steps):
        token_tour.step()
    head_pieces = square.gather(head_part, token_tour.current)
    w_head = square.place(head_pieces)

    small_all = received[:, depth:].reshape(count, small_depth * most).astype(F32)
    small_rows = small_all[:, : small_count * small_width].reshape(count, small_count, small_width)
    small_rows = small_rows.transpose(1, 0, 2).reshape(small_count, width)
    pos_all = small_all[:, small_count * small_width :][:, : 2 * rows].reshape(count, 2, rows)
    pos_all = (pos_all[:, 0] * 32.0 + pos_all[:, 1]).astype(jnp.int32)

    def own_heads(row):
        padded = jnp.pad(row, (0, slots * count * HD - width)).reshape(slots, count, HD)
        return lax.dynamic_index_in_dim(padded, me, 1, keepdims=False).reshape(wide)

    head_bias = jnp.concatenate(
        [own_heads(small_rows[0]), jnp.zeros((wide,), F32), own_heads(small_rows[1])]
    )
    fc_bias = lax.dynamic_slice_in_dim(small_rows[3:7].reshape(-1), me * hidden, hidden, 0)
    gain_one, shift_one = small_rows[8][None], small_rows[9][None]
    gain_two, shift_two = small_rows[10][None], small_rows[11][None]

    ready = head_pieces[3]
    out_part = lax.all_gather(
        after(out_weight, token_tour.current).astype(BF16), "seq", axis=1, tiled=True
    )
    fc_pieces = square.gather(after(fc_weight, ready).astype(BF16))
    proj_pieces = square.gather(after(proj_weight, fc_pieces[2]).T.astype(BF16))
    out_pieces = square.gather(after(by_rows(out_part), proj_pieces[2]))

    tokens_all, normal_all, qkv_rows = first_rows(
        token_tour.pieces, marks, w_head, gain_one, shift_one, head_bias[None]
    )
    qkv_all = qkv_rows.reshape(count, SEQS, seq_rows, 3 * wide)
    context, probs = attention_forward(qkv_all, pos_all)
    context = context.reshape(all_rows, wide)

    half = steps // 2
    cot_tour = Tour(ring, cotangent, back=True)
    cot_tour.step(token_tour.moved[-1])
    for t in range(1, half):
        cot_tour.step()
    context_tour = Tour(ring, after(context, cot_tour.moved[-1]))
    w_fc, w_proj = None, None
    for t in range(steps):
        if t == 1:
            context_tour.step(proj_pieces[2])
            w_fc = square.place(after(fc_pieces, context_tour.moved[0]))
        elif t == steps - 1:
            w_proj = square.place(after(proj_pieces, context_tour.moved[-2]))
            context_tour.step(out_pieces[2], w_fc)
        else:
            context_tour.step()
    cot_middle = cotangent
    for t in range(half, steps):
        cot_tour.step(context_tour.moved[-1])
        cot_middle = cot_tour.current if t == half else cot_middle
    w_out = heads_rows(square.me, out_pieces, count, slots)
    normed_all, residual = second_rows(
        tokens_all, context_tour.pieces, marks, w_out, small_rows[2][None], gain_two, shift_two
    )

    normed_all = after(normed_all, cot_middle)

    kept, parts = None, {}
    for taken in ([steps - 1], list(reversed(range(steps - 1)))):
        kept, more = hidden_rows(
            normed_all,
            [cot_tour.pieces[t] for t in taken],
            jnp.stack([ring.side] + [ring.position(t) for t in taken]),
            w_fc,
            w_proj,
            fc_bias[None],
            kept,
            taken,
            rows,
        )
        parts.update(more)
    hidden_low, grad_pre_low, cot_all = kept
    grad_fold = Fold(ring, parts)
    grad_fold.beside(*parts[0])
    grad_fold.step()
    output_partial = rows_product(after(hidden_low, grad_fold.carried), w_proj, "output_product")
    grad_fold.beside(output_partial)
    grad_fold.step()
    fc_sum = turned_product(after(normed_all, grad_fold.carried), grad_pre_low, "fc_product")
    grad_fold.beside(fc_sum)
    for _ in range(3, steps):
        grad_fold.step()
    grad_bias_fc = jnp.sum(after(grad_pre_low, grad_fold.carried).astype(F32), axis=0)
    grad_fold.beside(grad_bias_fc)
    fc_column = square.half_sum(after(fc_sum, grad_fold.carried))
    output_sum = lax.psum_scatter(output_partial, "seq", scatter_dimension=0, tiled=True)
    terms = grad_fold.terms
    grad_residual, grad_attn_low, row_sums, grad_context = second_back(
        residual, terms, cotangent, gain_two, w_out, count
    )

    proj_sum = turned_product(after(cot_all, grad_context), hidden_low, "proj_product")
    grad_context = after(lax.all_to_all(grad_context, "seq", 0, 0), proj_sum)
    proj_column = square.half_sum(after(proj_sum, grad_context))
    out_columns = out_weight.shape[1]
    attn_columns = after(grad_attn_low, grad_context)
    attn_columns = lax.all_to_all(
        attn_columns.reshape(rows, count, out_columns).transpose(1, 0, 2), "seq", 0, 0
    ).reshape(all_rows, out_columns)
    grad_qkv = attention_backward(
        qkv_all, grad_context.reshape(count, SEQS, seq_rows, wide), probs
    ).reshape(all_rows, 3 * wide)
    fc_grad = after(square.other_sum(fc_column), grad_qkv)
    proj_grad = square.other_sum(after(proj_column, grad_qkv))
    parts = ring_parts(after(grad_qkv, attn_columns), w_head, marks, steps, "input_parts")
    input_fold = Fold(ring, parts)
    head_sum, grad_gain_one, grad_shift_one, grad_qkv_sum = head_product(
        after(normal_all, *parts[0]), grad_qkv, w_head, small_rows[8][:, None], small_rows[9][:, None]
    )
    input_fold.beside(head_sum)
    input_fold.step()

    attn_columns = after(attn_columns, input_fold.carried)
    out_sum = out_product(context_tour.pieces, attn_columns, marks, count, slots)[:width]
    input_fold.beside(out_sum)
    head_column = square.half_sum(after(head_sum, input_fold.carried))
    input_fold.step()
    out_column = square.half_sum(after(out_sum, input_fold.carried))
    fc_new = adam_update(
        fc_weight, fc_first, fc_second, after(fc_grad, input_fold.carried), 0.02, 0.1
    )
    input_fold.beside(fc_new[0], head_column)
    for _ in range(3, steps):
        input_fold.step()
    small_begin = input_fold.carried
    head_grad = square.other_sum(head_column).astype(BF16)
    out_grad = square.other_sum(out_column)
    input_grad = first_back(tokens, input_fold.terms, grad_residual, gain_one)

    unpack_back = unpack_hot.reshape(3 * wide, count, most)
    head_packed = jnp.einsum("rk,ksl->srl", head_grad, unpack_back, preferred_element_type=BF16)
    head_back = lax.all_to_all(head_packed, "seq", 0, 0)
    qkv_grad = jnp.einsum(
        "drl,cdl->rc",
        head_back,
        pack_hot.reshape(window, count, most),
        preferred_element_type=F32,
    )
    output = (residual + output_sum.astype(F32) + small_rows[7]).astype(BF16)

    def place_heads(values):
        spread = (jnp.arange(count) == me).astype(F32)[None, :, None]
        placed = values.reshape(slots, 1, HD) * spread
        return placed.reshape(-1)[:width]

    grad_bias_fc = grad_bias_fc[None, :] * (jnp.arange(count) == me).astype(F32)[:, None]
    grad_qkv_sum = after(grad_qkv_sum, small_begin)[0]
    grad_small = jnp.concatenate(
        [
            place_heads(grad_qkv_sum[:wide])[None],
            place_heads(grad_qkv_sum[2 * wide :])[None],
            row_sums[2:3],
            grad_bias_fc.reshape(-1, width),
            row_sums[3:4],
            grad_gain_one[:, 0][None],
            grad_shift_one[:, 0][None],
            row_sums[0:1],
            row_sums[1:2],
        ],
        axis=0,
    )
    small_sent = grad_small.astype(BF16).reshape(small_count, count, small_width)
    small_part = jnp.sum(
        lax.all_to_all(small_sent.transpose(1, 0, 2), "seq", 0, 0).astype(F32), axis=0
    )
    small_grad = square.sum(after(small_part, head_grad))

    qkv_new = adam_update(qkv_weight, qkv_first, qkv_second, qkv_grad, 0.02, 0.1)
    out_new = adam_update(out_weight, out_first, out_second, out_grad, 0.3, 0.1)
    proj_new = adam_update(
        proj_weight.T, proj_first.T, proj_second.T, proj_grad, 0.02, 0.1
    )
    proj_new = [value.T for value in proj_new]
    small_new = adam_update(small_weight, small_first, small_second, small_grad, 0.3, 0.0)
    return (
        output,
        input_grad,
        *qkv_new,
        *out_new,
        *fc_new,
        *proj_new,
        *small_new,
        small_grad[7],
    )


def solution(mesh):
    rows = P(("dp", "seq"), None)
    matrix = P("dp", "seq")
    turned = P("seq", "dp")
    small = P(None, "seq")
    in_specs = (
        (rows, rows, P(("dp", "seq"))) + (matrix,) * 9 + (turned,) * 3 + (small,) * 3
    )
    out_specs = (rows, rows) + (matrix,) * 9 + (turned,) * 3 + (small,) * 3 + (P("seq"),)
    return jax.shard_map(shards, mesh=mesh, in_specs=in_specs, out_specs=out_specs, check_vma=False)
```

```python
import functools
import math

import jax
import jax.numpy as jnp
import numpy as np
from jax import lax
from jax.experimental import pallas as pl
from jax.experimental.layout import Layout, with_layout_constraint
from jax.experimental.pallas import tpu as pltpu
from jax.sharding import PartitionSpec as P

HEADS = 25
HD = 64
SEQS = 2
STEP = 10

NORM_EPS = 1e-05
SCORE_SCALE = 0.125
MASKED_SCORE = -1e30
BETA_ONE = 0.9
BETA_TWO = 0.95
ADAM_EPS = 1e-08
BF16 = jnp.bfloat16
F32 = jnp.float32
SMALL_COST = pl.CostEstimate(flops=1024, bytes_accessed=1024, transcendentals=0)
LARGE_COST = pl.CostEstimate(flops=8 * 10**9, bytes_accessed=8 * 10**6, transcendentals=0)


def adam_update(weight, first_moment, second, gradient, step_rate, decay_rate):
    moment_new = BETA_ONE * first_moment + (1.0 - BETA_ONE) * gradient
    second_new = BETA_TWO * second + (1.0 - BETA_TWO) * gradient * gradient
    direction = (
        moment_new
        / (1.0 - BETA_ONE**STEP)
        / (jnp.sqrt(second_new / (1.0 - BETA_TWO**STEP)) + ADAM_EPS)
    )
    return (moment_new, second_new, weight - step_rate * (direction + decay_rate * weight))


def dot(left, right):
    return jnp.dot(left, right, preferred_element_type=F32)


def dot_nt(left, right):
    return lax.dot_general(left, right, (((1,), (1,)), ((), ())), preferred_element_type=F32)


def dot_tn(left, right):
    return lax.dot_general(left, right, (((0,), (0,)), ((), ())), preferred_element_type=F32)


def after(value, *others):
    return lax.optimization_barrier((value,) + others)[0]


def by_rows(value):
    return with_layout_constraint(value, Layout(major_to_minor=(0, 1)))


def call(
    kernel, out, blocks, grid=None, in_blocks=None, scalars=None, alias=None, scratch=(), name=None
):
    operands = 0 if scalars is None else 1
    spec = dict(
        in_specs=in_blocks,
        out_specs=blocks,
        grid=grid or (1,),
        scratch_shapes=list(scratch),
    )
    if operands:
        spec = dict(grid_spec=pltpu.PrefetchScalarGridSpec(num_scalar_prefetch=1, **spec))
    run = pl.pallas_call(
        kernel,
        out_shape=out,
        input_output_aliases=alias or {},
        compiler_params=pltpu.CompilerParams(vmem_limit_bytes=60 * 1024 * 1024),
        cost_estimate=SMALL_COST,
        name=name,
        **spec,
    )
    if operands:
        return lambda *given: run(scalars, *given)
    return run


def whole(shape):
    return pl.BlockSpec(shape, lambda *_: (0,) * len(shape))


def struct(shape, dtype):
    return jax.ShapeDtypeStruct(shape, dtype)


class Ring:
    def __init__(self, count):
        self.sides = 2
        self.steps = count // 2
        steps = self.steps
        self.swap = [(j, j ^ 1) for j in range(count)]
        self.ahead = [(z * 2 + x, ((z + 1) % steps) * 2 + x) for z in range(steps) for x in range(2)]
        self.behind = [(dst, src) for src, dst in self.ahead]
        me = lax.axis_index("seq")
        self.place, self.side = me // 2, me % 2

    def position(self, t):
        return (self.place + self.steps - t) % self.steps

    def gather(self, block):
        tour = Tour(self, block)
        for _ in range(self.steps):
            tour.step()
        return tour


class Tour:
    def __init__(self, ring, block, back=False):
        self.ring, self.current, self.back = ring, block, back
        self.pieces = [None] * ring.steps
        self.moved = []

    def step(self, *begin, land=()):
        ring, t = self.ring, len(self.moved)
        if begin:
            self.current = after(self.current, *begin)
        if t:
            sent = after(self.current, self.moved[-2]) if t > 1 else self.current
            self.current = lax.ppermute(sent, "seq", ring.behind if self.back else ring.ahead)
            self.current = after(self.current, *land) if land else self.current
        crossing = after(self.current, self.moved[-1]) if t > 1 else self.current
        other = lax.ppermute(crossing, "seq", ring.swap)
        self.pieces[-t if self.back else t] = (self.current, other)
        self.moved.append(other)


class Fold:
    def __init__(self, ring, parts):
        self.ring, self.parts = ring, parts
        self.terms, self.count, self.carried = None, 0, None
        self.step()

    def step(self):
        ring = self.ring
        mine, other = self.parts[ring.steps - 1 - self.count]
        self.count += 1
        sent = None
        if self.terms is not None:
            sent = sum(term.astype(F32) for term in self.terms).astype(BF16)
            self.carried = sent
            other = after(other, sent)
        self.terms = [mine, lax.ppermute(other, "seq", ring.swap)]
        if sent is not None:
            self.terms.append(lax.ppermute(sent, "seq", ring.behind))

    def beside(self, *work):
        self.terms = list(lax.optimization_barrier((tuple(self.terms),) + work)[0])


class Square:
    def __init__(self):
        me = lax.axis_index("dp")
        self.me, self.far, self.near = me, me // 2, me % 2
        self.far_swap = [(j, j ^ 2) for j in range(4)]
        self.near_swap = [(j, j ^ 1) for j in range(4)]

    def gather(self, block, *begin):
        near = lax.ppermute(block, "dp", self.near_swap)
        far = lax.ppermute(block, "dp", self.far_swap)
        far = after(far, *begin) if begin else far
        return (block, near, far, lax.ppermute(far, "dp", self.near_swap))

    def place(self, pieces):
        rows, width = pieces[0].shape

        def kernel(me, *refs):
            for r in range(4):
                begin = pl.multiple_of((me[0] ^ r) * rows, 16)
                refs[4][pl.ds(begin, rows)] = refs[r][...]

        return call(
            kernel,
            struct((4 * rows, width), BF16),
            whole((4 * rows, width)),
            in_blocks=[whole((rows, width))] * 4,
            scalars=self.me[None],
            name="place_rows",
        )(*pieces)

    def half_sum(self, partial):
        parts = partial.reshape((2, 2, partial.shape[0] // 4) + partial.shape[1:])
        mine = lax.dynamic_index_in_dim(parts, self.near, 1, keepdims=False)
        other = lax.dynamic_index_in_dim(parts, 1 - self.near, 1, keepdims=False)
        return mine.astype(F32) + lax.ppermute(other, "dp", self.near_swap).astype(F32)

    def other_sum(self, column):
        mine = lax.dynamic_index_in_dim(column, self.far, 0, keepdims=False)
        other = lax.dynamic_index_in_dim(column, 1 - self.far, 0, keepdims=False)
        return mine + lax.ppermute(other.astype(BF16), "dp", self.far_swap).astype(F32)

    def sum(self, values):
        values = values + lax.ppermute(values, "dp", self.near_swap)
        return values + lax.ppermute(values, "dp", self.far_swap)


def head_tables(count, model_width, window):
    slots = -(-HEADS // count)
    wide = slots * HD
    lists = [[[] for _ in range(count)] for _ in range(count)]
    for column in range(3 * model_width):
        src, local = divmod(column, window)
        part, within = divmod(column, model_width)
        head, lane = divmod(within, HD)
        dst, slot = head % count, head // count
        lists[src][dst].append((local, part * wide + slot * HD + lane))
    most = max(len(entry) for row in lists for entry in row)
    most = -(-most // 64) * 64
    pack = np.full((count, count * most), -1, np.int32)
    unpack = np.full((count, count * most), -1, np.int32)
    for src in range(count):
        for dst in range(count):
            for place, (local, target) in enumerate(lists[src][dst]):
                pack[src, dst * most + place] = local
                unpack[dst, src * most + place] = target
    return pack, unpack, most


def pick_row(table, index):
    return lax.dynamic_index_in_dim(jnp.asarray(table), index, 0, keepdims=False)


def one_hot(rows, size):
    return (lax.broadcasted_iota(jnp.int32, (size, rows.shape[0]), 0) == rows[None, :]).astype(BF16)


def forward_kernel(pos_col, pos_row, query_ref, full_ref, context_ref, probs_ref, *, wide):
    slots, _, run, width = query_ref.shape
    rows = slots * run
    keys_total = full_ref.shape[0] * run
    query = query_ref[:, 0].reshape(rows, width)[:, :wide]
    full = full_ref[:, 0].reshape(keys_total, width)
    key, value = full[:, wide : 2 * wide], full[:, 2 * wide :]
    seen = pos_row[0] <= pos_col[0]
    lane_head = lax.broadcasted_iota(jnp.int32, (1, wide), 1) // HD
    context = jnp.zeros((rows, wide), F32)
    for head in range(wide // HD):
        mine = lane_head == head
        scores = dot_nt(jnp.where(mine, query, jnp.zeros_like(query)), key) * SCORE_SCALE
        scores = jnp.where(seen, scores, MASKED_SCORE)
        top = jnp.max(scores, axis=1, keepdims=True)
        raw = jnp.exp(scores - top)
        probs = (raw * (1.0 / jnp.sum(raw, axis=1, keepdims=True))).astype(BF16)
        probs_ref[0, head] = probs
        context = jnp.where(mine, dot(probs, value), context)
    context_ref[:, 0] = context.astype(BF16).reshape(slots, run, wide)


def backward_kernel(query_ref, full_ref, grad_ref, probs_ref, out_ref, key_sum, value_sum, *, wide):
    step = pl.program_id(1)
    slots, _, run, width = query_ref.shape
    rows = slots * run
    count = full_ref.shape[0]
    keys_total = count * run
    query = query_ref[:, 0].reshape(rows, width)[:, :wide]
    full = full_ref[:, 0].reshape(keys_total, width)
    key, value = full[:, wide : 2 * wide], full[:, 2 * wide :]
    grad = grad_ref[:, 0].reshape(rows, wide)
    lane_head = lax.broadcasted_iota(jnp.int32, (1, wide), 1) // HD

    @pl.when(step == 0)
    def _():
        key_sum[...] = jnp.zeros_like(key_sum)
        value_sum[...] = jnp.zeros_like(value_sum)

    query_grad = jnp.zeros((rows, wide), F32)
    key_grad = jnp.zeros((keys_total, wide), F32)
    value_grad = jnp.zeros((keys_total, wide), F32)
    for head in range(wide // HD):
        mine = lane_head == head
        probs_low = probs_ref[0, head]
        probs = probs_low.astype(F32)
        grad_probs = dot_nt(jnp.where(mine, grad, jnp.zeros_like(grad)), value)
        weighted = probs * grad_probs
        delta = jnp.sum(weighted, axis=1, keepdims=True)
        grad_scores = (weighted - probs * delta).astype(BF16)
        query_grad = jnp.where(mine, dot(grad_scores, key), query_grad)
        key_grad = jnp.where(mine, dot_tn(grad_scores, query), key_grad)
        value_grad = jnp.where(mine, dot_tn(probs_low, grad), value_grad)
    key_sum[...] += key_grad
    value_sum[...] += value_grad
    out_ref[pl.ds(step * slots, slots), 0, :, :wide] = (
        (query_grad * SCORE_SCALE).astype(BF16).reshape(slots, run, wide)
    )

    @pl.when(step == pl.num_programs(1) - 1)
    def _():
        out_ref[:, 0, :, wide : 2 * wide] = (
            (key_sum[...] * SCORE_SCALE).astype(BF16).reshape(count, run, wide)
        )
        out_ref[:, 0, :, 2 * wide :] = value_sum[...].astype(BF16).reshape(count, run, wide)


def attention_forward(qkv_rows, positions):
    count, _, run, width = qkv_rows.shape
    wide = width // 3
    heads = wide // HD
    length = count * run
    block = min(length, 512)
    slots = block // run
    steps = length // block
    by_sequence = positions.reshape(count, SEQS, run).transpose(1, 0, 2).reshape(SEQS, length)
    return pl.pallas_call(
        functools.partial(forward_kernel, wide=wide),
        grid=(SEQS, steps),
        in_specs=[
            pl.BlockSpec((1, block, 1), lambda s, i: (s, i, 0)),
            pl.BlockSpec((1, 1, length), lambda s, i: (s, 0, 0)),
            pl.BlockSpec((slots, 1, run, width), lambda s, i: (i, s, 0, 0)),
            pl.BlockSpec((count, 1, run, width), lambda s, i: (0, s, 0, 0)),
        ],
        out_specs=[
            pl.BlockSpec((slots, 1, run, wide), lambda s, i: (i, s, 0, 0)),
            pl.BlockSpec((1, heads, block, length), lambda s, i: (s, 0, i, 0)),
        ],
        out_shape=[
            jax.ShapeDtypeStruct((count, SEQS, run, wide), BF16),
            jax.ShapeDtypeStruct((SEQS, heads, length, length), BF16),
        ],
        compiler_params=pltpu.CompilerParams(vmem_limit_bytes=60 * 1024 * 1024),
        cost_estimate=LARGE_COST,
        name="attention_forward",
    )(by_sequence[:, :, None], by_sequence[:, None, :], qkv_rows, qkv_rows)


def attention_backward(qkv_rows, grad_context, probs):
    count, _, run, width = qkv_rows.shape
    wide = width // 3
    heads = wide // HD
    length = count * run
    block = min(length, 512)
    slots = block // run
    steps = length // block
    return pl.pallas_call(
        functools.partial(backward_kernel, wide=wide),
        grid=(SEQS, steps),
        in_specs=[
            pl.BlockSpec((slots, 1, run, width), lambda s, i: (i, s, 0, 0)),
            pl.BlockSpec((count, 1, run, width), lambda s, i: (0, s, 0, 0)),
            pl.BlockSpec((slots, 1, run, wide), lambda s, i: (i, s, 0, 0)),
            pl.BlockSpec((1, heads, block, length), lambda s, i: (s, 0, i, 0)),
        ],
        out_specs=pl.BlockSpec((count, 1, run, width), lambda s, i: (0, s, 0, 0)),
        out_shape=jax.ShapeDtypeStruct((count, SEQS, run, width), BF16),
        scratch_shapes=[pltpu.VMEM((length, wide), F32), pltpu.VMEM((length, wide), F32)],
        compiler_params=pltpu.CompilerParams(vmem_limit_bytes=60 * 1024 * 1024),
        cost_estimate=SMALL_COST,
        name="attention_backward",
    )(qkv_rows, qkv_rows, grad_context, probs)


def in_order(side, own, other, axis=0):
    first = jnp.where(side == 0, own, other)
    second = jnp.where(side == 0, other, own)
    return jnp.concatenate([first, second], axis=axis)


def normalize(values):
    centred = values - jnp.mean(values, axis=1, keepdims=True)
    spread = lax.rsqrt(jnp.mean(centred * centred, axis=1, keepdims=True) + NORM_EPS)
    return centred * spread, spread


def normalize_back(normal, spread, gain, grad):
    scaled = grad * gain
    along = jnp.mean(scaled * normal, axis=1, keepdims=True)
    return spread * (scaled - jnp.mean(scaled, axis=1, keepdims=True) - normal * along)


def first_rows(pieces, scalars, weight, gain, shift, bias):
    rows, width = pieces[0][0].shape
    steps = len(pieces)
    total = 2 * steps * rows
    columns = weight.shape[1]

    def kernel(marks, *refs):
        given, (w, g, s, b), outs = refs[: 2 * steps], refs[2 * steps : 2 * steps + 4], refs[-3:]
        for t in range(steps):

            @pl.when(pl.program_id(0) == t)
            def _(t=t):
                outs[0][...] = in_order(marks[0], given[2 * t][...], given[2 * t + 1][...])

        normal, _ = normalize(outs[0][...].astype(F32))
        outs[1][...] = normal.astype(BF16)
        scaled = (normal * g[...] + s[...]).astype(BF16)
        outs[2][...] = (dot(scaled, w[...]) + b[...]).astype(BF16)

    def block(width):
        return pl.BlockSpec((2 * rows, width), lambda t, marks: (marks[1 + t], 0))

    flat = [piece for pair in pieces for piece in pair]
    return call(
        kernel,
        [struct((total, width), BF16), struct((total, width), BF16), struct((total, columns), BF16)],
        [block(width), block(width), block(columns)],
        grid=(steps,),
        in_blocks=[whole((rows, width))] * (2 * steps)
        + [whole(weight.shape), whole((1, width)), whole((1, width)), whole((1, columns))],
        scalars=scalars,
        name="first_rows",
    )(*flat, weight, gain, shift, bias)


def second_rows(tokens_all, pieces, scalars, weight, bias, gain, shift):
    total, width = tokens_all.shape
    steps = len(pieces)
    wide = pieces[0][0].shape[1]
    own_rows = total // (2 * steps)
    rows = 2 * own_rows
    inside = rows // own_rows

    def kernel(marks, tokens, *refs):
        given = refs[: 2 * steps]
        w, b, g, s, normed, own, context = refs[2 * steps :]
        for t in range(steps):
            pair = in_order(marks[0], given[2 * t][...], given[2 * t + 1][...], axis=1)
            begin = pl.multiple_of(marks[1 + t] * (2 * wide), 2 * wide)
            context[:, pl.ds(begin, 2 * wide)] = pair
        residual = tokens[...].astype(F32) + dot(context[...], w[...]) + b[...]
        normal, _ = normalize(residual)
        normed[...] = (normal * g[...] + s[...]).astype(BF16)
        mine = marks[1] * 2 + marks[0]
        for i in range(inside):

            @pl.when(pl.program_id(0) * inside + i == mine)
            def _(i=i):
                own[...] = residual[i * own_rows : (i + 1) * own_rows]

    return pl.pallas_call(
        kernel,
        grid_spec=pltpu.PrefetchScalarGridSpec(
            num_scalar_prefetch=1,
            grid=(total // rows,),
            in_specs=[pl.BlockSpec((rows, width), lambda i, marks: (i, 0))]
            + [pl.BlockSpec((rows, wide), lambda i, marks: (i, 0))] * (2 * steps)
            + [whole(weight.shape), whole((1, width)), whole((1, width)), whole((1, width))],
            out_specs=[
                pl.BlockSpec((rows, width), lambda i, marks: (i, 0)),
                whole((own_rows, width)),
            ],
            scratch_shapes=[pltpu.VMEM((rows, 2 * steps * wide), BF16)],
        ),
        out_shape=[struct((total, width), BF16), struct((own_rows, width), F32)],
        compiler_params=pltpu.CompilerParams(vmem_limit_bytes=60 * 1024 * 1024),
        cost_estimate=SMALL_COST,
        name="second_rows",
    )(scalars, tokens_all, *[piece for pair in pieces for piece in pair], weight, bias, gain, shift)


def hidden_rows(normed, pairs, scalars, w_fc, w_proj, bias, kept, taken, rows):
    total, width = normed.shape
    hidden = w_fc.shape[1]
    many = len(taken)

    def kernel(marks, block, *refs):
        given, (fc, proj, b) = refs[: 2 * many], refs[2 * many : 2 * many + 3]
        act_ref, grad_ref, cot_ref = refs[-3 - 2 * many : -2 * many]
        parts = refs[-2 * many :]
        for i in range(many):

            @pl.when(pl.program_id(0) == i)
            def _(i=i):
                cot_ref[...] = in_order(marks[0], given[2 * i][...], given[2 * i + 1][...])

        z = dot(block[...], fc[...]) + b[...]
        square = z * z
        tanh = jnp.tanh(0.7978845608028654 * (z + 0.044715 * (square * z)))
        half = 0.5 * (1.0 + tanh)
        slope = half + 0.5 * z * (1.0 - tanh * tanh) * (
            0.7978845608028654 + (0.7978845608028654 * 3.0 * 0.044715) * square
        )
        act_ref[...] = (z * half).astype(BF16)
        grad = (dot(cot_ref[...], proj[...]) * slope).astype(BF16)
        grad_ref[...] = grad
        part = dot_nt(grad, fc[...])
        mine = jnp.where(marks[0] == 0, part[:rows], part[rows:])
        other = jnp.where(marks[0] == 0, part[rows:], part[:rows]).astype(BF16)
        for i in range(many):

            @pl.when(pl.program_id(0) == i)
            def _(i=i):
                parts[2 * i][...] = mine
                parts[2 * i + 1][...] = other

    def block(width):
        return pl.BlockSpec((2 * rows, width), lambda i, marks: (marks[1 + i], 0))

    operands = [normed] + [piece for pair in pairs for piece in pair] + [w_fc, w_proj, bias]
    blocks = [block(width)] + [whole((rows, width))] * (2 * many)
    blocks += [whole(w_fc.shape), whole(w_proj.shape), whole((1, hidden))]
    alias = {}
    if kept is not None:
        alias = {1 + len(operands) + i: i for i in range(3)}
        operands += list(kept)
        blocks += [pl.BlockSpec(memory_space=pl.ANY)] * 3
    outs = call(
        kernel,
        [struct((total, hidden), BF16), struct((total, hidden), BF16), struct((total, width), BF16)]
        + [struct((rows, width), dtype) for _ in taken for dtype in (F32, BF16)],
        [block(hidden), block(hidden), block(width)] + [whole((rows, width))] * (2 * many),
        grid=(many,),
        in_blocks=blocks,
        scalars=scalars,
        alias=alias,
        name="hidden_rows",
    )(*operands)
    return outs[:3], {t: (outs[3 + 2 * i], outs[4 + 2 * i]) for i, t in enumerate(taken)}


def turned_product(left, right, name):
    total, width = left.shape
    columns = right.shape[1]
    tile = 256

    def kernel(left_ref, right_ref, out_ref):
        out_ref[...] = dot(left_ref[...].T, right_ref[...]).astype(BF16)

    return call(
        kernel,
        struct((width, columns), BF16),
        pl.BlockSpec((tile, columns), lambda i: (i, 0)),
        grid=(pl.cdiv(width, tile),),
        in_blocks=[pl.BlockSpec((total, tile), lambda i: (0, i)), whole(right.shape)],
        name=name,
    )(left, right)


def head_product(normal, grad, weight, gain, shift):
    total, width = normal.shape
    columns = grad.shape[1]
    tile = 256

    def kernel(left, right, w, g, s, out, gain_sum, shift_sum, grad_sum):
        @pl.when(pl.program_id(0) == 0)
        def _():
            grad_sum[...] = jnp.sum(right[...].astype(F32), axis=0, keepdims=True)

        raw = dot(left[...].T, right[...])
        sums = grad_sum[...]
        low = w[...].astype(F32)
        gain_sum[...] = jnp.sum(raw * low, axis=1, keepdims=True)
        shift_sum[...] = jnp.sum(low * sums, axis=1, keepdims=True)
        out[...] = (raw * g[...] + s[...] * sums).astype(BF16)

    column = pl.BlockSpec((tile, 1), lambda i: (i, 0))
    return call(
        kernel,
        [
            struct((width, columns), BF16),
            struct((width, 1), F32),
            struct((width, 1), F32),
            struct((1, columns), F32),
        ],
        [pl.BlockSpec((tile, columns), lambda i: (i, 0)), column, column, whole((1, columns))],
        grid=(pl.cdiv(width, tile),),
        in_blocks=[
            pl.BlockSpec((total, tile), lambda i: (0, i)),
            whole(grad.shape),
            pl.BlockSpec((tile, columns), lambda i: (i, 0)),
            column,
            column,
        ],
        name="head_product",
    )(normal, grad, weight, gain, shift)


def ring_parts(left, right, scalars, steps, name):
    total, inner = left.shape
    width = right.shape[0]
    rows = total // (2 * steps)

    def kernel(marks, left_ref, right_ref, *outs):
        for t in range(steps):
            begin = pl.multiple_of(marks[1 + t] * (2 * rows), 2 * rows)
            part = dot_nt(left_ref[pl.ds(begin, 2 * rows)], right_ref[...])
            outs[2 * t][...] = jnp.where(marks[0] == 0, part[:rows], part[rows:])
            outs[2 * t + 1][...] = jnp.where(marks[0] == 0, part[rows:], part[:rows]).astype(BF16)

    outs = call(
        kernel,
        [struct((rows, width), dtype) for _ in range(steps) for dtype in (F32, BF16)],
        [whole((rows, width))] * (2 * steps),
        in_blocks=[whole(left.shape), whole(right.shape)],
        scalars=scalars,
        name=name,
    )(left, right)
    return [(outs[2 * t], outs[2 * t + 1]) for t in range(steps)]


def second_back(residual, terms, cotangent, gain, weight, count):
    rows, width = residual.shape
    wide = weight.shape[0] // count

    def kernel(res, mine, swapped, carried, cot, g, w, grad_ref, low_ref, sums_ref, out_ref):
        @pl.when(pl.program_id(0) == 0)
        def _():
            grad = mine[...] + swapped[...].astype(F32) + carried[...].astype(F32)
            normal, spread = normalize(res[...])
            total = cot[...].astype(F32) + normalize_back(normal, spread, g[...], grad)
            grad_ref[...] = total
            low = total.astype(BF16)
            low_ref[...] = low
            sums_ref[0:1] = jnp.sum(grad * normal, axis=0, keepdims=True)
            sums_ref[1:2] = jnp.sum(grad, axis=0, keepdims=True)
            sums_ref[2:3] = jnp.sum(low.astype(F32), axis=0, keepdims=True)
            sums_ref[3:4] = jnp.sum(cot[...].astype(F32), axis=0, keepdims=True)

        out_ref[0] = dot_nt(low_ref[...], w[...]).astype(BF16)

    row = whole((rows, width))
    return call(
        kernel,
        [
            struct((rows, width), F32),
            struct((rows, width), BF16),
            struct((4, width), F32),
            struct((count, rows, wide), BF16),
        ],
        [row, row, whole((4, width)), pl.BlockSpec((1, rows, wide), lambda i: (i, 0, 0))],
        grid=(count,),
        in_blocks=[row] * 5 + [whole((1, width)), pl.BlockSpec((wide, width), lambda i: (i, 0))],
        name="second_back",
    )(residual, *terms, cotangent, gain, weight)


def first_back(tokens, terms, residual_grad, gain):
    rows, width = tokens.shape

    def kernel(x, mine, swapped, carried, res, g, out_ref):
        grad = mine[...] + swapped[...].astype(F32) + carried[...].astype(F32)
        normal, spread = normalize(x[...].astype(F32))
        out_ref[...] = (res[...] + normalize_back(normal, spread, g[...], grad)).astype(BF16)

    row = whole((rows, width))
    return call(
        kernel,
        struct((rows, width), BF16),
        row,
        in_blocks=[row] * 5 + [whole((1, width))],
        name="first_back",
    )(tokens, *terms, residual_grad, gain)


def heads_rows(me, pieces, count, slots):
    rows, width = pieces[0].shape
    unit = math.gcd(rows, HD)

    def kernel(mark, *refs):
        out = refs[4]
        for h in range(HEADS, count * slots):
            place = ((h % count) * slots + h // count) * HD
            out[place : place + HD] = jnp.zeros((HD, width), BF16)
        for r in range(4):
            for piece in range(rows // unit):
                row = (mark[0] ^ r) * rows + piece * unit
                head = row // HD
                target = ((head % count) * slots + head // count) * HD + row % HD
                out[pl.ds(pl.multiple_of(target, unit), unit)] = refs[r][
                    piece * unit : (piece + 1) * unit
                ]

    return call(
        kernel,
        struct((count * slots * HD, width), BF16),
        whole((count * slots * HD, width)),
        in_blocks=[whole((rows, width))] * 4,
        scalars=me[None],
        name="heads_rows",
    )(*pieces)


def out_product(pieces, columns, scalars, count, slots):
    total, width = columns.shape
    wide = slots * HD
    steps = len(pieces)

    def kernel(marks, *refs):
        given, right, out = refs[: 2 * steps], refs[2 * steps], refs[-1]
        for t in range(steps):
            for b in range(2):
                owner = marks[1 + t] * 2 + (marks[0] if b == 0 else 1 - marks[0])
                value = dot_tn(given[2 * t + b][...], right[...]).astype(BF16)
                for slot in range(slots):
                    begin = pl.multiple_of((slot * count + owner) * HD, HD)
                    out[pl.ds(begin, HD)] = value[slot * HD : (slot + 1) * HD]

    return call(
        kernel,
        struct((slots * count * HD, width), BF16),
        whole((slots * count * HD, width)),
        in_blocks=[whole((total, wide))] * (2 * steps) + [whole(columns.shape)],
        scalars=scalars,
        name="out_product",
    )(*[piece for pair in pieces for piece in pair], columns)


def rows_product(left, right, name):
    total, inner = left.shape
    width = right.shape[0]
    block = min(total, 512)

    def kernel(left_ref, right_ref, out_ref):
        out_ref[...] = dot_nt(left_ref[...], right_ref[...]).astype(BF16)

    return call(
        kernel,
        struct((total, width), BF16),
        pl.BlockSpec((block, width), lambda i: (i, 0)),
        grid=(total // block,),
        in_blocks=[pl.BlockSpec((block, inner), lambda i: (i, 0)), whole(right.shape)],
        name=name,
    )(left, right)


def shards(
    tokens,
    cotangent,
    positions,
    qkv_weight,
    qkv_first,
    qkv_second,
    out_weight,
    out_first,
    out_second,
    fc_weight,
    fc_first,
    fc_second,
    proj_weight,
    proj_first,
    proj_second,
    small_weight,
    small_first,
    small_second,
):
    count = lax.axis_size("seq")
    ring = Ring(count)
    square = Square()
    me = lax.axis_index("seq")
    rows, width = tokens.shape
    seq_rows = rows // SEQS
    window = qkv_weight.shape[1]
    slots = -(-HEADS // count)
    wide = slots * HD
    small_count, small_width = small_weight.shape
    hidden = fc_weight.shape[1]
    all_rows = count * rows
    steps = ring.steps
    marks = jnp.stack([ring.side] + [ring.position(t) for t in range(steps)])
    tokens = by_rows(tokens)
    cotangent = by_rows(cotangent)

    token_tour = Tour(ring, tokens)
    token_tour.step()
    token_tour.step()
    pack, unpack, most = head_tables(count, width, window)
    pack_hot = one_hot(pick_row(pack, me), window)
    packed = jnp.einsum(
        "rc,cdl->drl",
        qkv_weight.astype(BF16),
        pack_hot.reshape(window, count, most),
        preferred_element_type=BF16,
    )
    depth = packed.shape[1]
    small_flat = jnp.concatenate(
        [
            small_weight.reshape(-1).astype(BF16),
            (positions // 32).astype(BF16),
            (positions % 32).astype(BF16),
        ]
    )
    small_depth = -(-small_flat.shape[0] // most)
    small_depth += -small_depth % 16
    small_flat = jnp.pad(small_flat, (0, small_depth * most - small_flat.shape[0]))
    small_pack = jnp.broadcast_to(
        small_flat.reshape(1, small_depth, most), (count, small_depth, most)
    )
    received = lax.all_to_all(jnp.concatenate([packed, small_pack], axis=1), "seq", 0, 0)
    token_tour.step()
    received = after(received, token_tour.moved[1], token_tour.current)

    unpack_hot = one_hot(pick_row(unpack, me), 3 * wide)
    head_part = jnp.einsum(
        "srl,ksl->rk",
        received[:, :depth],
        unpack_hot.reshape(3 * wide, count, most),
        preferred_element_type=BF16,
    )
    for t in range(3, steps):
        token_tour.step()
    head_pieces = square.gather(head_part, token_tour.current)
    w_head = square.place(head_pieces)

    small_all = received[:, depth:].reshape(count, small_depth * most).astype(F32)
    small_rows = small_all[:, : small_count * small_width].reshape(count, small_count, small_width)
    small_rows = small_rows.transpose(1, 0, 2).reshape(small_count, width)
    pos_all = small_all[:, small_count * small_width :][:, : 2 * rows].reshape(count, 2, rows)
    pos_all = (pos_all[:, 0] * 32.0 + pos_all[:, 1]).astype(jnp.int32)

    def own_heads(row):
        padded = jnp.pad(row, (0, slots * count * HD - width)).reshape(slots, count, HD)
        return lax.dynamic_index_in_dim(padded, me, 1, keepdims=False).reshape(wide)

    head_bias = jnp.concatenate(
        [own_heads(small_rows[0]), jnp.zeros((wide,), F32), own_heads(small_rows[1])]
    )
    fc_bias = lax.dynamic_slice_in_dim(small_rows[3:7].reshape(-1), me * hidden, hidden, 0)
    gain_one, shift_one = small_rows[8][None], small_rows[9][None]
    gain_two, shift_two = small_rows[10][None], small_rows[11][None]

    ready = (w_head, token_tour.moved[-1])
    out_part = lax.all_gather(
        after(out_weight, head_part).astype(BF16), "seq", axis=1, tiled=True
    )
    tokens_all, normal_all, qkv_rows = first_rows(
        token_tour.pieces, marks, w_head, gain_one, shift_one, head_bias[None]
    )
    qkv_all = qkv_rows.reshape(count, SEQS, seq_rows, 3 * wide)
    context, probs = attention_forward(qkv_all, pos_all)
    context = context.reshape(all_rows, wide)

    cot_zero = lax.ppermute(after(cotangent, *ready), "seq", ring.swap)
    cot_moving = lax.ppermute(after(cotangent, *ready), "seq", ring.behind)
    fc_low = after(fc_weight, *ready).astype(BF16)
    context = after(context, cot_zero, cot_moving)
    fc_pieces = square.gather(fc_low)
    proj_pieces = square.gather(after(proj_weight, fc_pieces[2], context).T.astype(BF16))
    out_pieces = square.gather(by_rows(out_part))
    context_tour = Tour(ring, context)
    w_fc, w_proj = None, None
    for t in range(steps):
        if t == 1:
            context_tour.step(land=(fc_pieces[2],))
            w_fc = square.place(after(fc_pieces, context_tour.moved[0]))
        elif t == 2:
            context_tour.step(land=(out_part, w_fc))
        elif t == steps - 1:
            context_tour.step(land=(proj_pieces[2],))
        else:
            context_tour.step()
    w_proj = square.place(after(proj_pieces, context_tour.current))
    w_out = heads_rows(square.me, out_pieces, count, slots)
    normed_all, residual = second_rows(
        tokens_all, context_tour.pieces, marks, w_out, small_rows[2][None], gain_two, shift_two
    )
    cot_pieces = {0: (cotangent, cot_zero)}
    cot_moving = after(cot_moving, context_tour.moved[-1])
    crossed = lax.ppermute(cot_moving, "seq", ring.swap)
    cot_pieces[steps - 1] = (cot_moving, crossed)
    cot_moving = after(lax.ppermute(cot_moving, "seq", ring.behind), residual)

    def feed_forward(kept, taken):
        return hidden_rows(
            normed_all,
            [cot_pieces[t] for t in taken],
            jnp.stack([ring.side] + [ring.position(t) for t in taken]),
            w_fc,
            w_proj,
            fc_bias[None],
            kept,
            taken,
            rows,
        )

    kept, parts = feed_forward(None, [steps - 1])
    for t in range(2, steps):
        crossed = lax.ppermute(after(cot_moving, crossed), "seq", ring.swap)
        crossed = after(crossed, parts[steps - 1][1])
        cot_pieces[steps - t] = (cot_moving, crossed)
        if t + 1 < steps:
            cot_moving = lax.ppermute(cot_moving, "seq", ring.behind)
            cot_moving = after(cot_moving, parts[steps - 1][1])
    kept, more = feed_forward(kept, list(reversed(range(steps - 1))))
    parts.update(more)
    hidden_low, grad_pre_low, cot_all = kept
    grad_fold = Fold(ring, parts)
    grad_fold.beside(*parts[0])
    grad_fold.step()
    output_partial = rows_product(after(hidden_low, grad_fold.carried), w_proj, "output_product")
    grad_fold.beside(output_partial)
    grad_fold.step()
    fc_sum = turned_product(after(normed_all, grad_fold.carried), grad_pre_low, "fc_product")
    grad_fold.beside(fc_sum)
    for _ in range(3, steps):
        grad_fold.step()
    grad_bias_fc = jnp.sum(after(grad_pre_low, grad_fold.carried).astype(F32), axis=0)
    grad_fold.beside(grad_bias_fc)
    fc_column = square.half_sum(after(fc_sum, grad_fold.carried))
    output_sum = lax.psum_scatter(output_partial, "seq", scatter_dimension=0, tiled=True)
    terms = grad_fold.terms
    grad_residual, grad_attn_low, row_sums, grad_context = second_back(
        residual, terms, cotangent, gain_two, w_out, count
    )

    proj_sum = turned_product(after(cot_all, grad_context), hidden_low, "proj_product")
    grad_context = after(lax.all_to_all(grad_context, "seq", 0, 0), proj_sum)
    proj_column = square.half_sum(after(proj_sum, grad_context))
    out_columns = out_weight.shape[1]
    attn_columns = after(grad_attn_low, grad_context)
    attn_columns = lax.all_to_all(
        attn_columns.reshape(rows, count, out_columns).transpose(1, 0, 2), "seq", 0, 0
    ).reshape(all_rows, out_columns)
    grad_qkv = attention_backward(
        qkv_all, grad_context.reshape(count, SEQS, seq_rows, wide), probs
    ).reshape(all_rows, 3 * wide)
    fc_grad = after(square.other_sum(fc_column), grad_qkv)
    proj_grad = square.other_sum(after(proj_column, grad_qkv))
    parts = ring_parts(after(grad_qkv, attn_columns), w_head, marks, steps, "input_parts")
    input_fold = Fold(ring, parts)
    head_sum, grad_gain_one, grad_shift_one, grad_qkv_sum = head_product(
        after(normal_all, *parts[0]), grad_qkv, w_head, small_rows[8][:, None], small_rows[9][:, None]
    )
    input_fold.beside(head_sum)
    input_fold.step()

    attn_columns = after(attn_columns, input_fold.carried)
    out_sum = out_product(context_tour.pieces, attn_columns, marks, count, slots)[:width]
    input_fold.beside(out_sum)
    head_column = square.half_sum(after(head_sum, input_fold.carried))
    input_fold.step()
    out_column = square.half_sum(after(out_sum, input_fold.carried))
    fc_new = adam_update(
        fc_weight, fc_first, fc_second, after(fc_grad, input_fold.carried), 0.02, 0.1
    )
    input_fold.beside(fc_new[0], head_column)
    for _ in range(3, steps):
        input_fold.step()
    head_grad = square.other_sum(after(head_column, input_fold.carried)).astype(BF16)
    unpack_back = unpack_hot.reshape(3 * wide, count, most)
    head_packed = jnp.einsum("rk,ksl->srl", head_grad, unpack_back, preferred_element_type=BF16)
    input_fold.beside(head_packed)
    out_grad = square.other_sum(out_column)
    input_grad = first_back(tokens, input_fold.terms, grad_residual, gain_one)

    head_back = lax.all_to_all(head_packed, "seq", 0, 0)
    qkv_grad = jnp.einsum(
        "drl,cdl->rc",
        head_back,
        pack_hot.reshape(window, count, most),
        preferred_element_type=F32,
    )
    output_sum = after(output_sum, input_grad)
    output = (residual + output_sum.astype(F32) + small_rows[7]).astype(BF16)

    def place_heads(values):
        spread = (jnp.arange(count) == me).astype(F32)[None, :, None]
        placed = values.reshape(slots, 1, HD) * spread
        return placed.reshape(-1)[:width]

    grad_bias_fc = grad_bias_fc[None, :] * (jnp.arange(count) == me).astype(F32)[:, None]
    grad_qkv_sum = after(grad_qkv_sum, head_packed)[0]
    grad_small = jnp.concatenate(
        [
            place_heads(grad_qkv_sum[:wide])[None],
            place_heads(grad_qkv_sum[2 * wide :])[None],
            row_sums[2:3],
            grad_bias_fc.reshape(-1, width),
            row_sums[3:4],
            grad_gain_one[:, 0][None],
            grad_shift_one[:, 0][None],
            row_sums[0:1],
            row_sums[1:2],
        ],
        axis=0,
    )
    small_sent = grad_small.astype(BF16).reshape(small_count, count, small_width)
    small_part = jnp.sum(
        lax.all_to_all(small_sent.transpose(1, 0, 2), "seq", 0, 0).astype(F32), axis=0
    )
    small_grad = square.sum(small_part)

    qkv_new = adam_update(qkv_weight, qkv_first, qkv_second, qkv_grad, 0.02, 0.1)
    out_new = adam_update(out_weight, out_first, out_second, out_grad, 0.3, 0.1)
    proj_new = adam_update(
        proj_weight.T, proj_first.T, proj_second.T, proj_grad, 0.02, 0.1
    )
    proj_new = [value.T for value in proj_new]
    small_new = adam_update(small_weight, small_first, small_second, small_grad, 0.3, 0.0)
    return (
        output,
        input_grad,
        *qkv_new,
        *out_new,
        *fc_new,
        *proj_new,
        *small_new,
        small_grad[7],
    )


def solution(mesh):
    rows = P(("dp", "seq"), None)
    matrix = P("dp", "seq")
    turned = P("seq", "dp")
    small = P(None, "seq")
    in_specs = (
        (rows, rows, P(("dp", "seq"))) + (matrix,) * 9 + (turned,) * 3 + (small,) * 3
    )
    out_specs = (rows, rows) + (matrix,) * 9 + (turned,) * 3 + (small,) * 3 + (P("seq"),)
    return jax.shard_map(shards, mesh=mesh, in_specs=in_specs, out_specs=out_specs, check_vma=False)
```

```python
import functools
import math

import jax
import jax.numpy as jnp
import numpy as np
from jax import lax
from jax.experimental import pallas as pl
from jax.experimental.layout import Layout, with_layout_constraint
from jax.experimental.pallas import tpu as pltpu
from jax.sharding import PartitionSpec as P

HEADS = 25
HD = 64
SEQS = 2
STEP = 10

NORM_EPS = 1e-05
SCORE_SCALE = 0.125
MASKED_SCORE = -1e30
BETA_ONE = 0.9
BETA_TWO = 0.95
ADAM_EPS = 1e-08
BF16 = jnp.bfloat16
F32 = jnp.float32
SMALL_COST = pl.CostEstimate(flops=1024, bytes_accessed=1024, transcendentals=0)
LARGE_COST = pl.CostEstimate(flops=8 * 10**9, bytes_accessed=8 * 10**6, transcendentals=0)


def adam_update(weight, first_moment, second, gradient, step_rate, decay_rate):
    moment_new = BETA_ONE * first_moment + (1.0 - BETA_ONE) * gradient
    second_new = BETA_TWO * second + (1.0 - BETA_TWO) * gradient * gradient
    direction = (
        moment_new
        / (1.0 - BETA_ONE**STEP)
        / (jnp.sqrt(second_new / (1.0 - BETA_TWO**STEP)) + ADAM_EPS)
    )
    return (moment_new, second_new, weight - step_rate * (direction + decay_rate * weight))


def dot(left, right):
    return jnp.dot(left, right, preferred_element_type=F32)


def dot_nt(left, right):
    return lax.dot_general(left, right, (((1,), (1,)), ((), ())), preferred_element_type=F32)


def dot_tn(left, right):
    return lax.dot_general(left, right, (((0,), (0,)), ((), ())), preferred_element_type=F32)


def after(value, *others):
    return lax.optimization_barrier((value,) + others)[0]


def by_rows(value):
    return with_layout_constraint(value, Layout(major_to_minor=(0, 1)))


def call(
    kernel, out, blocks, grid=None, in_blocks=None, scalars=None, alias=None, scratch=(), name=None
):
    operands = 0 if scalars is None else 1
    spec = dict(
        in_specs=in_blocks,
        out_specs=blocks,
        grid=grid or (1,),
        scratch_shapes=list(scratch),
    )
    if operands:
        spec = dict(grid_spec=pltpu.PrefetchScalarGridSpec(num_scalar_prefetch=1, **spec))
    run = pl.pallas_call(
        kernel,
        out_shape=out,
        input_output_aliases=alias or {},
        compiler_params=pltpu.CompilerParams(vmem_limit_bytes=60 * 1024 * 1024),
        cost_estimate=SMALL_COST,
        name=name,
        **spec,
    )
    if operands:
        return lambda *given: run(scalars, *given)
    return run


def whole(shape):
    return pl.BlockSpec(shape, lambda *_: (0,) * len(shape))


def struct(shape, dtype):
    return jax.ShapeDtypeStruct(shape, dtype)


class Ring:
    def __init__(self, count):
        self.sides = 2
        self.steps = count // 2
        steps = self.steps
        self.swap = [(j, j ^ 1) for j in range(count)]
        self.ahead = [(z * 2 + x, ((z + 1) % steps) * 2 + x) for z in range(steps) for x in range(2)]
        self.behind = [(dst, src) for src, dst in self.ahead]
        me = lax.axis_index("seq")
        self.place, self.side = me // 2, me % 2

    def position(self, t):
        return (self.place + self.steps - t) % self.steps

    def gather(self, block):
        tour = Tour(self, block)
        for _ in range(self.steps):
            tour.step()
        return tour


class Tour:
    def __init__(self, ring, block, back=False):
        self.ring, self.current, self.back = ring, block, back
        self.pieces = [None] * ring.steps
        self.moved = []

    def step(self, *begin, land=()):
        ring, t = self.ring, len(self.moved)
        if begin:
            self.current = after(self.current, *begin)
        if t:
            sent = after(self.current, self.moved[-2]) if t > 1 else self.current
            self.current = lax.ppermute(sent, "seq", ring.behind if self.back else ring.ahead)
            self.current = after(self.current, *land) if land else self.current
        crossing = after(self.current, self.moved[-1]) if t > 1 else self.current
        other = lax.ppermute(crossing, "seq", ring.swap)
        self.pieces[-t if self.back else t] = (self.current, other)
        self.moved.append(other)


class Fold:
    def __init__(self, ring, parts):
        self.ring, self.parts = ring, parts
        self.terms, self.count, self.carried = None, 0, None
        self.step()

    def step(self):
        ring = self.ring
        mine, other = self.parts[ring.steps - 1 - self.count]
        self.count += 1
        sent = None
        if self.terms is not None:
            sent = sum(term.astype(F32) for term in self.terms).astype(BF16)
            self.carried = sent
            other = after(other, sent)
        self.terms = [mine, lax.ppermute(other, "seq", ring.swap)]
        if sent is not None:
            self.terms.append(lax.ppermute(sent, "seq", ring.behind))

    def beside(self, *work):
        self.terms = list(lax.optimization_barrier((tuple(self.terms),) + work)[0])


class Square:
    def __init__(self):
        me = lax.axis_index("dp")
        self.me, self.far, self.near = me, me // 2, me % 2
        self.far_swap = [(j, j ^ 2) for j in range(4)]
        self.near_swap = [(j, j ^ 1) for j in range(4)]

    def gather(self, block, *begin):
        near = lax.ppermute(block, "dp", self.near_swap)
        far = lax.ppermute(block, "dp", self.far_swap)
        far = after(far, *begin) if begin else far
        return (block, near, far, lax.ppermute(far, "dp", self.near_swap))

    def place(self, pieces):
        rows, width = pieces[0].shape

        def kernel(me, *refs):
            for r in range(4):
                begin = pl.multiple_of((me[0] ^ r) * rows, 16)
                refs[4][pl.ds(begin, rows)] = refs[r][...]

        return call(
            kernel,
            struct((4 * rows, width), BF16),
            whole((4 * rows, width)),
            in_blocks=[whole((rows, width))] * 4,
            scalars=self.me[None],
            name="place_rows",
        )(*pieces)

    def half_sum(self, partial):
        parts = partial.reshape((2, 2, partial.shape[0] // 4) + partial.shape[1:])
        mine = lax.dynamic_index_in_dim(parts, self.near, 1, keepdims=False)
        other = lax.dynamic_index_in_dim(parts, 1 - self.near, 1, keepdims=False)
        return mine.astype(F32) + lax.ppermute(other, "dp", self.near_swap).astype(F32)

    def other_sum(self, column):
        mine = lax.dynamic_index_in_dim(column, self.far, 0, keepdims=False)
        other = lax.dynamic_index_in_dim(column, 1 - self.far, 0, keepdims=False)
        return mine + lax.ppermute(other.astype(BF16), "dp", self.far_swap).astype(F32)

    def sum(self, values):
        values = values + lax.ppermute(values, "dp", self.near_swap)
        return values + lax.ppermute(values, "dp", self.far_swap)


def head_tables(count, model_width, window):
    slots = -(-HEADS // count)
    wide = slots * HD
    lists = [[[] for _ in range(count)] for _ in range(count)]
    for column in range(3 * model_width):
        src, local = divmod(column, window)
        part, within = divmod(column, model_width)
        head, lane = divmod(within, HD)
        dst, slot = head % count, head // count
        lists[src][dst].append((local, part * wide + slot * HD + lane))
    most = max(len(entry) for row in lists for entry in row)
    most = -(-most // 64) * 64
    pack = np.full((count, count * most), -1, np.int32)
    unpack = np.full((count, count * most), -1, np.int32)
    for src in range(count):
        for dst in range(count):
            for place, (local, target) in enumerate(lists[src][dst]):
                pack[src, dst * most + place] = local
                unpack[dst, src * most + place] = target
    return pack, unpack, most


def pick_row(table, index):
    return lax.dynamic_index_in_dim(jnp.asarray(table), index, 0, keepdims=False)


def one_hot(rows, size):
    return (lax.broadcasted_iota(jnp.int32, (size, rows.shape[0]), 0) == rows[None, :]).astype(BF16)


def forward_kernel(pos_col, pos_row, query_ref, full_ref, context_ref, probs_ref, *, wide):
    slots, _, run, width = query_ref.shape
    rows = slots * run
    keys_total = full_ref.shape[0] * run
    query = query_ref[:, 0].reshape(rows, width)[:, :wide]
    full = full_ref[:, 0].reshape(keys_total, width)
    key, value = full[:, wide : 2 * wide], full[:, 2 * wide :]
    seen = pos_row[0] <= pos_col[0]
    lane_head = lax.broadcasted_iota(jnp.int32, (1, wide), 1) // HD
    context = jnp.zeros((rows, wide), F32)
    for head in range(wide // HD):
        mine = lane_head == head
        scores = dot_nt(jnp.where(mine, query, jnp.zeros_like(query)), key) * SCORE_SCALE
        scores = jnp.where(seen, scores, MASKED_SCORE)
        top = jnp.max(scores, axis=1, keepdims=True)
        raw = jnp.exp(scores - top)
        probs = (raw * (1.0 / jnp.sum(raw, axis=1, keepdims=True))).astype(BF16)
        probs_ref[0, head] = probs
        context = jnp.where(mine, dot(probs, value), context)
    context_ref[:, 0] = context.astype(BF16).reshape(slots, run, wide)


def backward_kernel(query_ref, full_ref, grad_ref, probs_ref, out_ref, key_sum, value_sum, *, wide):
    step = pl.program_id(1)
    slots, _, run, width = query_ref.shape
    rows = slots * run
    count = full_ref.shape[0]
    keys_total = count * run
    query = query_ref[:, 0].reshape(rows, width)[:, :wide]
    full = full_ref[:, 0].reshape(keys_total, width)
    key, value = full[:, wide : 2 * wide], full[:, 2 * wide :]
    grad = grad_ref[:, 0].reshape(rows, wide)
    lane_head = lax.broadcasted_iota(jnp.int32, (1, wide), 1) // HD

    @pl.when(step == 0)
    def _():
        key_sum[...] = jnp.zeros_like(key_sum)
        value_sum[...] = jnp.zeros_like(value_sum)

    query_grad = jnp.zeros((rows, wide), F32)
    key_grad = jnp.zeros((keys_total, wide), F32)
    value_grad = jnp.zeros((keys_total, wide), F32)
    for head in range(wide // HD):
        mine = lane_head == head
        probs_low = probs_ref[0, head]
        probs = probs_low.astype(F32)
        grad_probs = dot_nt(jnp.where(mine, grad, jnp.zeros_like(grad)), value)
        weighted = probs * grad_probs
        delta = jnp.sum(weighted, axis=1, keepdims=True)
        grad_scores = (weighted - probs * delta).astype(BF16)
        query_grad = jnp.where(mine, dot(grad_scores, key), query_grad)
        key_grad = jnp.where(mine, dot_tn(grad_scores, query), key_grad)
        value_grad = jnp.where(mine, dot_tn(probs_low, grad), value_grad)
    key_sum[...] += key_grad
    value_sum[...] += value_grad
    out_ref[pl.ds(step * slots, slots), 0, :, :wide] = (
        (query_grad * SCORE_SCALE).astype(BF16).reshape(slots, run, wide)
    )

    @pl.when(step == pl.num_programs(1) - 1)
    def _():
        out_ref[:, 0, :, wide : 2 * wide] = (
            (key_sum[...] * SCORE_SCALE).astype(BF16).reshape(count, run, wide)
        )
        out_ref[:, 0, :, 2 * wide :] = value_sum[...].astype(BF16).reshape(count, run, wide)


def attention_forward(qkv_rows, positions):
    count, _, run, width = qkv_rows.shape
    wide = width // 3
    heads = wide // HD
    length = count * run
    block = min(length, 512)
    slots = block // run
    steps = length // block
    by_sequence = positions.reshape(count, SEQS, run).transpose(1, 0, 2).reshape(SEQS, length)
    return pl.pallas_call(
        functools.partial(forward_kernel, wide=wide),
        grid=(SEQS, steps),
        in_specs=[
            pl.BlockSpec((1, block, 1), lambda s, i: (s, i, 0)),
            pl.BlockSpec((1, 1, length), lambda s, i: (s, 0, 0)),
            pl.BlockSpec((slots, 1, run, width), lambda s, i: (i, s, 0, 0)),
            pl.BlockSpec((count, 1, run, width), lambda s, i: (0, s, 0, 0)),
        ],
        out_specs=[
            pl.BlockSpec((slots, 1, run, wide), lambda s, i: (i, s, 0, 0)),
            pl.BlockSpec((1, heads, block, length), lambda s, i: (s, 0, i, 0)),
        ],
        out_shape=[
            jax.ShapeDtypeStruct((count, SEQS, run, wide), BF16),
            jax.ShapeDtypeStruct((SEQS, heads, length, length), BF16),
        ],
        compiler_params=pltpu.CompilerParams(vmem_limit_bytes=60 * 1024 * 1024),
        cost_estimate=LARGE_COST,
        name="attention_forward",
    )(by_sequence[:, :, None], by_sequence[:, None, :], qkv_rows, qkv_rows)


def attention_backward(qkv_rows, grad_context, probs):
    count, _, run, width = qkv_rows.shape
    wide = width // 3
    heads = wide // HD
    length = count * run
    block = min(length, 512)
    slots = block // run
    steps = length // block
    return pl.pallas_call(
        functools.partial(backward_kernel, wide=wide),
        grid=(SEQS, steps),
        in_specs=[
            pl.BlockSpec((slots, 1, run, width), lambda s, i: (i, s, 0, 0)),
            pl.BlockSpec((count, 1, run, width), lambda s, i: (0, s, 0, 0)),
            pl.BlockSpec((slots, 1, run, wide), lambda s, i: (i, s, 0, 0)),
            pl.BlockSpec((1, heads, block, length), lambda s, i: (s, 0, i, 0)),
        ],
        out_specs=pl.BlockSpec((count, 1, run, width), lambda s, i: (0, s, 0, 0)),
        out_shape=jax.ShapeDtypeStruct((count, SEQS, run, width), BF16),
        scratch_shapes=[pltpu.VMEM((length, wide), F32), pltpu.VMEM((length, wide), F32)],
        compiler_params=pltpu.CompilerParams(vmem_limit_bytes=60 * 1024 * 1024),
        cost_estimate=SMALL_COST,
        name="attention_backward",
    )(qkv_rows, qkv_rows, grad_context, probs)


def in_order(side, own, other, axis=0):
    first = jnp.where(side == 0, own, other)
    second = jnp.where(side == 0, other, own)
    return jnp.concatenate([first, second], axis=axis)


def normalize(values):
    centred = values - jnp.mean(values, axis=1, keepdims=True)
    spread = lax.rsqrt(jnp.mean(centred * centred, axis=1, keepdims=True) + NORM_EPS)
    return centred * spread, spread


def normalize_back(normal, spread, gain, grad):
    scaled = grad * gain
    along = jnp.mean(scaled * normal, axis=1, keepdims=True)
    return spread * (scaled - jnp.mean(scaled, axis=1, keepdims=True) - normal * along)


def first_rows(pieces, scalars, weight, gain, shift, bias):
    rows, width = pieces[0][0].shape
    steps = len(pieces)
    total = 2 * steps * rows
    columns = weight.shape[1]

    def kernel(marks, *refs):
        given, (w, g, s, b), outs = refs[: 2 * steps], refs[2 * steps : 2 * steps + 4], refs[-3:]
        for t in range(steps):

            @pl.when(pl.program_id(0) == t)
            def _(t=t):
                outs[0][...] = in_order(marks[0], given[2 * t][...], given[2 * t + 1][...])

        normal, _ = normalize(outs[0][...].astype(F32))
        outs[1][...] = normal.astype(BF16)
        scaled = (normal * g[...] + s[...]).astype(BF16)
        outs[2][...] = (dot(scaled, w[...]) + b[...]).astype(BF16)

    def block(width):
        return pl.BlockSpec((2 * rows, width), lambda t, marks: (marks[1 + t], 0))

    flat = [piece for pair in pieces for piece in pair]
    return call(
        kernel,
        [struct((total, width), BF16), struct((total, width), BF16), struct((total, columns), BF16)],
        [block(width), block(width), block(columns)],
        grid=(steps,),
        in_blocks=[whole((rows, width))] * (2 * steps)
        + [whole(weight.shape), whole((1, width)), whole((1, width)), whole((1, columns))],
        scalars=scalars,
        name="first_rows",
    )(*flat, weight, gain, shift, bias)


def residual_rows(tokens_all, pieces, scalars, weight, bias):
    total, width = tokens_all.shape
    many = len(pieces)
    wide = pieces[0][0].shape[1]
    rows = min(total, 256)

    def kernel(marks, tokens, *refs):
        given, (w, b, out) = refs[: 2 * many], refs[2 * many :]
        value = tokens[...].astype(F32) + b[...]
        for t in range(many):
            pair = in_order(marks[0], given[2 * t][...], given[2 * t + 1][...], axis=1)
            begin = pl.multiple_of(marks[1 + t] * (2 * wide), 2 * wide)
            value += dot(pair, w[pl.ds(begin, 2 * wide)])
        out[...] = value

    def block(width):
        return pl.BlockSpec((rows, width), lambda i, marks: (i, 0))

    return call(
        kernel,
        struct((total, width), F32),
        block(width),
        grid=(total // rows,),
        in_blocks=[block(width)] + [block(wide)] * (2 * many) + [whole(weight.shape), whole((1, width))],
        scalars=scalars,
        name="residual_rows",
    )(tokens_all, *[piece for pair in pieces for piece in pair], weight, bias)


def second_rows(partial, pair, scalars, weight, gain, shift, steps):
    total, width = partial.shape
    wide = pair[0].shape[1]
    own_rows = total // (2 * steps)
    rows = 2 * own_rows

    def kernel(marks, before, first, second, w, g, s, normed, own):
        both = in_order(marks[0], first[...], second[...], axis=1)
        residual = before[...] + dot(both, w[...])
        normal, _ = normalize(residual)
        normed[...] = (normal * g[...] + s[...]).astype(BF16)

        @pl.when(pl.program_id(0) == marks[1])
        def _():
            own[...] = jnp.where(marks[0] == 0, residual[:own_rows], residual[own_rows:])

    def block(width):
        return pl.BlockSpec((rows, width), lambda i, marks: (i, 0))

    return call(
        kernel,
        [struct((total, width), BF16), struct((own_rows, width), F32)],
        [block(width), whole((own_rows, width))],
        grid=(steps,),
        in_blocks=[
            block(width),
            block(wide),
            block(wide),
            pl.BlockSpec((2 * wide, width), lambda i, marks: (marks[steps], 0)),
            whole((1, width)),
            whole((1, width)),
        ],
        scalars=scalars,
        name="second_rows",
    )(partial, *pair, weight, gain, shift)


def hidden_rows(normed, pairs, scalars, w_fc, w_proj, bias, kept, taken, rows):
    total, width = normed.shape
    hidden = w_fc.shape[1]
    many = len(taken)

    def kernel(marks, block, *refs):
        given, (fc, proj, b) = refs[: 2 * many], refs[2 * many : 2 * many + 3]
        act_ref, grad_ref, cot_ref = refs[-3 - 2 * many : -2 * many]
        parts = refs[-2 * many :]
        for i in range(many):

            @pl.when(pl.program_id(0) == i)
            def _(i=i):
                cot_ref[...] = in_order(marks[0], given[2 * i][...], given[2 * i + 1][...])

        z = dot(block[...], fc[...]) + b[...]
        square = z * z
        tanh = jnp.tanh(0.7978845608028654 * (z + 0.044715 * (square * z)))
        half = 0.5 * (1.0 + tanh)
        slope = half + 0.5 * z * (1.0 - tanh * tanh) * (
            0.7978845608028654 + (0.7978845608028654 * 3.0 * 0.044715) * square
        )
        act_ref[...] = (z * half).astype(BF16)
        grad = (dot(cot_ref[...], proj[...]) * slope).astype(BF16)
        grad_ref[...] = grad
        part = dot_nt(grad, fc[...])
        mine = jnp.where(marks[0] == 0, part[:rows], part[rows:])
        other = jnp.where(marks[0] == 0, part[rows:], part[:rows]).astype(BF16)
        for i in range(many):

            @pl.when(pl.program_id(0) == i)
            def _(i=i):
                parts[2 * i][...] = mine
                parts[2 * i + 1][...] = other

    def block(width):
        return pl.BlockSpec((2 * rows, width), lambda i, marks: (marks[1 + i], 0))

    operands = [normed] + [piece for pair in pairs for piece in pair] + [w_fc, w_proj, bias]
    blocks = [block(width)] + [whole((rows, width))] * (2 * many)
    blocks += [whole(w_fc.shape), whole(w_proj.shape), whole((1, hidden))]
    alias = {}
    if kept is not None:
        alias = {1 + len(operands) + i: i for i in range(3)}
        operands += list(kept)
        blocks += [pl.BlockSpec(memory_space=pl.ANY)] * 3
    outs = call(
        kernel,
        [struct((total, hidden), BF16), struct((total, hidden), BF16), struct((total, width), BF16)]
        + [struct((rows, width), dtype) for _ in taken for dtype in (F32, BF16)],
        [block(hidden), block(hidden), block(width)] + [whole((rows, width))] * (2 * many),
        grid=(many,),
        in_blocks=blocks,
        scalars=scalars,
        alias=alias,
        name="hidden_rows",
    )(*operands)
    return outs[:3], {t: (outs[3 + 2 * i], outs[4 + 2 * i]) for i, t in enumerate(taken)}


def turned_product(left, right, name):
    total, width = left.shape
    columns = right.shape[1]
    tile = 256

    def kernel(left_ref, right_ref, out_ref):
        out_ref[...] = dot(left_ref[...].T, right_ref[...]).astype(BF16)

    return call(
        kernel,
        struct((width, columns), BF16),
        pl.BlockSpec((tile, columns), lambda i: (i, 0)),
        grid=(pl.cdiv(width, tile),),
        in_blocks=[pl.BlockSpec((total, tile), lambda i: (0, i)), whole(right.shape)],
        name=name,
    )(left, right)


def head_product(normal, grad, weight, gain, shift):
    total, width = normal.shape
    columns = grad.shape[1]
    tile = 256

    def kernel(left, right, w, g, s, out, gain_sum, shift_sum, grad_sum):
        @pl.when(pl.program_id(0) == 0)
        def _():
            grad_sum[...] = jnp.sum(right[...].astype(F32), axis=0, keepdims=True)

        raw = dot(left[...].T, right[...])
        sums = grad_sum[...]
        low = w[...].astype(F32)
        gain_sum[...] = jnp.sum(raw * low, axis=1, keepdims=True)
        shift_sum[...] = jnp.sum(low * sums, axis=1, keepdims=True)
        out[...] = (raw * g[...] + s[...] * sums).astype(BF16)

    column = pl.BlockSpec((tile, 1), lambda i: (i, 0))
    return call(
        kernel,
        [
            struct((width, columns), BF16),
            struct((width, 1), F32),
            struct((width, 1), F32),
            struct((1, columns), F32),
        ],
        [pl.BlockSpec((tile, columns), lambda i: (i, 0)), column, column, whole((1, columns))],
        grid=(pl.cdiv(width, tile),),
        in_blocks=[
            pl.BlockSpec((total, tile), lambda i: (0, i)),
            whole(grad.shape),
            pl.BlockSpec((tile, columns), lambda i: (i, 0)),
            column,
            column,
        ],
        name="head_product",
    )(normal, grad, weight, gain, shift)


def ring_parts(left, right, scalars, taken, steps, name):
    total, inner = left.shape
    width = right.shape[0]
    rows = total // (2 * steps)

    def kernel(marks, left_ref, right_ref, *outs):
        for i, t in enumerate(taken):
            begin = pl.multiple_of(marks[1 + t] * (2 * rows), 2 * rows)
            part = dot_nt(left_ref[pl.ds(begin, 2 * rows)], right_ref[...])
            outs[2 * i][...] = jnp.where(marks[0] == 0, part[:rows], part[rows:])
            outs[2 * i + 1][...] = jnp.where(marks[0] == 0, part[rows:], part[:rows]).astype(BF16)

    outs = call(
        kernel,
        [struct((rows, width), dtype) for _ in taken for dtype in (F32, BF16)],
        [whole((rows, width))] * (2 * len(taken)),
        in_blocks=[whole(left.shape), whole(right.shape)],
        scalars=scalars,
        name=name,
    )(left, right)
    return {t: (outs[2 * i], outs[2 * i + 1]) for i, t in enumerate(taken)}


def second_back(residual, terms, cotangent, gain, weight, count):
    rows, width = residual.shape
    wide = weight.shape[0] // count
    columns = width // count

    def kernel(res, mine, swapped, carried, cot, g, w, grad_ref, low_ref, sums_ref, out_ref):
        @pl.when(pl.program_id(0) == 0)
        def _():
            grad = mine[...] + swapped[...].astype(F32) + carried[...].astype(F32)
            normal, spread = normalize(res[...])
            total = cot[...].astype(F32) + normalize_back(normal, spread, g[...], grad)
            grad_ref[...] = total
            low = total.astype(BF16)
            low_ref[...] = low
            sums_ref[0:1] = jnp.sum(grad * normal, axis=0, keepdims=True)
            sums_ref[1:2] = jnp.sum(grad, axis=0, keepdims=True)
            sums_ref[2:3] = jnp.sum(low.astype(F32), axis=0, keepdims=True)
            sums_ref[3:4] = jnp.sum(cot[...].astype(F32), axis=0, keepdims=True)

        out_ref[0, :, :wide] = dot_nt(low_ref[...], w[...]).astype(BF16)
        for j in range(count):

            @pl.when(pl.program_id(0) == j)
            def _(j=j):
                out_ref[0, :, wide:] = low_ref[:, j * columns : (j + 1) * columns]

    row = whole((rows, width))
    return call(
        kernel,
        [
            struct((rows, width), F32),
            struct((rows, width), BF16),
            struct((4, width), F32),
            struct((count, rows, wide + columns), BF16),
        ],
        [row, row, whole((4, width)), pl.BlockSpec((1, rows, wide + columns), lambda i: (i, 0, 0))],
        grid=(count,),
        in_blocks=[row] * 5 + [whole((1, width)), pl.BlockSpec((wide, width), lambda i: (i, 0))],
        name="second_back",
    )(residual, *terms, cotangent, gain, weight)


def first_back(tokens, terms, residual_grad, gain):
    rows, width = tokens.shape

    def kernel(x, mine, swapped, carried, res, g, out_ref):
        grad = mine[...] + swapped[...].astype(F32) + carried[...].astype(F32)
        normal, spread = normalize(x[...].astype(F32))
        out_ref[...] = (res[...] + normalize_back(normal, spread, g[...], grad)).astype(BF16)

    row = whole((rows, width))
    return call(
        kernel,
        struct((rows, width), BF16),
        row,
        in_blocks=[row] * 5 + [whole((1, width))],
        name="first_back",
    )(tokens, *terms, residual_grad, gain)


def heads_rows(me, pieces, count, slots):
    rows, width = pieces[0].shape
    unit = math.gcd(rows, HD)

    def kernel(mark, *refs):
        out = refs[4]
        for h in range(HEADS, count * slots):
            place = ((h % count) * slots + h // count) * HD
            out[place : place + HD] = jnp.zeros((HD, width), BF16)
        for r in range(4):
            for piece in range(rows // unit):
                row = (mark[0] ^ r) * rows + piece * unit
                head = row // HD
                target = ((head % count) * slots + head // count) * HD + row % HD
                out[pl.ds(pl.multiple_of(target, unit), unit)] = refs[r][
                    piece * unit : (piece + 1) * unit
                ]

    return call(
        kernel,
        struct((count * slots * HD, width), BF16),
        whole((count * slots * HD, width)),
        in_blocks=[whole((rows, width))] * 4,
        scalars=me[None],
        name="heads_rows",
    )(*pieces)


def out_product(pieces, columns, scalars, count, slots):
    total, width = columns.shape
    wide = slots * HD
    steps = len(pieces)

    def kernel(marks, *refs):
        given, right, out = refs[: 2 * steps], refs[2 * steps], refs[-1]
        for t in range(steps):
            for b in range(2):
                owner = marks[1 + t] * 2 + (marks[0] if b == 0 else 1 - marks[0])
                value = dot_tn(given[2 * t + b][...], right[...]).astype(BF16)
                for slot in range(slots):
                    begin = pl.multiple_of((slot * count + owner) * HD, HD)
                    out[pl.ds(begin, HD)] = value[slot * HD : (slot + 1) * HD]

    return call(
        kernel,
        struct((slots * count * HD, width), BF16),
        whole((slots * count * HD, width)),
        in_blocks=[whole((total, wide))] * (2 * steps) + [whole(columns.shape)],
        scalars=scalars,
        name="out_product",
    )(*[piece for pair in pieces for piece in pair], columns)


def rows_product(left, right, name):
    total, inner = left.shape
    width = right.shape[0]
    block = min(total, 512)

    def kernel(left_ref, right_ref, out_ref):
        out_ref[...] = dot_nt(left_ref[...], right_ref[...]).astype(BF16)

    return call(
        kernel,
        struct((total, width), BF16),
        pl.BlockSpec((block, width), lambda i: (i, 0)),
        grid=(total // block,),
        in_blocks=[pl.BlockSpec((block, inner), lambda i: (i, 0)), whole(right.shape)],
        name=name,
    )(left, right)


def shards(
    tokens,
    cotangent,
    positions,
    qkv_weight,
    qkv_first,
    qkv_second,
    out_weight,
    out_first,
    out_second,
    fc_weight,
    fc_first,
    fc_second,
    proj_weight,
    proj_first,
    proj_second,
    small_weight,
    small_first,
    small_second,
):
    count = lax.axis_size("seq")
    ring = Ring(count)
    square = Square()
    me = lax.axis_index("seq")
    rows, width = tokens.shape
    seq_rows = rows // SEQS
    window = qkv_weight.shape[1]
    slots = -(-HEADS // count)
    wide = slots * HD
    small_count, small_width = small_weight.shape
    hidden = fc_weight.shape[1]
    all_rows = count * rows
    steps = ring.steps
    marks = jnp.stack([ring.side] + [ring.position(t) for t in range(steps)])
    tokens = by_rows(tokens)
    cotangent = by_rows(cotangent)

    token_tour = Tour(ring, tokens)
    token_tour.step()
    token_tour.step()
    pack, unpack, most = head_tables(count, width, window)
    pack_hot = one_hot(pick_row(pack, me), window)
    packed = jnp.einsum(
        "rc,cdl->drl",
        qkv_weight.astype(BF16),
        pack_hot.reshape(window, count, most),
        preferred_element_type=BF16,
    )
    packed = after(packed, token_tour.moved[0])
    depth = packed.shape[1]
    small_flat = jnp.concatenate(
        [
            small_weight.reshape(-1).astype(BF16),
            (positions // 32).astype(BF16),
            (positions % 32).astype(BF16),
        ]
    )
    small_depth = -(-small_flat.shape[0] // most)
    small_depth += -small_depth % 16
    small_flat = jnp.pad(small_flat, (0, small_depth * most - small_flat.shape[0]))
    small_pack = jnp.broadcast_to(
        small_flat.reshape(1, small_depth, most), (count, small_depth, most)
    )
    received = lax.all_to_all(jnp.concatenate([packed, small_pack], axis=1), "seq", 0, 0)
    token_tour.step()
    received = after(received, token_tour.moved[1], token_tour.current)

    unpack_hot = one_hot(pick_row(unpack, me), 3 * wide)
    head_part = jnp.einsum(
        "srl,ksl->rk",
        received[:, :depth],
        unpack_hot.reshape(3 * wide, count, most),
        preferred_element_type=BF16,
    )
    for t in range(3, steps):
        token_tour.step()
    head_pieces = square.gather(head_part, token_tour.current)
    w_head = square.place(head_pieces)

    small_all = received[:, depth:].reshape(count, small_depth * most).astype(F32)
    small_rows = small_all[:, : small_count * small_width].reshape(count, small_count, small_width)
    small_rows = small_rows.transpose(1, 0, 2).reshape(small_count, width)
    pos_all = small_all[:, small_count * small_width :][:, : 2 * rows].reshape(count, 2, rows)
    pos_all = (pos_all[:, 0] * 32.0 + pos_all[:, 1]).astype(jnp.int32)

    def own_heads(row):
        padded = jnp.pad(row, (0, slots * count * HD - width)).reshape(slots, count, HD)
        return lax.dynamic_index_in_dim(padded, me, 1, keepdims=False).reshape(wide)

    head_bias = jnp.concatenate(
        [own_heads(small_rows[0]), jnp.zeros((wide,), F32), own_heads(small_rows[1])]
    )
    fc_bias = lax.dynamic_slice_in_dim(small_rows[3:7].reshape(-1), me * hidden, hidden, 0)
    gain_one, shift_one = small_rows[8][None], small_rows[9][None]
    gain_two, shift_two = small_rows[10][None], small_rows[11][None]

    ready = (w_head, token_tour.moved[-1])
    out_part = lax.all_gather(
        after(out_weight, head_part).astype(BF16), "seq", axis=1, tiled=True
    )
    tokens_all, normal_all, qkv_rows = first_rows(
        token_tour.pieces, marks, w_head, gain_one, shift_one, head_bias[None]
    )
    qkv_all = qkv_rows.reshape(count, SEQS, seq_rows, 3 * wide)
    context, probs = attention_forward(qkv_all, pos_all)
    context = context.reshape(all_rows, wide)

    cot_zero = lax.ppermute(after(cotangent, *ready), "seq", ring.swap)
    cot_moving = lax.ppermute(after(cotangent, *ready), "seq", ring.behind)
    fc_low = after(fc_weight, *ready).astype(BF16)
    context = after(context, cot_zero, cot_moving)
    fc_pieces = square.gather(fc_low)
    proj_pieces = square.gather(after(proj_weight, fc_pieces[2], context).T.astype(BF16))
    context_tour = Tour(ring, context)
    w_fc, w_proj = None, None
    for t in range(steps):
        if t == 1:
            context_tour.step(land=(fc_pieces[2],))
            w_fc = square.place(after(fc_pieces, context_tour.moved[0]))
        elif t == 2:
            out_part = after(out_part, context_tour.current, context_tour.moved[0])
            out_pieces = square.gather(by_rows(out_part))
            context_tour.step(land=(out_part, w_fc))
        else:
            context_tour.step(land=(proj_pieces[2],) if t == steps - 1 else ())
    w_proj = square.place(after(proj_pieces, context_tour.current))
    w_out = heads_rows(square.me, out_pieces, count, slots)
    partial = residual_rows(
        tokens_all, context_tour.pieces[:-1], marks, w_out, small_rows[2][None]
    )
    last_pair = lax.optimization_barrier((context_tour.pieces[-1], partial, w_proj))[0]
    normed_all, residual = second_rows(
        partial, last_pair, marks, w_out, gain_two, shift_two, steps
    )
    cot_pieces = {0: (cotangent, cot_zero)}
    cot_moving = after(cot_moving, last_pair[1])
    crossed = lax.ppermute(cot_moving, "seq", ring.swap)
    cot_pieces[steps - 1] = (cot_moving, crossed)
    cot_moving = after(lax.ppermute(cot_moving, "seq", ring.behind), residual)

    def feed_forward(kept, taken, *begin):
        chosen = jnp.stack([ring.side] + [ring.position(t) for t in taken])
        return hidden_rows(
            normed_all,
            [cot_pieces[t] for t in taken],
            after(chosen, *begin) if begin else chosen,
            w_fc,
            w_proj,
            fc_bias[None],
            kept,
            taken,
            rows,
        )

    crossed = lax.ppermute(after(cot_moving, crossed), "seq", ring.swap)
    cot_pieces[steps - 2] = (cot_moving, crossed)
    cot_moving = lax.ppermute(cot_moving, "seq", ring.behind)
    kept, parts = feed_forward(None, [steps - 1])
    cot_moving, cot_pieces[steps - 2] = lax.optimization_barrier(
        (cot_moving, cot_pieces[steps - 2], parts[steps - 1][1])
    )[:2]
    for t in range(3, steps):
        crossed = lax.ppermute(after(cot_moving, crossed), "seq", ring.swap)
        cot_pieces[steps - t] = (cot_moving, crossed)
        if t + 1 < steps:
            cot_moving = lax.ppermute(cot_moving, "seq", ring.behind)
    grad_fold = Fold(ring, parts)
    kept, more = feed_forward(kept, [steps - 2])
    parts.update(more)
    grad_fold.beside(*parts[steps - 2], crossed)
    grad_fold.step()
    kept, more = feed_forward(kept, list(reversed(range(steps - 2))), grad_fold.carried)
    parts.update(more)
    grad_fold.beside(*parts[0])
    hidden_low, grad_pre_low, cot_all = kept
    grad_fold.step()
    output_partial = rows_product(after(hidden_low, grad_fold.carried), w_proj, "output_product")
    grad_fold.beside(output_partial)
    for _ in range(3, steps):
        grad_fold.step()
    fc_sum = turned_product(after(normed_all, grad_fold.carried), grad_pre_low, "fc_product")
    grad_fold.beside(fc_sum)
    output_sum = lax.psum_scatter(output_partial, "seq", scatter_dimension=0, tiled=True)
    terms = grad_fold.terms
    grad_residual, grad_attn_low, row_sums, grad_sent = second_back(
        residual, terms, cotangent, gain_two, w_out, count
    )
    grad_bias_fc = jnp.sum(after(grad_pre_low, grad_sent).astype(F32), axis=0)
    fc_column = square.half_sum(after(fc_sum, grad_sent))

    proj_sum = turned_product(after(cot_all, grad_sent), hidden_low, "proj_product")
    grad_back = after(lax.all_to_all(grad_sent, "seq", 0, 0), proj_sum, grad_bias_fc)
    proj_column = square.half_sum(after(proj_sum, grad_back))
    grad_context = grad_back[:, :, :wide]
    out_columns = out_weight.shape[1]
    attn_columns = grad_back[:, :, wide:].reshape(all_rows, out_columns)
    grad_qkv = attention_backward(
        qkv_all, grad_context.reshape(count, SEQS, seq_rows, wide), probs
    ).reshape(all_rows, 3 * wide)
    fc_grad = after(square.other_sum(fc_column), grad_qkv)
    proj_grad = square.other_sum(after(proj_column, grad_qkv))
    parts = ring_parts(grad_qkv, w_head, marks, [steps - 1], steps, "first_parts")
    input_fold = Fold(ring, parts)
    parts.update(
        ring_parts(
            after(grad_qkv, *parts[steps - 1]), w_head, marks, range(steps - 1), steps, "input_parts"
        )
    )
    head_sum, grad_gain_one, grad_shift_one, grad_qkv_sum = head_product(
        after(normal_all, *parts[0]), grad_qkv, w_head, small_rows[8][:, None], small_rows[9][:, None]
    )
    input_fold.beside(head_sum)
    input_fold.step()

    attn_columns = after(attn_columns, input_fold.carried)
    out_sum = out_product(context_tour.pieces, attn_columns, marks, count, slots)[:width]
    input_fold.beside(out_sum)
    head_column = square.half_sum(after(head_sum, input_fold.carried))
    input_fold.step()
    out_column = square.half_sum(after(out_sum, input_fold.carried))
    fc_new = adam_update(
        fc_weight, fc_first, fc_second, after(fc_grad, input_fold.carried), 0.02, 0.1
    )
    input_fold.beside(fc_new[0], head_column)
    for _ in range(3, steps):
        input_fold.step()
    head_far = square.other_sum(after(head_column, input_fold.carried))
    input_fold.beside(output_sum)
    out_grad = square.other_sum(out_column)
    input_grad = first_back(tokens, input_fold.terms, grad_residual, gain_one)
    head_grad = after(head_far, input_grad).astype(BF16)
    unpack_back = unpack_hot.reshape(3 * wide, count, most)
    head_packed = jnp.einsum("rk,ksl->srl", head_grad, unpack_back, preferred_element_type=BF16)
    head_back = lax.all_to_all(head_packed, "seq", 0, 0)
    qkv_grad = jnp.einsum(
        "drl,cdl->rc",
        head_back,
        pack_hot.reshape(window, count, most),
        preferred_element_type=F32,
    )
    output = (residual + output_sum.astype(F32) + small_rows[7]).astype(BF16)

    def place_heads(values):
        spread = (jnp.arange(count) == me).astype(F32)[None, :, None]
        placed = values.reshape(slots, 1, HD) * spread
        return placed.reshape(-1)[:width]

    grad_bias_fc = grad_bias_fc[None, :] * (jnp.arange(count) == me).astype(F32)[:, None]
    grad_qkv_sum = after(grad_qkv_sum, head_packed)[0]
    grad_small = jnp.concatenate(
        [
            place_heads(grad_qkv_sum[:wide])[None],
            place_heads(grad_qkv_sum[2 * wide :])[None],
            row_sums[2:3],
            grad_bias_fc.reshape(-1, width),
            row_sums[3:4],
            grad_gain_one[:, 0][None],
            grad_shift_one[:, 0][None],
            row_sums[0:1],
            row_sums[1:2],
        ],
        axis=0,
    )
    small_sent = grad_small.astype(BF16).reshape(small_count, count, small_width)
    small_part = jnp.sum(
        lax.all_to_all(small_sent.transpose(1, 0, 2), "seq", 0, 0).astype(F32), axis=0
    )
    small_grad = square.sum(small_part)

    qkv_new = adam_update(qkv_weight, qkv_first, qkv_second, qkv_grad, 0.02, 0.1)
    out_new = adam_update(out_weight, out_first, out_second, out_grad, 0.3, 0.1)
    proj_new = adam_update(
        proj_weight.T, proj_first.T, proj_second.T, proj_grad, 0.02, 0.1
    )
    proj_new = [value.T for value in proj_new]
    small_new = adam_update(small_weight, small_first, small_second, small_grad, 0.3, 0.0)
    return (
        output,
        input_grad,
        *qkv_new,
        *out_new,
        *fc_new,
        *proj_new,
        *small_new,
        small_grad[7],
    )


def solution(mesh):
    rows = P(("dp", "seq"), None)
    matrix = P("dp", "seq")
    turned = P("seq", "dp")
    small = P(None, "seq")
    in_specs = (
        (rows, rows, P(("dp", "seq"))) + (matrix,) * 9 + (turned,) * 3 + (small,) * 3
    )
    out_specs = (rows, rows) + (matrix,) * 9 + (turned,) * 3 + (small,) * 3 + (P("seq"),)
    return jax.shard_map(shards, mesh=mesh, in_specs=in_specs, out_specs=out_specs, check_vma=False)
```

```python
import functools
import math

import jax
import jax.numpy as jnp
import numpy as np
from jax import lax
from jax.experimental import pallas as pl
from jax.experimental.layout import Layout, with_layout_constraint
from jax.experimental.pallas import tpu as pltpu
from jax.sharding import PartitionSpec as P

HEADS = 25
HD = 64
SEQS = 2
STEP = 10

NORM_EPS = 1e-05
SCORE_SCALE = 0.125
MASKED_SCORE = -1e30
BETA_ONE = 0.9
BETA_TWO = 0.95
ADAM_EPS = 1e-08
BF16 = jnp.bfloat16
F32 = jnp.float32
SMALL_COST = pl.CostEstimate(flops=1024, bytes_accessed=1024, transcendentals=0)
LARGE_COST = pl.CostEstimate(flops=8 * 10**9, bytes_accessed=8 * 10**6, transcendentals=0)


def adam_update(weight, first_moment, second, gradient, step_rate, decay_rate):
    moment_new = BETA_ONE * first_moment + (1.0 - BETA_ONE) * gradient
    second_new = BETA_TWO * second + (1.0 - BETA_TWO) * gradient * gradient
    direction = (
        moment_new
        / (1.0 - BETA_ONE**STEP)
        / (jnp.sqrt(second_new / (1.0 - BETA_TWO**STEP)) + ADAM_EPS)
    )
    return (moment_new, second_new, weight - step_rate * (direction + decay_rate * weight))


def dot(left, right):
    return jnp.dot(left, right, preferred_element_type=F32)


def dot_nt(left, right):
    return lax.dot_general(left, right, (((1,), (1,)), ((), ())), preferred_element_type=F32)


def dot_tn(left, right):
    return lax.dot_general(left, right, (((0,), (0,)), ((), ())), preferred_element_type=F32)


def after(value, *others):
    return lax.optimization_barrier((value,) + others)[0]


def by_rows(value):
    return with_layout_constraint(value, Layout(major_to_minor=(0, 1)))


def call(
    kernel, out, blocks, grid=None, in_blocks=None, scalars=None, alias=None, scratch=(), name=None
):
    operands = 0 if scalars is None else 1
    spec = dict(
        in_specs=in_blocks,
        out_specs=blocks,
        grid=grid or (1,),
        scratch_shapes=list(scratch),
    )
    if operands:
        spec = dict(grid_spec=pltpu.PrefetchScalarGridSpec(num_scalar_prefetch=1, **spec))
    run = pl.pallas_call(
        kernel,
        out_shape=out,
        input_output_aliases=alias or {},
        compiler_params=pltpu.CompilerParams(vmem_limit_bytes=60 * 1024 * 1024),
        cost_estimate=SMALL_COST,
        name=name,
        **spec,
    )
    if operands:
        return lambda *given: run(scalars, *given)
    return run


def whole(shape):
    return pl.BlockSpec(shape, lambda *_: (0,) * len(shape))


def struct(shape, dtype):
    return jax.ShapeDtypeStruct(shape, dtype)


class Ring:
    def __init__(self, count):
        self.sides = 2
        self.steps = count // 2
        steps = self.steps
        self.swap = [(j, j ^ 1) for j in range(count)]
        self.ahead = [(z * 2 + x, ((z + 1) % steps) * 2 + x) for z in range(steps) for x in range(2)]
        self.behind = [(dst, src) for src, dst in self.ahead]
        me = lax.axis_index("seq")
        self.place, self.side = me // 2, me % 2

    def position(self, t):
        return (self.place + self.steps - t) % self.steps

    def gather(self, block):
        tour = Tour(self, block)
        for _ in range(self.steps):
            tour.step()
        return tour


class Tour:
    def __init__(self, ring, block, back=False):
        self.ring, self.current, self.back = ring, block, back
        self.pieces = [None] * ring.steps
        self.moved = []

    def step(self, *begin, land=()):
        ring, t = self.ring, len(self.moved)
        if begin:
            self.current = after(self.current, *begin)
        if t:
            moved = lax.ppermute(self.current, "seq", ring.behind if self.back else ring.ahead)
            self.current = after(moved, self.moved[-1], *land)
        other = lax.ppermute(self.current, "seq", ring.swap)
        self.pieces[-t if self.back else t] = (self.current, other)
        self.moved.append(other)


class Fold:
    def __init__(self, ring, parts):
        self.ring, self.parts = ring, parts
        self.terms, self.count, self.carried = None, 0, None
        self.step()

    def step(self):
        ring = self.ring
        mine, other = self.parts[ring.steps - 1 - self.count]
        self.count += 1
        sent = None
        if self.terms is not None:
            sent = sum(term.astype(F32) for term in self.terms).astype(BF16)
            self.carried = sent
            other = after(other, sent)
        self.terms = [mine, lax.ppermute(other, "seq", ring.swap)]
        if sent is not None:
            self.terms.append(lax.ppermute(sent, "seq", ring.behind))

    def beside(self, *work):
        self.terms = list(lax.optimization_barrier((tuple(self.terms),) + work)[0])


class Square:
    def __init__(self):
        me = lax.axis_index("dp")
        self.me, self.far, self.near = me, me // 2, me % 2
        self.far_swap = [(j, j ^ 2) for j in range(4)]
        self.near_swap = [(j, j ^ 1) for j in range(4)]

    def near_of(self, block):
        return lax.ppermute(block, "dp", self.near_swap)

    def far_of(self, block):
        return lax.ppermute(block, "dp", self.far_swap)

    def gather(self, block, *begin):
        near, far = self.near_of(block), self.far_of(block)
        far = after(far, *begin) if begin else far
        return (block, near, far, lax.ppermute(far, "dp", self.near_swap))

    def place(self, pieces):
        rows, width = pieces[0].shape

        def kernel(me, *refs):
            for r in range(4):
                begin = pl.multiple_of((me[0] ^ r) * rows, 16)
                refs[4][pl.ds(begin, rows)] = refs[r][...]

        return call(
            kernel,
            struct((4 * rows, width), BF16),
            whole((4 * rows, width)),
            in_blocks=[whole((rows, width))] * 4,
            scalars=self.me[None],
            name="place_rows",
        )(*pieces)

    def half_sum(self, partial):
        parts = partial.reshape((2, 2, partial.shape[0] // 4) + partial.shape[1:])
        mine = lax.dynamic_index_in_dim(parts, self.near, 1, keepdims=False)
        other = lax.dynamic_index_in_dim(parts, 1 - self.near, 1, keepdims=False)
        return mine.astype(F32) + lax.ppermute(other, "dp", self.near_swap).astype(F32)

    def other_sum(self, column):
        mine = lax.dynamic_index_in_dim(column, self.far, 0, keepdims=False)
        other = lax.dynamic_index_in_dim(column, 1 - self.far, 0, keepdims=False)
        return mine + lax.ppermute(other.astype(BF16), "dp", self.far_swap).astype(F32)

    def sum(self, values):
        values = values + lax.ppermute(values, "dp", self.near_swap)
        return values + lax.ppermute(values, "dp", self.far_swap)


def head_tables(count, model_width, window):
    slots = -(-HEADS // count)
    wide = slots * HD
    lists = [[[] for _ in range(count)] for _ in range(count)]
    for column in range(3 * model_width):
        src, local = divmod(column, window)
        part, within = divmod(column, model_width)
        head, lane = divmod(within, HD)
        dst, slot = head % count, head // count
        lists[src][dst].append((local, part * wide + slot * HD + lane))
    most = max(len(entry) for row in lists for entry in row)
    most = -(-most // 64) * 64
    pack = np.full((count, count * most), -1, np.int32)
    unpack = np.full((count, count * most), -1, np.int32)
    for src in range(count):
        for dst in range(count):
            for place, (local, target) in enumerate(lists[src][dst]):
                pack[src, dst * most + place] = local
                unpack[dst, src * most + place] = target
    return pack, unpack, most


def pick_row(table, index):
    return lax.dynamic_index_in_dim(jnp.asarray(table), index, 0, keepdims=False)


def one_hot(rows, size):
    return (lax.broadcasted_iota(jnp.int32, (size, rows.shape[0]), 0) == rows[None, :]).astype(BF16)


def forward_kernel(pos_col, pos_row, query_ref, full_ref, context_ref, probs_ref, *, wide):
    slots, _, run, width = query_ref.shape
    rows = slots * run
    keys_total = full_ref.shape[0] * run
    query = query_ref[:, 0].reshape(rows, width)[:, :wide]
    full = full_ref[:, 0].reshape(keys_total, width)
    key, value = full[:, wide : 2 * wide], full[:, 2 * wide :]
    seen = pos_row[0] <= pos_col[0]
    lane_head = lax.broadcasted_iota(jnp.int32, (1, wide), 1) // HD
    context = jnp.zeros((rows, wide), F32)
    for head in range(wide // HD):
        mine = lane_head == head
        scores = dot_nt(jnp.where(mine, query, jnp.zeros_like(query)), key) * SCORE_SCALE
        scores = jnp.where(seen, scores, MASKED_SCORE)
        top = jnp.max(scores, axis=1, keepdims=True)
        raw = jnp.exp(scores - top)
        probs = (raw * (1.0 / jnp.sum(raw, axis=1, keepdims=True))).astype(BF16)
        probs_ref[0, head] = probs
        context = jnp.where(mine, dot(probs, value), context)
    context_ref[:, 0] = context.astype(BF16).reshape(slots, run, wide)


def backward_kernel(query_ref, full_ref, grad_ref, probs_ref, out_ref, key_sum, value_sum, *, wide):
    step = pl.program_id(1)
    slots, _, run, width = query_ref.shape
    rows = slots * run
    count = full_ref.shape[0]
    keys_total = count * run
    query = query_ref[:, 0].reshape(rows, width)[:, :wide]
    full = full_ref[:, 0].reshape(keys_total, width)
    key, value = full[:, wide : 2 * wide], full[:, 2 * wide :]
    grad = grad_ref[:, 0].reshape(rows, wide)
    lane_head = lax.broadcasted_iota(jnp.int32, (1, wide), 1) // HD

    @pl.when(step == 0)
    def _():
        key_sum[...] = jnp.zeros_like(key_sum)
        value_sum[...] = jnp.zeros_like(value_sum)

    query_grad = jnp.zeros((rows, wide), F32)
    key_grad = jnp.zeros((keys_total, wide), F32)
    value_grad = jnp.zeros((keys_total, wide), F32)
    for head in range(wide // HD):
        mine = lane_head == head
        probs_low = probs_ref[0, head]
        probs = probs_low.astype(F32)
        grad_probs = dot_nt(jnp.where(mine, grad, jnp.zeros_like(grad)), value)
        weighted = probs * grad_probs
        delta = jnp.sum(weighted, axis=1, keepdims=True)
        grad_scores = (weighted - probs * delta).astype(BF16)
        query_grad = jnp.where(mine, dot(grad_scores, key), query_grad)
        key_grad = jnp.where(mine, dot_tn(grad_scores, query), key_grad)
        value_grad = jnp.where(mine, dot_tn(probs_low, grad), value_grad)
    key_sum[...] += key_grad
    value_sum[...] += value_grad
    out_ref[pl.ds(step * slots, slots), 0, :, :wide] = (
        (query_grad * SCORE_SCALE).astype(BF16).reshape(slots, run, wide)
    )

    @pl.when(step == pl.num_programs(1) - 1)
    def _():
        out_ref[:, 0, :, wide : 2 * wide] = (
            (key_sum[...] * SCORE_SCALE).astype(BF16).reshape(count, run, wide)
        )
        out_ref[:, 0, :, 2 * wide :] = value_sum[...].astype(BF16).reshape(count, run, wide)


def attention_forward(qkv_rows, positions):
    count, _, run, width = qkv_rows.shape
    wide = width // 3
    heads = wide // HD
    length = count * run
    block = min(length, 512)
    slots = block // run
    steps = length // block
    by_sequence = positions.reshape(count, SEQS, run).transpose(1, 0, 2).reshape(SEQS, length)
    return pl.pallas_call(
        functools.partial(forward_kernel, wide=wide),
        grid=(SEQS, steps),
        in_specs=[
            pl.BlockSpec((1, block, 1), lambda s, i: (s, i, 0)),
            pl.BlockSpec((1, 1, length), lambda s, i: (s, 0, 0)),
            pl.BlockSpec((slots, 1, run, width), lambda s, i: (i, s, 0, 0)),
            pl.BlockSpec((count, 1, run, width), lambda s, i: (0, s, 0, 0)),
        ],
        out_specs=[
            pl.BlockSpec((slots, 1, run, wide), lambda s, i: (i, s, 0, 0)),
            pl.BlockSpec((1, heads, block, length), lambda s, i: (s, 0, i, 0)),
        ],
        out_shape=[
            jax.ShapeDtypeStruct((count, SEQS, run, wide), BF16),
            jax.ShapeDtypeStruct((SEQS, heads, length, length), BF16),
        ],
        compiler_params=pltpu.CompilerParams(vmem_limit_bytes=60 * 1024 * 1024),
        cost_estimate=LARGE_COST,
        name="attention_forward",
    )(by_sequence[:, :, None], by_sequence[:, None, :], qkv_rows, qkv_rows)


def attention_backward(qkv_rows, grad_context, probs):
    count, _, run, width = qkv_rows.shape
    wide = width // 3
    heads = wide // HD
    length = count * run
    block = min(length, 512)
    slots = block // run
    steps = length // block
    return pl.pallas_call(
        functools.partial(backward_kernel, wide=wide),
        grid=(SEQS, steps),
        in_specs=[
            pl.BlockSpec((slots, 1, run, width), lambda s, i: (i, s, 0, 0)),
            pl.BlockSpec((count, 1, run, width), lambda s, i: (0, s, 0, 0)),
            pl.BlockSpec((slots, 1, run, wide), lambda s, i: (i, s, 0, 0)),
            pl.BlockSpec((1, heads, block, length), lambda s, i: (s, 0, i, 0)),
        ],
        out_specs=pl.BlockSpec((count, 1, run, width), lambda s, i: (0, s, 0, 0)),
        out_shape=jax.ShapeDtypeStruct((count, SEQS, run, width), BF16),
        scratch_shapes=[pltpu.VMEM((length, wide), F32), pltpu.VMEM((length, wide), F32)],
        compiler_params=pltpu.CompilerParams(vmem_limit_bytes=60 * 1024 * 1024),
        cost_estimate=SMALL_COST,
        name="attention_backward",
    )(qkv_rows, qkv_rows, grad_context, probs)


def in_order(side, own, other, axis=0):
    first = jnp.where(side == 0, own, other)
    second = jnp.where(side == 0, other, own)
    return jnp.concatenate([first, second], axis=axis)


def normalize(values):
    centred = values - jnp.mean(values, axis=1, keepdims=True)
    spread = lax.rsqrt(jnp.mean(centred * centred, axis=1, keepdims=True) + NORM_EPS)
    return centred * spread, spread


def normalize_back(normal, spread, gain, grad):
    scaled = grad * gain
    along = jnp.mean(scaled * normal, axis=1, keepdims=True)
    return spread * (scaled - jnp.mean(scaled, axis=1, keepdims=True) - normal * along)


def first_rows(pieces, scalars, weight, gain, shift, bias):
    rows, width = pieces[0][0].shape
    steps = len(pieces)
    total = 2 * steps * rows
    columns = weight.shape[1]

    def kernel(marks, *refs):
        given, (w, g, s, b), outs = refs[: 2 * steps], refs[2 * steps : 2 * steps + 4], refs[-3:]
        for t in range(steps):

            @pl.when(pl.program_id(0) == t)
            def _(t=t):
                outs[0][...] = in_order(marks[0], given[2 * t][...], given[2 * t + 1][...])

        normal, _ = normalize(outs[0][...].astype(F32))
        outs[1][...] = normal.astype(BF16)
        scaled = (normal * g[...] + s[...]).astype(BF16)
        outs[2][...] = (dot(scaled, w[...]) + b[...]).astype(BF16)

    def block(width):
        return pl.BlockSpec((2 * rows, width), lambda t, marks: (marks[1 + t], 0))

    flat = [piece for pair in pieces for piece in pair]
    return call(
        kernel,
        [struct((total, width), BF16), struct((total, width), BF16), struct((total, columns), BF16)],
        [block(width), block(width), block(columns)],
        grid=(steps,),
        in_blocks=[whole((rows, width))] * (2 * steps)
        + [whole(weight.shape), whole((1, width)), whole((1, width)), whole((1, columns))],
        scalars=scalars,
        name="first_rows",
    )(*flat, weight, gain, shift, bias)


def residual_rows(tokens_all, pieces, scalars, weight, bias):
    total, width = tokens_all.shape
    many = len(pieces)
    wide = pieces[0][0].shape[1]
    rows = min(total, 256)

    def kernel(marks, tokens, *refs):
        given, (w, b, out) = refs[: 2 * many], refs[2 * many :]
        value = tokens[...].astype(F32) + b[...]
        for t in range(many):
            pair = in_order(marks[0], given[2 * t][...], given[2 * t + 1][...], axis=1)
            begin = pl.multiple_of(marks[1 + t] * (2 * wide), 2 * wide)
            value += dot(pair, w[pl.ds(begin, 2 * wide)])
        out[...] = value

    def block(width):
        return pl.BlockSpec((rows, width), lambda i, marks: (i, 0))

    return call(
        kernel,
        struct((total, width), F32),
        block(width),
        grid=(total // rows,),
        in_blocks=[block(width)] + [block(wide)] * (2 * many) + [whole(weight.shape), whole((1, width))],
        scalars=scalars,
        name="residual_rows",
    )(tokens_all, *[piece for pair in pieces for piece in pair], weight, bias)


def second_rows(partial, pair, scalars, weight, gain, shift, steps):
    total, width = partial.shape
    wide = pair[0].shape[1]
    own_rows = total // (2 * steps)
    rows = 2 * own_rows

    def kernel(marks, before, first, second, w, g, s, normed, own):
        both = in_order(marks[0], first[...], second[...], axis=1)
        residual = before[...] + dot(both, w[...])
        normal, _ = normalize(residual)
        normed[...] = (normal * g[...] + s[...]).astype(BF16)

        @pl.when(pl.program_id(0) == marks[1])
        def _():
            own[...] = jnp.where(marks[0] == 0, residual[:own_rows], residual[own_rows:])

    def block(width):
        return pl.BlockSpec((rows, width), lambda i, marks: (i, 0))

    return call(
        kernel,
        [struct((total, width), BF16), struct((own_rows, width), F32)],
        [block(width), whole((own_rows, width))],
        grid=(steps,),
        in_blocks=[
            block(width),
            block(wide),
            block(wide),
            pl.BlockSpec((2 * wide, width), lambda i, marks: (marks[steps], 0)),
            whole((1, width)),
            whole((1, width)),
        ],
        scalars=scalars,
        name="second_rows",
    )(partial, *pair, weight, gain, shift)


def hidden_rows(normed, pairs, scalars, w_fc, w_proj, bias, kept, taken, rows):
    total, width = normed.shape
    hidden = w_fc.shape[1]
    many = len(taken)

    def kernel(marks, block, *refs):
        given, (fc, proj, b) = refs[: 2 * many], refs[2 * many : 2 * many + 3]
        act_ref, grad_ref, cot_ref = refs[-3 - 2 * many : -2 * many]
        parts = refs[-2 * many :]
        for i in range(many):

            @pl.when(pl.program_id(0) == i)
            def _(i=i):
                cot_ref[...] = in_order(marks[0], given[2 * i][...], given[2 * i + 1][...])

        z = dot(block[...], fc[...]) + b[...]
        square = z * z
        tanh = jnp.tanh(0.7978845608028654 * (z + 0.044715 * (square * z)))
        half = 0.5 * (1.0 + tanh)
        slope = half + 0.5 * z * (1.0 - tanh * tanh) * (
            0.7978845608028654 + (0.7978845608028654 * 3.0 * 0.044715) * square
        )
        act_ref[...] = (z * half).astype(BF16)
        grad = (dot(cot_ref[...], proj[...]) * slope).astype(BF16)
        grad_ref[...] = grad
        part = dot_nt(grad, fc[...])
        mine = jnp.where(marks[0] == 0, part[:rows], part[rows:])
        other = jnp.where(marks[0] == 0, part[rows:], part[:rows]).astype(BF16)
        for i in range(many):

            @pl.when(pl.program_id(0) == i)
            def _(i=i):
                parts[2 * i][...] = mine
                parts[2 * i + 1][...] = other

    def block(width):
        return pl.BlockSpec((2 * rows, width), lambda i, marks: (marks[1 + i], 0))

    operands = [normed] + [piece for pair in pairs for piece in pair] + [w_fc, w_proj, bias]
    blocks = [block(width)] + [whole((rows, width))] * (2 * many)
    blocks += [whole(w_fc.shape), whole(w_proj.shape), whole((1, hidden))]
    alias = {}
    if kept is not None:
        alias = {1 + len(operands) + i: i for i in range(3)}
        operands += list(kept)
        blocks += [pl.BlockSpec(memory_space=pl.ANY)] * 3
    outs = call(
        kernel,
        [struct((total, hidden), BF16), struct((total, hidden), BF16), struct((total, width), BF16)]
        + [struct((rows, width), dtype) for _ in taken for dtype in (F32, BF16)],
        [block(hidden), block(hidden), block(width)] + [whole((rows, width))] * (2 * many),
        grid=(many,),
        in_blocks=blocks,
        scalars=scalars,
        alias=alias,
        name="hidden_rows",
    )(*operands)
    return outs[:3], {t: (outs[3 + 2 * i], outs[4 + 2 * i]) for i, t in enumerate(taken)}


def turned_product(left, right, name):
    total, width = left.shape
    columns = right.shape[1]
    tile = 256

    def kernel(left_ref, right_ref, out_ref):
        out_ref[...] = dot(left_ref[...].T, right_ref[...]).astype(BF16)

    return call(
        kernel,
        struct((width, columns), BF16),
        pl.BlockSpec((tile, columns), lambda i: (i, 0)),
        grid=(pl.cdiv(width, tile),),
        in_blocks=[pl.BlockSpec((total, tile), lambda i: (0, i)), whole(right.shape)],
        name=name,
    )(left, right)


def head_product(normal, grad, weight, gain, shift):
    total, width = normal.shape
    columns = grad.shape[1]
    tile = 256

    def kernel(left, right, w, g, s, out, gain_sum, shift_sum, grad_sum):
        @pl.when(pl.program_id(0) == 0)
        def _():
            grad_sum[...] = jnp.sum(right[...].astype(F32), axis=0, keepdims=True)

        raw = dot(left[...].T, right[...])
        sums = grad_sum[...]
        low = w[...].astype(F32)
        gain_sum[...] = jnp.sum(raw * low, axis=1, keepdims=True)
        shift_sum[...] = jnp.sum(low * sums, axis=1, keepdims=True)
        out[...] = (raw * g[...] + s[...] * sums).astype(BF16)

    column = pl.BlockSpec((tile, 1), lambda i: (i, 0))
    return call(
        kernel,
        [
            struct((width, columns), BF16),
            struct((width, 1), F32),
            struct((width, 1), F32),
            struct((1, columns), F32),
        ],
        [pl.BlockSpec((tile, columns), lambda i: (i, 0)), column, column, whole((1, columns))],
        grid=(pl.cdiv(width, tile),),
        in_blocks=[
            pl.BlockSpec((total, tile), lambda i: (0, i)),
            whole(grad.shape),
            pl.BlockSpec((tile, columns), lambda i: (i, 0)),
            column,
            column,
        ],
        name="head_product",
    )(normal, grad, weight, gain, shift)


def ring_parts(left, right, scalars, taken, steps, name):
    total, inner = left.shape
    width = right.shape[0]
    rows = total // (2 * steps)

    def kernel(marks, left_ref, right_ref, *outs):
        for i, t in enumerate(taken):
            begin = pl.multiple_of(marks[1 + t] * (2 * rows), 2 * rows)
            part = dot_nt(left_ref[pl.ds(begin, 2 * rows)], right_ref[...])
            outs[2 * i][...] = jnp.where(marks[0] == 0, part[:rows], part[rows:])
            outs[2 * i + 1][...] = jnp.where(marks[0] == 0, part[rows:], part[:rows]).astype(BF16)

    outs = call(
        kernel,
        [struct((rows, width), dtype) for _ in taken for dtype in (F32, BF16)],
        [whole((rows, width))] * (2 * len(taken)),
        in_blocks=[whole(left.shape), whole(right.shape)],
        scalars=scalars,
        name=name,
    )(left, right)
    return {t: (outs[2 * i], outs[2 * i + 1]) for i, t in enumerate(taken)}


def second_back(residual, terms, cotangent, gain, weight, count):
    rows, width = residual.shape
    wide = weight.shape[0] // count
    columns = width // count

    def kernel(
        res, mine, swapped, carried, cot, g, w, grad_ref, low_ref, sums_ref, out_ref, cut_ref
    ):
        @pl.when(pl.program_id(0) == 0)
        def _():
            grad = mine[...] + swapped[...].astype(F32) + carried[...].astype(F32)
            normal, spread = normalize(res[...])
            total = cot[...].astype(F32) + normalize_back(normal, spread, g[...], grad)
            grad_ref[...] = total
            low = total.astype(BF16)
            low_ref[...] = low
            sums_ref[0:1] = jnp.sum(grad * normal, axis=0, keepdims=True)
            sums_ref[1:2] = jnp.sum(grad, axis=0, keepdims=True)
            sums_ref[2:3] = jnp.sum(low.astype(F32), axis=0, keepdims=True)
            sums_ref[3:4] = jnp.sum(cot[...].astype(F32), axis=0, keepdims=True)

        out_ref[0] = dot_nt(low_ref[...], w[...]).astype(BF16)
        for j in range(count):

            @pl.when(pl.program_id(0) == j)
            def _(j=j):
                cut_ref[0] = low_ref[:, j * columns : (j + 1) * columns]

    row = whole((rows, width))
    return call(
        kernel,
        [
            struct((rows, width), F32),
            struct((rows, width), BF16),
            struct((4, width), F32),
            struct((count, rows, wide), BF16),
            struct((count, rows, columns), BF16),
        ],
        [
            row,
            row,
            whole((4, width)),
            pl.BlockSpec((1, rows, wide), lambda i: (i, 0, 0)),
            pl.BlockSpec((1, rows, columns), lambda i: (i, 0, 0)),
        ],
        grid=(count,),
        in_blocks=[row] * 5 + [whole((1, width)), pl.BlockSpec((wide, width), lambda i: (i, 0))],
        name="second_back",
    )(residual, *terms, cotangent, gain, weight)


def first_back(tokens, terms, residual_grad, gain):
    rows, width = tokens.shape

    def kernel(x, mine, swapped, carried, res, g, out_ref):
        grad = mine[...] + swapped[...].astype(F32) + carried[...].astype(F32)
        normal, spread = normalize(x[...].astype(F32))
        out_ref[...] = (res[...] + normalize_back(normal, spread, g[...], grad)).astype(BF16)

    row = whole((rows, width))
    return call(
        kernel,
        struct((rows, width), BF16),
        row,
        in_blocks=[row] * 5 + [whole((1, width))],
        name="first_back",
    )(tokens, *terms, residual_grad, gain)


def heads_rows(me, pieces, count, slots):
    rows, width = pieces[0].shape
    unit = math.gcd(rows, HD)

    def kernel(mark, *refs):
        out = refs[4]
        for h in range(HEADS, count * slots):
            place = ((h % count) * slots + h // count) * HD
            out[place : place + HD] = jnp.zeros((HD, width), BF16)
        for r in range(4):
            for piece in range(rows // unit):
                row = (mark[0] ^ r) * rows + piece * unit
                head = row // HD
                target = ((head % count) * slots + head // count) * HD + row % HD
                out[pl.ds(pl.multiple_of(target, unit), unit)] = refs[r][
                    piece * unit : (piece + 1) * unit
                ]

    return call(
        kernel,
        struct((count * slots * HD, width), BF16),
        whole((count * slots * HD, width)),
        in_blocks=[whole((rows, width))] * 4,
        scalars=me[None],
        name="heads_rows",
    )(*pieces)


def out_product(pieces, columns, scalars, count, slots):
    total, width = columns.shape
    wide = slots * HD
    steps = len(pieces)

    def kernel(marks, *refs):
        given, right, out = refs[: 2 * steps], refs[2 * steps], refs[-1]
        for t in range(steps):
            for b in range(2):
                owner = marks[1 + t] * 2 + (marks[0] if b == 0 else 1 - marks[0])
                value = dot_tn(given[2 * t + b][...], right[...]).astype(BF16)
                for slot in range(slots):
                    begin = pl.multiple_of((slot * count + owner) * HD, HD)
                    out[pl.ds(begin, HD)] = value[slot * HD : (slot + 1) * HD]

    return call(
        kernel,
        struct((slots * count * HD, width), BF16),
        whole((slots * count * HD, width)),
        in_blocks=[whole((total, wide))] * (2 * steps) + [whole(columns.shape)],
        scalars=scalars,
        name="out_product",
    )(*[piece for pair in pieces for piece in pair], columns)


def rows_product(left, right, name):
    total, inner = left.shape
    width = right.shape[0]
    block = min(total, 512)

    def kernel(left_ref, right_ref, out_ref):
        out_ref[...] = dot_nt(left_ref[...], right_ref[...]).astype(BF16)

    return call(
        kernel,
        struct((total, width), BF16),
        pl.BlockSpec((block, width), lambda i: (i, 0)),
        grid=(total // block,),
        in_blocks=[pl.BlockSpec((block, inner), lambda i: (i, 0)), whole(right.shape)],
        name=name,
    )(left, right)


def shards(
    tokens,
    cotangent,
    positions,
    qkv_weight,
    qkv_first,
    qkv_second,
    out_weight,
    out_first,
    out_second,
    fc_weight,
    fc_first,
    fc_second,
    proj_weight,
    proj_first,
    proj_second,
    small_weight,
    small_first,
    small_second,
):
    count = lax.axis_size("seq")
    ring = Ring(count)
    square = Square()
    me = lax.axis_index("seq")
    rows, width = tokens.shape
    seq_rows = rows // SEQS
    window = qkv_weight.shape[1]
    slots = -(-HEADS // count)
    wide = slots * HD
    small_count, small_width = small_weight.shape
    hidden = fc_weight.shape[1]
    all_rows = count * rows
    steps = ring.steps
    marks = jnp.stack([ring.side] + [ring.position(t) for t in range(steps)])
    tokens = by_rows(tokens)
    cotangent = by_rows(cotangent)

    token_tour = Tour(ring, tokens)
    token_tour.step()
    token_tour.step()
    pack, unpack, most = head_tables(count, width, window)
    pack_hot = one_hot(pick_row(pack, me), window)
    packed = jnp.einsum(
        "rc,cdl->drl",
        qkv_weight.astype(BF16),
        pack_hot.reshape(window, count, most),
        preferred_element_type=BF16,
    )
    depth = packed.shape[1]
    small_flat = jnp.concatenate(
        [
            small_weight.reshape(-1).astype(BF16),
            (positions // 32).astype(BF16),
            (positions % 32).astype(BF16),
        ]
    )
    small_depth = -(-small_flat.shape[0] // most)
    small_depth += -small_depth % 16
    small_flat = jnp.pad(small_flat, (0, small_depth * most - small_flat.shape[0]))
    small_pack = jnp.broadcast_to(
        small_flat.reshape(1, small_depth, most), (count, small_depth, most)
    )
    received = lax.all_to_all(jnp.concatenate([packed, small_pack], axis=1), "seq", 0, 0)
    token_tour.step()
    received = after(received, token_tour.moved[1], token_tour.current)

    unpack_hot = one_hot(pick_row(unpack, me), 3 * wide)
    head_part = jnp.einsum(
        "srl,ksl->rk",
        received[:, :depth],
        unpack_hot.reshape(3 * wide, count, most),
        preferred_element_type=BF16,
    )
    for t in range(3, steps):
        token_tour.step()
    head_pieces = square.gather(head_part, token_tour.current)
    w_head = square.place(head_pieces)

    small_all = received[:, depth:].reshape(count, small_depth * most).astype(F32)
    small_rows = small_all[:, : small_count * small_width].reshape(count, small_count, small_width)
    small_rows = small_rows.transpose(1, 0, 2).reshape(small_count, width)
    pos_all = small_all[:, small_count * small_width :][:, : 2 * rows].reshape(count, 2, rows)
    pos_all = (pos_all[:, 0] * 32.0 + pos_all[:, 1]).astype(jnp.int32)

    def own_heads(row):
        padded = jnp.pad(row, (0, slots * count * HD - width)).reshape(slots, count, HD)
        return lax.dynamic_index_in_dim(padded, me, 1, keepdims=False).reshape(wide)

    head_bias = jnp.concatenate(
        [own_heads(small_rows[0]), jnp.zeros((wide,), F32), own_heads(small_rows[1])]
    )
    fc_bias = lax.dynamic_slice_in_dim(small_rows[3:7].reshape(-1), me * hidden, hidden, 0)
    gain_one, shift_one = small_rows[8][None], small_rows[9][None]
    gain_two, shift_two = small_rows[10][None], small_rows[11][None]

    ready = (w_head, token_tour.moved[-1])
    out_part = lax.all_gather(out_weight.astype(BF16), "seq", axis=1, tiled=True)
    tokens_all, normal_all, qkv_rows = first_rows(
        token_tour.pieces, marks, w_head, gain_one, shift_one, head_bias[None]
    )
    qkv_all = qkv_rows.reshape(count, SEQS, seq_rows, 3 * wide)
    context, probs = attention_forward(qkv_all, pos_all)
    context = context.reshape(all_rows, wide)

    cot_zero = lax.ppermute(after(cotangent, *ready), "seq", ring.swap)
    cot_moving = lax.ppermute(after(cotangent, *ready), "seq", ring.behind)
    fc_low = after(fc_weight, *ready).astype(BF16)
    context = after(context, cot_zero, cot_moving)
    out_part = by_rows(after(out_part, context))
    out_near, out_far = square.near_of(out_part), square.far_of(out_part)
    fc_near, fc_far = square.near_of(fc_low), square.far_of(fc_low)
    context_tour = Tour(ring, context)
    context_tour.step()
    context_tour.step(land=(out_part, fc_far))
    fc_pieces = (fc_low, fc_near, fc_far, square.near_of(after(fc_far, context_tour.current)))
    w_fc = square.place(fc_pieces)
    context_tour.step(land=(w_fc,))
    for t in range(3, steps):
        context_tour.step(land=(out_far,) if t == 3 else ())
    proj_low = after(proj_weight, context_tour.current).T.astype(BF16)
    proj_near, proj_far = square.near_of(proj_low), square.far_of(proj_low)
    out_pieces = (out_part, out_near, out_far, square.near_of(after(out_far, context_tour.current)))
    w_out = heads_rows(square.me, out_pieces, count, slots)
    partial = residual_rows(
        tokens_all, context_tour.pieces[:-1], marks, w_out, small_rows[2][None]
    )
    last_pair = after(context_tour.pieces[-1], partial)
    proj_far = after(proj_far, partial)
    normed_all, residual = second_rows(
        partial, last_pair, marks, w_out, gain_two, shift_two, steps
    )
    proj_pieces = (proj_low, proj_near, proj_far, after(square.near_of(proj_far), residual))
    w_proj = square.place(proj_pieces)
    cot_pieces = {0: (cotangent, cot_zero)}
    cot_moving = after(cot_moving, last_pair[1])
    crossed = lax.ppermute(cot_moving, "seq", ring.swap)
    cot_pieces[steps - 1] = (cot_moving, crossed)
    cot_moving = after(lax.ppermute(cot_moving, "seq", ring.behind), residual)

    def feed_forward(kept, taken, *begin):
        chosen = jnp.stack([ring.side] + [ring.position(t) for t in taken])
        return hidden_rows(
            normed_all,
            [cot_pieces[t] for t in taken],
            after(chosen, *begin) if begin else chosen,
            w_fc,
            w_proj,
            fc_bias[None],
            kept,
            taken,
            rows,
        )

    crossed = lax.ppermute(after(cot_moving, crossed), "seq", ring.swap)
    cot_pieces[steps - 2] = (cot_moving, crossed)
    cot_moving = lax.ppermute(cot_moving, "seq", ring.behind)
    kept, parts = feed_forward(None, [steps - 1])
    cot_moving, cot_pieces[steps - 2] = lax.optimization_barrier(
        (cot_moving, cot_pieces[steps - 2], parts[steps - 1][1])
    )[:2]
    for t in range(3, steps):
        crossed = lax.ppermute(after(cot_moving, crossed), "seq", ring.swap)
        cot_pieces[steps - t] = (cot_moving, crossed)
        if t + 1 < steps:
            cot_moving = lax.ppermute(cot_moving, "seq", ring.behind)
    grad_fold = Fold(ring, parts)
    kept, more = feed_forward(kept, [steps - 2])
    parts.update(more)
    grad_fold.beside(*parts[steps - 2], crossed)
    grad_fold.step()
    kept, more = feed_forward(kept, list(reversed(range(steps - 2))), grad_fold.carried)
    parts.update(more)
    grad_fold.beside(*parts[0])
    hidden_low, grad_pre_low, cot_all = kept
    grad_fold.step()
    output_partial = rows_product(after(hidden_low, grad_fold.carried), w_proj, "output_product")
    grad_fold.beside(output_partial)
    for _ in range(3, steps):
        grad_fold.step()
    fc_sum = turned_product(after(normed_all, grad_fold.carried), grad_pre_low, "fc_product")
    grad_fold.beside(fc_sum)
    output_sum = lax.psum_scatter(output_partial, "seq", scatter_dimension=0, tiled=True)
    terms = grad_fold.terms
    grad_residual, _, row_sums, grad_sent, attn_cut = second_back(
        residual, terms, cotangent, gain_two, w_out, count
    )
    grad_bias_fc = jnp.sum(after(grad_pre_low, grad_sent).astype(F32), axis=0)
    fc_column = square.half_sum(after(fc_sum, grad_sent))

    proj_sum = turned_product(after(cot_all, grad_sent), hidden_low, "proj_product")
    grad_context = after(lax.all_to_all(grad_sent, "seq", 0, 0), proj_sum, grad_bias_fc)
    proj_column = square.half_sum(after(proj_sum, grad_context))
    grad_qkv = attention_backward(
        qkv_all, grad_context.reshape(count, SEQS, seq_rows, wide), probs
    ).reshape(all_rows, 3 * wide)
    fc_grad = after(square.other_sum(fc_column), grad_qkv)
    proj_grad = square.other_sum(after(proj_column, grad_qkv))
    parts = ring_parts(grad_qkv, w_head, marks, [steps - 1], steps, "first_parts")
    input_fold = Fold(ring, parts)
    parts.update(
        ring_parts(
            after(grad_qkv, *parts[steps - 1]), w_head, marks, range(steps - 1), steps, "input_parts"
        )
    )
    input_fold.beside(*parts[0])
    input_fold.step()
    head_sum, grad_gain_one, grad_shift_one, grad_qkv_sum = head_product(
        after(normal_all, input_fold.carried),
        grad_qkv,
        w_head,
        small_rows[8][:, None],
        small_rows[9][:, None],
    )
    input_fold.beside(head_sum)
    input_fold.step()
    head_column = square.half_sum(after(head_sum, input_fold.carried))
    out_columns = out_weight.shape[1]
    attn_columns = lax.all_to_all(after(attn_cut, input_fold.carried), "seq", 0, 0)
    attn_columns = attn_columns.reshape(all_rows, out_columns)
    input_fold.beside(head_column)
    for _ in range(3, steps):
        input_fold.step()
    small_begin = input_fold.carried
    head_far = square.other_sum(after(head_column, input_fold.carried))
    out_sum = out_product(
        context_tour.pieces, after(attn_columns, input_fold.carried), marks, count, slots
    )[:width]
    input_fold.beside(output_sum, out_sum)
    input_grad = first_back(tokens, input_fold.terms, grad_residual, gain_one)
    out_column = square.half_sum(after(out_sum, input_grad))
    head_grad = after(head_far, input_grad).astype(BF16)
    unpack_back = unpack_hot.reshape(3 * wide, count, most)
    head_packed = jnp.einsum("rk,ksl->srl", head_grad, unpack_back, preferred_element_type=BF16)
    out_grad = square.other_sum(after(out_column, head_packed))
    fc_new = adam_update(
        fc_weight, fc_first, fc_second, after(fc_grad, head_packed), 0.02, 0.1
    )
    head_back = lax.all_to_all(head_packed, "seq", 0, 0)
    qkv_grad = jnp.einsum(
        "drl,cdl->rc",
        head_back,
        pack_hot.reshape(window, count, most),
        preferred_element_type=F32,
    )
    output = (residual + output_sum.astype(F32) + small_rows[7]).astype(BF16)

    def place_heads(values):
        spread = (jnp.arange(count) == me).astype(F32)[None, :, None]
        placed = values.reshape(slots, 1, HD) * spread
        return placed.reshape(-1)[:width]

    grad_bias_fc = grad_bias_fc[None, :] * (jnp.arange(count) == me).astype(F32)[:, None]
    grad_qkv_sum = after(grad_qkv_sum, small_begin)[0]
    grad_small = jnp.concatenate(
        [
            place_heads(grad_qkv_sum[:wide])[None],
            place_heads(grad_qkv_sum[2 * wide :])[None],
            row_sums[2:3],
            grad_bias_fc.reshape(-1, width),
            row_sums[3:4],
            grad_gain_one[:, 0][None],
            grad_shift_one[:, 0][None],
            row_sums[0:1],
            row_sums[1:2],
        ],
        axis=0,
    )
    small_sent = grad_small.astype(BF16).reshape(small_count, count, small_width)
    small_part = jnp.sum(
        lax.all_to_all(small_sent.transpose(1, 0, 2), "seq", 0, 0).astype(F32), axis=0
    )
    small_grad = square.sum(after(small_part, head_packed))

    qkv_new = adam_update(qkv_weight, qkv_first, qkv_second, qkv_grad, 0.02, 0.1)
    out_new = adam_update(out_weight, out_first, out_second, out_grad, 0.3, 0.1)
    proj_new = adam_update(
        proj_weight.T, proj_first.T, proj_second.T, proj_grad, 0.02, 0.1
    )
    proj_new = [value.T for value in proj_new]
    small_new = adam_update(small_weight, small_first, small_second, small_grad, 0.3, 0.0)
    return (
        output,
        input_grad,
        *qkv_new,
        *out_new,
        *fc_new,
        *proj_new,
        *small_new,
        small_grad[7],
    )


def solution(mesh):
    rows = P(("dp", "seq"), None)
    matrix = P("dp", "seq")
    turned = P("seq", "dp")
    small = P(None, "seq")
    in_specs = (
        (rows, rows, P(("dp", "seq"))) + (matrix,) * 9 + (turned,) * 3 + (small,) * 3
    )
    out_specs = (rows, rows) + (matrix,) * 9 + (turned,) * 3 + (small,) * 3 + (P("seq"),)
    return jax.shard_map(shards, mesh=mesh, in_specs=in_specs, out_specs=out_specs, check_vma=False)
```

```python
import functools
import math

import jax
import jax.numpy as jnp
import numpy as np
from jax import lax
from jax.experimental import pallas as pl
from jax.experimental.layout import Layout, with_layout_constraint
from jax.experimental.pallas import tpu as pltpu
from jax.sharding import PartitionSpec as P

HEADS = 25
HD = 64
SEQS = 2
STEP = 10

NORM_EPS = 1e-05
SCORE_SCALE = 0.125
MASKED_SCORE = -1e30
BETA_ONE = 0.9
BETA_TWO = 0.95
ADAM_EPS = 1e-08
BF16 = jnp.bfloat16
F32 = jnp.float32
SMALL_COST = pl.CostEstimate(flops=1024, bytes_accessed=1024, transcendentals=0)
LARGE_COST = pl.CostEstimate(flops=8 * 10**9, bytes_accessed=8 * 10**6, transcendentals=0)


def adam_update(weight, first_moment, second, gradient, step_rate, decay_rate):
    moment_new = BETA_ONE * first_moment + (1.0 - BETA_ONE) * gradient
    second_new = BETA_TWO * second + (1.0 - BETA_TWO) * gradient * gradient
    direction = (
        moment_new
        / (1.0 - BETA_ONE**STEP)
        / (jnp.sqrt(second_new / (1.0 - BETA_TWO**STEP)) + ADAM_EPS)
    )
    return (moment_new, second_new, weight - step_rate * (direction + decay_rate * weight))


def dot(left, right):
    return jnp.dot(left, right, preferred_element_type=F32)


def dot_nt(left, right):
    return lax.dot_general(left, right, (((1,), (1,)), ((), ())), preferred_element_type=F32)


def dot_tn(left, right):
    return lax.dot_general(left, right, (((0,), (0,)), ((), ())), preferred_element_type=F32)


def after(value, *others):
    return lax.optimization_barrier((value,) + others)[0]


def by_rows(value):
    return with_layout_constraint(value, Layout(major_to_minor=(0, 1)))


def call(
    kernel, out, blocks, grid=None, in_blocks=None, scalars=None, alias=None, scratch=(), name=None
):
    operands = 0 if scalars is None else 1
    spec = dict(
        in_specs=in_blocks,
        out_specs=blocks,
        grid=grid or (1,),
        scratch_shapes=list(scratch),
    )
    if operands:
        spec = dict(grid_spec=pltpu.PrefetchScalarGridSpec(num_scalar_prefetch=1, **spec))
    run = pl.pallas_call(
        kernel,
        out_shape=out,
        input_output_aliases=alias or {},
        compiler_params=pltpu.CompilerParams(vmem_limit_bytes=60 * 1024 * 1024),
        cost_estimate=SMALL_COST,
        name=name,
        **spec,
    )
    if operands:
        return lambda *given: run(scalars, *given)
    return run


def whole(shape):
    return pl.BlockSpec(shape, lambda *_: (0,) * len(shape))


def struct(shape, dtype):
    return jax.ShapeDtypeStruct(shape, dtype)


class Ring:
    def __init__(self, count):
        self.sides = 2
        self.steps = count // 2
        steps = self.steps
        self.swap = [(j, j ^ 1) for j in range(count)]
        self.ahead = [(z * 2 + x, ((z + 1) % steps) * 2 + x) for z in range(steps) for x in range(2)]
        self.behind = [(dst, src) for src, dst in self.ahead]
        me = lax.axis_index("seq")
        self.place, self.side = me // 2, me % 2

    def shift(self, t):
        steps = self.steps
        return [(z * 2 + x, ((z + t) % steps) * 2 + x) for z in range(steps) for x in range(2)]

    def position(self, t):
        return (self.place + self.steps - t) % self.steps

    def gather(self, block):
        tour = Tour(self, block)
        for _ in range(self.steps):
            tour.step()
        return tour


class Tour:
    def __init__(self, ring, block, back=False):
        self.ring, self.current, self.back = ring, block, back
        self.pieces = [None] * ring.steps
        self.moved = []

    def step(self, *begin, land=()):
        ring, t = self.ring, len(self.moved)
        if begin:
            self.current = after(self.current, *begin)
        if t:
            moved = lax.ppermute(self.current, "seq", ring.behind if self.back else ring.ahead)
            self.current = after(moved, self.moved[-1], *land)
        other = lax.ppermute(self.current, "seq", ring.swap)
        self.pieces[-t if self.back else t] = (self.current, other)
        self.moved.append(other)


class Fold:
    def __init__(self, ring, parts):
        self.ring, self.parts = ring, parts
        self.terms, self.count, self.carried = None, 0, None
        self.step()

    def step(self):
        ring = self.ring
        mine, other = self.parts[ring.steps - 1 - self.count]
        self.count += 1
        sent = None
        if self.terms is not None:
            sent = sum(term.astype(F32) for term in self.terms).astype(BF16)
            self.carried = sent
            other = after(other, sent)
        self.terms = [mine, lax.ppermute(other, "seq", ring.swap)]
        if sent is not None:
            self.terms.append(lax.ppermute(sent, "seq", ring.behind))

    def beside(self, *work):
        self.terms = list(lax.optimization_barrier((tuple(self.terms),) + work)[0])


class Square:
    def __init__(self):
        me = lax.axis_index("dp")
        self.me, self.far, self.near = me, me // 2, me % 2
        self.far_swap = [(j, j ^ 2) for j in range(4)]
        self.near_swap = [(j, j ^ 1) for j in range(4)]

    def near_of(self, block):
        return lax.ppermute(block, "dp", self.near_swap)

    def far_of(self, block):
        return lax.ppermute(block, "dp", self.far_swap)

    def gather(self, block, *begin):
        near, far = self.near_of(block), self.far_of(block)
        far = after(far, *begin) if begin else far
        return (block, near, far, lax.ppermute(far, "dp", self.near_swap))

    def place(self, pieces):
        rows, width = pieces[0].shape

        def kernel(me, *refs):
            for r in range(4):
                begin = pl.multiple_of((me[0] ^ r) * rows, 16)
                refs[4][pl.ds(begin, rows)] = refs[r][...]

        return call(
            kernel,
            struct((4 * rows, width), BF16),
            whole((4 * rows, width)),
            in_blocks=[whole((rows, width))] * 4,
            scalars=self.me[None],
            name="place_rows",
        )(*pieces)

    def half_sum(self, partial):
        parts = partial.reshape((2, 2, partial.shape[0] // 4) + partial.shape[1:])
        mine = lax.dynamic_index_in_dim(parts, self.near, 1, keepdims=False)
        other = lax.dynamic_index_in_dim(parts, 1 - self.near, 1, keepdims=False)
        near = lax.ppermute(other, "dp", self.near_swap)
        return (mine.astype(F32) + near.astype(F32)).astype(BF16)

    def other_sum(self, column):
        mine = lax.dynamic_index_in_dim(column, self.far, 0, keepdims=False)
        other = lax.dynamic_index_in_dim(column, 1 - self.far, 0, keepdims=False)
        return mine.astype(F32) + lax.ppermute(other, "dp", self.far_swap).astype(F32)

    def sum(self, values):
        values = values + lax.ppermute(values, "dp", self.near_swap)
        return values + lax.ppermute(values, "dp", self.far_swap)


def head_tables(count, model_width, window):
    slots = -(-HEADS // count)
    wide = slots * HD
    lists = [[[] for _ in range(count)] for _ in range(count)]
    for column in range(3 * model_width):
        src, local = divmod(column, window)
        part, within = divmod(column, model_width)
        head, lane = divmod(within, HD)
        dst, slot = head % count, head // count
        lists[src][dst].append((local, part * wide + slot * HD + lane))
    most = max(len(entry) for row in lists for entry in row)
    most = -(-most // 64) * 64
    pack = np.full((count, count * most), -1, np.int32)
    unpack = np.full((count, count * most), -1, np.int32)
    for src in range(count):
        for dst in range(count):
            for place, (local, target) in enumerate(lists[src][dst]):
                pack[src, dst * most + place] = local
                unpack[dst, src * most + place] = target
    return pack, unpack, most


def pick_row(table, index):
    return lax.dynamic_index_in_dim(jnp.asarray(table), index, 0, keepdims=False)


def one_hot(rows, size):
    return (lax.broadcasted_iota(jnp.int32, (size, rows.shape[0]), 0) == rows[None, :]).astype(BF16)


def forward_kernel(pos_col, pos_row, query_ref, full_ref, context_ref, probs_ref, *, wide):
    slots, _, run, width = query_ref.shape
    rows = slots * run
    keys_total = full_ref.shape[0] * run
    query = query_ref[:, 0].reshape(rows, width)[:, :wide]
    full = full_ref[:, 0].reshape(keys_total, width)
    key, value = full[:, wide : 2 * wide], full[:, 2 * wide :]
    seen = pos_row[0] <= pos_col[0]
    lane_head = lax.broadcasted_iota(jnp.int32, (1, wide), 1) // HD
    context = jnp.zeros((rows, wide), F32)
    for head in range(wide // HD):
        mine = lane_head == head
        scores = dot_nt(jnp.where(mine, query, jnp.zeros_like(query)), key) * SCORE_SCALE
        scores = jnp.where(seen, scores, MASKED_SCORE)
        top = jnp.max(scores, axis=1, keepdims=True)
        raw = jnp.exp(scores - top)
        probs = (raw * (1.0 / jnp.sum(raw, axis=1, keepdims=True))).astype(BF16)
        probs_ref[0, head] = probs
        context = jnp.where(mine, dot(probs, value), context)
    context_ref[:, 0] = context.astype(BF16).reshape(slots, run, wide)


def backward_kernel(query_ref, full_ref, grad_ref, probs_ref, out_ref, key_sum, value_sum, *, wide):
    step = pl.program_id(1)
    slots, _, run, width = query_ref.shape
    rows = slots * run
    count = full_ref.shape[0]
    keys_total = count * run
    query = query_ref[:, 0].reshape(rows, width)[:, :wide]
    full = full_ref[:, 0].reshape(keys_total, width)
    key, value = full[:, wide : 2 * wide], full[:, 2 * wide :]
    grad = grad_ref[:, 0].reshape(rows, wide)
    lane_head = lax.broadcasted_iota(jnp.int32, (1, wide), 1) // HD

    @pl.when(step == 0)
    def _():
        key_sum[...] = jnp.zeros_like(key_sum)
        value_sum[...] = jnp.zeros_like(value_sum)

    query_grad = jnp.zeros((rows, wide), F32)
    key_grad = jnp.zeros((keys_total, wide), F32)
    value_grad = jnp.zeros((keys_total, wide), F32)
    for head in range(wide // HD):
        mine = lane_head == head
        probs_low = probs_ref[0, head]
        probs = probs_low.astype(F32)
        grad_probs = dot_nt(jnp.where(mine, grad, jnp.zeros_like(grad)), value)
        weighted = probs * grad_probs
        delta = jnp.sum(weighted, axis=1, keepdims=True)
        grad_scores = (weighted - probs * delta).astype(BF16)
        query_grad = jnp.where(mine, dot(grad_scores, key), query_grad)
        key_grad = jnp.where(mine, dot_tn(grad_scores, query), key_grad)
        value_grad = jnp.where(mine, dot_tn(probs_low, grad), value_grad)
    key_sum[...] += key_grad
    value_sum[...] += value_grad
    out_ref[pl.ds(step * slots, slots), 0, :, :wide] = (
        (query_grad * SCORE_SCALE).astype(BF16).reshape(slots, run, wide)
    )

    @pl.when(step == pl.num_programs(1) - 1)
    def _():
        out_ref[:, 0, :, wide : 2 * wide] = (
            (key_sum[...] * SCORE_SCALE).astype(BF16).reshape(count, run, wide)
        )
        out_ref[:, 0, :, 2 * wide :] = value_sum[...].astype(BF16).reshape(count, run, wide)


def attention_forward(qkv_rows, positions):
    count, _, run, width = qkv_rows.shape
    wide = width // 3
    heads = wide // HD
    length = count * run
    block = min(length, 512)
    slots = block // run
    steps = length // block
    by_sequence = positions.reshape(count, SEQS, run).transpose(1, 0, 2).reshape(SEQS, length)
    return pl.pallas_call(
        functools.partial(forward_kernel, wide=wide),
        grid=(SEQS, steps),
        in_specs=[
            pl.BlockSpec((1, block, 1), lambda s, i: (s, i, 0)),
            pl.BlockSpec((1, 1, length), lambda s, i: (s, 0, 0)),
            pl.BlockSpec((slots, 1, run, width), lambda s, i: (i, s, 0, 0)),
            pl.BlockSpec((count, 1, run, width), lambda s, i: (0, s, 0, 0)),
        ],
        out_specs=[
            pl.BlockSpec((slots, 1, run, wide), lambda s, i: (i, s, 0, 0)),
            pl.BlockSpec((1, heads, block, length), lambda s, i: (s, 0, i, 0)),
        ],
        out_shape=[
            jax.ShapeDtypeStruct((count, SEQS, run, wide), BF16),
            jax.ShapeDtypeStruct((SEQS, heads, length, length), BF16),
        ],
        compiler_params=pltpu.CompilerParams(vmem_limit_bytes=60 * 1024 * 1024),
        cost_estimate=LARGE_COST,
        name="attention_forward",
    )(by_sequence[:, :, None], by_sequence[:, None, :], qkv_rows, qkv_rows)


def attention_backward(qkv_rows, grad_context, probs):
    count, _, run, width = qkv_rows.shape
    wide = width // 3
    heads = wide // HD
    length = count * run
    block = min(length, 512)
    slots = block // run
    steps = length // block
    return pl.pallas_call(
        functools.partial(backward_kernel, wide=wide),
        grid=(SEQS, steps),
        in_specs=[
            pl.BlockSpec((slots, 1, run, width), lambda s, i: (i, s, 0, 0)),
            pl.BlockSpec((count, 1, run, width), lambda s, i: (0, s, 0, 0)),
            pl.BlockSpec((slots, 1, run, wide), lambda s, i: (i, s, 0, 0)),
            pl.BlockSpec((1, heads, block, length), lambda s, i: (s, 0, i, 0)),
        ],
        out_specs=pl.BlockSpec((count, 1, run, width), lambda s, i: (0, s, 0, 0)),
        out_shape=jax.ShapeDtypeStruct((count, SEQS, run, width), BF16),
        scratch_shapes=[pltpu.VMEM((length, wide), F32), pltpu.VMEM((length, wide), F32)],
        compiler_params=pltpu.CompilerParams(vmem_limit_bytes=60 * 1024 * 1024),
        cost_estimate=SMALL_COST,
        name="attention_backward",
    )(qkv_rows, qkv_rows, grad_context, probs)


def in_order(side, own, other, axis=0):
    first = jnp.where(side == 0, own, other)
    second = jnp.where(side == 0, other, own)
    return jnp.concatenate([first, second], axis=axis)


def normalize(values):
    centred = values - jnp.mean(values, axis=1, keepdims=True)
    spread = lax.rsqrt(jnp.mean(centred * centred, axis=1, keepdims=True) + NORM_EPS)
    return centred * spread, spread


def normalize_back(normal, spread, gain, grad):
    scaled = grad * gain
    along = jnp.mean(scaled * normal, axis=1, keepdims=True)
    return spread * (scaled - jnp.mean(scaled, axis=1, keepdims=True) - normal * along)


def first_rows(pieces, scalars, weight, gain, shift, bias):
    rows, width = pieces[0][0].shape
    steps = len(pieces)
    total = 2 * steps * rows
    columns = weight.shape[1]

    def kernel(marks, *refs):
        given, (w, g, s, b), outs = refs[: 2 * steps], refs[2 * steps : 2 * steps + 4], refs[-3:]
        for t in range(steps):

            @pl.when(pl.program_id(0) == t)
            def _(t=t):
                outs[0][...] = in_order(marks[0], given[2 * t][...], given[2 * t + 1][...])

        normal, _ = normalize(outs[0][...].astype(F32))
        outs[1][...] = normal.astype(BF16)
        scaled = (normal * g[...] + s[...]).astype(BF16)
        outs[2][...] = (dot(scaled, w[...]) + b[...]).astype(BF16)

    def block(width):
        return pl.BlockSpec((2 * rows, width), lambda t, marks: (marks[1 + t], 0))

    flat = [piece for pair in pieces for piece in pair]
    return call(
        kernel,
        [struct((total, width), BF16), struct((total, width), BF16), struct((total, columns), BF16)],
        [block(width), block(width), block(columns)],
        grid=(steps,),
        in_blocks=[whole((rows, width))] * (2 * steps)
        + [whole(weight.shape), whole((1, width)), whole((1, width)), whole((1, columns))],
        scalars=scalars,
        name="first_rows",
    )(*flat, weight, gain, shift, bias)


def residual_rows(tokens_all, pieces, scalars, weight, bias):
    total, width = tokens_all.shape
    many = len(pieces)
    wide = pieces[0][0].shape[1]
    rows = min(total, 256)

    def kernel(marks, tokens, *refs):
        given, (w, b, out) = refs[: 2 * many], refs[2 * many :]
        value = tokens[...].astype(F32) + b[...]
        for t in range(many):
            pair = in_order(marks[0], given[2 * t][...], given[2 * t + 1][...], axis=1)
            begin = pl.multiple_of(marks[1 + t] * (2 * wide), 2 * wide)
            value += dot(pair, w[pl.ds(begin, 2 * wide)])
        out[...] = value

    def block(width):
        return pl.BlockSpec((rows, width), lambda i, marks: (i, 0))

    return call(
        kernel,
        struct((total, width), F32),
        block(width),
        grid=(total // rows,),
        in_blocks=[block(width)] + [block(wide)] * (2 * many) + [whole(weight.shape), whole((1, width))],
        scalars=scalars,
        name="residual_rows",
    )(tokens_all, *[piece for pair in pieces for piece in pair], weight, bias)


def second_rows(partial, pair, scalars, weight, gain, shift, steps):
    total, width = partial.shape
    wide = pair[0].shape[1]
    own_rows = total // (2 * steps)
    rows = 2 * own_rows

    def kernel(marks, before, first, second, w, g, s, normed, own):
        both = in_order(marks[0], first[...], second[...], axis=1)
        residual = before[...] + dot(both, w[...])
        normal, _ = normalize(residual)
        normed[...] = (normal * g[...] + s[...]).astype(BF16)

        @pl.when(pl.program_id(0) == marks[1])
        def _():
            own[...] = jnp.where(marks[0] == 0, residual[:own_rows], residual[own_rows:])

    def block(width):
        return pl.BlockSpec((rows, width), lambda i, marks: (i, 0))

    return call(
        kernel,
        [struct((total, width), BF16), struct((own_rows, width), F32)],
        [block(width), whole((own_rows, width))],
        grid=(steps,),
        in_blocks=[
            block(width),
            block(wide),
            block(wide),
            pl.BlockSpec((2 * wide, width), lambda i, marks: (marks[steps], 0)),
            whole((1, width)),
            whole((1, width)),
        ],
        scalars=scalars,
        name="second_rows",
    )(partial, *pair, weight, gain, shift)


def hidden_rows(normed, pairs, scalars, w_fc, w_proj, bias, kept, taken, rows):
    total, width = normed.shape
    hidden = w_fc.shape[1]
    many = len(taken)

    def kernel(marks, block, *refs):
        given, (fc, proj, b) = refs[: 2 * many], refs[2 * many : 2 * many + 3]
        act_ref, grad_ref, cot_ref = refs[-3 - 2 * many : -2 * many]
        parts = refs[-2 * many :]
        for i in range(many):

            @pl.when(pl.program_id(0) == i)
            def _(i=i):
                cot_ref[...] = in_order(marks[0], given[2 * i][...], given[2 * i + 1][...])

        z = dot(block[...], fc[...]) + b[...]
        square = z * z
        tanh = jnp.tanh(0.7978845608028654 * (z + 0.044715 * (square * z)))
        half = 0.5 * (1.0 + tanh)
        slope = half + 0.5 * z * (1.0 - tanh * tanh) * (
            0.7978845608028654 + (0.7978845608028654 * 3.0 * 0.044715) * square
        )
        act_ref[...] = (z * half).astype(BF16)
        grad = (dot(cot_ref[...], proj[...]) * slope).astype(BF16)
        grad_ref[...] = grad
        part = dot_nt(grad, fc[...])
        mine = jnp.where(marks[0] == 0, part[:rows], part[rows:])
        other = jnp.where(marks[0] == 0, part[rows:], part[:rows]).astype(BF16)
        for i in range(many):

            @pl.when(pl.program_id(0) == i)
            def _(i=i):
                parts[2 * i][...] = mine
                parts[2 * i + 1][...] = other

    def block(width):
        return pl.BlockSpec((2 * rows, width), lambda i, marks: (marks[1 + i], 0))

    operands = [normed] + [piece for pair in pairs for piece in pair] + [w_fc, w_proj, bias]
    blocks = [block(width)] + [whole((rows, width))] * (2 * many)
    blocks += [whole(w_fc.shape), whole(w_proj.shape), whole((1, hidden))]
    alias = {}
    if kept is not None:
        alias = {1 + len(operands) + i: i for i in range(3)}
        operands += list(kept)
        blocks += [pl.BlockSpec(memory_space=pl.ANY)] * 3
    outs = call(
        kernel,
        [struct((total, hidden), BF16), struct((total, hidden), BF16), struct((total, width), BF16)]
        + [struct((rows, width), dtype) for _ in taken for dtype in (F32, BF16)],
        [block(hidden), block(hidden), block(width)] + [whole((rows, width))] * (2 * many),
        grid=(many,),
        in_blocks=blocks,
        scalars=scalars,
        alias=alias,
        name="hidden_rows",
    )(*operands)
    return outs[:3], {t: (outs[3 + 2 * i], outs[4 + 2 * i]) for i, t in enumerate(taken)}


def turned_product(left, right, name):
    total, width = left.shape
    columns = right.shape[1]
    tile = 256

    def kernel(left_ref, right_ref, out_ref):
        out_ref[...] = dot(left_ref[...].T, right_ref[...]).astype(BF16)

    return call(
        kernel,
        struct((width, columns), BF16),
        pl.BlockSpec((tile, columns), lambda i: (i, 0)),
        grid=(pl.cdiv(width, tile),),
        in_blocks=[pl.BlockSpec((total, tile), lambda i: (0, i)), whole(right.shape)],
        name=name,
    )(left, right)


def head_product(normal, grad, weight, gain, shift):
    total, width = normal.shape
    columns = grad.shape[1]
    tile = 256

    def kernel(left, right, w, g, s, out, gain_sum, shift_sum, grad_sum):
        @pl.when(pl.program_id(0) == 0)
        def _():
            grad_sum[...] = jnp.sum(right[...].astype(F32), axis=0, keepdims=True)

        raw = dot(left[...].T, right[...])
        sums = grad_sum[...]
        low = w[...].astype(F32)
        gain_sum[...] = jnp.sum(raw * low, axis=1, keepdims=True)
        shift_sum[...] = jnp.sum(low * sums, axis=1, keepdims=True)
        out[...] = (raw * g[...] + s[...] * sums).astype(BF16)

    column = pl.BlockSpec((tile, 1), lambda i: (i, 0))
    return call(
        kernel,
        [
            struct((width, columns), BF16),
            struct((width, 1), F32),
            struct((width, 1), F32),
            struct((1, columns), F32),
        ],
        [pl.BlockSpec((tile, columns), lambda i: (i, 0)), column, column, whole((1, columns))],
        grid=(pl.cdiv(width, tile),),
        in_blocks=[
            pl.BlockSpec((total, tile), lambda i: (0, i)),
            whole(grad.shape),
            pl.BlockSpec((tile, columns), lambda i: (i, 0)),
            column,
            column,
        ],
        name="head_product",
    )(normal, grad, weight, gain, shift)


def ring_parts(left, right, scalars, taken, steps, name):
    total, inner = left.shape
    width = right.shape[0]
    rows = total // (2 * steps)

    def kernel(marks, left_ref, right_ref, *outs):
        for i, t in enumerate(taken):
            begin = pl.multiple_of(marks[1 + t] * (2 * rows), 2 * rows)
            part = dot_nt(left_ref[pl.ds(begin, 2 * rows)], right_ref[...])
            outs[2 * i][...] = jnp.where(marks[0] == 0, part[:rows], part[rows:])
            outs[2 * i + 1][...] = jnp.where(marks[0] == 0, part[rows:], part[:rows]).astype(BF16)

    outs = call(
        kernel,
        [struct((rows, width), dtype) for _ in taken for dtype in (F32, BF16)],
        [whole((rows, width))] * (2 * len(taken)),
        in_blocks=[whole(left.shape), whole(right.shape)],
        scalars=scalars,
        name=name,
    )(left, right)
    return {t: (outs[2 * i], outs[2 * i + 1]) for i, t in enumerate(taken)}


def second_back(residual, terms, cotangent, gain, weight, count):
    rows, width = residual.shape
    wide = weight.shape[0] // count
    columns = width // count

    def kernel(res, mine, swapped, carried, cot, g, w, grad_ref, low_ref, sums_ref, out_ref):
        @pl.when(pl.program_id(0) == 0)
        def _():
            grad = mine[...] + swapped[...].astype(F32) + carried[...].astype(F32)
            normal, spread = normalize(res[...])
            total = cot[...].astype(F32) + normalize_back(normal, spread, g[...], grad)
            grad_ref[...] = total
            low = total.astype(BF16)
            low_ref[...] = low
            sums_ref[0:1] = jnp.sum(grad * normal, axis=0, keepdims=True)
            sums_ref[1:2] = jnp.sum(grad, axis=0, keepdims=True)
            sums_ref[2:3] = jnp.sum(low.astype(F32), axis=0, keepdims=True)
            sums_ref[3:4] = jnp.sum(cot[...].astype(F32), axis=0, keepdims=True)

        out_ref[0, :, :wide] = dot_nt(low_ref[...], w[...]).astype(BF16)
        for j in range(count):

            @pl.when(pl.program_id(0) == j)
            def _(j=j):
                out_ref[0, :, wide:] = low_ref[:, j * columns : (j + 1) * columns]

    row = whole((rows, width))
    return call(
        kernel,
        [
            struct((rows, width), F32),
            struct((rows, width), BF16),
            struct((4, width), F32),
            struct((count, rows, wide + columns), BF16),
        ],
        [row, row, whole((4, width)), pl.BlockSpec((1, rows, wide + columns), lambda i: (i, 0, 0))],
        grid=(count,),
        in_blocks=[row] * 5 + [whole((1, width)), pl.BlockSpec((wide, width), lambda i: (i, 0))],
        name="second_back",
    )(residual, *terms, cotangent, gain, weight)


def first_back(tokens, terms, residual_grad, gain):
    rows, width = tokens.shape

    def kernel(x, mine, swapped, carried, res, g, out_ref):
        grad = mine[...] + swapped[...].astype(F32) + carried[...].astype(F32)
        normal, spread = normalize(x[...].astype(F32))
        out_ref[...] = (res[...] + normalize_back(normal, spread, g[...], grad)).astype(BF16)

    row = whole((rows, width))
    return call(
        kernel,
        struct((rows, width), BF16),
        row,
        in_blocks=[row] * 5 + [whole((1, width))],
        name="first_back",
    )(tokens, *terms, residual_grad, gain)


def gather_columns(own, other, scalars):
    steps, rows, columns = own.shape
    width = 2 * steps * columns

    def kernel(marks, own_ref, other_ref, out):
        offset = lax.broadcasted_iota(jnp.int32, (columns, width), 1)
        offset -= lax.broadcasted_iota(jnp.int32, (columns, width), 0)
        value = None
        for t in range(steps):
            for b in range(2):
                owner = marks[1 + t] * 2 + (marks[0] if b == 0 else 1 - marks[0])
                spread = jnp.where(offset == owner * columns, 1.0, 0.0).astype(BF16)
                part = dot((own_ref if b == 0 else other_ref)[t], spread)
                value = part if value is None else value + part
        out[...] = value.astype(BF16)

    return call(
        kernel,
        struct((rows, width), BF16),
        whole((rows, width)),
        in_blocks=[whole(own.shape)] * 2,
        scalars=scalars,
        name="gather_columns",
    )(own, other)


def heads_rows(me, pieces, count, slots):
    rows, width = pieces[0].shape
    unit = math.gcd(rows, HD)

    def kernel(mark, *refs):
        out = refs[4]
        for h in range(HEADS, count * slots):
            place = ((h % count) * slots + h // count) * HD
            out[place : place + HD] = jnp.zeros((HD, width), BF16)
        for r in range(4):
            for piece in range(rows // unit):
                row = (mark[0] ^ r) * rows + piece * unit
                head = row // HD
                target = ((head % count) * slots + head // count) * HD + row % HD
                out[pl.ds(pl.multiple_of(target, unit), unit)] = refs[r][
                    piece * unit : (piece + 1) * unit
                ]

    return call(
        kernel,
        struct((count * slots * HD, width), BF16),
        whole((count * slots * HD, width)),
        in_blocks=[whole((rows, width))] * 4,
        scalars=me[None],
        name="heads_rows",
    )(*pieces)


def out_product(pieces, columns, scalars, count, slots):
    total, width = columns.shape
    wide = slots * HD
    steps = len(pieces)

    def kernel(marks, *refs):
        given, right, out = refs[: 2 * steps], refs[2 * steps], refs[-1]
        for t in range(steps):
            for b in range(2):
                owner = marks[1 + t] * 2 + (marks[0] if b == 0 else 1 - marks[0])
                value = dot_tn(given[2 * t + b][...], right[...]).astype(BF16)
                for slot in range(slots):
                    head = slot * count + owner

                    @pl.when(head < HEADS)
                    def _(slot=slot, head=head, value=value):
                        begin = pl.multiple_of(head * HD, HD)
                        out[pl.ds(begin, HD)] = value[slot * HD : (slot + 1) * HD]

    return call(
        kernel,
        struct((HEADS * HD, width), BF16),
        whole((HEADS * HD, width)),
        in_blocks=[whole((total, wide))] * (2 * steps) + [whole(columns.shape)],
        scalars=scalars,
        name="out_product",
    )(*[piece for pair in pieces for piece in pair], columns)


def rows_product(left, right, name):
    total, inner = left.shape
    width = right.shape[0]
    block = min(total, 512)

    def kernel(left_ref, right_ref, out_ref):
        out_ref[...] = dot_nt(left_ref[...], right_ref[...]).astype(BF16)

    return call(
        kernel,
        struct((total, width), BF16),
        pl.BlockSpec((block, width), lambda i: (i, 0)),
        grid=(total // block,),
        in_blocks=[pl.BlockSpec((block, inner), lambda i: (i, 0)), whole(right.shape)],
        name=name,
    )(left, right)


def shards(
    tokens,
    cotangent,
    positions,
    qkv_weight,
    qkv_first,
    qkv_second,
    out_weight,
    out_first,
    out_second,
    fc_weight,
    fc_first,
    fc_second,
    proj_weight,
    proj_first,
    proj_second,
    small_weight,
    small_first,
    small_second,
):
    count = lax.axis_size("seq")
    ring = Ring(count)
    square = Square()
    me = lax.axis_index("seq")
    rows, width = tokens.shape
    seq_rows = rows // SEQS
    window = qkv_weight.shape[1]
    slots = -(-HEADS // count)
    wide = slots * HD
    small_count, small_width = small_weight.shape
    hidden = fc_weight.shape[1]
    all_rows = count * rows
    steps = ring.steps
    marks = jnp.stack([ring.side] + [ring.position(t) for t in range(steps)])
    tokens = by_rows(tokens)
    cotangent = by_rows(cotangent)

    token_tour = Tour(ring, tokens)
    token_tour.step()
    token_tour.step()
    pack, unpack, most = head_tables(count, width, window)
    pack_hot = one_hot(pick_row(pack, me), window)
    packed = jnp.einsum(
        "rc,cdl->drl",
        qkv_weight.astype(BF16),
        pack_hot.reshape(window, count, most),
        preferred_element_type=BF16,
    )
    depth = packed.shape[1]
    small_flat = jnp.concatenate(
        [
            small_weight.reshape(-1).astype(BF16),
            (positions // 32).astype(BF16),
            (positions % 32).astype(BF16),
        ]
    )
    small_depth = -(-small_flat.shape[0] // most)
    small_depth += -small_depth % 16
    small_flat = jnp.pad(small_flat, (0, small_depth * most - small_flat.shape[0]))
    small_pack = jnp.broadcast_to(
        small_flat.reshape(1, small_depth, most), (count, small_depth, most)
    )
    received = lax.all_to_all(jnp.concatenate([packed, small_pack], axis=1), "seq", 0, 0)
    token_tour.step()
    received = after(received, token_tour.moved[1], token_tour.current)

    unpack_hot = one_hot(pick_row(unpack, me), 3 * wide)
    head_part = jnp.einsum(
        "srl,ksl->rk",
        received[:, :depth],
        unpack_hot.reshape(3 * wide, count, most),
        preferred_element_type=BF16,
    )
    for t in range(3, steps):
        token_tour.step()
    head_pieces = square.gather(head_part, token_tour.current)
    out_low = by_rows(after(out_weight, head_part).astype(BF16))
    out_moved = [out_low] + [lax.ppermute(out_low, "seq", ring.shift(t)) for t in range(1, steps)]
    w_head = square.place(after(head_pieces, *out_moved))
    out_moved = jnp.stack(after(out_moved, w_head))
    out_crossed = lax.ppermute(out_moved, "seq", ring.swap)

    small_all = received[:, depth:].reshape(count, small_depth * most).astype(F32)
    small_rows = small_all[:, : small_count * small_width].reshape(count, small_count, small_width)
    small_rows = small_rows.transpose(1, 0, 2).reshape(small_count, width)
    pos_all = small_all[:, small_count * small_width :][:, : 2 * rows].reshape(count, 2, rows)
    pos_all = (pos_all[:, 0] * 32.0 + pos_all[:, 1]).astype(jnp.int32)

    def own_heads(row):
        padded = jnp.pad(row, (0, slots * count * HD - width)).reshape(slots, count, HD)
        return lax.dynamic_index_in_dim(padded, me, 1, keepdims=False).reshape(wide)

    head_bias = jnp.concatenate(
        [own_heads(small_rows[0]), jnp.zeros((wide,), F32), own_heads(small_rows[1])]
    )
    fc_bias = lax.dynamic_slice_in_dim(small_rows[3:7].reshape(-1), me * hidden, hidden, 0)
    gain_one, shift_one = small_rows[8][None], small_rows[9][None]
    gain_two, shift_two = small_rows[10][None], small_rows[11][None]

    ready = (w_head, token_tour.moved[-1])
    tokens_all, normal_all, qkv_rows = first_rows(
        token_tour.pieces, marks, w_head, gain_one, shift_one, head_bias[None]
    )
    qkv_all = qkv_rows.reshape(count, SEQS, seq_rows, 3 * wide)
    context, probs = attention_forward(qkv_all, pos_all)
    context = context.reshape(all_rows, wide)

    cot_zero = lax.ppermute(after(cotangent, *ready), "seq", ring.swap)
    cot_moving = lax.ppermute(after(cotangent, *ready), "seq", ring.behind)
    fc_low = after(fc_weight, *ready).astype(BF16)
    context = after(context, cot_zero, cot_moving)
    out_part = gather_columns(out_moved, after(out_crossed, context), marks)
    out_near, out_far = square.near_of(out_part), square.far_of(out_part)
    fc_near, fc_far = square.near_of(fc_low), square.far_of(fc_low)
    proj_low = after(proj_weight, context).T.astype(BF16)
    proj_near, proj_far = square.near_of(proj_low), square.far_of(proj_low)
    context_tour = Tour(ring, context)
    context_tour.step()
    context_tour.step(land=(out_part, fc_far))
    fc_pieces = (fc_low, fc_near, fc_far, square.near_of(after(fc_far, context_tour.current)))
    w_fc = square.place(fc_pieces)
    gain_column, shift_column = small_rows[8][:, None], small_rows[9][:, None]
    w_fc = after(w_fc, gain_column, shift_column)
    context_tour.step(land=(proj_far, w_fc))
    proj_pieces = (proj_low, proj_near, proj_far, square.near_of(after(proj_far, context_tour.current)))
    w_proj = square.place(proj_pieces)
    for t in range(3, steps):
        context_tour.step(land=(out_far, w_proj) if t == 3 else ())
    out_pieces = (out_part, out_near, out_far, square.near_of(after(out_far, context_tour.current)))
    w_out = heads_rows(square.me, out_pieces, count, slots)
    partial = residual_rows(
        tokens_all, context_tour.pieces[:-1], marks, w_out, small_rows[2][None]
    )
    last_pair = after(context_tour.pieces[-1], partial)
    normed_all, residual = second_rows(
        partial, last_pair, marks, w_out, gain_two, shift_two, steps
    )
    cot_pieces = {0: (cotangent, cot_zero)}
    cot_moving = [cot_moving]
    for t in range(2, steps):
        begin = context_tour.current if t == 2 else w_out
        moving = lax.ppermute(after(cot_moving[-1], begin), "seq", ring.behind)
        cot_moving.append(after(moving, w_out if t == 2 else residual))
    crossed = lax.ppermute(after(cot_moving[0], last_pair[1]), "seq", ring.swap)
    cot_pieces[steps - 1] = (cot_moving[0], crossed)

    def feed_forward(kept, taken, *begin):
        chosen = jnp.stack([ring.side] + [ring.position(t) for t in taken])
        return hidden_rows(
            normed_all,
            [cot_pieces[t] for t in taken],
            after(chosen, *begin) if begin else chosen,
            w_fc,
            w_proj,
            fc_bias[None],
            kept,
            taken,
            rows,
        )

    for t in range(2, steps):
        crossed = lax.ppermute(after(cot_moving[t - 1], crossed, residual), "seq", ring.swap)
        cot_pieces[steps - t] = (cot_moving[t - 1], crossed)
    kept, parts = feed_forward(None, [steps - 1])
    cot_pieces[steps - 2] = after(cot_pieces[steps - 2], parts[steps - 1][1])
    grad_fold = Fold(ring, parts)
    kept, more = feed_forward(kept, [steps - 2])
    parts.update(more)
    grad_fold.beside(*parts[steps - 2])
    for t in range(3, steps):
        cot_pieces[steps - t] = after(cot_pieces[steps - t], parts[steps - 2][1])
    grad_fold.step()
    kept, more = feed_forward(kept, list(reversed(range(steps - 2))), grad_fold.carried)
    parts.update(more)
    grad_fold.beside(*parts[0])
    hidden_low, grad_pre_low, cot_all = kept
    grad_fold.step()
    output_partial = rows_product(after(hidden_low, grad_fold.carried), w_proj, "output_product")
    grad_fold.beside(output_partial)
    for _ in range(3, steps):
        grad_fold.step()
    fc_sum = turned_product(after(normed_all, grad_fold.carried), grad_pre_low, "fc_product")
    grad_fold.beside(fc_sum)
    output_sum = lax.psum_scatter(output_partial, "seq", scatter_dimension=0, tiled=True)
    terms = grad_fold.terms
    grad_residual, _, row_sums, grad_sent = second_back(
        residual, terms, cotangent, gain_two, w_out, count
    )
    grad_bias_fc = jnp.sum(after(grad_pre_low, grad_sent).astype(F32), axis=0)
    fc_column = square.half_sum(after(fc_sum, grad_sent))

    proj_sum = turned_product(after(cot_all, grad_sent), hidden_low, "proj_product")
    grad_back = after(lax.all_to_all(grad_sent, "seq", 0, 0), proj_sum, grad_bias_fc)
    proj_column = square.half_sum(after(proj_sum, grad_back))
    grad_context = grad_back[:, :, :wide]
    attn_cut = grad_back[:, :, wide:]
    grad_qkv = attention_backward(
        qkv_all, grad_context.reshape(count, SEQS, seq_rows, wide), probs
    ).reshape(all_rows, 3 * wide)
    fc_grad = after(square.other_sum(fc_column), grad_qkv)
    proj_grad = square.other_sum(after(proj_column, grad_qkv))
    parts = ring_parts(grad_qkv, w_head, marks, [steps - 1], steps, "first_parts")
    input_fold = Fold(ring, parts)
    parts.update(
        ring_parts(
            after(grad_qkv, *parts[steps - 1]), w_head, marks, range(steps - 1), steps, "input_parts"
        )
    )
    input_fold.beside(*parts[0])
    input_fold.step()
    head_sum, grad_gain_one, grad_shift_one, grad_qkv_sum = head_product(
        after(normal_all, input_fold.carried),
        grad_qkv,
        w_head,
        gain_column,
        shift_column,
    )
    input_fold.beside(head_sum)
    input_fold.step()
    head_column = square.half_sum(after(head_sum, input_fold.carried))
    out_columns = out_weight.shape[1]
    attn_columns = after(attn_cut, input_fold.carried).reshape(all_rows, out_columns)
    out_sum = out_product(context_tour.pieces, attn_columns, marks, count, slots)
    input_fold.beside(head_column, out_sum)
    out_column = square.half_sum(out_sum)
    for _ in range(3, steps):
        input_fold.step()
    small_begin = input_fold.carried
    head_far = square.other_sum(after(head_column, input_fold.carried))
    input_fold.beside(output_sum)
    input_grad = first_back(tokens, input_fold.terms, grad_residual, gain_one)
    head_grad = after(head_far, input_grad).astype(BF16)
    unpack_back = unpack_hot.reshape(3 * wide, count, most)
    head_packed = jnp.einsum("rk,ksl->srl", head_grad, unpack_back, preferred_element_type=BF16)
    out_grad = square.other_sum(after(out_column, small_begin))
    fc_new = adam_update(
        fc_weight, fc_first, fc_second, after(fc_grad, head_packed), 0.02, 0.1
    )
    head_back = lax.all_to_all(head_packed, "seq", 0, 0)
    qkv_grad = jnp.einsum(
        "drl,cdl->rc",
        head_back,
        pack_hot.reshape(window, count, most),
        preferred_element_type=F32,
    )
    output = (residual + output_sum.astype(F32) + small_rows[7]).astype(BF16)

    def place_heads(values):
        spread = (jnp.arange(count) == me).astype(F32)[None, :, None]
        placed = values.reshape(slots, 1, HD) * spread
        return placed.reshape(-1)[:width]

    grad_bias_fc = grad_bias_fc[None, :] * (jnp.arange(count) == me).astype(F32)[:, None]
    grad_qkv_sum = after(grad_qkv_sum, small_begin)[0]
    grad_small = jnp.concatenate(
        [
            place_heads(grad_qkv_sum[:wide])[None],
            place_heads(grad_qkv_sum[2 * wide :])[None],
            row_sums[2:3],
            grad_bias_fc.reshape(-1, width),
            row_sums[3:4],
            grad_gain_one[:, 0][None],
            grad_shift_one[:, 0][None],
            row_sums[0:1],
            row_sums[1:2],
        ],
        axis=0,
    )
    small_sent = grad_small.astype(BF16).reshape(small_count, count, small_width)
    small_part = jnp.sum(
        lax.all_to_all(small_sent.transpose(1, 0, 2), "seq", 0, 0).astype(F32), axis=0
    )
    small_grad = square.sum(after(small_part, head_packed))

    qkv_new = adam_update(qkv_weight, qkv_first, qkv_second, qkv_grad, 0.02, 0.1)
    out_new = adam_update(out_weight, out_first, out_second, out_grad, 0.3, 0.1)
    proj_new = adam_update(
        proj_weight.T, proj_first.T, proj_second.T, proj_grad, 0.02, 0.1
    )
    proj_new = [value.T for value in proj_new]
    small_new = adam_update(small_weight, small_first, small_second, small_grad, 0.3, 0.0)
    return (
        output,
        input_grad,
        *qkv_new,
        *out_new,
        *fc_new,
        *proj_new,
        *small_new,
        small_grad[7],
    )


def solution(mesh):
    rows = P(("dp", "seq"), None)
    matrix = P("dp", "seq")
    turned = P("seq", "dp")
    small = P(None, "seq")
    in_specs = (
        (rows, rows, P(("dp", "seq"))) + (matrix,) * 9 + (turned,) * 3 + (small,) * 3
    )
    out_specs = (rows, rows) + (matrix,) * 9 + (turned,) * 3 + (small,) * 3 + (P("seq"),)
    return jax.shard_map(shards, mesh=mesh, in_specs=in_specs, out_specs=out_specs, check_vma=False)
```

```python
import functools
import math

import jax
import jax.numpy as jnp
import numpy as np
from jax import lax
from jax.experimental import pallas as pl
from jax.experimental.layout import Layout, with_layout_constraint
from jax.experimental.pallas import tpu as pltpu
from jax.sharding import PartitionSpec as P

HEADS = 25
HD = 64
SEQS = 2
STEP = 10

NORM_EPS = 1e-05
SCORE_SCALE = 0.125
MASKED_SCORE = -1e30
BETA_ONE = 0.9
BETA_TWO = 0.95
ADAM_EPS = 1e-08
BF16 = jnp.bfloat16
F32 = jnp.float32
SMALL_COST = pl.CostEstimate(flops=1024, bytes_accessed=1024, transcendentals=0)
LARGE_COST = pl.CostEstimate(flops=8 * 10**9, bytes_accessed=8 * 10**6, transcendentals=0)


def adam_update(weight, first_moment, second, gradient, step_rate, decay_rate):
    moment_new = BETA_ONE * first_moment + (1.0 - BETA_ONE) * gradient
    second_new = BETA_TWO * second + (1.0 - BETA_TWO) * gradient * gradient
    direction = (
        moment_new
        / (1.0 - BETA_ONE**STEP)
        / (jnp.sqrt(second_new / (1.0 - BETA_TWO**STEP)) + ADAM_EPS)
    )
    return (moment_new, second_new, weight - step_rate * (direction + decay_rate * weight))


def dot(left, right):
    return jnp.dot(left, right, preferred_element_type=F32)


def dot_nt(left, right):
    return lax.dot_general(left, right, (((1,), (1,)), ((), ())), preferred_element_type=F32)


def dot_tn(left, right):
    return lax.dot_general(left, right, (((0,), (0,)), ((), ())), preferred_element_type=F32)


def after(value, *others):
    return lax.optimization_barrier((value,) + others)[0]


def by_rows(value):
    return with_layout_constraint(value, Layout(major_to_minor=(0, 1)))


def call(
    kernel, out, blocks, grid=None, in_blocks=None, scalars=None, alias=None, scratch=(), name=None
):
    operands = 0 if scalars is None else 1
    spec = dict(
        in_specs=in_blocks,
        out_specs=blocks,
        grid=grid or (1,),
        scratch_shapes=list(scratch),
    )
    if operands:
        spec = dict(grid_spec=pltpu.PrefetchScalarGridSpec(num_scalar_prefetch=1, **spec))
    run = pl.pallas_call(
        kernel,
        out_shape=out,
        input_output_aliases=alias or {},
        compiler_params=pltpu.CompilerParams(vmem_limit_bytes=60 * 1024 * 1024),
        cost_estimate=SMALL_COST,
        name=name,
        **spec,
    )
    if operands:
        return lambda *given: run(scalars, *given)
    return run


def whole(shape):
    return pl.BlockSpec(shape, lambda *_: (0,) * len(shape))


def struct(shape, dtype):
    return jax.ShapeDtypeStruct(shape, dtype)


class Ring:
    def __init__(self, count):
        self.sides = 2
        self.steps = count // 2
        steps = self.steps
        self.swap = [(j, j ^ 1) for j in range(count)]
        self.ahead = [(z * 2 + x, ((z + 1) % steps) * 2 + x) for z in range(steps) for x in range(2)]
        self.behind = [(dst, src) for src, dst in self.ahead]
        me = lax.axis_index("seq")
        self.place, self.side = me // 2, me % 2

    def shift(self, t):
        steps = self.steps
        return [(z * 2 + x, ((z + t) % steps) * 2 + x) for z in range(steps) for x in range(2)]

    def position(self, t):
        return (self.place + self.steps - t) % self.steps

    def gather(self, block):
        tour = Tour(self, block)
        for _ in range(self.steps):
            tour.step()
        return tour


class Tour:
    def __init__(self, ring, block, back=False):
        self.ring, self.current, self.back = ring, block, back
        self.pieces = [None] * ring.steps
        self.moved = []

    def step(self, *begin, land=()):
        ring, t = self.ring, len(self.moved)
        if begin:
            self.current = after(self.current, *begin)
        if t:
            moved = lax.ppermute(self.current, "seq", ring.behind if self.back else ring.ahead)
            self.current = after(moved, self.moved[-1], *land)
        other = lax.ppermute(self.current, "seq", ring.swap)
        self.pieces[-t if self.back else t] = (self.current, other)
        self.moved.append(other)


class Fold:
    def __init__(self, ring, parts):
        self.ring, self.parts = ring, parts
        self.terms, self.count, self.carried = None, 0, None
        self.step()

    def step(self):
        ring = self.ring
        mine, other = self.parts[ring.steps - 1 - self.count]
        self.count += 1
        sent = None
        if self.terms is not None:
            sent = sum(term.astype(F32) for term in self.terms).astype(BF16)
            self.carried = sent
            other = after(other, sent)
        self.terms = [mine, lax.ppermute(other, "seq", ring.swap)]
        if sent is not None:
            self.terms.append(lax.ppermute(sent, "seq", ring.behind))

    def beside(self, *work):
        self.terms = list(lax.optimization_barrier((tuple(self.terms),) + work)[0])


class Square:
    def __init__(self):
        me = lax.axis_index("dp")
        self.me, self.far, self.near = me, me // 2, me % 2
        self.far_swap = [(j, j ^ 2) for j in range(4)]
        self.near_swap = [(j, j ^ 1) for j in range(4)]

    def near_of(self, block):
        return lax.ppermute(block, "dp", self.near_swap)

    def far_of(self, block):
        return lax.ppermute(block, "dp", self.far_swap)

    def gather(self, block, *begin):
        near, far = self.near_of(block), self.far_of(block)
        far = after(far, *begin) if begin else far
        return (block, near, far, lax.ppermute(far, "dp", self.near_swap))

    def place(self, pieces):
        rows, width = pieces[0].shape

        def kernel(me, *refs):
            for r in range(4):
                begin = pl.multiple_of((me[0] ^ r) * rows, 16)
                refs[4][pl.ds(begin, rows)] = refs[r][...]

        return call(
            kernel,
            struct((4 * rows, width), BF16),
            whole((4 * rows, width)),
            in_blocks=[whole((rows, width))] * 4,
            scalars=self.me[None],
            name="place_rows",
        )(*pieces)

    def half_sum(self, partial):
        parts = partial.reshape((2, 2, partial.shape[0] // 4) + partial.shape[1:])
        mine = lax.dynamic_index_in_dim(parts, self.near, 1, keepdims=False)
        other = lax.dynamic_index_in_dim(parts, 1 - self.near, 1, keepdims=False)
        near = lax.ppermute(other, "dp", self.near_swap)
        return (mine.astype(F32) + near.astype(F32)).astype(BF16)

    def other_sum(self, column):
        mine = lax.dynamic_index_in_dim(column, self.far, 0, keepdims=False)
        other = lax.dynamic_index_in_dim(column, 1 - self.far, 0, keepdims=False)
        return mine.astype(F32) + lax.ppermute(other, "dp", self.far_swap).astype(F32)

    def sum(self, values):
        values = values + lax.ppermute(values, "dp", self.near_swap)
        return values + lax.ppermute(values, "dp", self.far_swap)


def head_tables(count, model_width, window):
    slots = -(-HEADS // count)
    wide = slots * HD
    lists = [[[] for _ in range(count)] for _ in range(count)]
    for column in range(3 * model_width):
        src, local = divmod(column, window)
        part, within = divmod(column, model_width)
        head, lane = divmod(within, HD)
        dst, slot = head % count, head // count
        lists[src][dst].append((local, part * wide + slot * HD + lane))
    most = max(len(entry) for row in lists for entry in row)
    most = -(-most // 64) * 64
    pack = np.full((count, count * most), -1, np.int32)
    unpack = np.full((count, count * most), -1, np.int32)
    for src in range(count):
        for dst in range(count):
            for place, (local, target) in enumerate(lists[src][dst]):
                pack[src, dst * most + place] = local
                unpack[dst, src * most + place] = target
    return pack, unpack, most


def pick_row(table, index):
    return lax.dynamic_index_in_dim(jnp.asarray(table), index, 0, keepdims=False)


def one_hot(rows, size):
    return (lax.broadcasted_iota(jnp.int32, (size, rows.shape[0]), 0) == rows[None, :]).astype(BF16)


def forward_kernel(pos_col, pos_row, query_ref, full_ref, context_ref, probs_ref, *, wide):
    slots, _, run, width = query_ref.shape
    rows = slots * run
    keys_total = full_ref.shape[0] * run
    query = query_ref[:, 0].reshape(rows, width)[:, :wide]
    full = full_ref[:, 0].reshape(keys_total, width)
    key, value = full[:, wide : 2 * wide], full[:, 2 * wide :]
    seen = pos_row[0] <= pos_col[0]
    lane_head = lax.broadcasted_iota(jnp.int32, (1, wide), 1) // HD
    context = jnp.zeros((rows, wide), F32)
    for head in range(wide // HD):
        mine = lane_head == head
        scores = dot_nt(jnp.where(mine, query, jnp.zeros_like(query)), key) * SCORE_SCALE
        scores = jnp.where(seen, scores, MASKED_SCORE)
        top = jnp.max(scores, axis=1, keepdims=True)
        raw = jnp.exp(scores - top)
        probs = (raw * (1.0 / jnp.sum(raw, axis=1, keepdims=True))).astype(BF16)
        probs_ref[0, head] = probs
        context = jnp.where(mine, dot(probs, value), context)
    context_ref[:, 0] = context.astype(BF16).reshape(slots, run, wide)


def backward_kernel(query_ref, full_ref, grad_ref, probs_ref, out_ref, key_sum, value_sum, *, wide):
    step = pl.program_id(1)
    slots, _, run, width = query_ref.shape
    rows = slots * run
    count = full_ref.shape[0]
    keys_total = count * run
    query = query_ref[:, 0].reshape(rows, width)[:, :wide]
    full = full_ref[:, 0].reshape(keys_total, width)
    key, value = full[:, wide : 2 * wide], full[:, 2 * wide :]
    grad = grad_ref[:, 0].reshape(rows, wide)
    lane_head = lax.broadcasted_iota(jnp.int32, (1, wide), 1) // HD

    @pl.when(step == 0)
    def _():
        key_sum[...] = jnp.zeros_like(key_sum)
        value_sum[...] = jnp.zeros_like(value_sum)

    query_grad = jnp.zeros((rows, wide), F32)
    key_grad = jnp.zeros((keys_total, wide), F32)
    value_grad = jnp.zeros((keys_total, wide), F32)
    for head in range(wide // HD):
        mine = lane_head == head
        probs_low = probs_ref[0, head]
        probs = probs_low.astype(F32)
        grad_probs = dot_nt(jnp.where(mine, grad, jnp.zeros_like(grad)), value)
        weighted = probs * grad_probs
        delta = jnp.sum(weighted, axis=1, keepdims=True)
        grad_scores = (weighted - probs * delta).astype(BF16)
        query_grad = jnp.where(mine, dot(grad_scores, key), query_grad)
        key_grad = jnp.where(mine, dot_tn(grad_scores, query), key_grad)
        value_grad = jnp.where(mine, dot_tn(probs_low, grad), value_grad)
    key_sum[...] += key_grad
    value_sum[...] += value_grad
    out_ref[pl.ds(step * slots, slots), 0, :, :wide] = (
        (query_grad * SCORE_SCALE).astype(BF16).reshape(slots, run, wide)
    )

    @pl.when(step == pl.num_programs(1) - 1)
    def _():
        out_ref[:, 0, :, wide : 2 * wide] = (
            (key_sum[...] * SCORE_SCALE).astype(BF16).reshape(count, run, wide)
        )
        out_ref[:, 0, :, 2 * wide :] = value_sum[...].astype(BF16).reshape(count, run, wide)


def attention_forward(qkv_rows, positions):
    count, _, run, width = qkv_rows.shape
    wide = width // 3
    heads = wide // HD
    length = count * run
    block = min(length, 512)
    slots = block // run
    steps = length // block
    by_sequence = positions.reshape(count, SEQS, run).transpose(1, 0, 2).reshape(SEQS, length)
    return pl.pallas_call(
        functools.partial(forward_kernel, wide=wide),
        grid=(SEQS, steps),
        in_specs=[
            pl.BlockSpec((1, block, 1), lambda s, i: (s, i, 0)),
            pl.BlockSpec((1, 1, length), lambda s, i: (s, 0, 0)),
            pl.BlockSpec((slots, 1, run, width), lambda s, i: (i, s, 0, 0)),
            pl.BlockSpec((count, 1, run, width), lambda s, i: (0, s, 0, 0)),
        ],
        out_specs=[
            pl.BlockSpec((slots, 1, run, wide), lambda s, i: (i, s, 0, 0)),
            pl.BlockSpec((1, heads, block, length), lambda s, i: (s, 0, i, 0)),
        ],
        out_shape=[
            jax.ShapeDtypeStruct((count, SEQS, run, wide), BF16),
            jax.ShapeDtypeStruct((SEQS, heads, length, length), BF16),
        ],
        compiler_params=pltpu.CompilerParams(vmem_limit_bytes=60 * 1024 * 1024),
        cost_estimate=LARGE_COST,
        name="attention_forward",
    )(by_sequence[:, :, None], by_sequence[:, None, :], qkv_rows, qkv_rows)


def attention_backward(qkv_rows, grad_context, probs):
    count, _, run, width = qkv_rows.shape
    wide = width // 3
    heads = wide // HD
    length = count * run
    block = min(length, 512)
    slots = block // run
    steps = length // block
    return pl.pallas_call(
        functools.partial(backward_kernel, wide=wide),
        grid=(SEQS, steps),
        in_specs=[
            pl.BlockSpec((slots, 1, run, width), lambda s, i: (i, s, 0, 0)),
            pl.BlockSpec((count, 1, run, width), lambda s, i: (0, s, 0, 0)),
            pl.BlockSpec((slots, 1, run, wide), lambda s, i: (i, s, 0, 0)),
            pl.BlockSpec((1, heads, block, length), lambda s, i: (s, 0, i, 0)),
        ],
        out_specs=pl.BlockSpec((count, 1, run, width), lambda s, i: (0, s, 0, 0)),
        out_shape=jax.ShapeDtypeStruct((count, SEQS, run, width), BF16),
        scratch_shapes=[pltpu.VMEM((length, wide), F32), pltpu.VMEM((length, wide), F32)],
        compiler_params=pltpu.CompilerParams(vmem_limit_bytes=60 * 1024 * 1024),
        cost_estimate=SMALL_COST,
        name="attention_backward",
    )(qkv_rows, qkv_rows, grad_context, probs)


def in_order(side, own, other, axis=0):
    first = jnp.where(side == 0, own, other)
    second = jnp.where(side == 0, other, own)
    return jnp.concatenate([first, second], axis=axis)


def normalize(values):
    centred = values - jnp.mean(values, axis=1, keepdims=True)
    spread = lax.rsqrt(jnp.mean(centred * centred, axis=1, keepdims=True) + NORM_EPS)
    return centred * spread, spread


def normalize_back(normal, spread, gain, grad):
    scaled = grad * gain
    along = jnp.mean(scaled * normal, axis=1, keepdims=True)
    return spread * (scaled - jnp.mean(scaled, axis=1, keepdims=True) - normal * along)


def first_rows(pieces, scalars, weight, gain, shift, bias):
    rows, width = pieces[0][0].shape
    steps = len(pieces)
    total = 2 * steps * rows
    columns = weight.shape[1]

    def kernel(marks, *refs):
        given, (w, g, s, b), outs = refs[: 2 * steps], refs[2 * steps : 2 * steps + 4], refs[-3:]
        for t in range(steps):

            @pl.when(pl.program_id(0) == t)
            def _(t=t):
                outs[0][...] = in_order(marks[0], given[2 * t][...], given[2 * t + 1][...])

        normal, _ = normalize(outs[0][...].astype(F32))
        outs[1][...] = normal.astype(BF16)
        scaled = (normal * g[...] + s[...]).astype(BF16)
        outs[2][...] = (dot(scaled, w[...]) + b[...]).astype(BF16)

    def block(width):
        return pl.BlockSpec((2 * rows, width), lambda t, marks: (marks[1 + t], 0))

    flat = [piece for pair in pieces for piece in pair]
    return call(
        kernel,
        [struct((total, width), BF16), struct((total, width), BF16), struct((total, columns), BF16)],
        [block(width), block(width), block(columns)],
        grid=(steps,),
        in_blocks=[whole((rows, width))] * (2 * steps)
        + [whole(weight.shape), whole((1, width)), whole((1, width)), whole((1, columns))],
        scalars=scalars,
        name="first_rows",
    )(*flat, weight, gain, shift, bias)


def residual_rows(tokens_all, pieces, scalars, weight, bias):
    total, width = tokens_all.shape
    many = len(pieces)
    wide = pieces[0][0].shape[1]
    rows = min(total, 256)

    def kernel(marks, tokens, *refs):
        given, (w, b, out) = refs[: 2 * many], refs[2 * many :]
        value = tokens[...].astype(F32) + b[...]
        for t in range(many):
            pair = in_order(marks[0], given[2 * t][...], given[2 * t + 1][...], axis=1)
            begin = pl.multiple_of(marks[1 + t] * (2 * wide), 2 * wide)
            value += dot(pair, w[pl.ds(begin, 2 * wide)])
        out[...] = value

    def block(width):
        return pl.BlockSpec((rows, width), lambda i, marks: (i, 0))

    return call(
        kernel,
        struct((total, width), F32),
        block(width),
        grid=(total // rows,),
        in_blocks=[block(width)] + [block(wide)] * (2 * many) + [whole(weight.shape), whole((1, width))],
        scalars=scalars,
        name="residual_rows",
    )(tokens_all, *[piece for pair in pieces for piece in pair], weight, bias)


def second_rows(partial, pair, scalars, weight, gain, shift, steps):
    total, width = partial.shape
    wide = pair[0].shape[1]
    own_rows = total // (2 * steps)
    rows = 2 * own_rows

    def kernel(marks, before, first, second, w, g, s, normed, own):
        both = in_order(marks[0], first[...], second[...], axis=1)
        residual = before[...] + dot(both, w[...])
        normal, _ = normalize(residual)
        normed[...] = (normal * g[...] + s[...]).astype(BF16)

        @pl.when(pl.program_id(0) == marks[1])
        def _():
            own[...] = jnp.where(marks[0] == 0, residual[:own_rows], residual[own_rows:])

    def block(width):
        return pl.BlockSpec((rows, width), lambda i, marks: (i, 0))

    return call(
        kernel,
        [struct((total, width), BF16), struct((own_rows, width), F32)],
        [block(width), whole((own_rows, width))],
        grid=(steps,),
        in_blocks=[
            block(width),
            block(wide),
            block(wide),
            pl.BlockSpec((2 * wide, width), lambda i, marks: (marks[steps], 0)),
            whole((1, width)),
            whole((1, width)),
        ],
        scalars=scalars,
        name="second_rows",
    )(partial, *pair, weight, gain, shift)


def hidden_rows(normed, pairs, scalars, w_fc, w_proj, bias, kept, taken, rows):
    total, width = normed.shape
    hidden = w_fc.shape[1]
    many = len(taken)

    def kernel(marks, block, *refs):
        given, (fc, proj, b) = refs[: 2 * many], refs[2 * many : 2 * many + 3]
        act_ref, grad_ref, cot_ref = refs[-3 - 2 * many : -2 * many]
        parts = refs[-2 * many :]
        for i in range(many):

            @pl.when(pl.program_id(0) == i)
            def _(i=i):
                cot_ref[...] = in_order(marks[0], given[2 * i][...], given[2 * i + 1][...])

        z = dot(block[...], fc[...]) + b[...]
        square = z * z
        tanh = jnp.tanh(0.7978845608028654 * (z + 0.044715 * (square * z)))
        half = 0.5 * (1.0 + tanh)
        slope = half + 0.5 * z * (1.0 - tanh * tanh) * (
            0.7978845608028654 + (0.7978845608028654 * 3.0 * 0.044715) * square
        )
        act_ref[...] = (z * half).astype(BF16)
        grad = (dot(cot_ref[...], proj[...]) * slope).astype(BF16)
        grad_ref[...] = grad
        part = dot_nt(grad, fc[...])
        mine = jnp.where(marks[0] == 0, part[:rows], part[rows:])
        other = jnp.where(marks[0] == 0, part[rows:], part[:rows]).astype(BF16)
        for i in range(many):

            @pl.when(pl.program_id(0) == i)
            def _(i=i):
                parts[2 * i][...] = mine
                parts[2 * i + 1][...] = other

    def block(width):
        return pl.BlockSpec((2 * rows, width), lambda i, marks: (marks[1 + i], 0))

    operands = [normed] + [piece for pair in pairs for piece in pair] + [w_fc, w_proj, bias]
    blocks = [block(width)] + [whole((rows, width))] * (2 * many)
    blocks += [whole(w_fc.shape), whole(w_proj.shape), whole((1, hidden))]
    alias = {}
    if kept is not None:
        alias = {1 + len(operands) + i: i for i in range(3)}
        operands += list(kept)
        blocks += [pl.BlockSpec(memory_space=pl.ANY)] * 3
    outs = call(
        kernel,
        [struct((total, hidden), BF16), struct((total, hidden), BF16), struct((total, width), BF16)]
        + [struct((rows, width), dtype) for _ in taken for dtype in (F32, BF16)],
        [block(hidden), block(hidden), block(width)] + [whole((rows, width))] * (2 * many),
        grid=(many,),
        in_blocks=blocks,
        scalars=scalars,
        alias=alias,
        name="hidden_rows",
    )(*operands)
    return outs[:3], {t: (outs[3 + 2 * i], outs[4 + 2 * i]) for i, t in enumerate(taken)}


def turned_product(left, right, name):
    total, width = left.shape
    columns = right.shape[1]
    tile = 256

    def kernel(left_ref, right_ref, out_ref):
        out_ref[...] = dot(left_ref[...].T, right_ref[...]).astype(BF16)

    return call(
        kernel,
        struct((width, columns), BF16),
        pl.BlockSpec((tile, columns), lambda i: (i, 0)),
        grid=(pl.cdiv(width, tile),),
        in_blocks=[pl.BlockSpec((total, tile), lambda i: (0, i)), whole(right.shape)],
        name=name,
    )(left, right)


def head_product(normal, grad, weight, gain, shift):
    total, width = normal.shape
    columns = grad.shape[1]
    tile = 256

    def kernel(left, right, w, g, s, out, gain_sum, shift_sum, grad_sum):
        @pl.when(pl.program_id(0) == 0)
        def _():
            grad_sum[...] = jnp.sum(right[...].astype(F32), axis=0, keepdims=True)

        raw = dot(left[...].T, right[...])
        sums = grad_sum[...]
        low = w[...].astype(F32)
        gain_sum[...] = jnp.sum(raw * low, axis=1, keepdims=True)
        shift_sum[...] = jnp.sum(low * sums, axis=1, keepdims=True)
        out[...] = (raw * g[...] + s[...] * sums).astype(BF16)

    column = pl.BlockSpec((tile, 1), lambda i: (i, 0))
    return call(
        kernel,
        [
            struct((width, columns), BF16),
            struct((width, 1), F32),
            struct((width, 1), F32),
            struct((1, columns), F32),
        ],
        [pl.BlockSpec((tile, columns), lambda i: (i, 0)), column, column, whole((1, columns))],
        grid=(pl.cdiv(width, tile),),
        in_blocks=[
            pl.BlockSpec((total, tile), lambda i: (0, i)),
            whole(grad.shape),
            pl.BlockSpec((tile, columns), lambda i: (i, 0)),
            column,
            column,
        ],
        name="head_product",
    )(normal, grad, weight, gain, shift)


def ring_parts(left, right, scalars, taken, steps, name):
    total, inner = left.shape
    width = right.shape[0]
    rows = total // (2 * steps)

    def kernel(marks, left_ref, right_ref, *outs):
        for i, t in enumerate(taken):
            begin = pl.multiple_of(marks[1 + t] * (2 * rows), 2 * rows)
            part = dot_nt(left_ref[pl.ds(begin, 2 * rows)], right_ref[...])
            outs[2 * i][...] = jnp.where(marks[0] == 0, part[:rows], part[rows:])
            outs[2 * i + 1][...] = jnp.where(marks[0] == 0, part[rows:], part[:rows]).astype(BF16)

    outs = call(
        kernel,
        [struct((rows, width), dtype) for _ in taken for dtype in (F32, BF16)],
        [whole((rows, width))] * (2 * len(taken)),
        in_blocks=[whole(left.shape), whole(right.shape)],
        scalars=scalars,
        name=name,
    )(left, right)
    return {t: (outs[2 * i], outs[2 * i + 1]) for i, t in enumerate(taken)}


def second_back(residual, terms, cotangent, gain, weight, count):
    rows, width = residual.shape
    wide = weight.shape[0] // count
    columns = width // count

    def kernel(
        res, mine, swapped, carried, cot, g, w, grad_ref, low_ref, sums_ref, out_ref, cut_ref
    ):
        @pl.when(pl.program_id(0) == 0)
        def _():
            grad = mine[...] + swapped[...].astype(F32) + carried[...].astype(F32)
            normal, spread = normalize(res[...])
            total = cot[...].astype(F32) + normalize_back(normal, spread, g[...], grad)
            grad_ref[...] = total
            low = total.astype(BF16)
            low_ref[...] = low
            sums_ref[0:1] = jnp.sum(grad * normal, axis=0, keepdims=True)
            sums_ref[1:2] = jnp.sum(grad, axis=0, keepdims=True)
            sums_ref[2:3] = jnp.sum(low.astype(F32), axis=0, keepdims=True)
            sums_ref[3:4] = jnp.sum(cot[...].astype(F32), axis=0, keepdims=True)

        out_ref[0] = dot_nt(low_ref[...], w[...]).astype(BF16)
        for j in range(count):

            @pl.when(pl.program_id(0) == j)
            def _(j=j):
                cut_ref[0] = low_ref[:, j * columns : (j + 1) * columns]

    row = whole((rows, width))
    return call(
        kernel,
        [
            struct((rows, width), F32),
            struct((rows, width), BF16),
            struct((4, width), F32),
            struct((count, rows, wide), BF16),
            struct((count, rows, columns), BF16),
        ],
        [
            row,
            row,
            whole((4, width)),
            pl.BlockSpec((1, rows, wide), lambda i: (i, 0, 0)),
            pl.BlockSpec((1, rows, columns), lambda i: (i, 0, 0)),
        ],
        grid=(count,),
        in_blocks=[row] * 5 + [whole((1, width)), pl.BlockSpec((wide, width), lambda i: (i, 0))],
        name="second_back",
    )(residual, *terms, cotangent, gain, weight)


def first_back(tokens, terms, residual_grad, gain):
    rows, width = tokens.shape

    def kernel(x, mine, swapped, carried, res, g, out_ref):
        grad = mine[...] + swapped[...].astype(F32) + carried[...].astype(F32)
        normal, spread = normalize(x[...].astype(F32))
        out_ref[...] = (res[...] + normalize_back(normal, spread, g[...], grad)).astype(BF16)

    row = whole((rows, width))
    return call(
        kernel,
        struct((rows, width), BF16),
        row,
        in_blocks=[row] * 5 + [whole((1, width))],
        name="first_back",
    )(tokens, *terms, residual_grad, gain)


def gather_columns(own, other, scalars):
    steps, rows, columns = own.shape
    width = 2 * steps * columns

    def kernel(marks, own_ref, other_ref, out):
        offset = lax.broadcasted_iota(jnp.int32, (columns, width), 1)
        offset -= lax.broadcasted_iota(jnp.int32, (columns, width), 0)
        value = None
        for t in range(steps):
            for b in range(2):
                owner = marks[1 + t] * 2 + (marks[0] if b == 0 else 1 - marks[0])
                spread = jnp.where(offset == owner * columns, 1.0, 0.0).astype(BF16)
                part = dot((own_ref if b == 0 else other_ref)[t], spread)
                value = part if value is None else value + part
        out[...] = value.astype(BF16)

    return call(
        kernel,
        struct((rows, width), BF16),
        whole((rows, width)),
        in_blocks=[whole(own.shape)] * 2,
        scalars=scalars,
        name="gather_columns",
    )(own, other)


def heads_rows(me, pieces, count, slots):
    rows, width = pieces[0].shape
    unit = math.gcd(rows, HD)

    def kernel(mark, *refs):
        out = refs[4]
        for h in range(HEADS, count * slots):
            place = ((h % count) * slots + h // count) * HD
            out[place : place + HD] = jnp.zeros((HD, width), BF16)
        for r in range(4):
            for piece in range(rows // unit):
                row = (mark[0] ^ r) * rows + piece * unit
                head = row // HD
                target = ((head % count) * slots + head // count) * HD + row % HD
                out[pl.ds(pl.multiple_of(target, unit), unit)] = refs[r][
                    piece * unit : (piece + 1) * unit
                ]

    return call(
        kernel,
        struct((count * slots * HD, width), BF16),
        whole((count * slots * HD, width)),
        in_blocks=[whole((rows, width))] * 4,
        scalars=me[None],
        name="heads_rows",
    )(*pieces)


def out_product(pieces, columns, scalars, count, slots):
    total, width = columns.shape
    wide = slots * HD
    steps = len(pieces)

    def kernel(marks, *refs):
        given, right, out = refs[: 2 * steps], refs[2 * steps], refs[-1]
        for t in range(steps):
            for b in range(2):
                owner = marks[1 + t] * 2 + (marks[0] if b == 0 else 1 - marks[0])
                value = dot_tn(given[2 * t + b][...], right[...]).astype(BF16)
                for slot in range(slots):
                    head = slot * count + owner

                    @pl.when(head < HEADS)
                    def _(slot=slot, head=head, value=value):
                        begin = pl.multiple_of(head * HD, HD)
                        out[pl.ds(begin, HD)] = value[slot * HD : (slot + 1) * HD]

    return call(
        kernel,
        struct((HEADS * HD, width), BF16),
        whole((HEADS * HD, width)),
        in_blocks=[whole((total, wide))] * (2 * steps) + [whole(columns.shape)],
        scalars=scalars,
        name="out_product",
    )(*[piece for pair in pieces for piece in pair], columns)


def rows_product(left, right, name):
    total, inner = left.shape
    width = right.shape[0]
    block = min(total, 512)

    def kernel(left_ref, right_ref, out_ref):
        out_ref[...] = dot_nt(left_ref[...], right_ref[...]).astype(BF16)

    return call(
        kernel,
        struct((total, width), BF16),
        pl.BlockSpec((block, width), lambda i: (i, 0)),
        grid=(total // block,),
        in_blocks=[pl.BlockSpec((block, inner), lambda i: (i, 0)), whole(right.shape)],
        name=name,
    )(left, right)


def shards(
    tokens,
    cotangent,
    positions,
    qkv_weight,
    qkv_first,
    qkv_second,
    out_weight,
    out_first,
    out_second,
    fc_weight,
    fc_first,
    fc_second,
    proj_weight,
    proj_first,
    proj_second,
    small_weight,
    small_first,
    small_second,
):
    count = lax.axis_size("seq")
    ring = Ring(count)
    square = Square()
    me = lax.axis_index("seq")
    rows, width = tokens.shape
    seq_rows = rows // SEQS
    window = qkv_weight.shape[1]
    slots = -(-HEADS // count)
    wide = slots * HD
    small_count, small_width = small_weight.shape
    hidden = fc_weight.shape[1]
    all_rows = count * rows
    steps = ring.steps
    marks = jnp.stack([ring.side] + [ring.position(t) for t in range(steps)])
    tokens = by_rows(tokens)
    cotangent = by_rows(cotangent)

    token_tour = Tour(ring, tokens)
    token_tour.step()
    token_tour.step()
    pack, unpack, most = head_tables(count, width, window)
    pack_hot = one_hot(pick_row(pack, me), window)
    packed = jnp.einsum(
        "rc,cdl->drl",
        qkv_weight.astype(BF16),
        pack_hot.reshape(window, count, most),
        preferred_element_type=BF16,
    )
    depth = packed.shape[1]
    small_flat = jnp.concatenate(
        [
            small_weight.reshape(-1).astype(BF16),
            (positions // 32).astype(BF16),
            (positions % 32).astype(BF16),
        ]
    )
    small_depth = -(-small_flat.shape[0] // most)
    small_depth += -small_depth % 16
    small_flat = jnp.pad(small_flat, (0, small_depth * most - small_flat.shape[0]))
    small_pack = jnp.broadcast_to(
        small_flat.reshape(1, small_depth, most), (count, small_depth, most)
    )
    received = lax.all_to_all(jnp.concatenate([packed, small_pack], axis=1), "seq", 0, 0)
    token_tour.step()
    out_low = by_rows(out_weight.astype(BF16))
    out_moved = [out_low] + [lax.ppermute(out_low, "seq", ring.shift(t)) for t in range(1, steps)]
    received = after(received, token_tour.moved[1], token_tour.current, *out_moved)

    unpack_hot = one_hot(pick_row(unpack, me), 3 * wide)
    head_part = jnp.einsum(
        "srl,ksl->rk",
        received[:, :depth],
        unpack_hot.reshape(3 * wide, count, most),
        preferred_element_type=BF16,
    )
    for t in range(3, steps):
        token_tour.step()
    head_pieces = square.gather(head_part, token_tour.current)
    out_moved = jnp.stack(after(out_moved, head_part))
    out_part = gather_columns(out_moved, lax.ppermute(out_moved, "seq", ring.swap), marks)
    w_head = square.place(after(head_pieces, out_part))

    small_all = received[:, depth:].reshape(count, small_depth * most).astype(F32)
    small_rows = small_all[:, : small_count * small_width].reshape(count, small_count, small_width)
    small_rows = small_rows.transpose(1, 0, 2).reshape(small_count, width)
    pos_all = small_all[:, small_count * small_width :][:, : 2 * rows].reshape(count, 2, rows)
    pos_all = (pos_all[:, 0] * 32.0 + pos_all[:, 1]).astype(jnp.int32)

    def own_heads(row):
        padded = jnp.pad(row, (0, slots * count * HD - width)).reshape(slots, count, HD)
        return lax.dynamic_index_in_dim(padded, me, 1, keepdims=False).reshape(wide)

    head_bias = jnp.concatenate(
        [own_heads(small_rows[0]), jnp.zeros((wide,), F32), own_heads(small_rows[1])]
    )
    fc_bias = lax.dynamic_slice_in_dim(small_rows[3:7].reshape(-1), me * hidden, hidden, 0)
    gain_one, shift_one = small_rows[8][None], small_rows[9][None]
    gain_two, shift_two = small_rows[10][None], small_rows[11][None]

    ready = (w_head, token_tour.moved[-1])
    tokens_all, normal_all, qkv_rows = first_rows(
        token_tour.pieces, marks, w_head, gain_one, shift_one, head_bias[None]
    )
    qkv_all = qkv_rows.reshape(count, SEQS, seq_rows, 3 * wide)
    context, probs = attention_forward(qkv_all, pos_all)
    context = context.reshape(all_rows, wide)

    cot_zero = lax.ppermute(after(cotangent, *ready), "seq", ring.swap)
    cot_moving = lax.ppermute(after(cotangent, *ready), "seq", ring.behind)
    fc_low = after(fc_weight, *ready).astype(BF16)
    context = after(context, cot_zero, cot_moving)
    out_near, out_far = square.near_of(out_part), square.far_of(out_part)
    fc_near, fc_far = square.near_of(fc_low), square.far_of(after(fc_low, context))
    context_tour = Tour(ring, context)
    context_tour.step()
    context_tour.step(land=(out_far,))
    out_pieces = (out_part, out_near, out_far, square.near_of(after(out_far, context_tour.current)))
    proj_low = after(proj_weight, context_tour.current).T.astype(BF16)
    proj_near, proj_far = square.near_of(proj_low), square.far_of(proj_low)
    w_out = heads_rows(square.me, out_pieces, count, slots)
    context_tour.step(land=(fc_far, w_out))
    fc_pieces = (fc_low, fc_near, fc_far, square.near_of(after(fc_far, context_tour.current)))
    w_fc = square.place(fc_pieces)
    for t in range(3, steps):
        context_tour.step(land=(proj_far, w_fc) if t == 3 else ())
    proj_pieces = (proj_low, proj_near, proj_far, square.near_of(after(proj_far, context_tour.current)))
    w_proj = square.place(proj_pieces)
    partial = residual_rows(
        tokens_all, context_tour.pieces[:-1], marks, w_out, small_rows[2][None]
    )
    last_pair = after(context_tour.pieces[-1], partial, w_proj)
    normed_all, residual = second_rows(
        partial, last_pair, marks, w_out, gain_two, shift_two, steps
    )
    cot_moving = [cot_moving]
    for t in range(2, steps):
        begin = context_tour.current if t == 2 else w_proj
        moving = lax.ppermute(after(cot_moving[-1], begin), "seq", ring.behind)
        cot_moving.append(after(moving, w_proj if t == 2 else partial))
    cot_pieces = {0: (cotangent, cot_zero)}
    for t in range(1, steps):
        crossed = lax.ppermute(after(cot_moving[t - 1], last_pair[1]), "seq", ring.swap)
        cot_pieces[steps - t] = (cot_moving[t - 1], after(crossed, residual))

    def feed_forward(kept, taken, *begin):
        chosen = jnp.stack([ring.side] + [ring.position(t) for t in taken])
        return hidden_rows(
            normed_all,
            [cot_pieces[t] for t in taken],
            after(chosen, *begin) if begin else chosen,
            w_fc,
            w_proj,
            fc_bias[None],
            kept,
            taken,
            rows,
        )

    kept, parts = feed_forward(None, [steps - 1])
    grad_fold = Fold(ring, parts)
    kept, more = feed_forward(kept, [steps - 2])
    parts.update(more)
    grad_fold.beside(*parts[steps - 2])
    grad_fold.step()
    kept, more = feed_forward(kept, list(reversed(range(steps - 2))), grad_fold.carried)
    parts.update(more)
    grad_fold.beside(*parts[0])
    hidden_low, grad_pre_low, cot_all = kept
    grad_fold.step()
    output_partial = rows_product(after(hidden_low, grad_fold.carried), w_proj, "output_product")
    grad_fold.beside(output_partial)
    for _ in range(3, steps):
        grad_fold.step()
    fc_sum = turned_product(after(normed_all, grad_fold.carried), grad_pre_low, "fc_product")
    grad_fold.beside(fc_sum)
    output_sum = lax.psum_scatter(output_partial, "seq", scatter_dimension=0, tiled=True)
    terms = grad_fold.terms
    grad_residual, _, row_sums, grad_sent, attn_cut = second_back(
        residual, terms, cotangent, gain_two, w_out, count
    )
    grad_bias_fc = jnp.sum(after(grad_pre_low, grad_sent).astype(F32), axis=0)
    fc_column = square.half_sum(after(fc_sum, grad_sent))

    proj_sum = turned_product(after(cot_all, grad_sent), hidden_low, "proj_product")
    grad_context = after(lax.all_to_all(grad_sent, "seq", 0, 0), proj_sum, grad_bias_fc)
    proj_column = square.half_sum(after(proj_sum, grad_context))
    attn_columns = lax.all_to_all(after(attn_cut, grad_context), "seq", 0, 0)
    grad_qkv = attention_backward(
        qkv_all, grad_context.reshape(count, SEQS, seq_rows, wide), probs
    ).reshape(all_rows, 3 * wide)
    fc_grad = after(square.other_sum(fc_column), grad_qkv)
    proj_grad = square.other_sum(after(proj_column, grad_qkv))
    attn_columns = after(attn_columns, grad_qkv)
    parts = ring_parts(grad_qkv, w_head, marks, [steps - 1], steps, "first_parts")
    input_fold = Fold(ring, parts)
    parts.update(
        ring_parts(
            after(grad_qkv, *parts[steps - 1]), w_head, marks, range(steps - 1), steps, "input_parts"
        )
    )
    input_fold.beside(*parts[0])
    input_fold.step()
    head_sum, grad_gain_one, grad_shift_one, grad_qkv_sum = head_product(
        after(normal_all, input_fold.carried),
        grad_qkv,
        w_head,
        small_rows[8][:, None],
        small_rows[9][:, None],
    )
    input_fold.beside(head_sum)
    input_fold.step()
    head_column = square.half_sum(after(head_sum, input_fold.carried))
    out_columns = out_weight.shape[1]
    attn_columns = after(attn_columns, input_fold.carried).reshape(all_rows, out_columns)
    input_fold.beside(head_column)
    for _ in range(3, steps):
        input_fold.step()
    small_begin = input_fold.carried
    head_far = square.other_sum(after(head_column, input_fold.carried))
    out_sum = out_product(
        context_tour.pieces, after(attn_columns, input_fold.carried), marks, count, slots
    )
    input_fold.beside(output_sum, out_sum)
    input_grad = first_back(tokens, input_fold.terms, grad_residual, gain_one)
    out_column = square.half_sum(after(out_sum, input_grad))
    head_grad = after(head_far, input_grad).astype(BF16)
    unpack_back = unpack_hot.reshape(3 * wide, count, most)
    head_packed = jnp.einsum("rk,ksl->srl", head_grad, unpack_back, preferred_element_type=BF16)
    out_grad = square.other_sum(after(out_column, head_packed))
    fc_new = adam_update(
        fc_weight, fc_first, fc_second, after(fc_grad, head_packed), 0.02, 0.1
    )
    head_back = lax.all_to_all(head_packed, "seq", 0, 0)
    qkv_grad = jnp.einsum(
        "drl,cdl->rc",
        head_back,
        pack_hot.reshape(window, count, most),
        preferred_element_type=F32,
    )
    output = (residual + output_sum.astype(F32) + small_rows[7]).astype(BF16)

    def place_heads(values):
        spread = (jnp.arange(count) == me).astype(F32)[None, :, None]
        placed = values.reshape(slots, 1, HD) * spread
        return placed.reshape(-1)[:width]

    grad_bias_fc = grad_bias_fc[None, :] * (jnp.arange(count) == me).astype(F32)[:, None]
    grad_qkv_sum = after(grad_qkv_sum, small_begin)[0]
    grad_small = jnp.concatenate(
        [
            place_heads(grad_qkv_sum[:wide])[None],
            place_heads(grad_qkv_sum[2 * wide :])[None],
            row_sums[2:3],
            grad_bias_fc.reshape(-1, width),
            row_sums[3:4],
            grad_gain_one[:, 0][None],
            grad_shift_one[:, 0][None],
            row_sums[0:1],
            row_sums[1:2],
        ],
        axis=0,
    )
    small_sent = grad_small.astype(BF16).reshape(small_count, count, small_width)
    small_part = jnp.sum(
        lax.all_to_all(small_sent.transpose(1, 0, 2), "seq", 0, 0).astype(F32), axis=0
    )
    small_grad = square.sum(after(small_part, head_packed))

    qkv_new = adam_update(qkv_weight, qkv_first, qkv_second, qkv_grad, 0.02, 0.1)
    out_new = adam_update(out_weight, out_first, out_second, out_grad, 0.3, 0.1)
    proj_new = adam_update(
        proj_weight.T, proj_first.T, proj_second.T, proj_grad, 0.02, 0.1
    )
    proj_new = [value.T for value in proj_new]
    small_new = adam_update(small_weight, small_first, small_second, small_grad, 0.3, 0.0)
    return (
        output,
        input_grad,
        *qkv_new,
        *out_new,
        *fc_new,
        *proj_new,
        *small_new,
        small_grad[7],
    )


def solution(mesh):
    rows = P(("dp", "seq"), None)
    matrix = P("dp", "seq")
    turned = P("seq", "dp")
    small = P(None, "seq")
    in_specs = (
        (rows, rows, P(("dp", "seq"))) + (matrix,) * 9 + (turned,) * 3 + (small,) * 3
    )
    out_specs = (rows, rows) + (matrix,) * 9 + (turned,) * 3 + (small,) * 3 + (P("seq"),)
    return jax.shard_map(shards, mesh=mesh, in_specs=in_specs, out_specs=out_specs, check_vma=False)
```

```python
import functools
import math

import jax
import jax.numpy as jnp
import numpy as np
from jax import lax
from jax.experimental import pallas as pl
from jax.experimental.layout import Layout, with_layout_constraint
from jax.experimental.pallas import tpu as pltpu
from jax.sharding import PartitionSpec as P

HEADS = 25
HD = 64
SEQS = 2
STEP = 10

NORM_EPS = 1e-05
SCORE_SCALE = 0.125
MASKED_SCORE = -1e30
BETA_ONE = 0.9
BETA_TWO = 0.95
ADAM_EPS = 1e-08
BF16 = jnp.bfloat16
F32 = jnp.float32
SMALL_COST = pl.CostEstimate(flops=1024, bytes_accessed=1024, transcendentals=0)
LARGE_COST = pl.CostEstimate(flops=8 * 10**9, bytes_accessed=8 * 10**6, transcendentals=0)


def adam_update(weight, first_moment, second, gradient, step_rate, decay_rate):
    moment_new = BETA_ONE * first_moment + (1.0 - BETA_ONE) * gradient
    second_new = BETA_TWO * second + (1.0 - BETA_TWO) * gradient * gradient
    direction = (
        moment_new
        / (1.0 - BETA_ONE**STEP)
        / (jnp.sqrt(second_new / (1.0 - BETA_TWO**STEP)) + ADAM_EPS)
    )
    return (moment_new, second_new, weight - step_rate * (direction + decay_rate * weight))


def dot(left, right):
    return jnp.dot(left, right, preferred_element_type=F32)


def dot_nt(left, right):
    return lax.dot_general(left, right, (((1,), (1,)), ((), ())), preferred_element_type=F32)


def dot_tn(left, right):
    return lax.dot_general(left, right, (((0,), (0,)), ((), ())), preferred_element_type=F32)


def after(value, *others):
    return lax.optimization_barrier((value,) + others)[0]


def by_rows(value):
    return with_layout_constraint(value, Layout(major_to_minor=(0, 1)))


def call(
    kernel, out, blocks, grid=None, in_blocks=None, scalars=None, alias=None, scratch=(), name=None
):
    operands = 0 if scalars is None else 1
    spec = dict(
        in_specs=in_blocks,
        out_specs=blocks,
        grid=grid or (1,),
        scratch_shapes=list(scratch),
    )
    if operands:
        spec = dict(grid_spec=pltpu.PrefetchScalarGridSpec(num_scalar_prefetch=1, **spec))
    run = pl.pallas_call(
        kernel,
        out_shape=out,
        input_output_aliases=alias or {},
        compiler_params=pltpu.CompilerParams(vmem_limit_bytes=60 * 1024 * 1024),
        cost_estimate=SMALL_COST,
        name=name,
        **spec,
    )
    if operands:
        return lambda *given: run(scalars, *given)
    return run


def whole(shape):
    return pl.BlockSpec(shape, lambda *_: (0,) * len(shape))


def struct(shape, dtype):
    return jax.ShapeDtypeStruct(shape, dtype)


class Ring:
    def __init__(self, count):
        self.sides = 2
        self.steps = count // 2
        steps = self.steps
        self.swap = [(j, j ^ 1) for j in range(count)]
        self.ahead = [(z * 2 + x, ((z + 1) % steps) * 2 + x) for z in range(steps) for x in range(2)]
        self.behind = [(dst, src) for src, dst in self.ahead]
        me = lax.axis_index("seq")
        self.place, self.side = me // 2, me % 2

    def position(self, t):
        return (self.place + self.steps - t) % self.steps

    def gather(self, block):
        tour = Tour(self, block)
        for _ in range(self.steps):
            tour.step()
        return tour


class Tour:
    def __init__(self, ring, block, back=False):
        self.ring, self.current, self.back = ring, block, back
        self.pieces = [None] * ring.steps
        self.moved = []

    def step(self, *begin, land=()):
        ring, t = self.ring, len(self.moved)
        if begin:
            self.current = after(self.current, *begin)
        if t:
            moved = lax.ppermute(self.current, "seq", ring.behind if self.back else ring.ahead)
            self.current = after(moved, self.moved[-1], *land)
        other = lax.ppermute(self.current, "seq", ring.swap)
        self.pieces[-t if self.back else t] = (self.current, other)
        self.moved.append(other)


class Fold:
    def __init__(self, ring, parts):
        self.ring, self.parts = ring, parts
        self.terms, self.count, self.carried = None, 0, None
        self.step()

    def step(self):
        ring = self.ring
        mine, other = self.parts[ring.steps - 1 - self.count]
        self.count += 1
        sent = None
        if self.terms is not None:
            sent = sum(term.astype(F32) for term in self.terms).astype(BF16)
            self.carried = sent
            other = after(other, sent)
        self.terms = [mine, lax.ppermute(other, "seq", ring.swap)]
        if sent is not None:
            self.terms.append(lax.ppermute(sent, "seq", ring.behind))

    def beside(self, *work):
        self.terms = list(lax.optimization_barrier((tuple(self.terms),) + work)[0])


class Square:
    def __init__(self):
        me = lax.axis_index("dp")
        self.me, self.far, self.near = me, me // 2, me % 2
        self.far_swap = [(j, j ^ 2) for j in range(4)]
        self.near_swap = [(j, j ^ 1) for j in range(4)]

    def near_of(self, block):
        return lax.ppermute(block, "dp", self.near_swap)

    def far_of(self, block):
        return lax.ppermute(block, "dp", self.far_swap)

    def gather(self, block, *begin):
        near, far = self.near_of(block), self.far_of(block)
        far = after(far, *begin) if begin else far
        return (block, near, far, lax.ppermute(far, "dp", self.near_swap))

    def place(self, pieces):
        rows, width = pieces[0].shape

        def kernel(me, *refs):
            for r in range(4):
                begin = pl.multiple_of((me[0] ^ r) * rows, 16)
                refs[4][pl.ds(begin, rows)] = refs[r][...]

        return call(
            kernel,
            struct((4 * rows, width), BF16),
            whole((4 * rows, width)),
            in_blocks=[whole((rows, width))] * 4,
            scalars=self.me[None],
            name="place_rows",
        )(*pieces)

    def half_sum(self, partial):
        parts = partial.reshape((2, 2, partial.shape[0] // 4) + partial.shape[1:])
        mine = lax.dynamic_index_in_dim(parts, self.near, 1, keepdims=False)
        other = lax.dynamic_index_in_dim(parts, 1 - self.near, 1, keepdims=False)
        near = lax.ppermute(other, "dp", self.near_swap)
        return (mine.astype(F32) + near.astype(F32)).astype(BF16)

    def other_sum(self, column):
        mine = lax.dynamic_index_in_dim(column, self.far, 0, keepdims=False)
        other = lax.dynamic_index_in_dim(column, 1 - self.far, 0, keepdims=False)
        return mine.astype(F32) + lax.ppermute(other, "dp", self.far_swap).astype(F32)

    def sum(self, values):
        values = values + lax.ppermute(values, "dp", self.near_swap)
        return values + lax.ppermute(values, "dp", self.far_swap)


def head_tables(count, model_width, window):
    slots = -(-HEADS // count)
    wide = slots * HD
    lists = [[[] for _ in range(count)] for _ in range(count)]
    for column in range(3 * model_width):
        src, local = divmod(column, window)
        part, within = divmod(column, model_width)
        head, lane = divmod(within, HD)
        dst, slot = head % count, head // count
        lists[src][dst].append((local, part * wide + slot * HD + lane))
    most = max(len(entry) for row in lists for entry in row)
    most = -(-most // 64) * 64
    pack = np.full((count, count * most), -1, np.int32)
    unpack = np.full((count, count * most), -1, np.int32)
    for src in range(count):
        for dst in range(count):
            for place, (local, target) in enumerate(lists[src][dst]):
                pack[src, dst * most + place] = local
                unpack[dst, src * most + place] = target
    return pack, unpack, most


def pick_row(table, index):
    return lax.dynamic_index_in_dim(jnp.asarray(table), index, 0, keepdims=False)


def one_hot(rows, size):
    return (lax.broadcasted_iota(jnp.int32, (size, rows.shape[0]), 0) == rows[None, :]).astype(BF16)


def forward_kernel(pos_col, pos_row, query_ref, full_ref, context_ref, probs_ref, *, wide):
    slots, _, run, width = query_ref.shape
    rows = slots * run
    keys_total = full_ref.shape[0] * run
    query = query_ref[:, 0].reshape(rows, width)[:, :wide]
    full = full_ref[:, 0].reshape(keys_total, width)
    key, value = full[:, wide : 2 * wide], full[:, 2 * wide :]
    seen = pos_row[0] <= pos_col[0]
    lane_head = lax.broadcasted_iota(jnp.int32, (1, wide), 1) // HD
    context = jnp.zeros((rows, wide), F32)
    for head in range(wide // HD):
        mine = lane_head == head
        scores = dot_nt(jnp.where(mine, query, jnp.zeros_like(query)), key) * SCORE_SCALE
        scores = jnp.where(seen, scores, MASKED_SCORE)
        top = jnp.max(scores, axis=1, keepdims=True)
        raw = jnp.exp(scores - top)
        probs = (raw * (1.0 / jnp.sum(raw, axis=1, keepdims=True))).astype(BF16)
        probs_ref[0, head] = probs
        context = jnp.where(mine, dot(probs, value), context)
    context_ref[:, 0] = context.astype(BF16).reshape(slots, run, wide)


def backward_kernel(query_ref, full_ref, grad_ref, probs_ref, out_ref, key_sum, value_sum, *, wide):
    step = pl.program_id(1)
    slots, _, run, width = query_ref.shape
    rows = slots * run
    count = full_ref.shape[0]
    keys_total = count * run
    query = query_ref[:, 0].reshape(rows, width)[:, :wide]
    full = full_ref[:, 0].reshape(keys_total, width)
    key, value = full[:, wide : 2 * wide], full[:, 2 * wide :]
    grad = grad_ref[:, 0].reshape(rows, wide)
    lane_head = lax.broadcasted_iota(jnp.int32, (1, wide), 1) // HD

    @pl.when(step == 0)
    def _():
        key_sum[...] = jnp.zeros_like(key_sum)
        value_sum[...] = jnp.zeros_like(value_sum)

    query_grad = jnp.zeros((rows, wide), F32)
    key_grad = jnp.zeros((keys_total, wide), F32)
    value_grad = jnp.zeros((keys_total, wide), F32)
    for head in range(wide // HD):
        mine = lane_head == head
        probs_low = probs_ref[0, head]
        probs = probs_low.astype(F32)
        grad_probs = dot_nt(jnp.where(mine, grad, jnp.zeros_like(grad)), value)
        weighted = probs * grad_probs
        delta = jnp.sum(weighted, axis=1, keepdims=True)
        grad_scores = (weighted - probs * delta).astype(BF16)
        query_grad = jnp.where(mine, dot(grad_scores, key), query_grad)
        key_grad = jnp.where(mine, dot_tn(grad_scores, query), key_grad)
        value_grad = jnp.where(mine, dot_tn(probs_low, grad), value_grad)
    key_sum[...] += key_grad
    value_sum[...] += value_grad
    out_ref[pl.ds(step * slots, slots), 0, :, :wide] = (
        (query_grad * SCORE_SCALE).astype(BF16).reshape(slots, run, wide)
    )

    @pl.when(step == pl.num_programs(1) - 1)
    def _():
        out_ref[:, 0, :, wide : 2 * wide] = (
            (key_sum[...] * SCORE_SCALE).astype(BF16).reshape(count, run, wide)
        )
        out_ref[:, 0, :, 2 * wide :] = value_sum[...].astype(BF16).reshape(count, run, wide)


def attention_forward(qkv_rows, positions):
    count, _, run, width = qkv_rows.shape
    wide = width // 3
    heads = wide // HD
    length = count * run
    block = min(length, 512)
    slots = block // run
    steps = length // block
    by_sequence = positions.reshape(count, SEQS, run).transpose(1, 0, 2).reshape(SEQS, length)
    return pl.pallas_call(
        functools.partial(forward_kernel, wide=wide),
        grid=(SEQS, steps),
        in_specs=[
            pl.BlockSpec((1, block, 1), lambda s, i: (s, i, 0)),
            pl.BlockSpec((1, 1, length), lambda s, i: (s, 0, 0)),
            pl.BlockSpec((slots, 1, run, width), lambda s, i: (i, s, 0, 0)),
            pl.BlockSpec((count, 1, run, width), lambda s, i: (0, s, 0, 0)),
        ],
        out_specs=[
            pl.BlockSpec((slots, 1, run, wide), lambda s, i: (i, s, 0, 0)),
            pl.BlockSpec((1, heads, block, length), lambda s, i: (s, 0, i, 0)),
        ],
        out_shape=[
            jax.ShapeDtypeStruct((count, SEQS, run, wide), BF16),
            jax.ShapeDtypeStruct((SEQS, heads, length, length), BF16),
        ],
        compiler_params=pltpu.CompilerParams(vmem_limit_bytes=60 * 1024 * 1024),
        cost_estimate=LARGE_COST,
        name="attention_forward",
    )(by_sequence[:, :, None], by_sequence[:, None, :], qkv_rows, qkv_rows)


def attention_backward(qkv_rows, grad_context, probs):
    count, _, run, width = qkv_rows.shape
    wide = width // 3
    heads = wide // HD
    length = count * run
    block = min(length, 512)
    slots = block // run
    steps = length // block
    return pl.pallas_call(
        functools.partial(backward_kernel, wide=wide),
        grid=(SEQS, steps),
        in_specs=[
            pl.BlockSpec((slots, 1, run, width), lambda s, i: (i, s, 0, 0)),
            pl.BlockSpec((count, 1, run, width), lambda s, i: (0, s, 0, 0)),
            pl.BlockSpec((slots, 1, run, wide), lambda s, i: (i, s, 0, 0)),
            pl.BlockSpec((1, heads, block, length), lambda s, i: (s, 0, i, 0)),
        ],
        out_specs=pl.BlockSpec((count, 1, run, width), lambda s, i: (0, s, 0, 0)),
        out_shape=jax.ShapeDtypeStruct((count, SEQS, run, width), BF16),
        scratch_shapes=[pltpu.VMEM((length, wide), F32), pltpu.VMEM((length, wide), F32)],
        compiler_params=pltpu.CompilerParams(vmem_limit_bytes=60 * 1024 * 1024),
        cost_estimate=SMALL_COST,
        name="attention_backward",
    )(qkv_rows, qkv_rows, grad_context, probs)


def in_order(side, own, other, axis=0):
    first = jnp.where(side == 0, own, other)
    second = jnp.where(side == 0, other, own)
    return jnp.concatenate([first, second], axis=axis)


def normalize(values):
    centred = values - jnp.mean(values, axis=1, keepdims=True)
    spread = lax.rsqrt(jnp.mean(centred * centred, axis=1, keepdims=True) + NORM_EPS)
    return centred * spread, spread


def normalize_back(normal, spread, gain, grad):
    scaled = grad * gain
    along = jnp.mean(scaled * normal, axis=1, keepdims=True)
    return spread * (scaled - jnp.mean(scaled, axis=1, keepdims=True) - normal * along)


def first_rows(pieces, scalars, weight, gain, shift, bias):
    rows, width = pieces[0][0].shape
    steps = len(pieces)
    total = 2 * steps * rows
    columns = weight.shape[1]

    def kernel(marks, *refs):
        given, (w, g, s, b), outs = refs[: 2 * steps], refs[2 * steps : 2 * steps + 4], refs[-3:]
        for t in range(steps):

            @pl.when(pl.program_id(0) == t)
            def _(t=t):
                outs[0][...] = in_order(marks[0], given[2 * t][...], given[2 * t + 1][...])

        normal, _ = normalize(outs[0][...].astype(F32))
        outs[1][...] = normal.astype(BF16)
        scaled = (normal * g[...] + s[...]).astype(BF16)
        outs[2][...] = (dot(scaled, w[...]) + b[...]).astype(BF16)

    def block(width):
        return pl.BlockSpec((2 * rows, width), lambda t, marks: (marks[1 + t], 0))

    flat = [piece for pair in pieces for piece in pair]
    return call(
        kernel,
        [struct((total, width), BF16), struct((total, width), BF16), struct((total, columns), BF16)],
        [block(width), block(width), block(columns)],
        grid=(steps,),
        in_blocks=[whole((rows, width))] * (2 * steps)
        + [whole(weight.shape), whole((1, width)), whole((1, width)), whole((1, columns))],
        scalars=scalars,
        name="first_rows",
    )(*flat, weight, gain, shift, bias)


def residual_rows(tokens_all, pieces, scalars, weight, bias):
    total, width = tokens_all.shape
    many = len(pieces)
    wide = pieces[0][0].shape[1]
    rows = min(total, 256)

    def kernel(marks, tokens, *refs):
        given, (w, b, out) = refs[: 2 * many], refs[2 * many :]
        value = tokens[...].astype(F32) + b[...]
        for t in range(many):
            pair = in_order(marks[0], given[2 * t][...], given[2 * t + 1][...], axis=1)
            begin = pl.multiple_of(marks[1 + t] * (2 * wide), 2 * wide)
            value += dot(pair, w[pl.ds(begin, 2 * wide)])
        out[...] = value

    def block(width):
        return pl.BlockSpec((rows, width), lambda i, marks: (i, 0))

    return call(
        kernel,
        struct((total, width), F32),
        block(width),
        grid=(total // rows,),
        in_blocks=[block(width)] + [block(wide)] * (2 * many) + [whole(weight.shape), whole((1, width))],
        scalars=scalars,
        name="residual_rows",
    )(tokens_all, *[piece for pair in pieces for piece in pair], weight, bias)


def second_rows(partial, pair, scalars, weight, gain, shift, steps):
    total, width = partial.shape
    wide = pair[0].shape[1]
    own_rows = total // (2 * steps)
    rows = 2 * own_rows

    def kernel(marks, before, first, second, w, g, s, normed, own):
        both = in_order(marks[0], first[...], second[...], axis=1)
        residual = before[...] + dot(both, w[...])
        normal, _ = normalize(residual)
        normed[...] = (normal * g[...] + s[...]).astype(BF16)

        @pl.when(pl.program_id(0) == marks[1])
        def _():
            own[...] = jnp.where(marks[0] == 0, residual[:own_rows], residual[own_rows:])

    def block(width):
        return pl.BlockSpec((rows, width), lambda i, marks: (i, 0))

    return call(
        kernel,
        [struct((total, width), BF16), struct((own_rows, width), F32)],
        [block(width), whole((own_rows, width))],
        grid=(steps,),
        in_blocks=[
            block(width),
            block(wide),
            block(wide),
            pl.BlockSpec((2 * wide, width), lambda i, marks: (marks[steps], 0)),
            whole((1, width)),
            whole((1, width)),
        ],
        scalars=scalars,
        name="second_rows",
    )(partial, *pair, weight, gain, shift)


def hidden_rows(normed, pairs, scalars, w_fc, w_proj, bias, kept, taken, rows):
    total, width = normed.shape
    hidden = w_fc.shape[1]
    many = len(taken)

    def kernel(marks, block, *refs):
        given, (fc, proj, b) = refs[: 2 * many], refs[2 * many : 2 * many + 3]
        act_ref, grad_ref, cot_ref = refs[-3 - 2 * many : -2 * many]
        parts = refs[-2 * many :]
        for i in range(many):

            @pl.when(pl.program_id(0) == i)
            def _(i=i):
                cot_ref[...] = in_order(marks[0], given[2 * i][...], given[2 * i + 1][...])

        z = dot(block[...], fc[...]) + b[...]
        square = z * z
        tanh = jnp.tanh(0.7978845608028654 * (z + 0.044715 * (square * z)))
        half = 0.5 * (1.0 + tanh)
        slope = half + 0.5 * z * (1.0 - tanh * tanh) * (
            0.7978845608028654 + (0.7978845608028654 * 3.0 * 0.044715) * square
        )
        act_ref[...] = (z * half).astype(BF16)
        grad = (dot(cot_ref[...], proj[...]) * slope).astype(BF16)
        grad_ref[...] = grad
        part = dot_nt(grad, fc[...])
        mine = jnp.where(marks[0] == 0, part[:rows], part[rows:])
        other = jnp.where(marks[0] == 0, part[rows:], part[:rows]).astype(BF16)
        for i in range(many):

            @pl.when(pl.program_id(0) == i)
            def _(i=i):
                parts[2 * i][...] = mine
                parts[2 * i + 1][...] = other

    def block(width):
        return pl.BlockSpec((2 * rows, width), lambda i, marks: (marks[1 + i], 0))

    operands = [normed] + [piece for pair in pairs for piece in pair] + [w_fc, w_proj, bias]
    blocks = [block(width)] + [whole((rows, width))] * (2 * many)
    blocks += [whole(w_fc.shape), whole(w_proj.shape), whole((1, hidden))]
    alias = {}
    if kept is not None:
        alias = {1 + len(operands) + i: i for i in range(3)}
        operands += list(kept)
        blocks += [pl.BlockSpec(memory_space=pl.ANY)] * 3
    outs = call(
        kernel,
        [struct((total, hidden), BF16), struct((total, hidden), BF16), struct((total, width), BF16)]
        + [struct((rows, width), dtype) for _ in taken for dtype in (F32, BF16)],
        [block(hidden), block(hidden), block(width)] + [whole((rows, width))] * (2 * many),
        grid=(many,),
        in_blocks=blocks,
        scalars=scalars,
        alias=alias,
        name="hidden_rows",
    )(*operands)
    return outs[:3], {t: (outs[3 + 2 * i], outs[4 + 2 * i]) for i, t in enumerate(taken)}


def turned_product(left, right, name):
    total, width = left.shape
    columns = right.shape[1]
    tile = 256

    def kernel(left_ref, right_ref, out_ref):
        out_ref[...] = dot(left_ref[...].T, right_ref[...]).astype(BF16)

    return call(
        kernel,
        struct((width, columns), BF16),
        pl.BlockSpec((tile, columns), lambda i: (i, 0)),
        grid=(pl.cdiv(width, tile),),
        in_blocks=[pl.BlockSpec((total, tile), lambda i: (0, i)), whole(right.shape)],
        name=name,
    )(left, right)


def head_product(normal, grad, weight, gain, shift):
    total, width = normal.shape
    columns = grad.shape[1]
    tile = 256

    def kernel(left, right, w, g, s, out, gain_sum, shift_sum, grad_sum):
        @pl.when(pl.program_id(0) == 0)
        def _():
            grad_sum[...] = jnp.sum(right[...].astype(F32), axis=0, keepdims=True)

        raw = dot(left[...].T, right[...])
        sums = grad_sum[...]
        low = w[...].astype(F32)
        gain_sum[...] = jnp.sum(raw * low, axis=1, keepdims=True)
        shift_sum[...] = jnp.sum(low * sums, axis=1, keepdims=True)
        out[...] = (raw * g[...] + s[...] * sums).astype(BF16)

    column = pl.BlockSpec((tile, 1), lambda i: (i, 0))
    return call(
        kernel,
        [
            struct((width, columns), BF16),
            struct((width, 1), F32),
            struct((width, 1), F32),
            struct((1, columns), F32),
        ],
        [pl.BlockSpec((tile, columns), lambda i: (i, 0)), column, column, whole((1, columns))],
        grid=(pl.cdiv(width, tile),),
        in_blocks=[
            pl.BlockSpec((total, tile), lambda i: (0, i)),
            whole(grad.shape),
            pl.BlockSpec((tile, columns), lambda i: (i, 0)),
            column,
            column,
        ],
        name="head_product",
    )(normal, grad, weight, gain, shift)


def ring_parts(left, right, scalars, taken, steps, name):
    total, inner = left.shape
    width = right.shape[0]
    rows = total // (2 * steps)

    def kernel(marks, left_ref, right_ref, *outs):
        for i, t in enumerate(taken):
            begin = pl.multiple_of(marks[1 + t] * (2 * rows), 2 * rows)
            part = dot_nt(left_ref[pl.ds(begin, 2 * rows)], right_ref[...])
            outs[2 * i][...] = jnp.where(marks[0] == 0, part[:rows], part[rows:])
            outs[2 * i + 1][...] = jnp.where(marks[0] == 0, part[rows:], part[:rows]).astype(BF16)

    outs = call(
        kernel,
        [struct((rows, width), dtype) for _ in taken for dtype in (F32, BF16)],
        [whole((rows, width))] * (2 * len(taken)),
        in_blocks=[whole(left.shape), whole(right.shape)],
        scalars=scalars,
        name=name,
    )(left, right)
    return {t: (outs[2 * i], outs[2 * i + 1]) for i, t in enumerate(taken)}


def second_back(residual, terms, cotangent, gain, weight, count):
    rows, width = residual.shape
    wide = weight.shape[0] // count
    columns = width // count

    def kernel(
        res, mine, swapped, carried, cot, g, w, grad_ref, low_ref, sums_ref, out_ref, cut_ref
    ):
        @pl.when(pl.program_id(0) == 0)
        def _():
            grad = mine[...] + swapped[...].astype(F32) + carried[...].astype(F32)
            normal, spread = normalize(res[...])
            total = cot[...].astype(F32) + normalize_back(normal, spread, g[...], grad)
            grad_ref[...] = total
            low = total.astype(BF16)
            low_ref[...] = low
            sums_ref[0:1] = jnp.sum(grad * normal, axis=0, keepdims=True)
            sums_ref[1:2] = jnp.sum(grad, axis=0, keepdims=True)
            sums_ref[2:3] = jnp.sum(low.astype(F32), axis=0, keepdims=True)
            sums_ref[3:4] = jnp.sum(cot[...].astype(F32), axis=0, keepdims=True)

        out_ref[0] = dot_nt(low_ref[...], w[...]).astype(BF16)
        for j in range(count):

            @pl.when(pl.program_id(0) == j)
            def _(j=j):
                cut_ref[0] = low_ref[:, j * columns : (j + 1) * columns]

    row = whole((rows, width))
    return call(
        kernel,
        [
            struct((rows, width), F32),
            struct((rows, width), BF16),
            struct((4, width), F32),
            struct((count, rows, wide), BF16),
            struct((count, rows, columns), BF16),
        ],
        [
            row,
            row,
            whole((4, width)),
            pl.BlockSpec((1, rows, wide), lambda i: (i, 0, 0)),
            pl.BlockSpec((1, rows, columns), lambda i: (i, 0, 0)),
        ],
        grid=(count,),
        in_blocks=[row] * 5 + [whole((1, width)), pl.BlockSpec((wide, width), lambda i: (i, 0))],
        name="second_back",
    )(residual, *terms, cotangent, gain, weight)


def first_back(tokens, terms, residual_grad, gain):
    rows, width = tokens.shape

    def kernel(x, mine, swapped, carried, res, g, out_ref):
        grad = mine[...] + swapped[...].astype(F32) + carried[...].astype(F32)
        normal, spread = normalize(x[...].astype(F32))
        out_ref[...] = (res[...] + normalize_back(normal, spread, g[...], grad)).astype(BF16)

    row = whole((rows, width))
    return call(
        kernel,
        struct((rows, width), BF16),
        row,
        in_blocks=[row] * 5 + [whole((1, width))],
        name="first_back",
    )(tokens, *terms, residual_grad, gain)


def heads_rows(me, pieces, count, slots):
    rows, width = pieces[0].shape
    unit = math.gcd(rows, HD)

    def kernel(mark, *refs):
        out = refs[4]
        for h in range(HEADS, count * slots):
            place = ((h % count) * slots + h // count) * HD
            out[place : place + HD] = jnp.zeros((HD, width), BF16)
        for r in range(4):
            for piece in range(rows // unit):
                row = (mark[0] ^ r) * rows + piece * unit
                head = row // HD
                target = ((head % count) * slots + head // count) * HD + row % HD
                out[pl.ds(pl.multiple_of(target, unit), unit)] = refs[r][
                    piece * unit : (piece + 1) * unit
                ]

    return call(
        kernel,
        struct((count * slots * HD, width), BF16),
        whole((count * slots * HD, width)),
        in_blocks=[whole((rows, width))] * 4,
        scalars=me[None],
        name="heads_rows",
    )(*pieces)


def out_product(pieces, columns, scalars, count, slots):
    total, width = columns.shape
    wide = slots * HD
    steps = len(pieces)

    def kernel(marks, *refs):
        given, right, out = refs[: 2 * steps], refs[2 * steps], refs[-1]
        for t in range(steps):
            for b in range(2):
                owner = marks[1 + t] * 2 + (marks[0] if b == 0 else 1 - marks[0])
                value = dot_tn(given[2 * t + b][...], right[...]).astype(BF16)
                for slot in range(slots):
                    head = slot * count + owner

                    @pl.when(head < HEADS)
                    def _(slot=slot, head=head, value=value):
                        begin = pl.multiple_of(head * HD, HD)
                        out[pl.ds(begin, HD)] = value[slot * HD : (slot + 1) * HD]

    return call(
        kernel,
        struct((HEADS * HD, width), BF16),
        whole((HEADS * HD, width)),
        in_blocks=[whole((total, wide))] * (2 * steps) + [whole(columns.shape)],
        scalars=scalars,
        name="out_product",
    )(*[piece for pair in pieces for piece in pair], columns)


def rows_product(left, right, name):
    total, inner = left.shape
    width = right.shape[0]
    block = min(total, 512)

    def kernel(left_ref, right_ref, out_ref):
        out_ref[...] = dot_nt(left_ref[...], right_ref[...]).astype(BF16)

    return call(
        kernel,
        struct((total, width), BF16),
        pl.BlockSpec((block, width), lambda i: (i, 0)),
        grid=(total // block,),
        in_blocks=[pl.BlockSpec((block, inner), lambda i: (i, 0)), whole(right.shape)],
        name=name,
    )(left, right)


def shards(
    tokens,
    cotangent,
    positions,
    qkv_weight,
    qkv_first,
    qkv_second,
    out_weight,
    out_first,
    out_second,
    fc_weight,
    fc_first,
    fc_second,
    proj_weight,
    proj_first,
    proj_second,
    small_weight,
    small_first,
    small_second,
):
    count = lax.axis_size("seq")
    ring = Ring(count)
    square = Square()
    me = lax.axis_index("seq")
    rows, width = tokens.shape
    seq_rows = rows // SEQS
    window = qkv_weight.shape[1]
    slots = -(-HEADS // count)
    wide = slots * HD
    small_count, small_width = small_weight.shape
    hidden = fc_weight.shape[1]
    all_rows = count * rows
    steps = ring.steps
    marks = jnp.stack([ring.side] + [ring.position(t) for t in range(steps)])
    tokens = by_rows(tokens)
    cotangent = by_rows(cotangent)

    token_tour = Tour(ring, tokens)
    token_tour.step()
    token_tour.step()
    pack, unpack, most = head_tables(count, width, window)
    pack_hot = one_hot(pick_row(pack, me), window)
    packed = jnp.einsum(
        "rc,cdl->drl",
        qkv_weight.astype(BF16),
        pack_hot.reshape(window, count, most),
        preferred_element_type=BF16,
    )
    depth = packed.shape[1]
    small_flat = jnp.concatenate(
        [
            small_weight.reshape(-1).astype(BF16),
            (positions // 32).astype(BF16),
            (positions % 32).astype(BF16),
        ]
    )
    small_depth = -(-small_flat.shape[0] // most)
    small_depth += -small_depth % 16
    small_flat = jnp.pad(small_flat, (0, small_depth * most - small_flat.shape[0]))
    small_pack = jnp.broadcast_to(
        small_flat.reshape(1, small_depth, most), (count, small_depth, most)
    )
    received = lax.all_to_all(jnp.concatenate([packed, small_pack], axis=1), "seq", 0, 0)
    token_tour.step()
    received = after(received, token_tour.moved[1], token_tour.current)

    unpack_hot = one_hot(pick_row(unpack, me), 3 * wide)
    head_part = jnp.einsum(
        "srl,ksl->rk",
        received[:, :depth],
        unpack_hot.reshape(3 * wide, count, most),
        preferred_element_type=BF16,
    )
    for t in range(3, steps):
        token_tour.step()
    head_pieces = square.gather(head_part, token_tour.current)
    w_head = square.place(head_pieces)

    small_all = received[:, depth:].reshape(count, small_depth * most).astype(F32)
    small_rows = small_all[:, : small_count * small_width].reshape(count, small_count, small_width)
    small_rows = small_rows.transpose(1, 0, 2).reshape(small_count, width)
    pos_all = small_all[:, small_count * small_width :][:, : 2 * rows].reshape(count, 2, rows)
    pos_all = (pos_all[:, 0] * 32.0 + pos_all[:, 1]).astype(jnp.int32)

    def own_heads(row):
        padded = jnp.pad(row, (0, slots * count * HD - width)).reshape(slots, count, HD)
        return lax.dynamic_index_in_dim(padded, me, 1, keepdims=False).reshape(wide)

    head_bias = jnp.concatenate(
        [own_heads(small_rows[0]), jnp.zeros((wide,), F32), own_heads(small_rows[1])]
    )
    fc_bias = lax.dynamic_slice_in_dim(small_rows[3:7].reshape(-1), me * hidden, hidden, 0)
    gain_one, shift_one = small_rows[8][None], small_rows[9][None]
    gain_two, shift_two = small_rows[10][None], small_rows[11][None]

    ready = (w_head, token_tour.moved[-1])
    tokens_all, normal_all, qkv_rows = first_rows(
        token_tour.pieces, marks, w_head, gain_one, shift_one, head_bias[None]
    )
    qkv_all = qkv_rows.reshape(count, SEQS, seq_rows, 3 * wide)
    context, probs = attention_forward(qkv_all, pos_all)
    context = context.reshape(all_rows, wide)

    cot_zero = lax.ppermute(after(cotangent, *ready), "seq", ring.swap)
    cot_moving = lax.ppermute(after(cotangent, *ready), "seq", ring.behind)
    out_part = lax.all_gather(out_weight.astype(BF16), "seq", axis=1, tiled=True)
    fc_low = after(fc_weight, *ready).astype(BF16)
    context = after(context, cot_zero, cot_moving)
    out_part = by_rows(after(out_part, context))
    out_near, out_far = square.near_of(out_part), square.far_of(out_part)
    fc_near, fc_far = square.near_of(fc_low), square.far_of(fc_low)
    proj_low = after(proj_weight, context).T.astype(BF16)
    proj_near, proj_far = square.near_of(proj_low), square.far_of(proj_low)
    context_tour = Tour(ring, context)
    context_tour.step()
    context_tour.step(land=(out_part, fc_far, proj_far))
    fc_pieces = (fc_low, fc_near, fc_far, square.near_of(after(fc_far, context_tour.current)))
    proj_pieces = (proj_low, proj_near, proj_far, square.near_of(after(proj_far, context_tour.current)))
    w_fc, w_proj = square.place(fc_pieces), square.place(proj_pieces)
    context_tour.step(land=(w_fc, w_proj))
    for t in range(3, steps):
        context_tour.step(land=(out_far,) if t == 3 else ())
    out_pieces = (out_part, out_near, out_far, square.near_of(after(out_far, context_tour.current)))
    w_out = heads_rows(square.me, out_pieces, count, slots)
    partial = residual_rows(
        tokens_all, context_tour.pieces[:-1], marks, w_out, small_rows[2][None]
    )
    last_pair = after(context_tour.pieces[-1], partial)
    normed_all, residual = second_rows(
        partial, last_pair, marks, w_out, gain_two, shift_two, steps
    )
    cot_moving = [cot_moving]
    for t in range(2, steps):
        begin = context_tour.current if t == 2 else w_out
        moving = lax.ppermute(after(cot_moving[-1], begin), "seq", ring.behind)
        cot_moving.append(after(moving, w_out if t == 2 else partial))
    cot_pieces = {0: (cotangent, cot_zero)}
    for t in range(1, steps):
        crossed = lax.ppermute(after(cot_moving[t - 1], last_pair[1]), "seq", ring.swap)
        cot_pieces[steps - t] = (cot_moving[t - 1], after(crossed, residual))

    def feed_forward(kept, taken, *begin):
        chosen = jnp.stack([ring.side] + [ring.position(t) for t in taken])
        return hidden_rows(
            normed_all,
            [cot_pieces[t] for t in taken],
            after(chosen, *begin) if begin else chosen,
            w_fc,
            w_proj,
            fc_bias[None],
            kept,
            taken,
            rows,
        )

    kept, parts = feed_forward(None, [steps - 1])
    grad_fold = Fold(ring, parts)
    kept, more = feed_forward(kept, [steps - 2])
    parts.update(more)
    grad_fold.beside(*parts[steps - 2])
    grad_fold.step()
    kept, more = feed_forward(kept, list(reversed(range(steps - 2))), grad_fold.carried)
    parts.update(more)
    grad_fold.beside(*parts[0])
    hidden_low, grad_pre_low, cot_all = kept
    grad_fold.step()
    output_partial = rows_product(after(hidden_low, grad_fold.carried), w_proj, "output_product")
    grad_fold.beside(output_partial)
    for _ in range(3, steps):
        grad_fold.step()
    fc_sum = turned_product(after(normed_all, grad_fold.carried), grad_pre_low, "fc_product")
    grad_fold.beside(fc_sum)
    output_sum = lax.psum_scatter(output_partial, "seq", scatter_dimension=0, tiled=True)
    terms = grad_fold.terms
    grad_residual, _, row_sums, grad_sent, attn_cut = second_back(
        residual, terms, cotangent, gain_two, w_out, count
    )
    grad_bias_fc = jnp.sum(after(grad_pre_low, grad_sent).astype(F32), axis=0)
    fc_column = square.half_sum(after(fc_sum, grad_sent))

    proj_sum = turned_product(after(cot_all, grad_sent), hidden_low, "proj_product")
    grad_context = after(lax.all_to_all(grad_sent, "seq", 0, 0), proj_sum, grad_bias_fc)
    proj_column = square.half_sum(after(proj_sum, grad_context))
    attn_columns = lax.all_to_all(after(attn_cut, grad_context), "seq", 0, 0)
    grad_qkv = attention_backward(
        qkv_all, grad_context.reshape(count, SEQS, seq_rows, wide), probs
    ).reshape(all_rows, 3 * wide)
    fc_grad = after(square.other_sum(fc_column), grad_qkv)
    proj_grad = square.other_sum(after(proj_column, grad_qkv))
    attn_columns = after(attn_columns, grad_qkv)
    parts = ring_parts(grad_qkv, w_head, marks, [steps - 1], steps, "first_parts")
    input_fold = Fold(ring, parts)
    parts.update(
        ring_parts(
            after(grad_qkv, *parts[steps - 1]), w_head, marks, range(steps - 1), steps, "input_parts"
        )
    )
    input_fold.beside(*parts[0])
    input_fold.step()
    head_sum, grad_gain_one, grad_shift_one, grad_qkv_sum = head_product(
        after(normal_all, input_fold.carried),
        grad_qkv,
        w_head,
        small_rows[8][:, None],
        small_rows[9][:, None],
    )
    input_fold.beside(head_sum)
    input_fold.step()
    head_column = square.half_sum(after(head_sum, input_fold.carried))
    out_columns = out_weight.shape[1]
    attn_columns = after(attn_columns, input_fold.carried).reshape(all_rows, out_columns)
    input_fold.beside(head_column)
    for _ in range(3, steps):
        input_fold.step()
    small_begin = input_fold.carried
    head_far = square.other_sum(after(head_column, input_fold.carried))
    out_sum = out_product(
        context_tour.pieces, after(attn_columns, input_fold.carried), marks, count, slots
    )
    input_fold.beside(output_sum, out_sum)
    head_grad = after(head_far, *input_fold.terms).astype(BF16)
    unpack_back = unpack_hot.reshape(3 * wide, count, most)
    head_packed = jnp.einsum("rk,ksl->srl", head_grad, unpack_back, preferred_element_type=BF16)
    last_terms = after(tuple(input_fold.terms), head_packed)
    input_grad = first_back(tokens, last_terms, grad_residual, gain_one)
    out_column = square.half_sum(after(out_sum, head_packed))
    out_grad = square.other_sum(out_column)
    fc_new = adam_update(
        fc_weight, fc_first, fc_second, after(fc_grad, head_packed), 0.02, 0.1
    )
    head_back = lax.all_to_all(head_packed, "seq", 0, 0)
    output = (residual + output_sum.astype(F32) + small_rows[7]).astype(BF16)

    def place_heads(values):
        spread = (jnp.arange(count) == me).astype(F32)[None, :, None]
        placed = values.reshape(slots, 1, HD) * spread
        return placed.reshape(-1)[:width]

    grad_bias_fc = grad_bias_fc[None, :] * (jnp.arange(count) == me).astype(F32)[:, None]
    grad_qkv_sum = after(grad_qkv_sum, small_begin)[0]
    grad_small = jnp.concatenate(
        [
            place_heads(grad_qkv_sum[:wide])[None],
            place_heads(grad_qkv_sum[2 * wide :])[None],
            row_sums[2:3],
            grad_bias_fc.reshape(-1, width),
            row_sums[3:4],
            grad_gain_one[:, 0][None],
            grad_shift_one[:, 0][None],
            row_sums[0:1],
            row_sums[1:2],
        ],
        axis=0,
    )
    small_sent = grad_small.astype(BF16).reshape(small_count, count, small_width)
    small_part = jnp.sum(
        lax.all_to_all(small_sent.transpose(1, 0, 2), "seq", 0, 0).astype(F32), axis=0
    )
    small_grad = square.sum(after(small_part, head_packed))

    out_new = adam_update(out_weight, out_first, out_second, out_grad, 0.3, 0.1)
    proj_new = adam_update(
        proj_weight.T, proj_first.T, proj_second.T, proj_grad, 0.02, 0.1
    )
    proj_new = [value.T for value in proj_new]
    small_new = adam_update(small_weight, small_first, small_second, small_grad, 0.3, 0.0)
    head_back = after(head_back, fc_new[0], out_new[0], small_new[0])
    qkv_grad = jnp.einsum(
        "drl,cdl->rc",
        head_back,
        pack_hot.reshape(window, count, most),
        preferred_element_type=F32,
    )
    qkv_new = adam_update(qkv_weight, qkv_first, qkv_second, qkv_grad, 0.02, 0.1)
    return (
        output,
        input_grad,
        *qkv_new,
        *out_new,
        *fc_new,
        *proj_new,
        *small_new,
        small_grad[7],
    )


def solution(mesh):
    rows = P(("dp", "seq"), None)
    matrix = P("dp", "seq")
    turned = P("seq", "dp")
    small = P(None, "seq")
    in_specs = (
        (rows, rows, P(("dp", "seq"))) + (matrix,) * 9 + (turned,) * 3 + (small,) * 3
    )
    out_specs = (rows, rows) + (matrix,) * 9 + (turned,) * 3 + (small,) * 3 + (P("seq"),)
    return jax.shard_map(shards, mesh=mesh, in_specs=in_specs, out_specs=out_specs, check_vma=False)
```

```python
import functools
import math

import jax
import jax.numpy as jnp
import numpy as np
from jax import lax
from jax.experimental import pallas as pl
from jax.experimental.layout import Layout, with_layout_constraint
from jax.experimental.pallas import tpu as pltpu
from jax.sharding import PartitionSpec as P

HEADS = 25
HD = 64
SEQS = 2
STEP = 10

NORM_EPS = 1e-05
SCORE_SCALE = 0.125
MASKED_SCORE = -1e30
BETA_ONE = 0.9
BETA_TWO = 0.95
ADAM_EPS = 1e-08
BF16 = jnp.bfloat16
F32 = jnp.float32
SMALL_COST = pl.CostEstimate(flops=1024, bytes_accessed=1024, transcendentals=0)
LARGE_COST = pl.CostEstimate(flops=8 * 10**9, bytes_accessed=8 * 10**6, transcendentals=0)


def adam_update(weight, first_moment, second, gradient, step_rate, decay_rate):
    moment_new = BETA_ONE * first_moment + (1.0 - BETA_ONE) * gradient
    second_new = BETA_TWO * second + (1.0 - BETA_TWO) * gradient * gradient
    direction = (
        moment_new
        / (1.0 - BETA_ONE**STEP)
        / (jnp.sqrt(second_new / (1.0 - BETA_TWO**STEP)) + ADAM_EPS)
    )
    return (moment_new, second_new, weight - step_rate * (direction + decay_rate * weight))


def dot(left, right):
    return jnp.dot(left, right, preferred_element_type=F32)


def dot_nt(left, right):
    return lax.dot_general(left, right, (((1,), (1,)), ((), ())), preferred_element_type=F32)


def dot_tn(left, right):
    return lax.dot_general(left, right, (((0,), (0,)), ((), ())), preferred_element_type=F32)


def after(value, *others):
    return lax.optimization_barrier((value,) + others)[0]


def by_rows(value):
    return with_layout_constraint(value, Layout(major_to_minor=(0, 1)))


def call(
    kernel, out, blocks, grid=None, in_blocks=None, scalars=None, alias=None, scratch=(), name=None
):
    operands = 0 if scalars is None else 1
    spec = dict(
        in_specs=in_blocks,
        out_specs=blocks,
        grid=grid or (1,),
        scratch_shapes=list(scratch),
    )
    if operands:
        spec = dict(grid_spec=pltpu.PrefetchScalarGridSpec(num_scalar_prefetch=1, **spec))
    run = pl.pallas_call(
        kernel,
        out_shape=out,
        input_output_aliases=alias or {},
        compiler_params=pltpu.CompilerParams(vmem_limit_bytes=60 * 1024 * 1024),
        cost_estimate=SMALL_COST,
        name=name,
        **spec,
    )
    if operands:
        return lambda *given: run(scalars, *given)
    return run


def whole(shape):
    return pl.BlockSpec(shape, lambda *_: (0,) * len(shape))


def struct(shape, dtype):
    return jax.ShapeDtypeStruct(shape, dtype)


class Ring:
    def __init__(self, count):
        self.sides = 2
        self.steps = count // 2
        steps = self.steps
        self.swap = [(j, j ^ 1) for j in range(count)]
        self.ahead = [(z * 2 + x, ((z + 1) % steps) * 2 + x) for z in range(steps) for x in range(2)]
        self.behind = [(dst, src) for src, dst in self.ahead]
        me = lax.axis_index("seq")
        self.place, self.side = me // 2, me % 2

    def position(self, t):
        return (self.place + self.steps - t) % self.steps

    def gather(self, block):
        tour = Tour(self, block)
        for _ in range(self.steps):
            tour.step()
        return tour


class Tour:
    def __init__(self, ring, block, back=False):
        self.ring, self.current, self.back = ring, block, back
        self.pieces = [None] * ring.steps
        self.moved = []

    def step(self, *begin, land=()):
        ring, t = self.ring, len(self.moved)
        if begin:
            self.current = after(self.current, *begin)
        if t:
            moved = lax.ppermute(self.current, "seq", ring.behind if self.back else ring.ahead)
            self.current = after(moved, self.moved[-1], *land)
        other = lax.ppermute(self.current, "seq", ring.swap)
        self.pieces[-t if self.back else t] = (self.current, other)
        self.moved.append(other)


class Fold:
    def __init__(self, ring, parts):
        self.ring, self.parts = ring, parts
        self.terms, self.count, self.carried = None, 0, None
        self.step()

    def step(self):
        ring = self.ring
        mine, other = self.parts[ring.steps - 1 - self.count]
        self.count += 1
        sent = None
        if self.terms is not None:
            sent = sum(term.astype(F32) for term in self.terms).astype(BF16)
            self.carried = sent
            other = after(other, sent)
        self.terms = [mine, lax.ppermute(other, "seq", ring.swap)]
        if sent is not None:
            self.terms.append(lax.ppermute(sent, "seq", ring.behind))

    def beside(self, *work):
        self.terms = list(lax.optimization_barrier((tuple(self.terms),) + work)[0])


class Square:
    def __init__(self):
        me = lax.axis_index("dp")
        self.me, self.far, self.near = me, me // 2, me % 2
        self.far_swap = [(j, j ^ 2) for j in range(4)]
        self.near_swap = [(j, j ^ 1) for j in range(4)]

    def near_of(self, block):
        return lax.ppermute(block, "dp", self.near_swap)

    def far_of(self, block):
        return lax.ppermute(block, "dp", self.far_swap)

    def gather(self, block, *begin):
        near, far = self.near_of(block), self.far_of(block)
        far = after(far, *begin) if begin else far
        return (block, near, far, lax.ppermute(far, "dp", self.near_swap))

    def place(self, pieces):
        rows, width = pieces[0].shape

        def kernel(me, *refs):
            for r in range(4):
                begin = pl.multiple_of((me[0] ^ r) * rows, 16)
                refs[4][pl.ds(begin, rows)] = refs[r][...]

        return call(
            kernel,
            struct((4 * rows, width), BF16),
            whole((4 * rows, width)),
            in_blocks=[whole((rows, width))] * 4,
            scalars=self.me[None],
            name="place_rows",
        )(*pieces)

    def half_sum(self, partial):
        parts = partial.reshape((2, 2, partial.shape[0] // 4) + partial.shape[1:])
        mine = lax.dynamic_index_in_dim(parts, self.near, 1, keepdims=False)
        other = lax.dynamic_index_in_dim(parts, 1 - self.near, 1, keepdims=False)
        near = lax.ppermute(other, "dp", self.near_swap)
        return (mine.astype(F32) + near.astype(F32)).astype(BF16)

    def other_sum(self, column):
        mine = lax.dynamic_index_in_dim(column, self.far, 0, keepdims=False)
        other = lax.dynamic_index_in_dim(column, 1 - self.far, 0, keepdims=False)
        return mine.astype(F32) + lax.ppermute(other, "dp", self.far_swap).astype(F32)

    def sum(self, values):
        values = values + lax.ppermute(values, "dp", self.near_swap)
        return values + lax.ppermute(values, "dp", self.far_swap)


def head_tables(count, model_width, window):
    slots = -(-HEADS // count)
    wide = slots * HD
    lists = [[[] for _ in range(count)] for _ in range(count)]
    for column in range(3 * model_width):
        src, local = divmod(column, window)
        part, within = divmod(column, model_width)
        head, lane = divmod(within, HD)
        dst, slot = head % count, head // count
        lists[src][dst].append((local, part * wide + slot * HD + lane))
    most = max(len(entry) for row in lists for entry in row)
    most = -(-most // 64) * 64
    pack = np.full((count, count * most), -1, np.int32)
    unpack = np.full((count, count * most), -1, np.int32)
    for src in range(count):
        for dst in range(count):
            for place, (local, target) in enumerate(lists[src][dst]):
                pack[src, dst * most + place] = local
                unpack[dst, src * most + place] = target
    return pack, unpack, most


def pick_row(table, index):
    return lax.dynamic_index_in_dim(jnp.asarray(table), index, 0, keepdims=False)


def one_hot(rows, size):
    return (lax.broadcasted_iota(jnp.int32, (size, rows.shape[0]), 0) == rows[None, :]).astype(BF16)


def forward_kernel(pos_col, pos_row, query_ref, full_ref, context_ref, probs_ref, *, wide):
    slots, _, run, width = query_ref.shape
    rows = slots * run
    keys_total = full_ref.shape[0] * run
    query = query_ref[:, 0].reshape(rows, width)[:, :wide]
    full = full_ref[:, 0].reshape(keys_total, width)
    key, value = full[:, wide : 2 * wide], full[:, 2 * wide :]
    seen = pos_row[0] <= pos_col[0]
    lane_head = lax.broadcasted_iota(jnp.int32, (1, wide), 1) // HD
    context = jnp.zeros((rows, wide), F32)
    for head in range(wide // HD):
        mine = lane_head == head
        scores = dot_nt(jnp.where(mine, query, jnp.zeros_like(query)), key) * SCORE_SCALE
        scores = jnp.where(seen, scores, MASKED_SCORE)
        top = jnp.max(scores, axis=1, keepdims=True)
        raw = jnp.exp(scores - top)
        probs = (raw * (1.0 / jnp.sum(raw, axis=1, keepdims=True))).astype(BF16)
        probs_ref[0, head] = probs
        context = jnp.where(mine, dot(probs, value), context)
    context_ref[:, 0] = context.astype(BF16).reshape(slots, run, wide)


def backward_kernel(query_ref, full_ref, grad_ref, probs_ref, out_ref, key_sum, value_sum, *, wide):
    step = pl.program_id(1)
    slots, _, run, width = query_ref.shape
    rows = slots * run
    count = full_ref.shape[0]
    keys_total = count * run
    query = query_ref[:, 0].reshape(rows, width)[:, :wide]
    full = full_ref[:, 0].reshape(keys_total, width)
    key, value = full[:, wide : 2 * wide], full[:, 2 * wide :]
    grad = grad_ref[:, 0].reshape(rows, wide)
    lane_head = lax.broadcasted_iota(jnp.int32, (1, wide), 1) // HD

    @pl.when(step == 0)
    def _():
        key_sum[...] = jnp.zeros_like(key_sum)
        value_sum[...] = jnp.zeros_like(value_sum)

    query_grad = jnp.zeros((rows, wide), F32)
    key_grad = jnp.zeros((keys_total, wide), F32)
    value_grad = jnp.zeros((keys_total, wide), F32)
    for head in range(wide // HD):
        mine = lane_head == head
        probs_low = probs_ref[0, head]
        probs = probs_low.astype(F32)
        grad_probs = dot_nt(jnp.where(mine, grad, jnp.zeros_like(grad)), value)
        weighted = probs * grad_probs
        delta = jnp.sum(weighted, axis=1, keepdims=True)
        grad_scores = (weighted - probs * delta).astype(BF16)
        query_grad = jnp.where(mine, dot(grad_scores, key), query_grad)
        key_grad = jnp.where(mine, dot_tn(grad_scores, query), key_grad)
        value_grad = jnp.where(mine, dot_tn(probs_low, grad), value_grad)
    key_sum[...] += key_grad
    value_sum[...] += value_grad
    out_ref[pl.ds(step * slots, slots), 0, :, :wide] = (
        (query_grad * SCORE_SCALE).astype(BF16).reshape(slots, run, wide)
    )

    @pl.when(step == pl.num_programs(1) - 1)
    def _():
        out_ref[:, 0, :, wide : 2 * wide] = (
            (key_sum[...] * SCORE_SCALE).astype(BF16).reshape(count, run, wide)
        )
        out_ref[:, 0, :, 2 * wide :] = value_sum[...].astype(BF16).reshape(count, run, wide)


def attention_forward(qkv_rows, positions):
    count, _, run, width = qkv_rows.shape
    wide = width // 3
    heads = wide // HD
    length = count * run
    block = min(length, 512)
    slots = block // run
    steps = length // block
    by_sequence = positions.reshape(count, SEQS, run).transpose(1, 0, 2).reshape(SEQS, length)
    return pl.pallas_call(
        functools.partial(forward_kernel, wide=wide),
        grid=(SEQS, steps),
        in_specs=[
            pl.BlockSpec((1, block, 1), lambda s, i: (s, i, 0)),
            pl.BlockSpec((1, 1, length), lambda s, i: (s, 0, 0)),
            pl.BlockSpec((slots, 1, run, width), lambda s, i: (i, s, 0, 0)),
            pl.BlockSpec((count, 1, run, width), lambda s, i: (0, s, 0, 0)),
        ],
        out_specs=[
            pl.BlockSpec((slots, 1, run, wide), lambda s, i: (i, s, 0, 0)),
            pl.BlockSpec((1, heads, block, length), lambda s, i: (s, 0, i, 0)),
        ],
        out_shape=[
            jax.ShapeDtypeStruct((count, SEQS, run, wide), BF16),
            jax.ShapeDtypeStruct((SEQS, heads, length, length), BF16),
        ],
        compiler_params=pltpu.CompilerParams(vmem_limit_bytes=60 * 1024 * 1024),
        cost_estimate=LARGE_COST,
        name="attention_forward",
    )(by_sequence[:, :, None], by_sequence[:, None, :], qkv_rows, qkv_rows)


def attention_backward(qkv_rows, grad_context, probs):
    count, _, run, width = qkv_rows.shape
    wide = width // 3
    heads = wide // HD
    length = count * run
    block = min(length, 512)
    slots = block // run
    steps = length // block
    return pl.pallas_call(
        functools.partial(backward_kernel, wide=wide),
        grid=(SEQS, steps),
        in_specs=[
            pl.BlockSpec((slots, 1, run, width), lambda s, i: (i, s, 0, 0)),
            pl.BlockSpec((count, 1, run, width), lambda s, i: (0, s, 0, 0)),
            pl.BlockSpec((slots, 1, run, wide), lambda s, i: (i, s, 0, 0)),
            pl.BlockSpec((1, heads, block, length), lambda s, i: (s, 0, i, 0)),
        ],
        out_specs=pl.BlockSpec((count, 1, run, width), lambda s, i: (0, s, 0, 0)),
        out_shape=jax.ShapeDtypeStruct((count, SEQS, run, width), BF16),
        scratch_shapes=[pltpu.VMEM((length, wide), F32), pltpu.VMEM((length, wide), F32)],
        compiler_params=pltpu.CompilerParams(vmem_limit_bytes=60 * 1024 * 1024),
        cost_estimate=SMALL_COST,
        name="attention_backward",
    )(qkv_rows, qkv_rows, grad_context, probs)


def in_order(side, own, other, axis=0):
    first = jnp.where(side == 0, own, other)
    second = jnp.where(side == 0, other, own)
    return jnp.concatenate([first, second], axis=axis)


def normalize(values):
    centred = values - jnp.mean(values, axis=1, keepdims=True)
    spread = lax.rsqrt(jnp.mean(centred * centred, axis=1, keepdims=True) + NORM_EPS)
    return centred * spread, spread


def normalize_back(normal, spread, gain, grad):
    scaled = grad * gain
    along = jnp.mean(scaled * normal, axis=1, keepdims=True)
    return spread * (scaled - jnp.mean(scaled, axis=1, keepdims=True) - normal * along)


def first_rows(pieces, scalars, weight, gain, shift, bias):
    rows, width = pieces[0][0].shape
    steps = len(pieces)
    total = 2 * steps * rows
    columns = weight.shape[1]

    def kernel(marks, *refs):
        given, (w, g, s, b), outs = refs[: 2 * steps], refs[2 * steps : 2 * steps + 4], refs[-3:]
        for t in range(steps):

            @pl.when(pl.program_id(0) == t)
            def _(t=t):
                outs[0][...] = in_order(marks[0], given[2 * t][...], given[2 * t + 1][...])

        normal, _ = normalize(outs[0][...].astype(F32))
        outs[1][...] = normal.astype(BF16)
        scaled = (normal * g[...] + s[...]).astype(BF16)
        outs[2][...] = (dot(scaled, w[...]) + b[...]).astype(BF16)

    def block(width):
        return pl.BlockSpec((2 * rows, width), lambda t, marks: (marks[1 + t], 0))

    flat = [piece for pair in pieces for piece in pair]
    return call(
        kernel,
        [struct((total, width), BF16), struct((total, width), BF16), struct((total, columns), BF16)],
        [block(width), block(width), block(columns)],
        grid=(steps,),
        in_blocks=[whole((rows, width))] * (2 * steps)
        + [whole(weight.shape), whole((1, width)), whole((1, width)), whole((1, columns))],
        scalars=scalars,
        name="first_rows",
    )(*flat, weight, gain, shift, bias)


def second_rows(tokens_all, pieces, scalars, weight, bias, gain, shift):
    total, width = tokens_all.shape
    steps = len(pieces)
    wide = pieces[0][0].shape[1]
    own_rows = total // (2 * steps)
    rows = 2 * own_rows
    inside = rows // own_rows

    def kernel(marks, tokens, *refs):
        given = refs[: 2 * steps]
        w, b, g, s, normed, own, context = refs[2 * steps :]
        for t in range(steps):
            pair = in_order(marks[0], given[2 * t][...], given[2 * t + 1][...], axis=1)
            begin = pl.multiple_of(marks[1 + t] * (2 * wide), 2 * wide)
            context[:, pl.ds(begin, 2 * wide)] = pair
        residual = tokens[...].astype(F32) + dot(context[...], w[...]) + b[...]
        normal, _ = normalize(residual)
        normed[...] = (normal * g[...] + s[...]).astype(BF16)
        mine = marks[1] * 2 + marks[0]
        for i in range(inside):

            @pl.when(pl.program_id(0) * inside + i == mine)
            def _(i=i):
                own[...] = residual[i * own_rows : (i + 1) * own_rows]

    return pl.pallas_call(
        kernel,
        grid_spec=pltpu.PrefetchScalarGridSpec(
            num_scalar_prefetch=1,
            grid=(total // rows,),
            in_specs=[pl.BlockSpec((rows, width), lambda i, marks: (i, 0))]
            + [pl.BlockSpec((rows, wide), lambda i, marks: (i, 0))] * (2 * steps)
            + [whole(weight.shape), whole((1, width)), whole((1, width)), whole((1, width))],
            out_specs=[
                pl.BlockSpec((rows, width), lambda i, marks: (i, 0)),
                whole((own_rows, width)),
            ],
            scratch_shapes=[pltpu.VMEM((rows, 2 * steps * wide), BF16)],
        ),
        out_shape=[struct((total, width), BF16), struct((own_rows, width), F32)],
        compiler_params=pltpu.CompilerParams(vmem_limit_bytes=60 * 1024 * 1024),
        cost_estimate=SMALL_COST,
        name="second_rows",
    )(scalars, tokens_all, *[piece for pair in pieces for piece in pair], weight, bias, gain, shift)


def hidden_rows(normed, pairs, scalars, w_fc, w_proj, bias, kept, taken, rows):
    total, width = normed.shape
    hidden = w_fc.shape[1]
    many = len(taken)

    def kernel(marks, block, *refs):
        given, (fc, proj, b) = refs[: 2 * many], refs[2 * many : 2 * many + 3]
        act_ref, grad_ref, cot_ref = refs[-3 - 2 * many : -2 * many]
        parts = refs[-2 * many :]
        for i in range(many):

            @pl.when(pl.program_id(0) == i)
            def _(i=i):
                cot_ref[...] = in_order(marks[0], given[2 * i][...], given[2 * i + 1][...])

        z = dot(block[...], fc[...]) + b[...]
        square = z * z
        tanh = jnp.tanh(0.7978845608028654 * (z + 0.044715 * (square * z)))
        half = 0.5 * (1.0 + tanh)
        slope = half + 0.5 * z * (1.0 - tanh * tanh) * (
            0.7978845608028654 + (0.7978845608028654 * 3.0 * 0.044715) * square
        )
        act_ref[...] = (z * half).astype(BF16)
        grad = (dot(cot_ref[...], proj[...]) * slope).astype(BF16)
        grad_ref[...] = grad
        part = dot_nt(grad, fc[...])
        mine = jnp.where(marks[0] == 0, part[:rows], part[rows:])
        other = jnp.where(marks[0] == 0, part[rows:], part[:rows]).astype(BF16)
        for i in range(many):

            @pl.when(pl.program_id(0) == i)
            def _(i=i):
                parts[2 * i][...] = mine
                parts[2 * i + 1][...] = other

    def block(width):
        return pl.BlockSpec((2 * rows, width), lambda i, marks: (marks[1 + i], 0))

    operands = [normed] + [piece for pair in pairs for piece in pair] + [w_fc, w_proj, bias]
    blocks = [block(width)] + [whole((rows, width))] * (2 * many)
    blocks += [whole(w_fc.shape), whole(w_proj.shape), whole((1, hidden))]
    alias = {}
    if kept is not None:
        alias = {1 + len(operands) + i: i for i in range(3)}
        operands += list(kept)
        blocks += [pl.BlockSpec(memory_space=pl.ANY)] * 3
    outs = call(
        kernel,
        [struct((total, hidden), BF16), struct((total, hidden), BF16), struct((total, width), BF16)]
        + [struct((rows, width), dtype) for _ in taken for dtype in (F32, BF16)],
        [block(hidden), block(hidden), block(width)] + [whole((rows, width))] * (2 * many),
        grid=(many,),
        in_blocks=blocks,
        scalars=scalars,
        alias=alias,
        name="hidden_rows",
    )(*operands)
    return outs[:3], {t: (outs[3 + 2 * i], outs[4 + 2 * i]) for i, t in enumerate(taken)}


def turned_product(left, right, name):
    total, width = left.shape
    columns = right.shape[1]
    tile = 256

    def kernel(left_ref, right_ref, out_ref):
        out_ref[...] = dot(left_ref[...].T, right_ref[...]).astype(BF16)

    return call(
        kernel,
        struct((width, columns), BF16),
        pl.BlockSpec((tile, columns), lambda i: (i, 0)),
        grid=(pl.cdiv(width, tile),),
        in_blocks=[pl.BlockSpec((total, tile), lambda i: (0, i)), whole(right.shape)],
        name=name,
    )(left, right)


def head_product(normal, grad, weight, gain, shift):
    total, width = normal.shape
    columns = grad.shape[1]
    tile = 256

    def kernel(left, right, w, g, s, out, gain_sum, shift_sum, grad_sum):
        @pl.when(pl.program_id(0) == 0)
        def _():
            grad_sum[...] = jnp.sum(right[...].astype(F32), axis=0, keepdims=True)

        raw = dot(left[...].T, right[...])
        sums = grad_sum[...]
        low = w[...].astype(F32)
        gain_sum[...] = jnp.sum(raw * low, axis=1, keepdims=True)
        shift_sum[...] = jnp.sum(low * sums, axis=1, keepdims=True)
        out[...] = (raw * g[...] + s[...] * sums).astype(BF16)

    column = pl.BlockSpec((tile, 1), lambda i: (i, 0))
    return call(
        kernel,
        [
            struct((width, columns), BF16),
            struct((width, 1), F32),
            struct((width, 1), F32),
            struct((1, columns), F32),
        ],
        [pl.BlockSpec((tile, columns), lambda i: (i, 0)), column, column, whole((1, columns))],
        grid=(pl.cdiv(width, tile),),
        in_blocks=[
            pl.BlockSpec((total, tile), lambda i: (0, i)),
            whole(grad.shape),
            pl.BlockSpec((tile, columns), lambda i: (i, 0)),
            column,
            column,
        ],
        name="head_product",
    )(normal, grad, weight, gain, shift)


def ring_parts(left, right, scalars, taken, steps, name):
    total, inner = left.shape
    width = right.shape[0]
    rows = total // (2 * steps)

    def kernel(marks, left_ref, right_ref, *outs):
        for i, t in enumerate(taken):
            begin = pl.multiple_of(marks[1 + t] * (2 * rows), 2 * rows)
            part = dot_nt(left_ref[pl.ds(begin, 2 * rows)], right_ref[...])
            outs[2 * i][...] = jnp.where(marks[0] == 0, part[:rows], part[rows:])
            outs[2 * i + 1][...] = jnp.where(marks[0] == 0, part[rows:], part[:rows]).astype(BF16)

    outs = call(
        kernel,
        [struct((rows, width), dtype) for _ in taken for dtype in (F32, BF16)],
        [whole((rows, width))] * (2 * len(taken)),
        in_blocks=[whole(left.shape), whole(right.shape)],
        scalars=scalars,
        name=name,
    )(left, right)
    return {t: (outs[2 * i], outs[2 * i + 1]) for i, t in enumerate(taken)}


def second_back(residual, terms, cotangent, gain, weight, count):
    rows, width = residual.shape
    wide = weight.shape[0] // count
    columns = width // count

    def kernel(
        res, mine, swapped, carried, cot, g, w, grad_ref, low_ref, sums_ref, out_ref, cut_ref
    ):
        @pl.when(pl.program_id(0) == 0)
        def _():
            grad = mine[...] + swapped[...].astype(F32) + carried[...].astype(F32)
            normal, spread = normalize(res[...])
            total = cot[...].astype(F32) + normalize_back(normal, spread, g[...], grad)
            grad_ref[...] = total
            low = total.astype(BF16)
            low_ref[...] = low
            sums_ref[0:1] = jnp.sum(grad * normal, axis=0, keepdims=True)
            sums_ref[1:2] = jnp.sum(grad, axis=0, keepdims=True)
            sums_ref[2:3] = jnp.sum(low.astype(F32), axis=0, keepdims=True)
            sums_ref[3:4] = jnp.sum(cot[...].astype(F32), axis=0, keepdims=True)

        out_ref[0] = dot_nt(low_ref[...], w[...]).astype(BF16)
        for j in range(count):

            @pl.when(pl.program_id(0) == j)
            def _(j=j):
                cut_ref[0] = low_ref[:, j * columns : (j + 1) * columns]

    row = whole((rows, width))
    return call(
        kernel,
        [
            struct((rows, width), F32),
            struct((rows, width), BF16),
            struct((4, width), F32),
            struct((count, rows, wide), BF16),
            struct((count, rows, columns), BF16),
        ],
        [
            row,
            row,
            whole((4, width)),
            pl.BlockSpec((1, rows, wide), lambda i: (i, 0, 0)),
            pl.BlockSpec((1, rows, columns), lambda i: (i, 0, 0)),
        ],
        grid=(count,),
        in_blocks=[row] * 5 + [whole((1, width)), pl.BlockSpec((wide, width), lambda i: (i, 0))],
        name="second_back",
    )(residual, *terms, cotangent, gain, weight)


def first_back(tokens, terms, residual_grad, gain):
    rows, width = tokens.shape

    def kernel(x, mine, swapped, carried, res, g, out_ref):
        grad = mine[...] + swapped[...].astype(F32) + carried[...].astype(F32)
        normal, spread = normalize(x[...].astype(F32))
        out_ref[...] = (res[...] + normalize_back(normal, spread, g[...], grad)).astype(BF16)

    row = whole((rows, width))
    return call(
        kernel,
        struct((rows, width), BF16),
        row,
        in_blocks=[row] * 5 + [whole((1, width))],
        name="first_back",
    )(tokens, *terms, residual_grad, gain)


def heads_rows(me, pieces, count, slots):
    rows, width = pieces[0].shape
    unit = math.gcd(rows, HD)

    def kernel(mark, *refs):
        out = refs[4]
        for h in range(HEADS, count * slots):
            place = ((h % count) * slots + h // count) * HD
            out[place : place + HD] = jnp.zeros((HD, width), BF16)
        for r in range(4):
            for piece in range(rows // unit):
                row = (mark[0] ^ r) * rows + piece * unit
                head = row // HD
                target = ((head % count) * slots + head // count) * HD + row % HD
                out[pl.ds(pl.multiple_of(target, unit), unit)] = refs[r][
                    piece * unit : (piece + 1) * unit
                ]

    return call(
        kernel,
        struct((count * slots * HD, width), BF16),
        whole((count * slots * HD, width)),
        in_blocks=[whole((rows, width))] * 4,
        scalars=me[None],
        name="heads_rows",
    )(*pieces)


def out_product(pieces, columns, scalars, count, slots):
    total, width = columns.shape
    wide = slots * HD
    steps = len(pieces)

    def kernel(marks, *refs):
        given, right, out = refs[: 2 * steps], refs[2 * steps], refs[-1]
        for t in range(steps):
            for b in range(2):
                owner = marks[1 + t] * 2 + (marks[0] if b == 0 else 1 - marks[0])
                value = dot_tn(given[2 * t + b][...], right[...]).astype(BF16)
                for slot in range(slots):
                    head = slot * count + owner

                    @pl.when(head < HEADS)
                    def _(slot=slot, head=head, value=value):
                        begin = pl.multiple_of(head * HD, HD)
                        out[pl.ds(begin, HD)] = value[slot * HD : (slot + 1) * HD]

    return call(
        kernel,
        struct((HEADS * HD, width), BF16),
        whole((HEADS * HD, width)),
        in_blocks=[whole((total, wide))] * (2 * steps) + [whole(columns.shape)],
        scalars=scalars,
        name="out_product",
    )(*[piece for pair in pieces for piece in pair], columns)


def rows_product(left, right, name):
    total, inner = left.shape
    width = right.shape[0]
    block = min(total, 512)

    def kernel(left_ref, right_ref, out_ref):
        out_ref[...] = dot_nt(left_ref[...], right_ref[...]).astype(BF16)

    return call(
        kernel,
        struct((total, width), BF16),
        pl.BlockSpec((block, width), lambda i: (i, 0)),
        grid=(total // block,),
        in_blocks=[pl.BlockSpec((block, inner), lambda i: (i, 0)), whole(right.shape)],
        name=name,
    )(left, right)


def shards(
    tokens,
    cotangent,
    positions,
    qkv_weight,
    qkv_first,
    qkv_second,
    out_weight,
    out_first,
    out_second,
    fc_weight,
    fc_first,
    fc_second,
    proj_weight,
    proj_first,
    proj_second,
    small_weight,
    small_first,
    small_second,
):
    count = lax.axis_size("seq")
    ring = Ring(count)
    square = Square()
    me = lax.axis_index("seq")
    rows, width = tokens.shape
    seq_rows = rows // SEQS
    window = qkv_weight.shape[1]
    slots = -(-HEADS // count)
    wide = slots * HD
    small_count, small_width = small_weight.shape
    hidden = fc_weight.shape[1]
    all_rows = count * rows
    steps = ring.steps
    marks = jnp.stack([ring.side] + [ring.position(t) for t in range(steps)])
    tokens = by_rows(tokens)
    cotangent = by_rows(cotangent)

    token_tour = Tour(ring, tokens)
    token_tour.step()
    token_tour.step()
    pack, unpack, most = head_tables(count, width, window)
    pack_hot = one_hot(pick_row(pack, me), window)
    packed = jnp.einsum(
        "rc,cdl->drl",
        qkv_weight.astype(BF16),
        pack_hot.reshape(window, count, most),
        preferred_element_type=BF16,
    )
    depth = packed.shape[1]
    small_flat = jnp.concatenate(
        [
            small_weight.reshape(-1).astype(BF16),
            (positions // 32).astype(BF16),
            (positions % 32).astype(BF16),
        ]
    )
    small_depth = -(-small_flat.shape[0] // most)
    small_depth += -small_depth % 16
    small_flat = jnp.pad(small_flat, (0, small_depth * most - small_flat.shape[0]))
    small_pack = jnp.broadcast_to(
        small_flat.reshape(1, small_depth, most), (count, small_depth, most)
    )
    received = lax.all_to_all(jnp.concatenate([packed, small_pack], axis=1), "seq", 0, 0)
    token_tour.step()
    received = after(received, token_tour.moved[1], token_tour.current)

    unpack_hot = one_hot(pick_row(unpack, me), 3 * wide)
    head_part = jnp.einsum(
        "srl,ksl->rk",
        received[:, :depth],
        unpack_hot.reshape(3 * wide, count, most),
        preferred_element_type=BF16,
    )
    for t in range(3, steps):
        token_tour.step()
    head_pieces = square.gather(head_part, token_tour.current)
    w_head = square.place(head_pieces)

    small_all = received[:, depth:].reshape(count, small_depth * most).astype(F32)
    small_rows = small_all[:, : small_count * small_width].reshape(count, small_count, small_width)
    small_rows = small_rows.transpose(1, 0, 2).reshape(small_count, width)
    pos_all = small_all[:, small_count * small_width :][:, : 2 * rows].reshape(count, 2, rows)
    pos_all = (pos_all[:, 0] * 32.0 + pos_all[:, 1]).astype(jnp.int32)

    def own_heads(row):
        padded = jnp.pad(row, (0, slots * count * HD - width)).reshape(slots, count, HD)
        return lax.dynamic_index_in_dim(padded, me, 1, keepdims=False).reshape(wide)

    head_bias = jnp.concatenate(
        [own_heads(small_rows[0]), jnp.zeros((wide,), F32), own_heads(small_rows[1])]
    )
    fc_bias = lax.dynamic_slice_in_dim(small_rows[3:7].reshape(-1), me * hidden, hidden, 0)
    gain_one, shift_one = small_rows[8][None], small_rows[9][None]
    gain_two, shift_two = small_rows[10][None], small_rows[11][None]

    ready = (w_head, token_tour.moved[-1])
    tokens_all, normal_all, qkv_rows = first_rows(
        token_tour.pieces, marks, w_head, gain_one, shift_one, head_bias[None]
    )
    qkv_all = qkv_rows.reshape(count, SEQS, seq_rows, 3 * wide)
    context, probs = attention_forward(qkv_all, pos_all)
    context = context.reshape(all_rows, wide)

    cot_zero = lax.ppermute(after(cotangent, *ready), "seq", ring.swap)
    cot_moving = lax.ppermute(after(cotangent, *ready), "seq", ring.behind)
    out_part = lax.all_gather(out_weight.astype(BF16), "seq", axis=1, tiled=True)
    fc_low = after(fc_weight, *ready).astype(BF16)
    context = after(context, cot_zero, cot_moving)
    out_part = by_rows(after(out_part, context))
    out_near, out_far = square.near_of(out_part), square.far_of(out_part)
    fc_near, fc_far = square.near_of(fc_low), square.far_of(fc_low)
    proj_low = after(proj_weight, context).T.astype(BF16)
    proj_near, proj_far = square.near_of(proj_low), square.far_of(proj_low)
    context_tour = Tour(ring, context)
    context_tour.step()
    context_tour.step(land=(out_part, fc_far, proj_far))
    fc_pieces = (fc_low, fc_near, fc_far, square.near_of(after(fc_far, context_tour.current)))
    proj_pieces = (proj_low, proj_near, proj_far, square.near_of(after(proj_far, context_tour.current)))
    w_fc, w_proj = square.place(fc_pieces), square.place(proj_pieces)
    context_tour.step(land=(w_fc, w_proj))
    for t in range(3, steps):
        context_tour.step(land=(out_far,) if t == 3 else ())
    out_pieces = (out_part, out_near, out_far, square.near_of(after(out_far, context_tour.current)))
    w_out = heads_rows(square.me, out_pieces, count, slots)
    normed_all, residual = second_rows(
        tokens_all, context_tour.pieces, marks, w_out, small_rows[2][None], gain_two, shift_two
    )
    cot_moving = [cot_moving]
    for t in range(2, steps):
        begin = context_tour.current if t == 2 else w_out
        moving = lax.ppermute(after(cot_moving[-1], begin), "seq", ring.behind)
        cot_moving.append(after(moving, w_out if t == 2 else residual))
    cot_pieces = {0: (cotangent, cot_zero)}
    crossing = after(context_tour.moved[-1], w_out)
    for t in range(1, steps):
        crossed = lax.ppermute(after(cot_moving[t - 1], crossing), "seq", ring.swap)
        cot_pieces[steps - t] = (cot_moving[t - 1], after(crossed, residual))

    def feed_forward(kept, taken, *begin):
        chosen = jnp.stack([ring.side] + [ring.position(t) for t in taken])
        return hidden_rows(
            normed_all,
            [cot_pieces[t] for t in taken],
            after(chosen, *begin) if begin else chosen,
            w_fc,
            w_proj,
            fc_bias[None],
            kept,
            taken,
            rows,
        )

    kept, parts = feed_forward(None, [steps - 1])
    grad_fold = Fold(ring, parts)
    kept, more = feed_forward(kept, [steps - 2])
    parts.update(more)
    grad_fold.beside(*parts[steps - 2])
    grad_fold.step()
    kept, more = feed_forward(kept, list(reversed(range(steps - 2))), grad_fold.carried)
    parts.update(more)
    grad_fold.beside(*parts[0])
    hidden_low, grad_pre_low, cot_all = kept
    grad_fold.step()
    output_partial = rows_product(after(hidden_low, grad_fold.carried), w_proj, "output_product")
    grad_fold.beside(output_partial)
    for _ in range(3, steps):
        grad_fold.step()
    fc_sum = turned_product(after(normed_all, grad_fold.carried), grad_pre_low, "fc_product")
    grad_fold.beside(fc_sum)
    output_sum = lax.psum_scatter(output_partial, "seq", scatter_dimension=0, tiled=True)
    terms = grad_fold.terms
    grad_residual, _, row_sums, grad_sent, attn_cut = second_back(
        residual, terms, cotangent, gain_two, w_out, count
    )
    grad_bias_fc = jnp.sum(after(grad_pre_low, grad_sent).astype(F32), axis=0)
    fc_column = square.half_sum(after(fc_sum, grad_sent))

    proj_sum = turned_product(after(cot_all, grad_sent), hidden_low, "proj_product")
    gain_column, shift_column = after((small_rows[8][:, None], small_rows[9][:, None]), grad_sent)
    grad_context = after(
        lax.all_to_all(grad_sent, "seq", 0, 0),
        proj_sum,
        grad_bias_fc,
        gain_column,
        shift_column,
    )
    proj_column = square.half_sum(proj_sum)
    attn_columns = lax.all_to_all(after(attn_cut, grad_context), "seq", 0, 0)
    grad_qkv = attention_backward(
        qkv_all, grad_context.reshape(count, SEQS, seq_rows, wide), probs
    ).reshape(all_rows, 3 * wide)
    fc_grad = after(square.other_sum(fc_column), grad_qkv)
    proj_grad = square.other_sum(after(proj_column, grad_qkv))
    attn_columns = after(attn_columns, grad_qkv)
    parts = ring_parts(grad_qkv, w_head, marks, [steps - 1], steps, "first_parts")
    input_fold = Fold(ring, parts)
    parts.update(
        ring_parts(
            after(grad_qkv, *parts[steps - 1]), w_head, marks, range(steps - 1), steps, "input_parts"
        )
    )
    input_fold.beside(*parts[0])
    input_fold.step()
    head_sum, grad_gain_one, grad_shift_one, grad_qkv_sum = head_product(
        after(normal_all, input_fold.carried),
        grad_qkv,
        w_head,
        gain_column,
        shift_column,
    )
    input_fold.beside(head_sum)
    input_fold.step()
    head_column = square.half_sum(after(head_sum, input_fold.carried))
    out_columns = out_weight.shape[1]
    attn_columns = after(attn_columns, input_fold.carried).reshape(all_rows, out_columns)
    input_fold.beside(head_column)
    for _ in range(3, steps):
        input_fold.step()
    small_begin = input_fold.carried
    head_far = square.other_sum(after(head_column, input_fold.carried))
    out_sum = out_product(
        context_tour.pieces, after(attn_columns, input_fold.carried), marks, count, slots
    )
    input_fold.beside(output_sum, out_sum)
    head_grad = after(head_far, *input_fold.terms).astype(BF16)
    unpack_back = unpack_hot.reshape(3 * wide, count, most)
    head_packed = jnp.einsum("rk,ksl->srl", head_grad, unpack_back, preferred_element_type=BF16)
    last_terms = after(tuple(input_fold.terms), head_packed)
    input_grad = first_back(tokens, last_terms, grad_residual, gain_one)
    out_column = square.half_sum(after(out_sum, head_packed))
    out_grad = square.other_sum(out_column)
    fc_new = adam_update(
        fc_weight, fc_first, fc_second, after(fc_grad, head_packed), 0.02, 0.1
    )
    head_back = lax.all_to_all(head_packed, "seq", 0, 0)
    output = (residual + output_sum.astype(F32) + small_rows[7]).astype(BF16)

    def place_heads(values):
        spread = (jnp.arange(count) == me).astype(F32)[None, :, None]
        placed = values.reshape(slots, 1, HD) * spread
        return placed.reshape(-1)[:width]

    grad_bias_fc = grad_bias_fc[None, :] * (jnp.arange(count) == me).astype(F32)[:, None]
    grad_qkv_sum = after(grad_qkv_sum, small_begin)[0]
    grad_small = jnp.concatenate(
        [
            place_heads(grad_qkv_sum[:wide])[None],
            place_heads(grad_qkv_sum[2 * wide :])[None],
            row_sums[2:3],
            grad_bias_fc.reshape(-1, width),
            row_sums[3:4],
            grad_gain_one[:, 0][None],
            grad_shift_one[:, 0][None],
            row_sums[0:1],
            row_sums[1:2],
        ],
        axis=0,
    )
    small_sent = grad_small.astype(BF16).reshape(small_count, count, small_width)
    small_part = jnp.sum(
        lax.all_to_all(small_sent.transpose(1, 0, 2), "seq", 0, 0).astype(F32), axis=0
    )
    small_grad = square.sum(after(small_part, head_packed))

    out_new = adam_update(out_weight, out_first, out_second, out_grad, 0.3, 0.1)
    proj_new = adam_update(
        proj_weight.T, proj_first.T, proj_second.T, proj_grad, 0.02, 0.1
    )
    proj_new = [value.T for value in proj_new]
    small_new = adam_update(small_weight, small_first, small_second, small_grad, 0.3, 0.0)
    head_back = after(head_back, fc_new[0], out_new[0], small_new[0])
    qkv_grad = jnp.einsum(
        "drl,cdl->rc",
        head_back,
        pack_hot.reshape(window, count, most),
        preferred_element_type=F32,
    )
    qkv_new = adam_update(qkv_weight, qkv_first, qkv_second, qkv_grad, 0.02, 0.1)
    return (
        output,
        input_grad,
        *qkv_new,
        *out_new,
        *fc_new,
        *proj_new,
        *small_new,
        small_grad[7],
    )


def solution(mesh):
    rows = P(("dp", "seq"), None)
    matrix = P("dp", "seq")
    turned = P("seq", "dp")
    small = P(None, "seq")
    in_specs = (
        (rows, rows, P(("dp", "seq"))) + (matrix,) * 9 + (turned,) * 3 + (small,) * 3
    )
    out_specs = (rows, rows) + (matrix,) * 9 + (turned,) * 3 + (small,) * 3 + (P("seq"),)
    return jax.shard_map(shards, mesh=mesh, in_specs=in_specs, out_specs=out_specs, check_vma=False)
```

```python
import functools
import math

import jax
import jax.numpy as jnp
import numpy as np
from jax import lax
from jax.experimental import pallas as pl
from jax.experimental.layout import Layout, with_layout_constraint
from jax.experimental.pallas import tpu as pltpu
from jax.sharding import PartitionSpec as P

HEADS = 25
HD = 64
SEQS = 2
STEP = 10

NORM_EPS = 1e-05
SCORE_SCALE = 0.125
MASKED_SCORE = -1e30
BETA_ONE = 0.9
BETA_TWO = 0.95
ADAM_EPS = 1e-08
BF16 = jnp.bfloat16
F32 = jnp.float32
SMALL_COST = pl.CostEstimate(flops=1024, bytes_accessed=1024, transcendentals=0)
LARGE_COST = pl.CostEstimate(flops=8 * 10**9, bytes_accessed=8 * 10**6, transcendentals=0)


def adam_update(weight, first_moment, second, gradient, step_rate, decay_rate):
    moment_new = BETA_ONE * first_moment + (1.0 - BETA_ONE) * gradient
    second_new = BETA_TWO * second + (1.0 - BETA_TWO) * gradient * gradient
    direction = (
        moment_new
        / (1.0 - BETA_ONE**STEP)
        / (jnp.sqrt(second_new / (1.0 - BETA_TWO**STEP)) + ADAM_EPS)
    )
    return (moment_new, second_new, weight - step_rate * (direction + decay_rate * weight))


def dot(left, right):
    return jnp.dot(left, right, preferred_element_type=F32)


def dot_nt(left, right):
    return lax.dot_general(left, right, (((1,), (1,)), ((), ())), preferred_element_type=F32)


def dot_tn(left, right):
    return lax.dot_general(left, right, (((0,), (0,)), ((), ())), preferred_element_type=F32)


def after(value, *others):
    return lax.optimization_barrier((value,) + others)[0]


def by_rows(value):
    return with_layout_constraint(value, Layout(major_to_minor=(0, 1)))


def call(
    kernel, out, blocks, grid=None, in_blocks=None, scalars=None, alias=None, scratch=(), name=None
):
    operands = 0 if scalars is None else 1
    spec = dict(
        in_specs=in_blocks,
        out_specs=blocks,
        grid=grid or (1,),
        scratch_shapes=list(scratch),
    )
    if operands:
        spec = dict(grid_spec=pltpu.PrefetchScalarGridSpec(num_scalar_prefetch=1, **spec))
    run = pl.pallas_call(
        kernel,
        out_shape=out,
        input_output_aliases=alias or {},
        compiler_params=pltpu.CompilerParams(vmem_limit_bytes=60 * 1024 * 1024),
        cost_estimate=SMALL_COST,
        name=name,
        **spec,
    )
    if operands:
        return lambda *given: run(scalars, *given)
    return run


def whole(shape):
    return pl.BlockSpec(shape, lambda *_: (0,) * len(shape))


def struct(shape, dtype):
    return jax.ShapeDtypeStruct(shape, dtype)


class Ring:
    def __init__(self, count):
        self.sides = 2
        self.steps = count // 2
        steps = self.steps
        self.swap = [(j, j ^ 1) for j in range(count)]
        self.ahead = [(z * 2 + x, ((z + 1) % steps) * 2 + x) for z in range(steps) for x in range(2)]
        self.behind = [(dst, src) for src, dst in self.ahead]
        me = lax.axis_index("seq")
        self.place, self.side = me // 2, me % 2

    def position(self, t):
        return (self.place + self.steps - t) % self.steps

    def gather(self, block):
        tour = Tour(self, block)
        for _ in range(self.steps):
            tour.step()
        return tour


class Tour:
    def __init__(self, ring, block, back=False):
        self.ring, self.current, self.back = ring, block, back
        self.pieces = [None] * ring.steps
        self.moved = []

    def step(self, *begin, land=()):
        ring, t = self.ring, len(self.moved)
        if begin:
            self.current = after(self.current, *begin)
        if t:
            moved = lax.ppermute(self.current, "seq", ring.behind if self.back else ring.ahead)
            self.current = after(moved, self.moved[-1], *land)
        other = lax.ppermute(self.current, "seq", ring.swap)
        self.pieces[-t if self.back else t] = (self.current, other)
        self.moved.append(other)


class Fold:
    def __init__(self, ring, parts):
        self.ring, self.parts = ring, parts
        self.terms, self.count, self.carried = None, 0, None
        self.step()

    def step(self):
        ring = self.ring
        mine, other = self.parts[ring.steps - 1 - self.count]
        self.count += 1
        sent = None
        if self.terms is not None:
            sent = sum(term.astype(F32) for term in self.terms).astype(BF16)
            self.carried = sent
            other = after(other, sent)
        self.terms = [mine, lax.ppermute(other, "seq", ring.swap)]
        if sent is not None:
            self.terms.append(lax.ppermute(sent, "seq", ring.behind))

    def beside(self, *work):
        self.terms = list(lax.optimization_barrier((tuple(self.terms),) + work)[0])


class Square:
    def __init__(self):
        me = lax.axis_index("dp")
        self.me, self.far, self.near = me, me // 2, me % 2
        self.far_swap = [(j, j ^ 2) for j in range(4)]
        self.near_swap = [(j, j ^ 1) for j in range(4)]

    def near_of(self, block):
        return lax.ppermute(block, "dp", self.near_swap)

    def far_of(self, block):
        return lax.ppermute(block, "dp", self.far_swap)

    def gather(self, block, *begin):
        near, far = self.near_of(block), self.far_of(block)
        far = after(far, *begin) if begin else far
        return (block, near, far, lax.ppermute(far, "dp", self.near_swap))

    def place(self, pieces):
        rows, width = pieces[0].shape

        def kernel(me, *refs):
            for r in range(4):
                begin = pl.multiple_of((me[0] ^ r) * rows, 16)
                refs[4][pl.ds(begin, rows)] = refs[r][...]

        return call(
            kernel,
            struct((4 * rows, width), BF16),
            whole((4 * rows, width)),
            in_blocks=[whole((rows, width))] * 4,
            scalars=self.me[None],
            name="place_rows",
        )(*pieces)

    def half_sum(self, partial):
        parts = partial.reshape((2, 2, partial.shape[0] // 4) + partial.shape[1:])
        mine = lax.dynamic_index_in_dim(parts, self.near, 1, keepdims=False)
        other = lax.dynamic_index_in_dim(parts, 1 - self.near, 1, keepdims=False)
        near = lax.ppermute(other, "dp", self.near_swap)
        return (mine.astype(F32) + near.astype(F32)).astype(BF16)

    def other_sum(self, column):
        mine = lax.dynamic_index_in_dim(column, self.far, 0, keepdims=False)
        other = lax.dynamic_index_in_dim(column, 1 - self.far, 0, keepdims=False)
        return mine.astype(F32) + lax.ppermute(other, "dp", self.far_swap).astype(F32)

    def sum(self, values):
        values = values + lax.ppermute(values, "dp", self.near_swap)
        return values + lax.ppermute(values, "dp", self.far_swap)


def head_tables(count, model_width, window):
    slots = -(-HEADS // count)
    wide = slots * HD
    lists = [[[] for _ in range(count)] for _ in range(count)]
    for column in range(3 * model_width):
        src, local = divmod(column, window)
        part, within = divmod(column, model_width)
        head, lane = divmod(within, HD)
        dst, slot = head % count, head // count
        lists[src][dst].append((local, part * wide + slot * HD + lane))
    most = max(len(entry) for row in lists for entry in row)
    most = -(-most // 64) * 64
    pack = np.full((count, count * most), -1, np.int32)
    unpack = np.full((count, count * most), -1, np.int32)
    for src in range(count):
        for dst in range(count):
            for place, (local, target) in enumerate(lists[src][dst]):
                pack[src, dst * most + place] = local
                unpack[dst, src * most + place] = target
    return pack, unpack, most


def pick_row(table, index):
    return lax.dynamic_index_in_dim(jnp.asarray(table), index, 0, keepdims=False)


def one_hot(rows, size):
    return (lax.broadcasted_iota(jnp.int32, (size, rows.shape[0]), 0) == rows[None, :]).astype(BF16)


def forward_kernel(pos_col, pos_row, query_ref, full_ref, context_ref, probs_ref, *, wide):
    slots, _, run, width = query_ref.shape
    rows = slots * run
    keys_total = full_ref.shape[0] * run
    query = query_ref[:, 0].reshape(rows, width)[:, :wide]
    full = full_ref[:, 0].reshape(keys_total, width)
    key, value = full[:, wide : 2 * wide], full[:, 2 * wide :]
    seen = pos_row[0] <= pos_col[0]
    lane_head = lax.broadcasted_iota(jnp.int32, (1, wide), 1) // HD
    context = jnp.zeros((rows, wide), F32)
    for head in range(wide // HD):
        mine = lane_head == head
        scores = dot_nt(jnp.where(mine, query, jnp.zeros_like(query)), key) * SCORE_SCALE
        scores = jnp.where(seen, scores, MASKED_SCORE)
        top = jnp.max(scores, axis=1, keepdims=True)
        raw = jnp.exp(scores - top)
        probs = (raw * (1.0 / jnp.sum(raw, axis=1, keepdims=True))).astype(BF16)
        probs_ref[0, head] = probs
        context = jnp.where(mine, dot(probs, value), context)
    context_ref[:, 0] = context.astype(BF16).reshape(slots, run, wide)


def backward_kernel(query_ref, full_ref, grad_ref, probs_ref, out_ref, key_sum, value_sum, *, wide):
    step = pl.program_id(1)
    slots, _, run, width = query_ref.shape
    rows = slots * run
    count = full_ref.shape[0]
    keys_total = count * run
    query = query_ref[:, 0].reshape(rows, width)[:, :wide]
    full = full_ref[:, 0].reshape(keys_total, width)
    key, value = full[:, wide : 2 * wide], full[:, 2 * wide :]
    grad = grad_ref[:, 0].reshape(rows, wide)
    lane_head = lax.broadcasted_iota(jnp.int32, (1, wide), 1) // HD

    @pl.when(step == 0)
    def _():
        key_sum[...] = jnp.zeros_like(key_sum)
        value_sum[...] = jnp.zeros_like(value_sum)

    query_grad = jnp.zeros((rows, wide), F32)
    key_grad = jnp.zeros((keys_total, wide), F32)
    value_grad = jnp.zeros((keys_total, wide), F32)
    for head in range(wide // HD):
        mine = lane_head == head
        probs_low = probs_ref[0, head]
        probs = probs_low.astype(F32)
        grad_probs = dot_nt(jnp.where(mine, grad, jnp.zeros_like(grad)), value)
        weighted = probs * grad_probs
        delta = jnp.sum(weighted, axis=1, keepdims=True)
        grad_scores = (weighted - probs * delta).astype(BF16)
        query_grad = jnp.where(mine, dot(grad_scores, key), query_grad)
        key_grad = jnp.where(mine, dot_tn(grad_scores, query), key_grad)
        value_grad = jnp.where(mine, dot_tn(probs_low, grad), value_grad)
    key_sum[...] += key_grad
    value_sum[...] += value_grad
    out_ref[pl.ds(step * slots, slots), 0, :, :wide] = (
        (query_grad * SCORE_SCALE).astype(BF16).reshape(slots, run, wide)
    )

    @pl.when(step == pl.num_programs(1) - 1)
    def _():
        out_ref[:, 0, :, wide : 2 * wide] = (
            (key_sum[...] * SCORE_SCALE).astype(BF16).reshape(count, run, wide)
        )
        out_ref[:, 0, :, 2 * wide :] = value_sum[...].astype(BF16).reshape(count, run, wide)


def attention_forward(qkv_rows, positions):
    count, _, run, width = qkv_rows.shape
    wide = width // 3
    heads = wide // HD
    length = count * run
    block = min(length, 512)
    slots = block // run
    steps = length // block
    by_sequence = positions.reshape(count, SEQS, run).transpose(1, 0, 2).reshape(SEQS, length)
    return pl.pallas_call(
        functools.partial(forward_kernel, wide=wide),
        grid=(SEQS, steps),
        in_specs=[
            pl.BlockSpec((1, block, 1), lambda s, i: (s, i, 0)),
            pl.BlockSpec((1, 1, length), lambda s, i: (s, 0, 0)),
            pl.BlockSpec((slots, 1, run, width), lambda s, i: (i, s, 0, 0)),
            pl.BlockSpec((count, 1, run, width), lambda s, i: (0, s, 0, 0)),
        ],
        out_specs=[
            pl.BlockSpec((slots, 1, run, wide), lambda s, i: (i, s, 0, 0)),
            pl.BlockSpec((1, heads, block, length), lambda s, i: (s, 0, i, 0)),
        ],
        out_shape=[
            jax.ShapeDtypeStruct((count, SEQS, run, wide), BF16),
            jax.ShapeDtypeStruct((SEQS, heads, length, length), BF16),
        ],
        compiler_params=pltpu.CompilerParams(vmem_limit_bytes=60 * 1024 * 1024),
        cost_estimate=LARGE_COST,
        name="attention_forward",
    )(by_sequence[:, :, None], by_sequence[:, None, :], qkv_rows, qkv_rows)


def attention_backward(qkv_rows, grad_context, probs):
    count, _, run, width = qkv_rows.shape
    wide = width // 3
    heads = wide // HD
    length = count * run
    block = min(length, 512)
    slots = block // run
    steps = length // block
    return pl.pallas_call(
        functools.partial(backward_kernel, wide=wide),
        grid=(SEQS, steps),
        in_specs=[
            pl.BlockSpec((slots, 1, run, width), lambda s, i: (i, s, 0, 0)),
            pl.BlockSpec((count, 1, run, width), lambda s, i: (0, s, 0, 0)),
            pl.BlockSpec((slots, 1, run, wide), lambda s, i: (i, s, 0, 0)),
            pl.BlockSpec((1, heads, block, length), lambda s, i: (s, 0, i, 0)),
        ],
        out_specs=pl.BlockSpec((count, 1, run, width), lambda s, i: (0, s, 0, 0)),
        out_shape=jax.ShapeDtypeStruct((count, SEQS, run, width), BF16),
        scratch_shapes=[pltpu.VMEM((length, wide), F32), pltpu.VMEM((length, wide), F32)],
        compiler_params=pltpu.CompilerParams(vmem_limit_bytes=60 * 1024 * 1024),
        cost_estimate=SMALL_COST,
        name="attention_backward",
    )(qkv_rows, qkv_rows, grad_context, probs)


def in_order(side, own, other, axis=0):
    first = jnp.where(side == 0, own, other)
    second = jnp.where(side == 0, other, own)
    return jnp.concatenate([first, second], axis=axis)


def normalize(values):
    centred = values - jnp.mean(values, axis=1, keepdims=True)
    spread = lax.rsqrt(jnp.mean(centred * centred, axis=1, keepdims=True) + NORM_EPS)
    return centred * spread, spread


def normalize_back(normal, spread, gain, grad):
    scaled = grad * gain
    along = jnp.mean(scaled * normal, axis=1, keepdims=True)
    return spread * (scaled - jnp.mean(scaled, axis=1, keepdims=True) - normal * along)


def first_rows(pieces, scalars, weight, small, bias):
    rows, width = pieces[0][0].shape
    steps = len(pieces)
    total = 2 * steps * rows
    columns = weight.shape[1]

    def kernel(marks, *refs):
        given, (w, small_ref, b), outs = refs[: 2 * steps], refs[2 * steps : -3], refs[-3:]
        for t in range(steps):

            @pl.when(pl.program_id(0) == t)
            def _(t=t):
                outs[0][...] = in_order(marks[0], given[2 * t][...], given[2 * t + 1][...])

        normal, _ = normalize(outs[0][...].astype(F32))
        outs[1][...] = normal.astype(BF16)
        scaled = (normal * small_ref[8:9] + small_ref[9:10]).astype(BF16)
        outs[2][...] = (dot(scaled, w[...]) + b[...]).astype(BF16)

    def block(width):
        return pl.BlockSpec((2 * rows, width), lambda t, marks: (marks[1 + t], 0))

    flat = [piece for pair in pieces for piece in pair]
    return call(
        kernel,
        [struct((total, width), BF16), struct((total, width), BF16), struct((total, columns), BF16)],
        [block(width), block(width), block(columns)],
        grid=(steps,),
        in_blocks=[whole((rows, width))] * (2 * steps)
        + [whole(weight.shape), whole(small.shape), whole((1, columns))],
        scalars=scalars,
        name="first_rows",
    )(*flat, weight, small, bias)


def second_rows(tokens_all, pieces, scalars, weight, small):
    total, width = tokens_all.shape
    steps = len(pieces)
    wide = pieces[0][0].shape[1]
    own_rows = total // (2 * steps)
    rows = 2 * own_rows
    inside = rows // own_rows

    def kernel(marks, tokens, *refs):
        given = refs[: 2 * steps]
        w, small_ref, normed, own, context = refs[2 * steps :]
        for t in range(steps):
            pair = in_order(marks[0], given[2 * t][...], given[2 * t + 1][...], axis=1)
            begin = pl.multiple_of(marks[1 + t] * (2 * wide), 2 * wide)
            context[:, pl.ds(begin, 2 * wide)] = pair
        residual = tokens[...].astype(F32) + dot(context[...], w[...]) + small_ref[2:3]
        normal, _ = normalize(residual)
        normed[...] = (normal * small_ref[10:11] + small_ref[11:12]).astype(BF16)
        mine = marks[1] * 2 + marks[0]
        for i in range(inside):

            @pl.when(pl.program_id(0) * inside + i == mine)
            def _(i=i):
                own[...] = residual[i * own_rows : (i + 1) * own_rows]

    return pl.pallas_call(
        kernel,
        grid_spec=pltpu.PrefetchScalarGridSpec(
            num_scalar_prefetch=1,
            grid=(total // rows,),
            in_specs=[pl.BlockSpec((rows, width), lambda i, marks: (i, 0))]
            + [pl.BlockSpec((rows, wide), lambda i, marks: (i, 0))] * (2 * steps)
            + [whole(weight.shape), whole(small.shape)],
            out_specs=[
                pl.BlockSpec((rows, width), lambda i, marks: (i, 0)),
                whole((own_rows, width)),
            ],
            scratch_shapes=[pltpu.VMEM((rows, 2 * steps * wide), BF16)],
        ),
        out_shape=[struct((total, width), BF16), struct((own_rows, width), F32)],
        compiler_params=pltpu.CompilerParams(vmem_limit_bytes=60 * 1024 * 1024),
        cost_estimate=SMALL_COST,
        name="second_rows",
    )(scalars, tokens_all, *[piece for pair in pieces for piece in pair], weight, small)


def hidden_rows(normed, pairs, scalars, w_fc, w_proj, bias, kept, taken, rows):
    total, width = normed.shape
    hidden = w_fc.shape[1]
    many = len(taken)

    def kernel(marks, block, *refs):
        given, (fc, proj, b) = refs[: 2 * many], refs[2 * many : 2 * many + 3]
        act_ref, grad_ref, cot_ref = refs[-3 - 2 * many : -2 * many]
        parts = refs[-2 * many :]
        for i in range(many):

            @pl.when(pl.program_id(0) == i)
            def _(i=i):
                cot_ref[...] = in_order(marks[0], given[2 * i][...], given[2 * i + 1][...])

        z = dot(block[...], fc[...]) + b[...]
        square = z * z
        tanh = jnp.tanh(0.7978845608028654 * (z + 0.044715 * (square * z)))
        half = 0.5 * (1.0 + tanh)
        slope = half + 0.5 * z * (1.0 - tanh * tanh) * (
            0.7978845608028654 + (0.7978845608028654 * 3.0 * 0.044715) * square
        )
        act_ref[...] = (z * half).astype(BF16)
        grad = (dot(cot_ref[...], proj[...]) * slope).astype(BF16)
        grad_ref[...] = grad
        part = dot_nt(grad, fc[...])
        mine = jnp.where(marks[0] == 0, part[:rows], part[rows:])
        other = jnp.where(marks[0] == 0, part[rows:], part[:rows]).astype(BF16)
        for i in range(many):

            @pl.when(pl.program_id(0) == i)
            def _(i=i):
                parts[2 * i][...] = mine
                parts[2 * i + 1][...] = other

    def block(width):
        return pl.BlockSpec((2 * rows, width), lambda i, marks: (marks[1 + i], 0))

    operands = [normed] + [piece for pair in pairs for piece in pair] + [w_fc, w_proj, bias]
    blocks = [block(width)] + [whole((rows, width))] * (2 * many)
    blocks += [whole(w_fc.shape), whole(w_proj.shape), whole((1, hidden))]
    alias = {}
    if kept is not None:
        alias = {1 + len(operands) + i: i for i in range(3)}
        operands += list(kept)
        blocks += [pl.BlockSpec(memory_space=pl.ANY)] * 3
    outs = call(
        kernel,
        [struct((total, hidden), BF16), struct((total, hidden), BF16), struct((total, width), BF16)]
        + [struct((rows, width), dtype) for _ in taken for dtype in (F32, BF16)],
        [block(hidden), block(hidden), block(width)] + [whole((rows, width))] * (2 * many),
        grid=(many,),
        in_blocks=blocks,
        scalars=scalars,
        alias=alias,
        name="hidden_rows",
    )(*operands)
    return outs[:3], {t: (outs[3 + 2 * i], outs[4 + 2 * i]) for i, t in enumerate(taken)}


def turned_product(left, right, name):
    total, width = left.shape
    columns = right.shape[1]
    tile = 256

    def kernel(left_ref, right_ref, out_ref):
        out_ref[...] = dot(left_ref[...].T, right_ref[...]).astype(BF16)

    return call(
        kernel,
        struct((width, columns), BF16),
        pl.BlockSpec((tile, columns), lambda i: (i, 0)),
        grid=(pl.cdiv(width, tile),),
        in_blocks=[pl.BlockSpec((total, tile), lambda i: (0, i)), whole(right.shape)],
        name=name,
    )(left, right)


def head_product(normal, grad, weight, small):
    total, width = normal.shape
    columns = grad.shape[1]
    tile = 256

    def kernel(left, right, w, small_ref, out, gain_sum, shift_sum, grad_sum):
        @pl.when(pl.program_id(0) == 0)
        def _():
            grad_sum[...] = jnp.sum(right[...].astype(F32), axis=0, keepdims=True)

        raw = dot(left[...].T, right[...])
        sums = grad_sum[...]
        low = w[...].astype(F32)
        gain_sum[...] = jnp.sum(raw * low, axis=1, keepdims=True)
        shift_sum[...] = jnp.sum(low * sums, axis=1, keepdims=True)
        turned = small_ref[8:16].T
        out[...] = (raw * turned[:, 0:1] + turned[:, 1:2] * sums).astype(BF16)

    column = pl.BlockSpec((tile, 1), lambda i: (i, 0))
    return call(
        kernel,
        [
            struct((width, columns), BF16),
            struct((width, 1), F32),
            struct((width, 1), F32),
            struct((1, columns), F32),
        ],
        [pl.BlockSpec((tile, columns), lambda i: (i, 0)), column, column, whole((1, columns))],
        grid=(pl.cdiv(width, tile),),
        in_blocks=[
            pl.BlockSpec((total, tile), lambda i: (0, i)),
            whole(grad.shape),
            pl.BlockSpec((tile, columns), lambda i: (i, 0)),
            pl.BlockSpec((small.shape[0], tile), lambda i: (0, i)),
        ],
        name="head_product",
    )(normal, grad, weight, small)


def ring_parts(left, right, scalars, taken, steps, name):
    total, inner = left.shape
    width = right.shape[0]
    rows = total // (2 * steps)

    def kernel(marks, left_ref, right_ref, *outs):
        for i, t in enumerate(taken):
            begin = pl.multiple_of(marks[1 + t] * (2 * rows), 2 * rows)
            part = dot_nt(left_ref[pl.ds(begin, 2 * rows)], right_ref[...])
            outs[2 * i][...] = jnp.where(marks[0] == 0, part[:rows], part[rows:])
            outs[2 * i + 1][...] = jnp.where(marks[0] == 0, part[rows:], part[:rows]).astype(BF16)

    outs = call(
        kernel,
        [struct((rows, width), dtype) for _ in taken for dtype in (F32, BF16)],
        [whole((rows, width))] * (2 * len(taken)),
        in_blocks=[whole(left.shape), whole(right.shape)],
        scalars=scalars,
        name=name,
    )(left, right)
    return {t: (outs[2 * i], outs[2 * i + 1]) for i, t in enumerate(taken)}


def second_back(residual, terms, cotangent, small, weight, count):
    rows, width = residual.shape
    wide = weight.shape[0] // count
    columns = width // count

    def kernel(
        res, mine, swapped, carried, cot, g, w, grad_ref, low_ref, sums_ref, out_ref, cut_ref
    ):
        @pl.when(pl.program_id(0) == 0)
        def _():
            grad = mine[...] + swapped[...].astype(F32) + carried[...].astype(F32)
            normal, spread = normalize(res[...])
            total = cot[...].astype(F32) + normalize_back(normal, spread, g[10:11], grad)
            grad_ref[...] = total
            low = total.astype(BF16)
            low_ref[...] = low
            sums_ref[0:1] = jnp.sum(grad * normal, axis=0, keepdims=True)
            sums_ref[1:2] = jnp.sum(grad, axis=0, keepdims=True)
            sums_ref[2:3] = jnp.sum(low.astype(F32), axis=0, keepdims=True)
            sums_ref[3:4] = jnp.sum(cot[...].astype(F32), axis=0, keepdims=True)

        out_ref[0] = dot_nt(low_ref[...], w[...]).astype(BF16)
        for j in range(count):

            @pl.when(pl.program_id(0) == j)
            def _(j=j):
                cut_ref[0] = low_ref[:, j * columns : (j + 1) * columns]

    row = whole((rows, width))
    return call(
        kernel,
        [
            struct((rows, width), F32),
            struct((rows, width), BF16),
            struct((4, width), F32),
            struct((count, rows, wide), BF16),
            struct((count, rows, columns), BF16),
        ],
        [
            row,
            row,
            whole((4, width)),
            pl.BlockSpec((1, rows, wide), lambda i: (i, 0, 0)),
            pl.BlockSpec((1, rows, columns), lambda i: (i, 0, 0)),
        ],
        grid=(count,),
        in_blocks=[row] * 5 + [whole(small.shape), pl.BlockSpec((wide, width), lambda i: (i, 0))],
        name="second_back",
    )(residual, *terms, cotangent, small, weight)


def first_back(tokens, terms, residual_grad, small):
    rows, width = tokens.shape

    def kernel(x, mine, swapped, carried, res, g, out_ref):
        grad = mine[...] + swapped[...].astype(F32) + carried[...].astype(F32)
        normal, spread = normalize(x[...].astype(F32))
        out_ref[...] = (res[...] + normalize_back(normal, spread, g[8:9], grad)).astype(BF16)

    row = whole((rows, width))
    return call(
        kernel,
        struct((rows, width), BF16),
        row,
        in_blocks=[row] * 5 + [whole(small.shape)],
        name="first_back",
    )(tokens, *terms, residual_grad, small)


def heads_rows(me, pieces, count, slots):
    rows, width = pieces[0].shape
    unit = math.gcd(rows, HD)

    def kernel(mark, *refs):
        out = refs[4]
        for h in range(HEADS, count * slots):
            place = ((h % count) * slots + h // count) * HD
            out[place : place + HD] = jnp.zeros((HD, width), BF16)
        for r in range(4):
            for piece in range(rows // unit):
                row = (mark[0] ^ r) * rows + piece * unit
                head = row // HD
                target = ((head % count) * slots + head // count) * HD + row % HD
                out[pl.ds(pl.multiple_of(target, unit), unit)] = refs[r][
                    piece * unit : (piece + 1) * unit
                ]

    return call(
        kernel,
        struct((count * slots * HD, width), BF16),
        whole((count * slots * HD, width)),
        in_blocks=[whole((rows, width))] * 4,
        scalars=me[None],
        name="heads_rows",
    )(*pieces)


def out_product(pieces, columns, scalars, count, slots):
    total, width = columns.shape
    wide = slots * HD
    steps = len(pieces)

    def kernel(marks, *refs):
        given, right, out = refs[: 2 * steps], refs[2 * steps], refs[-1]
        for t in range(steps):
            for b in range(2):
                owner = marks[1 + t] * 2 + (marks[0] if b == 0 else 1 - marks[0])
                value = dot_tn(given[2 * t + b][...], right[...]).astype(BF16)
                for slot in range(slots):
                    head = slot * count + owner

                    def store(slot=slot, head=head, value=value):
                        begin = pl.multiple_of(head * HD, HD)
                        out[pl.ds(begin, HD)] = value[slot * HD : (slot + 1) * HD]

                    if (slot + 1) * count <= HEADS:
                        store()
                    else:
                        pl.when(head < HEADS)(store)

    return call(
        kernel,
        struct((HEADS * HD, width), BF16),
        whole((HEADS * HD, width)),
        in_blocks=[whole((total, wide))] * (2 * steps) + [whole(columns.shape)],
        scalars=scalars,
        name="out_product",
    )(*[piece for pair in pieces for piece in pair], columns)


def rows_product(left, right, name):
    total, inner = left.shape
    width = right.shape[0]
    block = min(total, 512)

    def kernel(left_ref, right_ref, out_ref):
        out_ref[...] = dot_nt(left_ref[...], right_ref[...]).astype(BF16)

    return call(
        kernel,
        struct((total, width), BF16),
        pl.BlockSpec((block, width), lambda i: (i, 0)),
        grid=(total // block,),
        in_blocks=[pl.BlockSpec((block, inner), lambda i: (i, 0)), whole(right.shape)],
        name=name,
    )(left, right)


def shards(
    tokens,
    cotangent,
    positions,
    qkv_weight,
    qkv_first,
    qkv_second,
    out_weight,
    out_first,
    out_second,
    fc_weight,
    fc_first,
    fc_second,
    proj_weight,
    proj_first,
    proj_second,
    small_weight,
    small_first,
    small_second,
):
    count = lax.axis_size("seq")
    ring = Ring(count)
    square = Square()
    me = lax.axis_index("seq")
    rows, width = tokens.shape
    seq_rows = rows // SEQS
    window = qkv_weight.shape[1]
    slots = -(-HEADS // count)
    wide = slots * HD
    small_count, small_width = small_weight.shape
    hidden = fc_weight.shape[1]
    all_rows = count * rows
    steps = ring.steps
    marks = jnp.stack([ring.side] + [ring.position(t) for t in range(steps)])
    tokens = by_rows(tokens)
    cotangent = by_rows(cotangent)

    token_tour = Tour(ring, tokens)
    token_tour.step()
    token_tour.step()
    pack, unpack, most = head_tables(count, width, window)
    pack_hot = one_hot(pick_row(pack, me), window)
    packed = jnp.einsum(
        "rc,cdl->drl",
        qkv_weight.astype(BF16),
        pack_hot.reshape(window, count, most),
        preferred_element_type=BF16,
    )
    depth = packed.shape[1]
    small_flat = jnp.concatenate(
        [
            small_weight.reshape(-1).astype(BF16),
            (positions // 32).astype(BF16),
            (positions % 32).astype(BF16),
        ]
    )
    small_depth = -(-small_flat.shape[0] // most)
    small_depth += -small_depth % 16
    small_flat = jnp.pad(small_flat, (0, small_depth * most - small_flat.shape[0]))
    small_pack = jnp.broadcast_to(
        small_flat.reshape(1, small_depth, most), (count, small_depth, most)
    )
    received = lax.all_to_all(jnp.concatenate([packed, small_pack], axis=1), "seq", 0, 0)
    token_tour.step()
    received = after(received, token_tour.moved[1], token_tour.current)

    unpack_hot = one_hot(pick_row(unpack, me), 3 * wide)
    head_part = jnp.einsum(
        "srl,ksl->rk",
        received[:, :depth],
        unpack_hot.reshape(3 * wide, count, most),
        preferred_element_type=BF16,
    )
    for t in range(3, steps):
        token_tour.step()
    head_pieces = square.gather(head_part, token_tour.current)
    w_head = square.place(head_pieces)

    small_all = received[:, depth:].reshape(count, small_depth * most).astype(F32)
    small_rows = small_all[:, : small_count * small_width].reshape(count, small_count, small_width)
    small_rows = small_rows.transpose(1, 0, 2).reshape(small_count, width)
    small_rows = jnp.pad(small_rows, ((0, 4), (0, 0)))
    pos_all = small_all[:, small_count * small_width :][:, : 2 * rows].reshape(count, 2, rows)
    pos_all = (pos_all[:, 0] * 32.0 + pos_all[:, 1]).astype(jnp.int32)

    def own_heads(row):
        padded = jnp.pad(row, (0, slots * count * HD - width)).reshape(slots, count, HD)
        return lax.dynamic_index_in_dim(padded, me, 1, keepdims=False).reshape(wide)

    head_bias = jnp.concatenate(
        [own_heads(small_rows[0]), jnp.zeros((wide,), F32), own_heads(small_rows[1])]
    )
    fc_bias = lax.dynamic_slice_in_dim(small_rows[3:7].reshape(-1), me * hidden, hidden, 0)

    ready = (w_head, token_tour.moved[-1])
    tokens_all, normal_all, qkv_rows = first_rows(
        token_tour.pieces, marks, w_head, small_rows, head_bias[None]
    )
    qkv_all = qkv_rows.reshape(count, SEQS, seq_rows, 3 * wide)
    context, probs = attention_forward(qkv_all, pos_all)
    context = context.reshape(all_rows, wide)

    cot_zero = lax.ppermute(after(cotangent, *ready), "seq", ring.swap)
    cot_moving = lax.ppermute(after(cotangent, *ready), "seq", ring.behind)
    out_part = lax.all_gather(out_weight.astype(BF16), "seq", axis=1, tiled=True)
    fc_low = after(fc_weight, *ready).astype(BF16)
    context = after(context, cot_zero, cot_moving)
    out_part = by_rows(after(out_part, context))
    out_near, out_far = square.near_of(out_part), square.far_of(out_part)
    fc_near, fc_far = square.near_of(fc_low), square.far_of(fc_low)
    proj_low = after(proj_weight, context).T.astype(BF16)
    proj_near, proj_far = square.near_of(proj_low), square.far_of(proj_low)
    context_tour = Tour(ring, context)
    context_tour.step()
    context_tour.step(land=(out_part, fc_far, proj_far))
    fc_pieces = (fc_low, fc_near, fc_far, square.near_of(after(fc_far, context_tour.current)))
    proj_pieces = (proj_low, proj_near, proj_far, square.near_of(after(proj_far, context_tour.current)))
    w_fc, w_proj = square.place(fc_pieces), square.place(proj_pieces)
    context_tour.step(land=(w_fc, w_proj))
    for t in range(3, steps):
        context_tour.step(land=(out_far,) if t == 3 else ())
    out_pieces = (out_part, out_near, out_far, square.near_of(after(out_far, context_tour.current)))
    w_out = heads_rows(square.me, out_pieces, count, slots)
    normed_all, residual = second_rows(
        tokens_all, context_tour.pieces, marks, w_out, small_rows
    )
    cot_moving = [cot_moving]
    for t in range(2, steps):
        begin = context_tour.current if t == 2 else w_out
        moving = lax.ppermute(after(cot_moving[-1], begin), "seq", ring.behind)
        cot_moving.append(after(moving, w_out if t == 2 else residual))
    cot_pieces = {0: (cotangent, cot_zero)}
    crossing = after(context_tour.moved[-1], w_out)
    for t in range(1, steps):
        crossed = lax.ppermute(after(cot_moving[t - 1], crossing), "seq", ring.swap)
        cot_pieces[steps - t] = (cot_moving[t - 1], after(crossed, residual))

    def feed_forward(kept, taken, *begin):
        chosen = jnp.stack([ring.side] + [ring.position(t) for t in taken])
        return hidden_rows(
            normed_all,
            [cot_pieces[t] for t in taken],
            after(chosen, *begin) if begin else chosen,
            w_fc,
            w_proj,
            fc_bias[None],
            kept,
            taken,
            rows,
        )

    kept, parts = feed_forward(None, [steps - 1])
    grad_fold = Fold(ring, parts)
    kept, more = feed_forward(kept, [steps - 2])
    parts.update(more)
    grad_fold.beside(*parts[steps - 2])
    grad_fold.step()
    kept, more = feed_forward(kept, list(reversed(range(steps - 2))), grad_fold.carried)
    parts.update(more)
    grad_fold.beside(*parts[0])
    hidden_low, grad_pre_low, cot_all = kept
    grad_fold.step()
    output_partial = rows_product(after(hidden_low, grad_fold.carried), w_proj, "output_product")
    grad_fold.beside(output_partial)
    for _ in range(3, steps):
        grad_fold.step()
    fc_sum = turned_product(after(normed_all, grad_fold.carried), grad_pre_low, "fc_product")
    grad_fold.beside(fc_sum)
    output_sum = lax.psum_scatter(output_partial, "seq", scatter_dimension=0, tiled=True)
    terms = grad_fold.terms
    grad_residual, _, row_sums, grad_sent, attn_cut = second_back(
        residual, terms, cotangent, small_rows, w_out, count
    )
    grad_bias_fc = jnp.sum(after(grad_pre_low, grad_sent).astype(F32), axis=0)
    fc_column = square.half_sum(after(fc_sum, grad_sent))

    proj_sum = turned_product(after(cot_all, grad_sent), hidden_low, "proj_product")
    grad_context = after(
        lax.all_to_all(grad_sent, "seq", 0, 0),
        proj_sum,
        grad_bias_fc,
    )
    proj_column = square.half_sum(proj_sum)
    attn_columns = lax.all_to_all(after(attn_cut, grad_context), "seq", 0, 0)
    grad_qkv = attention_backward(
        qkv_all, grad_context.reshape(count, SEQS, seq_rows, wide), probs
    ).reshape(all_rows, 3 * wide)
    fc_grad = after(square.other_sum(fc_column), grad_qkv)
    proj_grad = square.other_sum(after(proj_column, grad_qkv))
    attn_columns = after(attn_columns, grad_qkv)
    parts = ring_parts(grad_qkv, w_head, marks, [steps - 1], steps, "first_parts")
    input_fold = Fold(ring, parts)
    parts.update(
        ring_parts(
            after(grad_qkv, *parts[steps - 1]), w_head, marks, range(steps - 1), steps, "input_parts"
        )
    )
    input_fold.beside(*parts[0])
    input_fold.step()
    head_sum, grad_gain_one, grad_shift_one, grad_qkv_sum = head_product(
        after(normal_all, input_fold.carried),
        grad_qkv,
        w_head,
        small_rows,
    )
    input_fold.beside(head_sum)
    input_fold.step()
    head_column = square.half_sum(after(head_sum, input_fold.carried))
    out_columns = out_weight.shape[1]
    attn_columns = after(attn_columns, input_fold.carried).reshape(all_rows, out_columns)
    input_fold.beside(head_column)
    for _ in range(3, steps):
        input_fold.step()
    small_begin = input_fold.carried
    head_far = square.other_sum(after(head_column, input_fold.carried))
    out_sum = out_product(
        context_tour.pieces, after(attn_columns, input_fold.carried), marks, count, slots
    )
    input_fold.beside(output_sum, out_sum)
    head_grad = after(head_far, *input_fold.terms).astype(BF16)
    unpack_back = unpack_hot.reshape(3 * wide, count, most)
    head_packed = jnp.einsum("rk,ksl->srl", head_grad, unpack_back, preferred_element_type=BF16)
    last_terms = after(tuple(input_fold.terms), head_packed)
    input_grad = first_back(tokens, last_terms, grad_residual, small_rows)
    out_column = square.half_sum(after(out_sum, head_packed))
    out_grad = square.other_sum(out_column)
    fc_new = adam_update(
        fc_weight, fc_first, fc_second, after(fc_grad, head_packed), 0.02, 0.1
    )
    head_back = lax.all_to_all(head_packed, "seq", 0, 0)
    output = (residual + output_sum.astype(F32) + small_rows[7]).astype(BF16)

    def place_heads(values):
        spread = (jnp.arange(count) == me).astype(F32)[None, :, None]
        placed = values.reshape(slots, 1, HD) * spread
        return placed.reshape(-1)[:width]

    grad_bias_fc = grad_bias_fc[None, :] * (jnp.arange(count) == me).astype(F32)[:, None]
    grad_qkv_sum = after(grad_qkv_sum, small_begin)[0]
    grad_small = jnp.concatenate(
        [
            place_heads(grad_qkv_sum[:wide])[None],
            place_heads(grad_qkv_sum[2 * wide :])[None],
            row_sums[2:3],
            grad_bias_fc.reshape(-1, width),
            row_sums[3:4],
            grad_gain_one[:, 0][None],
            grad_shift_one[:, 0][None],
            row_sums[0:1],
            row_sums[1:2],
        ],
        axis=0,
    )
    small_sent = grad_small.astype(BF16).reshape(small_count, count, small_width)
    small_part = jnp.sum(
        lax.all_to_all(small_sent.transpose(1, 0, 2), "seq", 0, 0).astype(F32), axis=0
    )
    small_grad = square.sum(after(small_part, head_packed))

    out_new = adam_update(out_weight, out_first, out_second, out_grad, 0.3, 0.1)
    proj_new = adam_update(
        proj_weight.T, proj_first.T, proj_second.T, proj_grad, 0.02, 0.1
    )
    proj_new = [value.T for value in proj_new]
    small_new = adam_update(small_weight, small_first, small_second, small_grad, 0.3, 0.0)
    head_back = after(head_back, fc_new[0], out_new[0], small_new[0])
    qkv_grad = jnp.einsum(
        "drl,cdl->rc",
        head_back,
        pack_hot.reshape(window, count, most),
        preferred_element_type=F32,
    )
    qkv_new = adam_update(qkv_weight, qkv_first, qkv_second, qkv_grad, 0.02, 0.1)
    return (
        output,
        input_grad,
        *qkv_new,
        *out_new,
        *fc_new,
        *proj_new,
        *small_new,
        small_grad[7],
    )


def solution(mesh):
    rows = P(("dp", "seq"), None)
    matrix = P("dp", "seq")
    turned = P("seq", "dp")
    small = P(None, "seq")
    in_specs = (
        (rows, rows, P(("dp", "seq"))) + (matrix,) * 9 + (turned,) * 3 + (small,) * 3
    )
    out_specs = (rows, rows) + (matrix,) * 9 + (turned,) * 3 + (small,) * 3 + (P("seq"),)
    return jax.shard_map(shards, mesh=mesh, in_specs=in_specs, out_specs=out_specs, check_vma=False)
```

```python
import functools
import math

import jax
import jax.numpy as jnp
import numpy as np
from jax import lax
from jax.experimental import pallas as pl
from jax.experimental.layout import Layout, with_layout_constraint
from jax.experimental.pallas import tpu as pltpu
from jax.sharding import PartitionSpec as P

HEADS = 25
HD = 64
SEQS = 2
STEP = 10

NORM_EPS = 1e-05
SCORE_SCALE = 0.125
MASKED_SCORE = -1e30
BETA_ONE = 0.9
BETA_TWO = 0.95
ADAM_EPS = 1e-08
BF16 = jnp.bfloat16
F32 = jnp.float32
SMALL_COST = pl.CostEstimate(flops=1024, bytes_accessed=1024, transcendentals=0)
LARGE_COST = pl.CostEstimate(flops=8 * 10**9, bytes_accessed=8 * 10**6, transcendentals=0)


def adam_update(weight, first_moment, second, gradient, step_rate, decay_rate):
    moment_new = BETA_ONE * first_moment + (1.0 - BETA_ONE) * gradient
    second_new = BETA_TWO * second + (1.0 - BETA_TWO) * gradient * gradient
    direction = (
        moment_new
        / (1.0 - BETA_ONE**STEP)
        / (jnp.sqrt(second_new / (1.0 - BETA_TWO**STEP)) + ADAM_EPS)
    )
    return (moment_new, second_new, weight - step_rate * (direction + decay_rate * weight))


def dot(left, right):
    return jnp.dot(left, right, preferred_element_type=F32)


def dot_nt(left, right):
    return lax.dot_general(left, right, (((1,), (1,)), ((), ())), preferred_element_type=F32)


def dot_tn(left, right):
    return lax.dot_general(left, right, (((0,), (0,)), ((), ())), preferred_element_type=F32)


def after(value, *others):
    return lax.optimization_barrier((value,) + others)[0]


def by_rows(value):
    return with_layout_constraint(value, Layout(major_to_minor=(0, 1)))


def call(
    kernel, out, blocks, grid=None, in_blocks=None, scalars=None, alias=None, scratch=(), name=None
):
    operands = 0 if scalars is None else 1
    spec = dict(
        in_specs=in_blocks,
        out_specs=blocks,
        grid=grid or (1,),
        scratch_shapes=list(scratch),
    )
    if operands:
        spec = dict(grid_spec=pltpu.PrefetchScalarGridSpec(num_scalar_prefetch=1, **spec))
    run = pl.pallas_call(
        kernel,
        out_shape=out,
        input_output_aliases=alias or {},
        compiler_params=pltpu.CompilerParams(vmem_limit_bytes=60 * 1024 * 1024),
        cost_estimate=SMALL_COST,
        name=name,
        **spec,
    )
    if operands:
        return lambda *given: run(scalars, *given)
    return run


def whole(shape):
    return pl.BlockSpec(shape, lambda *_: (0,) * len(shape))


def struct(shape, dtype):
    return jax.ShapeDtypeStruct(shape, dtype)


class Ring:
    def __init__(self, count):
        self.sides = 2
        self.steps = count // 2
        steps = self.steps
        self.swap = [(j, j ^ 1) for j in range(count)]
        self.ahead = [(z * 2 + x, ((z + 1) % steps) * 2 + x) for z in range(steps) for x in range(2)]
        self.behind = [(dst, src) for src, dst in self.ahead]
        me = lax.axis_index("seq")
        self.place, self.side = me // 2, me % 2

    def position(self, t):
        return (self.place + self.steps - t) % self.steps

    def gather(self, block):
        tour = Tour(self, block)
        for _ in range(self.steps):
            tour.step()
        return tour


class Tour:
    def __init__(self, ring, block, back=False):
        self.ring, self.current, self.back = ring, block, back
        self.pieces = [None] * ring.steps
        self.moved = []

    def step(self, *begin, land=()):
        ring, t = self.ring, len(self.moved)
        if begin:
            self.current = after(self.current, *begin)
        if t:
            moved = lax.ppermute(self.current, "seq", ring.behind if self.back else ring.ahead)
            self.current = after(moved, self.moved[-1], *land)
        other = lax.ppermute(self.current, "seq", ring.swap)
        self.pieces[-t if self.back else t] = (self.current, other)
        self.moved.append(other)


class Fold:
    def __init__(self, ring, parts):
        self.ring, self.parts = ring, parts
        self.terms, self.count, self.carried = None, 0, None
        self.step()

    def step(self):
        ring = self.ring
        mine, other = self.parts[ring.steps - 1 - self.count]
        self.count += 1
        sent = None
        if self.terms is not None:
            sent = sum(term.astype(F32) for term in self.terms).astype(BF16)
            self.carried = sent
            other = after(other, sent)
        self.terms = [mine, lax.ppermute(other, "seq", ring.swap)]
        if sent is not None:
            self.terms.append(lax.ppermute(sent, "seq", ring.behind))

    def beside(self, *work):
        self.terms = list(lax.optimization_barrier((tuple(self.terms),) + work)[0])


class Square:
    def __init__(self):
        me = lax.axis_index("dp")
        self.me, self.far, self.near = me, me // 2, me % 2
        self.far_swap = [(j, j ^ 2) for j in range(4)]
        self.near_swap = [(j, j ^ 1) for j in range(4)]

    def near_of(self, block):
        return lax.ppermute(block, "dp", self.near_swap)

    def far_of(self, block):
        return lax.ppermute(block, "dp", self.far_swap)

    def gather(self, block, *begin):
        near, far = self.near_of(block), self.far_of(block)
        far = after(far, *begin) if begin else far
        return (block, near, far, lax.ppermute(far, "dp", self.near_swap))

    def place(self, pieces):
        rows, width = pieces[0].shape

        def kernel(me, *refs):
            for r in range(4):
                begin = pl.multiple_of((me[0] ^ r) * rows, 16)
                refs[4][pl.ds(begin, rows)] = refs[r][...]

        return call(
            kernel,
            struct((4 * rows, width), BF16),
            whole((4 * rows, width)),
            in_blocks=[whole((rows, width))] * 4,
            scalars=self.me[None],
            name="place_rows",
        )(*pieces)

    def half_sum(self, partial):
        parts = partial.reshape((2, 2, partial.shape[0] // 4) + partial.shape[1:])
        mine = lax.dynamic_index_in_dim(parts, self.near, 1, keepdims=False)
        other = lax.dynamic_index_in_dim(parts, 1 - self.near, 1, keepdims=False)
        near = lax.ppermute(other, "dp", self.near_swap)
        return (mine.astype(F32) + near.astype(F32)).astype(BF16)

    def other_sum(self, column):
        mine = lax.dynamic_index_in_dim(column, self.far, 0, keepdims=False)
        other = lax.dynamic_index_in_dim(column, 1 - self.far, 0, keepdims=False)
        return mine.astype(F32) + lax.ppermute(other, "dp", self.far_swap).astype(F32)

    def sum(self, values):
        values = values + lax.ppermute(values, "dp", self.near_swap)
        return values + lax.ppermute(values, "dp", self.far_swap)


def head_tables(count, model_width, window):
    slots = -(-HEADS // count)
    wide = slots * HD
    lists = [[[] for _ in range(count)] for _ in range(count)]
    for column in range(3 * model_width):
        src, local = divmod(column, window)
        part, within = divmod(column, model_width)
        head, lane = divmod(within, HD)
        dst, slot = head % count, head // count
        lists[src][dst].append((local, part * wide + slot * HD + lane))
    most = max(len(entry) for row in lists for entry in row)
    most = -(-most // 64) * 64
    pack = np.full((count, count * most), -1, np.int32)
    unpack = np.full((count, count * most), -1, np.int32)
    for src in range(count):
        for dst in range(count):
            for place, (local, target) in enumerate(lists[src][dst]):
                pack[src, dst * most + place] = local
                unpack[dst, src * most + place] = target
    return pack, unpack, most


def pick_row(table, index):
    return lax.dynamic_index_in_dim(jnp.asarray(table), index, 0, keepdims=False)


def one_hot(rows, size):
    return (lax.broadcasted_iota(jnp.int32, (size, rows.shape[0]), 0) == rows[None, :]).astype(BF16)


def forward_kernel(pos_col, pos_row, query_ref, full_ref, context_ref, probs_ref, *, wide):
    slots, _, run, width = query_ref.shape
    rows = slots * run
    keys_total = full_ref.shape[0] * run
    query = query_ref[:, 0].reshape(rows, width)[:, :wide]
    full = full_ref[:, 0].reshape(keys_total, width)
    key, value = full[:, wide : 2 * wide], full[:, 2 * wide :]
    seen = pos_row[0] <= pos_col[0]
    lane_head = lax.broadcasted_iota(jnp.int32, (1, wide), 1) // HD
    context = jnp.zeros((rows, wide), F32)
    for head in range(wide // HD):
        mine = lane_head == head
        scores = dot_nt(jnp.where(mine, query, jnp.zeros_like(query)), key) * SCORE_SCALE
        scores = jnp.where(seen, scores, MASKED_SCORE)
        top = jnp.max(scores, axis=1, keepdims=True)
        raw = jnp.exp(scores - top)
        probs = (raw * (1.0 / jnp.sum(raw, axis=1, keepdims=True))).astype(BF16)
        probs_ref[0, head] = probs
        context = jnp.where(mine, dot(probs, value), context)
    context_ref[:, 0] = context.astype(BF16).reshape(slots, run, wide)


def backward_kernel(query_ref, full_ref, grad_ref, probs_ref, out_ref, key_sum, value_sum, *, wide):
    step = pl.program_id(1)
    slots, _, run, width = query_ref.shape
    rows = slots * run
    count = full_ref.shape[0]
    keys_total = count * run
    query = query_ref[:, 0].reshape(rows, width)[:, :wide]
    full = full_ref[:, 0].reshape(keys_total, width)
    key, value = full[:, wide : 2 * wide], full[:, 2 * wide :]
    grad = grad_ref[:, 0].reshape(rows, wide)
    lane_head = lax.broadcasted_iota(jnp.int32, (1, wide), 1) // HD

    @pl.when(step == 0)
    def _():
        key_sum[...] = jnp.zeros_like(key_sum)
        value_sum[...] = jnp.zeros_like(value_sum)

    query_grad = jnp.zeros((rows, wide), F32)
    key_grad = jnp.zeros((keys_total, wide), F32)
    value_grad = jnp.zeros((keys_total, wide), F32)
    for head in range(wide // HD):
        mine = lane_head == head
        probs_low = probs_ref[0, head]
        probs = probs_low.astype(F32)
        grad_probs = dot_nt(jnp.where(mine, grad, jnp.zeros_like(grad)), value)
        weighted = probs * grad_probs
        delta = jnp.sum(weighted, axis=1, keepdims=True)
        grad_scores = (weighted - probs * delta).astype(BF16)
        query_grad = jnp.where(mine, dot(grad_scores, key), query_grad)
        key_grad = jnp.where(mine, dot_tn(grad_scores, query), key_grad)
        value_grad = jnp.where(mine, dot_tn(probs_low, grad), value_grad)
    key_sum[...] += key_grad
    value_sum[...] += value_grad
    out_ref[pl.ds(step * slots, slots), 0, :, :wide] = (
        (query_grad * SCORE_SCALE).astype(BF16).reshape(slots, run, wide)
    )

    @pl.when(step == pl.num_programs(1) - 1)
    def _():
        out_ref[:, 0, :, wide : 2 * wide] = (
            (key_sum[...] * SCORE_SCALE).astype(BF16).reshape(count, run, wide)
        )
        out_ref[:, 0, :, 2 * wide :] = value_sum[...].astype(BF16).reshape(count, run, wide)


def attention_forward(qkv_rows, positions):
    count, _, run, width = qkv_rows.shape
    wide = width // 3
    heads = wide // HD
    length = count * run
    block = min(length, 512)
    slots = block // run
    steps = length // block
    by_sequence = positions.reshape(count, SEQS, run).transpose(1, 0, 2).reshape(SEQS, length)
    return pl.pallas_call(
        functools.partial(forward_kernel, wide=wide),
        grid=(SEQS, steps),
        in_specs=[
            pl.BlockSpec((1, block, 1), lambda s, i: (s, i, 0)),
            pl.BlockSpec((1, 1, length), lambda s, i: (s, 0, 0)),
            pl.BlockSpec((slots, 1, run, width), lambda s, i: (i, s, 0, 0)),
            pl.BlockSpec((count, 1, run, width), lambda s, i: (0, s, 0, 0)),
        ],
        out_specs=[
            pl.BlockSpec((slots, 1, run, wide), lambda s, i: (i, s, 0, 0)),
            pl.BlockSpec((1, heads, block, length), lambda s, i: (s, 0, i, 0)),
        ],
        out_shape=[
            jax.ShapeDtypeStruct((count, SEQS, run, wide), BF16),
            jax.ShapeDtypeStruct((SEQS, heads, length, length), BF16),
        ],
        compiler_params=pltpu.CompilerParams(vmem_limit_bytes=60 * 1024 * 1024),
        cost_estimate=LARGE_COST,
        name="attention_forward",
    )(by_sequence[:, :, None], by_sequence[:, None, :], qkv_rows, qkv_rows)


def attention_backward(qkv_rows, grad_context, probs):
    count, _, run, width = qkv_rows.shape
    wide = width // 3
    heads = wide // HD
    length = count * run
    block = min(length, 512)
    slots = block // run
    steps = length // block
    return pl.pallas_call(
        functools.partial(backward_kernel, wide=wide),
        grid=(SEQS, steps),
        in_specs=[
            pl.BlockSpec((slots, 1, run, width), lambda s, i: (i, s, 0, 0)),
            pl.BlockSpec((count, 1, run, width), lambda s, i: (0, s, 0, 0)),
            pl.BlockSpec((slots, 1, run, wide), lambda s, i: (i, s, 0, 0)),
            pl.BlockSpec((1, heads, block, length), lambda s, i: (s, 0, i, 0)),
        ],
        out_specs=pl.BlockSpec((count, 1, run, width), lambda s, i: (0, s, 0, 0)),
        out_shape=jax.ShapeDtypeStruct((count, SEQS, run, width), BF16),
        scratch_shapes=[pltpu.VMEM((length, wide), F32), pltpu.VMEM((length, wide), F32)],
        compiler_params=pltpu.CompilerParams(vmem_limit_bytes=60 * 1024 * 1024),
        cost_estimate=SMALL_COST,
        name="attention_backward",
    )(qkv_rows, qkv_rows, grad_context, probs)


def in_order(side, own, other, axis=0):
    first = jnp.where(side == 0, own, other)
    second = jnp.where(side == 0, other, own)
    return jnp.concatenate([first, second], axis=axis)


def normalize(values):
    centred = values - jnp.mean(values, axis=1, keepdims=True)
    spread = lax.rsqrt(jnp.mean(centred * centred, axis=1, keepdims=True) + NORM_EPS)
    return centred * spread, spread


def normalize_back(normal, spread, gain, grad):
    scaled = grad * gain
    along = jnp.mean(scaled * normal, axis=1, keepdims=True)
    return spread * (scaled - jnp.mean(scaled, axis=1, keepdims=True) - normal * along)


def first_rows(pieces, scalars, weight, small, bias):
    rows, width = pieces[0][0].shape
    steps = len(pieces)
    total = 2 * steps * rows
    columns = weight.shape[1]

    def kernel(marks, *refs):
        given, (w, small_ref, b), outs = refs[: 2 * steps], refs[2 * steps : -3], refs[-3:]
        for t in range(steps):

            @pl.when(pl.program_id(0) == t)
            def _(t=t):
                outs[0][...] = in_order(marks[0], given[2 * t][...], given[2 * t + 1][...])

        normal, _ = normalize(outs[0][...].astype(F32))
        outs[1][...] = normal.astype(BF16)
        scaled = (normal * small_ref[8:9] + small_ref[9:10]).astype(BF16)
        outs[2][...] = (dot(scaled, w[...]) + b[...]).astype(BF16)

    def block(width):
        return pl.BlockSpec((2 * rows, width), lambda t, marks: (marks[1 + t], 0))

    flat = [piece for pair in pieces for piece in pair]
    return call(
        kernel,
        [struct((total, width), BF16), struct((total, width), BF16), struct((total, columns), BF16)],
        [block(width), block(width), block(columns)],
        grid=(steps,),
        in_blocks=[whole((rows, width))] * (2 * steps)
        + [whole(weight.shape), whole(small.shape), whole((1, columns))],
        scalars=scalars,
        name="first_rows",
    )(*flat, weight, small, bias)


def second_rows(tokens_all, pieces, scalars, weight, small):
    total, width = tokens_all.shape
    steps = len(pieces)
    wide = pieces[0][0].shape[1]
    own_rows = total // (2 * steps)
    rows = 2 * own_rows
    inside = rows // own_rows

    def kernel(marks, tokens, *refs):
        given = refs[: 2 * steps]
        w, small_ref, normed, own, context = refs[2 * steps :]
        for t in range(steps):
            pair = in_order(marks[0], given[2 * t][...], given[2 * t + 1][...], axis=1)
            begin = pl.multiple_of(marks[1 + t] * (2 * wide), 2 * wide)
            context[:, pl.ds(begin, 2 * wide)] = pair
        residual = tokens[...].astype(F32) + dot(context[...], w[...]) + small_ref[2:3]
        normal, _ = normalize(residual)
        normed[...] = (normal * small_ref[10:11] + small_ref[11:12]).astype(BF16)
        mine = marks[1] * 2 + marks[0]
        for i in range(inside):

            @pl.when(pl.program_id(0) * inside + i == mine)
            def _(i=i):
                own[...] = residual[i * own_rows : (i + 1) * own_rows]

    return pl.pallas_call(
        kernel,
        grid_spec=pltpu.PrefetchScalarGridSpec(
            num_scalar_prefetch=1,
            grid=(total // rows,),
            in_specs=[pl.BlockSpec((rows, width), lambda i, marks: (i, 0))]
            + [pl.BlockSpec((rows, wide), lambda i, marks: (i, 0))] * (2 * steps)
            + [whole(weight.shape), whole(small.shape)],
            out_specs=[
                pl.BlockSpec((rows, width), lambda i, marks: (i, 0)),
                whole((own_rows, width)),
            ],
            scratch_shapes=[pltpu.VMEM((rows, 2 * steps * wide), BF16)],
        ),
        out_shape=[struct((total, width), BF16), struct((own_rows, width), F32)],
        compiler_params=pltpu.CompilerParams(vmem_limit_bytes=60 * 1024 * 1024),
        cost_estimate=SMALL_COST,
        name="second_rows",
    )(scalars, tokens_all, *[piece for pair in pieces for piece in pair], weight, small)


def hidden_rows(normed, pairs, scalars, w_fc, w_proj, bias, kept, taken, rows):
    total, width = normed.shape
    hidden = w_fc.shape[1]
    many = len(taken)

    def kernel(marks, block, *refs):
        given, (fc, proj, b) = refs[: 2 * many], refs[2 * many : 2 * many + 3]
        act_ref, grad_ref, cot_ref = refs[-3 - 2 * many : -2 * many]
        parts = refs[-2 * many :]
        for i in range(many):

            @pl.when(pl.program_id(0) == i)
            def _(i=i):
                cot_ref[...] = in_order(marks[0], given[2 * i][...], given[2 * i + 1][...])

        z = dot(block[...], fc[...]) + b[...]
        square = z * z
        tanh = jnp.tanh(0.7978845608028654 * (z + 0.044715 * (square * z)))
        half = 0.5 * (1.0 + tanh)
        slope = half + 0.5 * z * (1.0 - tanh * tanh) * (
            0.7978845608028654 + (0.7978845608028654 * 3.0 * 0.044715) * square
        )
        act_ref[...] = (z * half).astype(BF16)
        grad = (dot(cot_ref[...], proj[...]) * slope).astype(BF16)
        grad_ref[...] = grad
        part = dot_nt(grad, fc[...])
        mine = jnp.where(marks[0] == 0, part[:rows], part[rows:])
        other = jnp.where(marks[0] == 0, part[rows:], part[:rows]).astype(BF16)
        for i in range(many):

            @pl.when(pl.program_id(0) == i)
            def _(i=i):
                parts[2 * i][...] = mine
                parts[2 * i + 1][...] = other

    def block(width):
        return pl.BlockSpec((2 * rows, width), lambda i, marks: (marks[1 + i], 0))

    operands = [normed] + [piece for pair in pairs for piece in pair] + [w_fc, w_proj, bias]
    blocks = [block(width)] + [whole((rows, width))] * (2 * many)
    blocks += [whole(w_fc.shape), whole(w_proj.shape), whole((1, hidden))]
    alias = {}
    if kept is not None:
        alias = {1 + len(operands) + i: i for i in range(3)}
        operands += list(kept)
        blocks += [pl.BlockSpec(memory_space=pl.ANY)] * 3
    outs = call(
        kernel,
        [struct((total, hidden), BF16), struct((total, hidden), BF16), struct((total, width), BF16)]
        + [struct((rows, width), dtype) for _ in taken for dtype in (F32, BF16)],
        [block(hidden), block(hidden), block(width)] + [whole((rows, width))] * (2 * many),
        grid=(many,),
        in_blocks=blocks,
        scalars=scalars,
        alias=alias,
        name="hidden_rows",
    )(*operands)
    return outs[:3], {t: (outs[3 + 2 * i], outs[4 + 2 * i]) for i, t in enumerate(taken)}


def turned_product(left, right, name):
    total, width = left.shape
    columns = right.shape[1]
    tile = 256

    def kernel(left_ref, right_ref, out_ref):
        out_ref[...] = dot(left_ref[...].T, right_ref[...]).astype(BF16)

    return call(
        kernel,
        struct((width, columns), BF16),
        pl.BlockSpec((tile, columns), lambda i: (i, 0)),
        grid=(pl.cdiv(width, tile),),
        in_blocks=[pl.BlockSpec((total, tile), lambda i: (0, i)), whole(right.shape)],
        name=name,
    )(left, right)


def head_product(normal, grad, weight, small):
    total, width = normal.shape
    columns = grad.shape[1]
    tile = 256

    def kernel(left, right, w, small_ref, out, gain_sum, shift_sum, grad_sum):
        @pl.when(pl.program_id(0) == 0)
        def _():
            grad_sum[...] = jnp.sum(right[...].astype(F32), axis=0, keepdims=True)

        raw = dot(left[...].T, right[...])
        sums = grad_sum[...]
        low = w[...].astype(F32)
        gain_sum[...] = jnp.sum(raw * low, axis=1, keepdims=True)
        shift_sum[...] = jnp.sum(low * sums, axis=1, keepdims=True)
        turned = small_ref[8:16].T
        out[...] = (raw * turned[:, 0:1] + turned[:, 1:2] * sums).astype(BF16)

    column = pl.BlockSpec((tile, 1), lambda i: (i, 0))
    return call(
        kernel,
        [
            struct((width, columns), BF16),
            struct((width, 1), F32),
            struct((width, 1), F32),
            struct((1, columns), F32),
        ],
        [pl.BlockSpec((tile, columns), lambda i: (i, 0)), column, column, whole((1, columns))],
        grid=(pl.cdiv(width, tile),),
        in_blocks=[
            pl.BlockSpec((total, tile), lambda i: (0, i)),
            whole(grad.shape),
            pl.BlockSpec((tile, columns), lambda i: (i, 0)),
            pl.BlockSpec((small.shape[0], tile), lambda i: (0, i)),
        ],
        name="head_product",
    )(normal, grad, weight, small)


def ring_parts(left, right, scalars, taken, steps, name):
    total, inner = left.shape
    width = right.shape[0]
    rows = total // (2 * steps)

    def kernel(marks, left_ref, right_ref, *outs):
        for i, t in enumerate(taken):
            begin = pl.multiple_of(marks[1 + t] * (2 * rows), 2 * rows)
            part = dot_nt(left_ref[pl.ds(begin, 2 * rows)], right_ref[...])
            outs[2 * i][...] = jnp.where(marks[0] == 0, part[:rows], part[rows:])
            outs[2 * i + 1][...] = jnp.where(marks[0] == 0, part[rows:], part[:rows]).astype(BF16)

    outs = call(
        kernel,
        [struct((rows, width), dtype) for _ in taken for dtype in (F32, BF16)],
        [whole((rows, width))] * (2 * len(taken)),
        in_blocks=[whole(left.shape), whole(right.shape)],
        scalars=scalars,
        name=name,
    )(left, right)
    return {t: (outs[2 * i], outs[2 * i + 1]) for i, t in enumerate(taken)}


def second_back(residual, terms, cotangent, small, weight, count):
    rows, width = residual.shape
    wide = weight.shape[0] // count
    columns = width // count

    def kernel(
        res, mine, swapped, carried, cot, g, w, grad_ref, low_ref, sums_ref, out_ref, cut_ref
    ):
        @pl.when(pl.program_id(0) == 0)
        def _():
            grad = mine[...] + swapped[...].astype(F32) + carried[...].astype(F32)
            normal, spread = normalize(res[...])
            total = cot[...].astype(F32) + normalize_back(normal, spread, g[10:11], grad)
            grad_ref[...] = total
            low = total.astype(BF16)
            low_ref[...] = low
            sums_ref[0:1] = jnp.sum(grad * normal, axis=0, keepdims=True)
            sums_ref[1:2] = jnp.sum(grad, axis=0, keepdims=True)
            sums_ref[2:3] = jnp.sum(low.astype(F32), axis=0, keepdims=True)
            sums_ref[3:4] = jnp.sum(cot[...].astype(F32), axis=0, keepdims=True)

        out_ref[0] = dot_nt(low_ref[...], w[...]).astype(BF16)
        for j in range(count):

            @pl.when(pl.program_id(0) == j)
            def _(j=j):
                cut_ref[0] = low_ref[:, j * columns : (j + 1) * columns]

    row = whole((rows, width))
    return call(
        kernel,
        [
            struct((rows, width), F32),
            struct((rows, width), BF16),
            struct((4, width), F32),
            struct((count, rows, wide), BF16),
            struct((count, rows, columns), BF16),
        ],
        [
            row,
            row,
            whole((4, width)),
            pl.BlockSpec((1, rows, wide), lambda i: (i, 0, 0)),
            pl.BlockSpec((1, rows, columns), lambda i: (i, 0, 0)),
        ],
        grid=(count,),
        in_blocks=[row] * 5 + [whole(small.shape), pl.BlockSpec((wide, width), lambda i: (i, 0))],
        name="second_back",
    )(residual, *terms, cotangent, small, weight)


def first_back(tokens, terms, residual_grad, small):
    rows, width = tokens.shape

    def kernel(x, mine, swapped, carried, res, g, out_ref):
        grad = mine[...] + swapped[...].astype(F32) + carried[...].astype(F32)
        normal, spread = normalize(x[...].astype(F32))
        out_ref[...] = (res[...] + normalize_back(normal, spread, g[8:9], grad)).astype(BF16)

    row = whole((rows, width))
    return call(
        kernel,
        struct((rows, width), BF16),
        row,
        in_blocks=[row] * 5 + [whole(small.shape)],
        name="first_back",
    )(tokens, *terms, residual_grad, small)


def heads_rows(me, pieces, count, slots):
    rows, width = pieces[0].shape
    unit = math.gcd(rows, HD)

    def kernel(mark, *refs):
        out = refs[4]
        for h in range(HEADS, count * slots):
            place = ((h % count) * slots + h // count) * HD
            out[place : place + HD] = jnp.zeros((HD, width), BF16)
        for r in range(4):
            for piece in range(rows // unit):
                row = (mark[0] ^ r) * rows + piece * unit
                head = row // HD
                target = ((head % count) * slots + head // count) * HD + row % HD
                out[pl.ds(pl.multiple_of(target, unit), unit)] = refs[r][
                    piece * unit : (piece + 1) * unit
                ]

    return call(
        kernel,
        struct((count * slots * HD, width), BF16),
        whole((count * slots * HD, width)),
        in_blocks=[whole((rows, width))] * 4,
        scalars=me[None],
        name="heads_rows",
    )(*pieces)


def out_product(pieces, columns, scalars, count, slots):
    total, width = columns.shape
    wide = slots * HD
    steps = len(pieces)

    def kernel(marks, *refs):
        given, right, out = refs[: 2 * steps], refs[2 * steps], refs[-1]
        for t in range(steps):
            for b in range(2):
                owner = marks[1 + t] * 2 + (marks[0] if b == 0 else 1 - marks[0])
                value = dot_tn(given[2 * t + b][...], right[...]).astype(BF16)
                for slot in range(slots):
                    head = slot * count + owner

                    def store(slot=slot, head=head, value=value):
                        begin = pl.multiple_of(head * HD, HD)
                        out[pl.ds(begin, HD)] = value[slot * HD : (slot + 1) * HD]

                    if (slot + 1) * count <= HEADS:
                        store()
                    else:
                        pl.when(head < HEADS)(store)

    return call(
        kernel,
        struct((HEADS * HD, width), BF16),
        whole((HEADS * HD, width)),
        in_blocks=[whole((total, wide))] * (2 * steps) + [whole(columns.shape)],
        scalars=scalars,
        name="out_product",
    )(*[piece for pair in pieces for piece in pair], columns)


def rows_product(left, right, name):
    total, inner = left.shape
    width = right.shape[0]
    block = min(total, 512)

    def kernel(left_ref, right_ref, out_ref):
        out_ref[...] = dot_nt(left_ref[...], right_ref[...]).astype(BF16)

    return call(
        kernel,
        struct((total, width), BF16),
        pl.BlockSpec((block, width), lambda i: (i, 0)),
        grid=(total // block,),
        in_blocks=[pl.BlockSpec((block, inner), lambda i: (i, 0)), whole(right.shape)],
        name=name,
    )(left, right)


def shards(
    tokens,
    cotangent,
    positions,
    qkv_weight,
    qkv_first,
    qkv_second,
    out_weight,
    out_first,
    out_second,
    fc_weight,
    fc_first,
    fc_second,
    proj_weight,
    proj_first,
    proj_second,
    small_weight,
    small_first,
    small_second,
):
    count = lax.axis_size("seq")
    ring = Ring(count)
    square = Square()
    me = lax.axis_index("seq")
    rows, width = tokens.shape
    seq_rows = rows // SEQS
    window = qkv_weight.shape[1]
    slots = -(-HEADS // count)
    wide = slots * HD
    small_count, small_width = small_weight.shape
    hidden = fc_weight.shape[1]
    all_rows = count * rows
    steps = ring.steps
    marks = jnp.stack([ring.side] + [ring.position(t) for t in range(steps)])
    tokens = by_rows(tokens)
    cotangent = by_rows(cotangent)

    token_tour = Tour(ring, tokens)
    token_tour.step()
    token_tour.step()
    pack, unpack, most = head_tables(count, width, window)
    pack_hot = one_hot(pick_row(pack, me), window)
    packed = jnp.einsum(
        "rc,cdl->drl",
        qkv_weight.astype(BF16),
        pack_hot.reshape(window, count, most),
        preferred_element_type=BF16,
    )
    depth = packed.shape[1]
    small_flat = jnp.concatenate(
        [
            small_weight.reshape(-1).astype(BF16),
            (positions // 32).astype(BF16),
            (positions % 32).astype(BF16),
        ]
    )
    small_depth = -(-small_flat.shape[0] // most)
    small_depth += -small_depth % 16
    small_flat = jnp.pad(small_flat, (0, small_depth * most - small_flat.shape[0]))
    small_pack = jnp.broadcast_to(
        small_flat.reshape(1, small_depth, most), (count, small_depth, most)
    )
    received = lax.all_to_all(jnp.concatenate([packed, small_pack], axis=1), "seq", 0, 0)
    token_tour.step()
    received = after(received, token_tour.moved[1], token_tour.current)

    unpack_hot = one_hot(pick_row(unpack, me), 3 * wide)
    head_part = jnp.einsum(
        "srl,ksl->rk",
        received[:, :depth],
        unpack_hot.reshape(3 * wide, count, most),
        preferred_element_type=BF16,
    )
    for t in range(3, steps):
        token_tour.step()
    head_pieces = square.gather(head_part, token_tour.current)
    w_head = square.place(head_pieces)

    small_all = received[:, depth:].reshape(count, small_depth * most).astype(F32)
    small_rows = small_all[:, : small_count * small_width].reshape(count, small_count, small_width)
    small_rows = small_rows.transpose(1, 0, 2).reshape(small_count, width)
    small_rows = jnp.pad(small_rows, ((0, 4), (0, 0)))
    pos_all = small_all[:, small_count * small_width :][:, : 2 * rows].reshape(count, 2, rows)
    pos_all = (pos_all[:, 0] * 32.0 + pos_all[:, 1]).astype(jnp.int32)

    def own_heads(row):
        padded = jnp.pad(row, (0, slots * count * HD - width)).reshape(slots, count, HD)
        return lax.dynamic_index_in_dim(padded, me, 1, keepdims=False).reshape(wide)

    head_bias = jnp.concatenate(
        [own_heads(small_rows[0]), jnp.zeros((wide,), F32), own_heads(small_rows[1])]
    )
    fc_bias = lax.dynamic_slice_in_dim(small_rows[3:7].reshape(-1), me * hidden, hidden, 0)

    ready = (w_head, token_tour.moved[-1])
    tokens_all, normal_all, qkv_rows = first_rows(
        token_tour.pieces, marks, w_head, small_rows, head_bias[None]
    )
    qkv_all = qkv_rows.reshape(count, SEQS, seq_rows, 3 * wide)
    context, probs = attention_forward(qkv_all, pos_all)
    context = context.reshape(all_rows, wide)

    cot_zero = lax.ppermute(after(cotangent, *ready), "seq", ring.swap)
    cot_moving = lax.ppermute(after(cotangent, *ready), "seq", ring.behind)
    out_part = lax.all_gather(out_weight.astype(BF16), "seq", axis=1, tiled=True)
    fc_low = after(fc_weight, *ready).astype(BF16)
    context = after(context, cot_zero, cot_moving)
    out_part = by_rows(after(out_part, context))
    out_near, out_far = square.near_of(out_part), square.far_of(out_part)
    fc_near, fc_far = square.near_of(fc_low), square.far_of(fc_low)
    proj_low = after(proj_weight, context).T.astype(BF16)
    proj_near, proj_far = square.near_of(proj_low), square.far_of(proj_low)
    context_tour = Tour(ring, context)
    context_tour.step()
    context_tour.step(land=(out_part, fc_far, proj_far))
    fc_pieces = (fc_low, fc_near, fc_far, square.near_of(after(fc_far, context_tour.current)))
    proj_pieces = (proj_low, proj_near, proj_far, square.near_of(after(proj_far, context_tour.current)))
    w_fc, w_proj = square.place(fc_pieces), square.place(proj_pieces)
    context_tour.step(land=(w_fc, w_proj))
    for t in range(3, steps):
        context_tour.step(land=(out_far,) if t == 3 else ())
    out_pieces = (out_part, out_near, out_far, square.near_of(after(out_far, context_tour.current)))
    w_out = heads_rows(square.me, out_pieces, count, slots)
    normed_all, residual = second_rows(
        tokens_all, context_tour.pieces, marks, w_out, small_rows
    )
    cot_moving = [cot_moving]
    for t in range(2, steps):
        begin = context_tour.current if t == 2 else w_out
        moving = lax.ppermute(after(cot_moving[-1], begin), "seq", ring.behind)
        cot_moving.append(after(moving, w_out if t == 2 else residual))
    cot_pieces = {0: (cotangent, cot_zero)}
    crossing = after(context_tour.moved[-1], w_out)
    for t in range(1, steps):
        crossed = lax.ppermute(after(cot_moving[t - 1], crossing), "seq", ring.swap)
        cot_pieces[steps - t] = (cot_moving[t - 1], after(crossed, residual))

    def feed_forward(kept, taken, *begin):
        chosen = jnp.stack([ring.side] + [ring.position(t) for t in taken])
        return hidden_rows(
            normed_all,
            [cot_pieces[t] for t in taken],
            after(chosen, *begin) if begin else chosen,
            w_fc,
            w_proj,
            fc_bias[None],
            kept,
            taken,
            rows,
        )

    kept, parts = feed_forward(None, [steps - 1])
    grad_fold = Fold(ring, parts)
    kept, more = feed_forward(kept, [steps - 2])
    parts.update(more)
    grad_fold.beside(*parts[steps - 2])
    grad_fold.step()
    kept, more = feed_forward(kept, [0], grad_fold.carried)
    parts.update(more)
    kept, more = feed_forward(kept, list(reversed(range(1, steps - 2))), *parts[0])
    parts.update(more)
    grad_fold.beside(*parts[1])
    hidden_low, grad_pre_low, cot_all = kept
    grad_fold.step()
    output_partial = rows_product(after(hidden_low, grad_fold.carried), w_proj, "output_product")
    grad_fold.beside(output_partial)
    for _ in range(3, steps):
        grad_fold.step()
    fc_sum = turned_product(after(normed_all, grad_fold.carried), grad_pre_low, "fc_product")
    grad_fold.beside(fc_sum)
    output_sum = lax.psum_scatter(output_partial, "seq", scatter_dimension=0, tiled=True)
    terms = grad_fold.terms
    grad_residual, _, row_sums, grad_sent, attn_cut = second_back(
        residual, terms, cotangent, small_rows, w_out, count
    )
    grad_bias_fc = jnp.sum(after(grad_pre_low, grad_sent).astype(F32), axis=0)
    fc_column = square.half_sum(after(fc_sum, grad_sent))

    proj_sum = turned_product(after(cot_all, grad_sent), hidden_low, "proj_product")
    grad_context = after(
        lax.all_to_all(grad_sent, "seq", 0, 0),
        proj_sum,
        grad_bias_fc,
    )
    proj_column = square.half_sum(proj_sum)
    attn_columns = lax.all_to_all(after(attn_cut, grad_context), "seq", 0, 0)
    grad_qkv = attention_backward(
        qkv_all, grad_context.reshape(count, SEQS, seq_rows, wide), probs
    ).reshape(all_rows, 3 * wide)
    fc_grad = after(square.other_sum(fc_column), grad_qkv)
    proj_grad = square.other_sum(after(proj_column, grad_qkv))
    attn_columns = after(attn_columns, grad_qkv)
    parts = ring_parts(grad_qkv, w_head, marks, [steps - 1], steps, "first_parts")
    input_fold = Fold(ring, parts)
    parts.update(
        ring_parts(
            after(grad_qkv, *parts[steps - 1]), w_head, marks, range(steps - 1), steps, "input_parts"
        )
    )
    input_fold.beside(*parts[0])
    input_fold.step()
    head_sum, grad_gain_one, grad_shift_one, grad_qkv_sum = head_product(
        after(normal_all, input_fold.carried),
        grad_qkv,
        w_head,
        small_rows,
    )
    input_fold.beside(head_sum)
    input_fold.step()
    head_column = square.half_sum(after(head_sum, input_fold.carried))
    out_columns = out_weight.shape[1]
    attn_columns = after(attn_columns, input_fold.carried).reshape(all_rows, out_columns)
    input_fold.beside(head_column)
    for _ in range(3, steps):
        input_fold.step()
    small_begin = input_fold.carried
    head_far = square.other_sum(after(head_column, input_fold.carried))
    out_sum = out_product(
        context_tour.pieces, after(attn_columns, input_fold.carried), marks, count, slots
    )
    input_fold.beside(output_sum, out_sum)
    head_grad = after(head_far, *input_fold.terms).astype(BF16)
    unpack_back = unpack_hot.reshape(3 * wide, count, most)
    head_packed = jnp.einsum("rk,ksl->srl", head_grad, unpack_back, preferred_element_type=BF16)
    last_terms = after(tuple(input_fold.terms), head_packed)
    input_grad = first_back(tokens, last_terms, grad_residual, small_rows)
    out_column = square.half_sum(after(out_sum, head_packed))
    out_grad = square.other_sum(out_column)
    fc_new = adam_update(
        fc_weight, fc_first, fc_second, after(fc_grad, head_packed), 0.02, 0.1
    )
    head_back = lax.all_to_all(head_packed, "seq", 0, 0)
    output = (residual + output_sum.astype(F32) + small_rows[7]).astype(BF16)

    def place_heads(values):
        spread = (jnp.arange(count) == me).astype(F32)[None, :, None]
        placed = values.reshape(slots, 1, HD) * spread
        return placed.reshape(-1)[:width]

    grad_bias_fc = grad_bias_fc[None, :] * (jnp.arange(count) == me).astype(F32)[:, None]
    grad_qkv_sum = after(grad_qkv_sum, small_begin)[0]
    grad_small = jnp.concatenate(
        [
            place_heads(grad_qkv_sum[:wide])[None],
            place_heads(grad_qkv_sum[2 * wide :])[None],
            row_sums[2:3],
            grad_bias_fc.reshape(-1, width),
            row_sums[3:4],
            grad_gain_one[:, 0][None],
            grad_shift_one[:, 0][None],
            row_sums[0:1],
            row_sums[1:2],
        ],
        axis=0,
    )
    small_sent = grad_small.astype(BF16).reshape(small_count, count, small_width)
    small_part = jnp.sum(
        lax.all_to_all(small_sent.transpose(1, 0, 2), "seq", 0, 0).astype(F32), axis=0
    )
    small_grad = square.sum(after(small_part, head_packed))

    out_new = adam_update(out_weight, out_first, out_second, out_grad, 0.3, 0.1)
    proj_new = adam_update(
        proj_weight.T, proj_first.T, proj_second.T, proj_grad, 0.02, 0.1
    )
    proj_new = [value.T for value in proj_new]
    small_new = adam_update(small_weight, small_first, small_second, small_grad, 0.3, 0.0)
    head_back = after(head_back, fc_new[0], out_new[0], small_new[0])
    qkv_grad = jnp.einsum(
        "drl,cdl->rc",
        head_back,
        pack_hot.reshape(window, count, most),
        preferred_element_type=F32,
    )
    qkv_new = adam_update(qkv_weight, qkv_first, qkv_second, qkv_grad, 0.02, 0.1)
    return (
        output,
        input_grad,
        *qkv_new,
        *out_new,
        *fc_new,
        *proj_new,
        *small_new,
        small_grad[7],
    )


def solution(mesh):
    rows = P(("dp", "seq"), None)
    matrix = P("dp", "seq")
    turned = P("seq", "dp")
    small = P(None, "seq")
    in_specs = (
        (rows, rows, P(("dp", "seq"))) + (matrix,) * 9 + (turned,) * 3 + (small,) * 3
    )
    out_specs = (rows, rows) + (matrix,) * 9 + (turned,) * 3 + (small,) * 3 + (P("seq"),)
    return jax.shard_map(shards, mesh=mesh, in_specs=in_specs, out_specs=out_specs, check_vma=False)
```
